32 devices in a mesh: dp: 16 (over z, y, x), seq: 2 (over core).
Axes of the slice: x: 2, y: 2, z: 4, core: 2. Of those that a mesh axis runs over, the one named last changes fastest.
Arguments:
- frames: bfloat16 [2, 4096, 768], P(None, ('dp', 'seq')), may hold values from -6 to 6
- clip_lengths: int32 [2, 16, 3], P(None, 'dp'), may hold values from 1 to 192, 256 in all within a row
- conv_weight: bfloat16 [128, 48, 768], P(None, None, 'dp'), may hold values from -0.078125 to 0.078125
- front_gain: bfloat16 [768], P('dp'), may hold values from 0.25 to 1.75
- qkv_weight: bfloat16 [768, 2304], P('dp'), may hold values from -0.3125 to 0.3125
- out_weight: bfloat16 [768, 768], P('dp'), may hold values from -0.875 to 0.875
- middle_gain: bfloat16 [768], P('dp'), may hold values from 0.25 to 1.75
- up_weight: bfloat16 [768, 3072], P('dp'), may hold values from -0.21875 to 0.21875
- down_weight: bfloat16 [3072, 768], P('dp'), may hold values from -0.109375 to 0.109375
- final_gain: bfloat16 [768], P('dp'), may hold values from 0.25 to 1.75
- cotangent: bfloat16 [2, 4096, 768], P(None, ('dp', 'seq')), may hold values from -6 to 6
Outputs:
- output: bfloat16 [2, 4096, 768], P(None, ('dp', 'seq'))
- frames_grad: float32 [2, 4096, 768], P(None, ('dp', 'seq'))
- conv_weight_grad: float32 [128, 48, 768], P(None, None, 'dp')
- front_gain_grad: float32 [768], P('dp')
- qkv_weight_grad: float32 [768, 2304], P('dp')
- out_weight_grad: float32 [768, 768], P('dp')
- middle_gain_grad: float32 [768], P('dp')
- up_weight_grad: float32 [768, 3072], P('dp')
- down_weight_grad: float32 [3072, 768], P('dp')
- final_gain_grad: float32 [768], P('dp')
The draws below stay inside these ranges and needn't reach their ends.
Inputs may be any that keep to these rules, and one draw needn't show every extreme that they name: `clip_lengths`: the 3 lengths of each pack sum to 256; the longest clip of every pack has exactly 192 frames.
All inputs are finite; a program needn't handle non-finite values.
Results may differ from the reference program's by a relative error of at most 0.019.
Values may be sent and summed in bfloat16 or wider, within the bound.
A program may use at most 176 MiB of HBM per device.

```python
import math
import jax
import jax.numpy as jnp
import numpy as np
from jax import lax

HEADS = 12
HEAD_DIM = 64
D = 768
FF = 3072
GROUPS = 16
CG = 48
KERNEL = 128
MICRO = 2
CLIPS = 3
PACK = 256
LONG = 192
PACKS = 16
FRAMES = 4096


def with_spikes(values, key, source, target, parts, factor):
    owner, partner = [(jnp.arange(values.shape[dim]) // (values.shape[dim] // parts)).reshape([-1 if axis == dim else 1 for axis in range(values.ndim)]) for dim in (source, target)]
    chosen = jax.random.permutation(key, parts)[partner]
    strong = (owner == chosen) | (owner == (partner + parts // 2) % parts)
    return jnp.where(strong, factor * values, values)


def block_scale(rng, shape, split, low, top_value):
    def one(dim, blocks):
        heights = jax.random.uniform(jax.random.fold_in(jax.random.fold_in(rng, 6), dim), (blocks,), jnp.float32, low / len(split), top_value / len(split))
        return jnp.repeat(jnp.exp(heights), shape[dim] // blocks).reshape((-1,) + (1,) * (len(shape) - dim - 1))

    factor_of = one(*split[0])
    for cut in split[1:]:
        factor_of = factor_of * one(*cut)
    return factor_of


def split_up(amount, total, reach, lean):
    weights = [(1 << 20) // math.isqrt(grade ** lean) + 1 for grade in range(2, amount + 1)]
    rest, given = total - reach - (amount - 1), [1] * (amount - 1)
    while rest > 0:
        movable = [i for i in range(amount - 1) if given[i] < reach]
        pool, budget = sum([weights[i] for i in movable]), rest
        for i in movable:
            extra = min(reach - given[i], max(1, budget * weights[i] // pool), rest)
            given[i] = given[i] + extra
            rest = rest - extra
    return np.array([reach] + given)


def ragged_sizes(rng, count, total, most, lean):
    if count == 2:
        one = jax.random.randint(rng, (), max(1, total - most), min(most, total - 1) + 1)
        return jnp.stack([one, total - one])
    tallies = jnp.asarray(split_up(count, total, most, lean), jnp.int32)
    twos = (count - 1) // 2
    donor, taker = tallies[1:1 + 2 * twos:2], tallies[2:2 + 2 * twos:2]
    margin = jnp.minimum(donor - 1, most - taker)
    passed = jax.random.randint(jax.random.fold_in(rng, 1), (twos,), 0, 1 << 20) % (margin + 1)
    tallies = tallies.at[1:1 + 2 * twos:2].set(donor - passed).at[2:2 + 2 * twos:2].set(taker + passed)
    return tallies[jax.random.permutation(jax.random.fold_in(rng, 2), count)]


def normal_values(rng, extent, width, most, pieces=(), kind=jnp.bfloat16):
    factor_of = block_scale(rng, extent, pieces, -0.22, 0.18) if pieces else 1.0
    values = jax.random.normal(rng, extent, jnp.float32) * width * factor_of
    return jnp.minimum(jnp.maximum(values, -most), most).astype(kind)


def heavy_noise(rng, dims, spread, limit, split, heavy, kind=jnp.bfloat16):
    values = spread * jax.random.normal(rng, dims, jnp.float32)
    if split:
        values = values * block_scale(rng, dims, split, -0.22, 0.18)
    return jnp.clip(with_spikes(values, jax.random.fold_in(rng, 3), *heavy), -limit, limit).astype(kind)


def setup_inputs(seed: int = 0) -> dict:
    key_list = jax.random.split(jax.random.key(seed), 12)
    frames = normal_values(key_list[0], (MICRO, FRAMES, D), 1.0, 6.0, ((1, 32),))
    clip_lengths = jax.vmap(lambda own: ragged_sizes(own, CLIPS, PACK, LONG, 2))(jax.random.split(key_list[1], MICRO * PACKS)).reshape((MICRO, PACKS, CLIPS)).astype(jnp.int32)
    conv_weight = normal_values(key_list[2], (KERNEL, CG, D), (KERNEL * CG) ** -0.5, 0.078125, ((2, 16),))
    front_gain = jnp.clip(1.0 + 0.15 * jax.random.normal(key_list[3], (D,), jnp.float32), 0.25, 1.75).astype(jnp.bfloat16)
    qkv_weight = normal_values(key_list[4], (D, 3 * D), (D // 2) ** -0.5, 0.3125, ((0, 16),))
    out_weight = normal_values(key_list[5], (D, D), (D // 16) ** -0.5, 0.875, ((0, 16),))
    middle_gain = jnp.clip(1.0 + 0.15 * jax.random.normal(key_list[6], (D,), jnp.float32), 0.25, 1.75).astype(jnp.bfloat16)
    up_weight = normal_values(key_list[7], (D, FF), D ** -0.5, 0.21875, ((0, 16),))
    down_weight = normal_values(key_list[8], (FF, D), FF ** -0.5, 0.109375, ((0, 16),))
    final_gain = jnp.clip(1.0 + 0.15 * jax.random.normal(key_list[9], (D,), jnp.float32), 0.25, 1.75).astype(jnp.bfloat16)
    cotangent = heavy_noise(key_list[10], (MICRO, FRAMES, D), 1.0, 6.0, ((1, 32),), (1, 2, 32, 2.75))
    return dict(frames=frames, clip_lengths=clip_lengths, conv_weight=conv_weight, front_gain=front_gain, qkv_weight=qkv_weight, out_weight=out_weight, middle_gain=middle_gain, up_weight=up_weight, down_weight=down_weight, final_gain=final_gain, cotangent=cotangent)


@jax.custom_vjp
def low(v):
    return lax.optimization_barrier(v.astype(jnp.bfloat16)).astype(jnp.float32)

@jax.custom_vjp
def low_back(v):
    return v

def low_keep(v):
    return (low(v), None)

def low_pass(kept, grad):
    return (grad,)

def back_keep(v):
    return (v, None)

def back_low(kept, grad):
    return (low(grad),)
low.defvjp(low_keep, low_pass)
low_back.defvjp(back_keep, back_low)
epsilon = 1e-05
highest = lax.Precision.HIGHEST

def layer_norm(values, gain_vector):
    centered = values - lax.optimization_barrier(jnp.mean(values, axis=-1, keepdims=True))
    variance = lax.optimization_barrier(jnp.mean(centered * centered, axis=-1, keepdims=True))
    return centered * lax.rsqrt(variance + epsilon) * gain_vector

def segment_numbers(lengths):
    ends = jnp.cumsum(lengths.astype(jnp.int32))
    position = jnp.arange(PACK, dtype=jnp.int32)
    return lax.optimization_barrier(jnp.sum((position[:, None] >= ends[None, :]).astype(jnp.int32), axis=1))

def layer(frames_pack, segments, conv_weight, front_gain, qkv_weight, out_weight, middle_gain, up_weight, down_weight, final_gain):
    padded = jnp.pad(frames_pack, ((KERNEL // 2, KERNEL // 2), (0, 0)))
    convolved = lax.conv_general_dilated(padded[None], conv_weight, (1,), 'VALID', dimension_numbers=('NWC', 'WIO', 'NWC'), feature_group_count=GROUPS, precision=highest)[0, :PACK]
    convolved = low_back(convolved)
    mixed = frames_pack + jax.nn.gelu(convolved, approximate=False)
    normed = layer_norm(mixed, front_gain)
    projected = low(low_back(jnp.dot(low(normed), qkv_weight, precision=highest)))
    heads_shape = (PACK, HEADS, HEAD_DIM)
    queries = projected[:, :D].reshape(heads_shape)
    key_heads = projected[:, D:2 * D].reshape(heads_shape)
    value_heads = projected[:, 2 * D:].reshape(heads_shape)
    scores = low_back(jnp.einsum('qhd,khd->hqk', queries, key_heads, precision=highest) * HEAD_DIM ** (-0.5))
    same_clip = segments[:, None] == segments[None, :]
    scores = jnp.where(same_clip[None], scores, -1e+30)
    row_max = lax.optimization_barrier(jnp.max(scores, axis=-1, keepdims=True))
    shifted = jnp.exp(scores - row_max)
    softmax_probs = shifted / lax.optimization_barrier(jnp.sum(shifted, axis=-1, keepdims=True))
    attended = jnp.einsum('hqk,khd->qhd', low(softmax_probs), value_heads, precision=highest).reshape(PACK, D)
    attended = low(low_back(attended))
    branch = low_back(jnp.dot(attended, out_weight, precision=highest))
    middle = layer_norm(normed + branch, middle_gain)
    hidden = low_back(jnp.dot(low(middle), up_weight, precision=highest))
    activated = low(jax.nn.gelu(hidden, approximate=False))
    feed = low_back(jnp.dot(activated, down_weight, precision=highest))
    return layer_norm(middle + feed, final_gain)

def reference(frames, clip_lengths, conv_weight, front_gain, qkv_weight, out_weight, middle_gain, up_weight, down_weight, final_gain, cotangent):
    params = tuple((item.astype(jnp.float32) for item in (conv_weight, front_gain, qkv_weight, out_weight, middle_gain, up_weight, down_weight, final_gain)))
    frames_all = frames.astype(jnp.float32).reshape(MICRO * PACKS, PACK, D)
    cotangent_all = cotangent.astype(jnp.float32).reshape(MICRO * PACKS, PACK, D)
    lengths_all = clip_lengths.reshape(MICRO * PACKS, CLIPS)

    def one_pack(running, items):
        pack_frames, pack_lengths, pack_cotangent = items
        segments = segment_numbers(pack_lengths)

        def forward(pack_input, *weights):
            return layer(pack_input, segments, *weights)
        result, pullback = jax.vjp(forward, pack_frames, *params)
        gradients = pullback(pack_cotangent)
        running = tuple((total + part for total, part in zip(running, gradients[1:])))
        return (running, (result.astype(jnp.bfloat16), gradients[0]))
    zeros = tuple((jnp.zeros(item.shape, jnp.float32) for item in params))
    running, (outputs, frame_grads) = lax.scan(one_pack, zeros, (frames_all, lengths_all, cotangent_all))
    return (outputs.reshape(MICRO, FRAMES, D), frame_grads.reshape(MICRO, FRAMES, D), running[0], running[1], running[2], running[3], running[4], running[5], running[6], running[7])
```

```python
import functools

import jax
import jax.numpy as jnp
from jax import lax
from jax.experimental import pallas as pl
from jax.experimental.pallas import tpu as pltpu
from jax.sharding import PartitionSpec as P

MESH = pl.DeviceIdType.MESH


def dp_factors(size):
    return {16: (4, 2, 2), 128: (4, 4, 8)}.get(size, (size, 1, 1))


def offsets_of(dims):
    return [(i, j, k) for i in range(dims[0]) for j in range(dims[1]) for k in range(dims[2])]


def place(dims, order, position, offsets):
    coords = list(position)
    for axis, offset in zip(order, offsets):
        if offset:
            coords[axis] = lax.rem(coords[axis] + offset, dims[axis])
    return (coords[0] * dims[1] + coords[1]) * dims[2] + coords[2]


def position_of(dims):
    me = lax.axis_index("dp")
    return (me // (dims[1] * dims[2]), lax.rem(me // dims[2], dims[1]), lax.rem(me, dims[2]))


def greet(dims, position, core):
    barrier = pltpu.get_barrier_semaphore()
    count = 1
    pl.semaphore_signal(barrier, inc=1, device_id={"seq": 1 - core}, device_id_type=MESH)
    for axis in range(3):
        for offset in range(1, dims[axis]):
            other = place(dims, (axis,), position, (offset,))
            pl.semaphore_signal(barrier, inc=1, device_id={"dp": other}, device_id_type=MESH)
            count += 1
    pl.semaphore_wait(barrier, count)


ORDERS = ((0, 1, 2), (0, 2, 1))


def gather_kernel(dims, chunks, *refs):
    n_arr = len(refs[:-5]) // 2
    ins, outs = refs[:n_arr], refs[n_arr : 2 * n_arr]
    send_sems, recv_sems, push_send, push_recv, local_sems = refs[2 * n_arr :]
    position = position_of(dims)
    me = lax.axis_index("dp")
    core_index = lax.axis_index("seq")
    greet(dims, position, core_index)
    locals_ = []
    for i in range(n_arr):
        copy = pltpu.make_async_copy(ins[i], outs[i].at[me], local_sems.at[i])
        copy.start()
        locals_.append(copy)

    def run(core):
        order = ORDERS[core]
        sizes = [dims[axis] for axis in order]
        started = []
        counters = [0] * len(chunks)

        def part(which, chunk, side):
            array, rows, lanes = chunks[chunk][side]
            return outs[array].at[which, pl.ds(*rows), pl.ds(*lanes)]

        def own(chunk):
            array, rows, lanes = chunks[chunk][core]
            return ins[array].at[pl.ds(*rows), pl.ds(*lanes)]

        def send(chunk, offsets, level, distance):
            gid = place(dims, order, position, offsets)
            target = place(dims, (order[level],), position, (distance,))
            copy = pltpu.make_async_remote_copy(
                src_ref=own(chunk) if offsets == (0, 0, 0) else part(gid, chunk, core),
                dst_ref=part(gid, chunk, core),
                send_sem=send_sems.at[chunk, counters[chunk]],
                recv_sem=recv_sems.at[chunk, gid],
                device_id={"dp": target},
                device_id_type=MESH,
            )
            counters[chunk] += 1
            copy.start()
            started.append(copy)

        def arrive(chunk, offsets):
            gid = place(dims, order, position, offsets)
            ref = part(gid, chunk, core)
            pltpu.make_async_copy(ref, ref, recv_sems.at[chunk, gid]).wait()

        def push(chunk, offsets):
            gid = place(dims, order, position, offsets)
            ref = part(gid, chunk, core)
            copy = pltpu.make_async_remote_copy(
                src_ref=ref,
                dst_ref=ref,
                send_sem=push_send.at[chunk, gid],
                recv_sem=push_recv.at[chunk, gid],
                device_id={"seq": 1 - core},
                device_id_type=MESH,
            )
            copy.start()
            started.append(copy)

        def spread(chunk, offsets, first):
            for level in range(first, 3):
                for distance in range(1, sizes[level]):
                    send(chunk, offsets, level, distance)

        def stage(chunk, number):
            if number == 0:
                spread(chunk, (0, 0, 0), 0)
            if number == 1:
                for i in range(1, sizes[0]):
                    arrive(chunk, (i, 0, 0))
                    spread(chunk, (i, 0, 0), 1)
                    push(chunk, (i, 0, 0))
            if number == 2:
                for i in range(sizes[0]):
                    for j in range(1, sizes[1]):
                        arrive(chunk, (i, j, 0))
                        spread(chunk, (i, j, 0), 2)
                        push(chunk, (i, j, 0))
            if number == 3:
                for i in range(sizes[0]):
                    for j in range(sizes[1]):
                        for k in range(1, sizes[2]):
                            arrive(chunk, (i, j, k))
                            push(chunk, (i, j, k))

        count = len(chunks)
        for step in range(count + 3):
            for number in range(4):
                if 0 <= step - number < count:
                    stage(step - number, number)
        for chunk in range(count):
            for offsets in offsets_of(dims):
                if offsets != (0, 0, 0):
                    gid = place(dims, (0, 1, 2), position, offsets)
                    ref = part(gid, chunk, 1 - core)
                    pltpu.make_async_copy(ref, ref, push_recv.at[chunk, gid]).wait()
        for copy in started:
            copy.wait_send()

    for core in range(2):
        pl.when(core_index == core)(functools.partial(run, core))
    for copy in locals_:
        copy.wait()


def all_gather(arrays, chunks, dp, collective_id=0):
    dims = dp_factors(dp)
    n = len(chunks)
    any_ = pl.BlockSpec(memory_space=pl.ANY)
    return pl.pallas_call(
        functools.partial(gather_kernel, dims, chunks),
        out_shape=[jax.ShapeDtypeStruct((dp,) + a.shape, a.dtype) for a in arrays],
        in_specs=[any_] * len(arrays),
        out_specs=[any_] * len(arrays),
        scratch_shapes=[
            pltpu.SemaphoreType.DMA((n, dp)),
            pltpu.SemaphoreType.DMA((n, dp)),
            pltpu.SemaphoreType.DMA((n, dp)),
            pltpu.SemaphoreType.DMA((n, dp)),
            pltpu.SemaphoreType.DMA((len(arrays),)),
        ],
        compiler_params=pltpu.CompilerParams(collective_id=collective_id, has_side_effects=True),
    )(*arrays)


def scatter_kernel(dims, chunks, n_arr, *refs):
    ins, outs = refs[:n_arr], refs[n_arr : 2 * n_arr]
    scratch = list(refs[2 * n_arr :])
    n = len(chunks)
    stage_refs, pair_refs = scratch[:n], scratch[n : 2 * n]
    hop_refs = [scratch[(2 + level) * n : (3 + level) * n] for level in range(3)]
    (load_sems, pair_send, pair_recv, hop_send, hop_recv, last_send, last_recv) = scratch[5 * n :]
    position = position_of(dims)
    core_index = lax.axis_index("seq")
    greet(dims, position, core_index)

    def run(core):
        order = ORDERS[core]
        sizes = [dims[axis] for axis in order]
        started = []
        other_order = ORDERS[1 - core]
        other_sizes = [dims[axis] for axis in other_order]

        def part(array_refs, which, chunk, side):
            array, rows, lanes = chunks[chunk][side]
            return array_refs[array].at[which, pl.ds(*rows), pl.ds(*lanes)]

        def slot(level, offsets, distance):
            index = distance - 1
            for i in range(level):
                index = index * sizes[i] + offsets[i]
            return index

        def semaphore(level, index):
            return (1, sizes[0], sizes[0] * sizes[1])[level] + index - 1

        def begin(chunk):
            array = chunks[chunk][core][0]
            theirs = sorted(offsets_of(other_sizes), key=lambda o: (o[2] == 0, o[1] == 0, o[0] == 0))
            mine = sorted(offsets_of(sizes), key=lambda o: (o[2] == 0, o[1] == 0, o[0] == 0))
            for given, kept in zip(theirs, mine):
                gid = place(dims, other_order, position, given)
                copy = pltpu.make_async_remote_copy(
                    src_ref=part(ins, gid, chunk, 1 - core),
                    dst_ref=pair_refs[chunk].at[gid],
                    send_sem=pair_send.at[chunk],
                    recv_sem=pair_recv.at[chunk, gid],
                    device_id={"seq": 1 - core},
                    device_id_type=MESH,
                )
                copy.start()
                gid = place(dims, order, position, kept)
                pltpu.make_async_copy(
                    part(ins, gid, chunk, core), stage_refs[chunk].at[gid], load_sems.at[chunk, gid]
                ).start()

        def combine(chunk, offsets, target):
            gid = place(dims, order, position, offsets)
            own = stage_refs[chunk].at[gid]
            pair = pair_refs[chunk].at[gid]
            pltpu.make_async_copy(own, own, load_sems.at[chunk, gid]).wait()
            pltpu.make_async_copy(pair, pair, pair_recv.at[chunk, gid]).wait()
            terms = [own, pair]
            for level in (2, 1, 0):
                if offsets[level]:
                    break
                for distance in range(1, sizes[level]):
                    index = slot(level, offsets, distance)
                    ref = hop_refs[level][chunk].at[index]
                    pltpu.make_async_copy(ref, ref, hop_recv.at[chunk, semaphore(level, index)]).wait()
                    terms.append(ref)
            height = own.shape[0]

            tall = 16 if height % 16 == 0 else height

            @pl.loop(0, height // tall)
            def _(tile):
                rows = pl.ds(pl.multiple_of(tile * tall, tall), tall)
                total = terms[0][rows, :].astype(jnp.float32)
                for term in terms[1:]:
                    total = total + term[rows, :].astype(jnp.float32)
                if target is None:
                    own[rows, :] = total.astype(own.dtype)
                else:
                    target[rows, :] = total

            return gid

        def send(chunk, offsets):
            level = max(i for i in range(3) if offsets[i])
            gid = combine(chunk, offsets, None)
            index = slot(level, offsets, offsets[level])
            target = place(dims, (order[level],), position, (offsets[level],))
            copy = pltpu.make_async_remote_copy(
                src_ref=stage_refs[chunk].at[gid],
                dst_ref=hop_refs[level][chunk].at[index],
                send_sem=hop_send.at[chunk, semaphore(level, index)],
                recv_sem=hop_recv.at[chunk, semaphore(level, index)],
                device_id={"dp": target},
                device_id_type=MESH,
            )
            copy.start()
            started.append(copy)

        def final(chunk):
            array, rows, lanes = chunks[chunk][core]
            half = outs[array].at[pl.ds(*rows), pl.ds(*lanes)]
            combine(chunk, (0, 0, 0), half)
            copy = pltpu.make_async_remote_copy(
                src_ref=half,
                dst_ref=half,
                send_sem=last_send.at[chunk],
                recv_sem=last_recv.at[chunk],
                device_id={"seq": 1 - core},
                device_id_type=MESH,
            )
            copy.start()
            started.append(copy)

        for chunk in range(n):
            begin(chunk)

        def stage(chunk, number):
            if number == 0:
                for d in range(1, sizes[2]):
                    for i in range(sizes[0]):
                        for j in range(sizes[1]):
                            send(chunk, (i, (j + 1) % sizes[1], d))
            if number == 1:
                for d in range(1, sizes[1]):
                    for i in range(sizes[0]):
                        send(chunk, ((i + 1) % sizes[0], d, 0))
            if number == 2:
                for d in range(1, sizes[0]):
                    send(chunk, (d, 0, 0))
            if number == 3:
                final(chunk)

        for step in range(n + 3):
            for number in range(4):
                if 0 <= step - number < n:
                    stage(step - number, number)
        for chunk in range(n):
            array, rows, lanes = chunks[chunk][1 - core]
            half = outs[array].at[pl.ds(*rows), pl.ds(*lanes)]
            pltpu.make_async_copy(half, half, last_recv.at[chunk]).wait()
            sent = pair_refs[chunk]
            pltpu.make_async_copy(sent, sent, pair_send.at[chunk]).wait()
        for copy in started:
            copy.wait_send()

    for core in range(2):
        pl.when(core_index == core)(functools.partial(run, core))


def hop_slots(dims, core):
    a, b, c = [dims[axis] for axis in ORDERS[core]]
    return (a - 1, a * (b - 1), a * b * (c - 1))


def reduce_scatter(arrays, chunks, dp, collective_id=1):
    dims = dp_factors(dp)
    n = len(chunks)
    any_ = pl.BlockSpec(memory_space=pl.ANY)
    shapes = [(chunk[0][1][1], chunk[0][2][1]) for chunk in chunks]
    slots = [max(pair) for pair in zip(hop_slots(dims, 0), hop_slots(dims, 1))]
    low = jnp.bfloat16
    scratch = [pltpu.VMEM((dp,) + s, low) for s in shapes] * 2
    for level in range(3):
        scratch += [pltpu.VMEM((slots[level],) + s, low) for s in shapes]
    return pl.pallas_call(
        functools.partial(scatter_kernel, dims, chunks, len(arrays)),
        out_shape=[jax.ShapeDtypeStruct(a.shape[1:], jnp.float32) for a in arrays],
        in_specs=[any_] * len(arrays),
        out_specs=[pl.BlockSpec(memory_space=pltpu.VMEM)] * len(arrays),
        scratch_shapes=scratch
        + [
            pltpu.SemaphoreType.DMA((n, dp)),
            pltpu.SemaphoreType.DMA((n,)),
            pltpu.SemaphoreType.DMA((n, dp)),
            pltpu.SemaphoreType.DMA((n, dp)),
            pltpu.SemaphoreType.DMA((n, dp)),
            pltpu.SemaphoreType.DMA((n,)),
            pltpu.SemaphoreType.DMA((n,)),
        ],
        compiler_params=pltpu.CompilerParams(
            collective_id=collective_id, has_side_effects=True, vmem_limit_bytes=58 << 20
        ),
    )(*arrays)


GROUPS = 16
KERNEL = 128
FINE = 16
COARSE = KERNEL // FINE
LANES = 128


def lane_numbers(rows):
    return lax.broadcasted_iota(jnp.int32, (rows, LANES), 1)


def take_group(ref, rows, group, width):
    start = group * width
    base = pl.multiple_of(start // LANES * LANES, LANES)
    window = ref[rows, pl.ds(base, 2 * LANES)]
    turned = pltpu.roll(window, lax.rem(2 * LANES - (start - base), 2 * LANES), 1)[:, :LANES]
    return jnp.where(lane_numbers(turned.shape[0]) < width, turned, 0.0)


def add_group(ref, values, group, width):
    start = group * width
    base = pl.multiple_of(start // LANES * LANES, LANES)
    wide = jnp.concatenate([values, jnp.zeros_like(values)], axis=1)
    ref[:, pl.ds(base, 2 * LANES)] += pltpu.roll(wide, start - base, 1)


def double_96(pair, moved):
    lane = lane_numbers(pair.shape[0])
    turned = pltpu.roll(moved, 96, 1)
    return jnp.where(lane < 96, pair, turned), jnp.where(lane < 64, turned, 0.0)


def double_192(first, second, moved_first, moved_second):
    lane = lane_numbers(first.shape[0])
    a, b = pltpu.roll(moved_first, 64, 1), pltpu.roll(moved_second, 64, 1)
    return first, jnp.where(lane < 64, second, a), jnp.where(lane < 64, a, b)


def fold_lanes(tiles, shift):
    a, b, c = tiles
    lane = lane_numbers(a.shape[0])
    tb, tc = pltpu.roll(b, 64, 1), pltpu.roll(c, 64, 1)
    a, b = shift(a, jnp.where(lane < 64, tb, tc), 4), shift(b, tc, 4)
    lane = lane_numbers(a.shape[0])
    far = jnp.where(lane < 32, pltpu.roll(a, 32, 1), pltpu.roll(b, 32, 1))
    a = shift(a, far, 2)
    a = shift(a, pltpu.roll(a, 80, 1), 1)
    return jnp.where(lane_numbers(a.shape[0]) < 48, a, 0.0)


def forward_kernel(pack, frames, weight, out, patches, padded, total):
    group = pl.program_id(0)
    half = KERNEL // 2
    reach = pack + FINE

    @pl.when(group == 0)
    def _():
        padded[...] = jnp.zeros_like(padded)
        padded[half : half + pack, 0 : frames.shape[1]] = frames[...].astype(jnp.float32)
        total[...] = jnp.zeros_like(total)

    rows = reach + KERNEL - FINE
    one = take_group(padded, slice(0, rows), group, 48)
    lane = lane_numbers(rows - FINE)
    two = one[: rows - FINE] + pltpu.roll(one[FINE:], 48, 1)
    low, high = double_96(two[: rows - 3 * FINE], two[2 * FINE :])
    tiles = double_192(low[:reach], high[:reach], low[4 * FINE :], high[4 * FINE :])
    patch = jnp.concatenate(tiles, axis=1).astype(jnp.bfloat16)
    patches[0] = patch
    product = jnp.dot(patch, weight[0], preferred_element_type=jnp.float32)
    size = pack + 8
    near = product[:size, :384] + product[8 : 8 + size, 384:]

    def shift(base, moved, amount):
        return base + pltpu.roll(moved, size - amount, 0)

    tiles = [near[:, i * LANES : (i + 1) * LANES] for i in range(3)]
    add_group(total, fold_lanes(tiles, shift)[:pack], group, 48)

    @pl.when(group == GROUPS - 1)
    def _():
        out[...] = total[:, : frames.shape[1]]


def conv_forward(frames, weight):
    pack, width = frames.shape
    reach = pack + FINE
    return pl.pallas_call(
        functools.partial(forward_kernel, pack),
        grid=(GROUPS,),
        out_shape=[
            jax.ShapeDtypeStruct((pack, width), jnp.float32),
            jax.ShapeDtypeStruct((GROUPS, reach, 384), jnp.bfloat16),
        ],
        in_specs=[
            pl.BlockSpec((pack, width), lambda g: (0, 0)),
            pl.BlockSpec((1, 384, 768), lambda g: (g, 0, 0)),
        ],
        out_specs=[
            pl.BlockSpec((pack, width), lambda g: (0, 0)),
            pl.BlockSpec((1, reach, 384), lambda g: (g, 0, 0)),
        ],
        scratch_shapes=[
            pltpu.VMEM((pack + KERNEL, width + LANES), jnp.float32),
            pltpu.VMEM((pack, width + LANES), jnp.float32),
        ],
        compiler_params=pltpu.CompilerParams(vmem_limit_bytes=40 << 20),
    )(frames, weight)


def backward_kernel(pack, grads, direct, weight, patches, out, weight_grad, padded, tall, total):
    group = pl.program_id(0)
    reach = pack + FINE
    edge = KERNEL // 2 - FINE

    @pl.when(group == 0)
    def _():
        padded[...] = jnp.zeros_like(padded)
        padded[:pack, : grads.shape[1]] = grads[...].astype(jnp.float32)
        tall[...] = jnp.zeros_like(tall)
        total[...] = jnp.zeros_like(total)
        total[:, : direct.shape[1]] = direct[...]

    def later(values, amount):
        return pltpu.roll(values, amount, 0)

    one = take_group(padded, slice(0, reach), group, 48)
    two = one + pltpu.roll(later(one, 1), 48, 1)
    low, high = double_96(two, later(two, 2))
    tiles = double_192(low, high, later(low, 4), later(high, 4))
    near = jnp.concatenate(tiles, axis=1)
    spread = jnp.concatenate([near, later(near, 8)], axis=1).astype(jnp.bfloat16)
    weight_grad[0] = lax.dot_general(
        patches[0], spread, (((0,), (0,)), ((), ())), preferred_element_type=jnp.float32
    ).astype(jnp.bfloat16)
    tall[edge : edge + reach] = lax.dot_general(
        spread, weight[0], (((1,), (1,)), ((), ())), preferred_element_type=jnp.float32
    )

    def shift(base, moved, amount):
        return base[amount * FINE :] + moved[: base.shape[0] - amount * FINE]

    tiles = [tall[:, i * LANES : (i + 1) * LANES] for i in range(3)]
    add_group(total, fold_lanes(tiles, shift), group, 48)

    @pl.when(group == GROUPS - 1)
    def _():
        out[...] = total[:, : grads.shape[1]]


def conv_backward(grads, direct, weight, patches):
    pack, width = grads.shape
    reach = pack + FINE
    whole = lambda g: (0, 0)
    each = lambda g: (g, 0, 0)
    return pl.pallas_call(
        functools.partial(backward_kernel, pack),
        grid=(GROUPS,),
        out_shape=[
            jax.ShapeDtypeStruct((pack, width), jnp.float32),
            jax.ShapeDtypeStruct(weight.shape, jnp.bfloat16),
        ],
        in_specs=[
            pl.BlockSpec((pack, width), whole),
            pl.BlockSpec((pack, width), whole),
            pl.BlockSpec((1, 384, 768), each),
            pl.BlockSpec((1, reach, 384), each),
        ],
        out_specs=[
            pl.BlockSpec((pack, width), whole),
            pl.BlockSpec((1, 384, 768), each),
        ],
        scratch_shapes=[
            pltpu.VMEM((reach, width + LANES), jnp.float32),
            pltpu.VMEM((pack + KERNEL - FINE, 384), jnp.float32),
            pltpu.VMEM((pack, width + LANES), jnp.float32),
        ],
        compiler_params=pltpu.CompilerParams(vmem_limit_bytes=40 << 20),
    )(grads, direct, weight, patches)


HEAD_DIM = 64
CLIP_EPS = 1e-05
GAIN_ROWS = 16


def norm_forward(values, gain_vector):
    centered = values - jnp.mean(values, axis=-1, keepdims=True)
    inverse = lax.rsqrt(jnp.mean(centered * centered, axis=-1, keepdims=True) + CLIP_EPS)
    unit_rows = centered * inverse
    return (unit_rows * gain_vector, unit_rows, inverse)


def norm_backward(grad_out, unit_rows, inverse, gain_vector):
    scaled = grad_out * gain_vector
    inner = jnp.mean(scaled, axis=-1, keepdims=True)
    along = jnp.mean(scaled * unit_rows, axis=-1, keepdims=True)
    return (inverse * (scaled - inner - unit_rows * along), jnp.sum(grad_out * unit_rows, axis=0))


def gelu_slope(values):
    cumulative = 0.5 * (1.0 + lax.erf(values * 0.7071067811865476))
    density = jnp.exp(-0.5 * values * values) * 0.3989422804014327
    return cumulative + values * density


def segment_numbers(lengths, pack_rows):
    ends = jnp.cumsum(lengths)
    position = jnp.arange(pack_rows, dtype=jnp.int32)
    return jnp.sum((position[:, None] >= ends[None, :]).astype(jnp.int32), axis=1)


def dot(a, b, contract):
    return lax.dot_general(a, b, ((contract[:1], contract[1:]), ((), ())), preferred_element_type=jnp.float32)


def middle_part(frames, convolved, segments, gains, wide, down, cotangent):
    pack, width = frames.shape
    heads = width // HEAD_DIM
    low = jnp.bfloat16
    front_gain, middle_gain, final_gain = gains
    qkv, out_weight, up = wide[:, : 3 * width], wide[:, 3 * width : 4 * width], wide[:, 4 * width :]
    mixed = frames.astype(jnp.float32) + jax.nn.gelu(convolved, approximate=False)
    normed, unit_front, inverse_front = norm_forward(mixed, front_gain)
    normed_low = normed.astype(low)
    projected = dot(normed_low, qkv, (1, 0)).astype(low).reshape(pack, 3, heads, HEAD_DIM)
    queries, keys, values = projected[:, 0], projected[:, 1], projected[:, 2]
    scale = HEAD_DIM ** (-0.5)
    scores = jnp.einsum("qhd,khd->hqk", queries, keys, preferred_element_type=jnp.float32) * scale
    same_clip = segments[:, None] == segments[None, :]
    scores = jnp.where(same_clip[None], scores, -1e30)
    shifted = jnp.exp(scores - jnp.max(scores, axis=-1, keepdims=True))
    probs = shifted / jnp.sum(shifted, axis=-1, keepdims=True)
    probs_low = probs.astype(low)
    attended = (
        jnp.einsum("hqk,khd->qhd", probs_low, values, preferred_element_type=jnp.float32)
        .astype(low)
        .reshape(pack, width)
    )
    branch = dot(attended, out_weight, (1, 0))
    middle, unit_middle, inverse_middle = norm_forward(normed + branch, middle_gain)
    middle_low = middle.astype(low)
    hidden = dot(middle_low, up, (1, 0))
    activated = jax.nn.gelu(hidden, approximate=False).astype(low)
    feed = dot(activated, down, (1, 0))
    output, unit_final, inverse_final = norm_forward(middle + feed, final_gain)
    grad_final, final_gain_grad = norm_backward(
        cotangent.astype(jnp.float32), unit_final, inverse_final, final_gain
    )
    grad_feed = grad_final.astype(low)
    down_grad = dot(activated, grad_feed, (0, 0))
    grad_hidden = (dot(grad_feed, down, (1, 1)) * gelu_slope(hidden)).astype(low)
    up_grad = dot(middle_low, grad_hidden, (0, 0))
    grad_middle = grad_final + dot(grad_hidden, up, (1, 1))
    grad_mid_in, middle_gain_grad = norm_backward(
        grad_middle, unit_middle, inverse_middle, middle_gain
    )
    grad_branch = grad_mid_in.astype(low)
    out_grad = dot(attended, grad_branch, (0, 0))
    grad_attended = dot(grad_branch, out_weight, (1, 1)).astype(low).reshape(pack, heads, HEAD_DIM)
    grad_values = jnp.einsum("hqk,qhd->khd", probs_low, grad_attended, preferred_element_type=jnp.float32)
    grad_probs = jnp.einsum("qhd,khd->hqk", grad_attended, values, preferred_element_type=jnp.float32)
    grad_scores = (
        probs * (grad_probs - jnp.sum(probs * grad_probs, axis=-1, keepdims=True))
    ).astype(low)
    grad_queries = jnp.einsum("hqk,khd->qhd", grad_scores, keys, preferred_element_type=jnp.float32) * scale
    grad_keys = jnp.einsum("hqk,qhd->khd", grad_scores, queries, preferred_element_type=jnp.float32) * scale
    grad_projected = (
        jnp.stack([grad_queries, grad_keys, grad_values], axis=1).astype(low).reshape(pack, 3 * width)
    )
    qkv_grad = dot(normed_low, grad_projected, (0, 0))
    grad_normed = grad_mid_in + dot(grad_projected, qkv, (1, 1))
    grad_mixed, front_gain_grad = norm_backward(grad_normed, unit_front, inverse_front, front_gain)
    grad_convolved = (grad_mixed * gelu_slope(convolved)).astype(low)
    wide_grad = jnp.concatenate([qkv_grad, out_grad, up_grad], axis=1).astype(low)
    gain_grads = jnp.stack([front_gain_grad, middle_gain_grad, final_gain_grad])
    return output.astype(low), grad_mixed, grad_convolved, wide_grad, down_grad.astype(low), gain_grads


def chunks_of(conv_rows, conv_lanes, wide_rows, width, down_rows):
    both = range(2)
    quarter, half = conv_rows // 4, width // 2
    conv = [
        [(0, ((2 * part + core) * quarter, quarter), (0, conv_lanes)) for core in both] for part in both
    ]
    wide = [
        [(1, (0, wide_rows), ((2 * part + core) * 2 * width, 2 * width)) for core in both] for part in both
    ]
    down = [[(2, (0, down_rows), (core * half, half)) for core in both]]
    gain = [[(3, (core * GAIN_ROWS, GAIN_ROWS), (0, LANES)) for core in both]]
    return gain, conv, wide, down


def shards(
    frames,
    clip_lengths,
    conv_weight,
    front_gain,
    qkv_weight,
    out_weight,
    middle_gain,
    up_weight,
    down_weight,
    final_gain,
    cotangent,
):
    dp = lax.axis_size("dp")
    low = jnp.bfloat16
    width = frames.shape[2]
    columns = conv_weight.shape[2]
    group_width = conv_weight.shape[1]
    gain_width = front_gain.shape[0]
    conv_shard = (
        conv_weight.reshape(COARSE, FINE, group_width, columns)
        .transpose(0, 2, 1, 3)
        .reshape(COARSE * group_width, FINE * columns)
    )
    wide_shard = jnp.concatenate([qkv_weight, out_weight, up_weight], axis=1)
    gain_shard = jnp.pad(
        jnp.stack([front_gain, middle_gain, final_gain]),
        ((0, 2 * GAIN_ROWS - 3), (0, LANES - gain_width)),
    )
    parts = (conv_shard, wide_shard, down_weight, gain_shard)
    gain_chunk, conv_chunks, wide_chunks, down_chunk = chunks_of(
        *conv_shard.shape, wide_shard.shape[0], width, down_weight.shape[0]
    )
    conv_all, wide_all, down_all, gain_all = all_gather(
        parts, gain_chunk + conv_chunks + wide_chunks + down_chunk, dp
    )
    split = group_width // columns
    weight = (
        conv_all.reshape(GROUPS, split, COARSE * group_width, FINE, columns)
        .transpose(0, 2, 3, 1, 4)
        .reshape(GROUPS, COARSE * group_width, FINE * group_width)
    )
    wide = wide_all.reshape(width, wide_shard.shape[1])
    down = down_all.reshape(-1, width)
    gains = gain_all[:, :3, :gain_width].transpose(1, 0, 2).reshape(3, width).astype(jnp.float32)

    both = lax.all_to_all(
        jnp.stack([frames, cotangent], axis=1), "seq", split_axis=0, concat_axis=2, tiled=True
    )
    pack_frames, pack_cotangent = both[0, 0], both[0, 1]
    pack = pack_frames.shape[0]
    lengths = lax.dynamic_index_in_dim(clip_lengths[:, 0], lax.axis_index("seq"), 0, False)
    segments = segment_numbers(lengths, pack)

    convolved, patches = conv_forward(pack_frames, weight)
    output, grad_mixed, grad_convolved, wide_grad, down_grad, gain_grads = middle_part(
        pack_frames, convolved, segments, gains, wide, down, pack_cotangent
    )
    frame_grad, conv_grad = conv_backward(grad_convolved, grad_mixed, weight, patches)

    conv_blocks = (
        conv_grad.reshape(GROUPS, COARSE * group_width, FINE, split, columns)
        .transpose(0, 3, 1, 2, 4)
        .reshape((dp,) + conv_shard.shape)
    )
    gain_blocks = jnp.pad(
        gain_grads.astype(low).reshape(3, dp, gain_width).transpose(1, 0, 2),
        ((0, 0), (0, 2 * GAIN_ROWS - 3), (0, LANES - gain_width)),
    )
    conv_sum, wide_sum, down_sum, gain_sum = reduce_scatter(
        (
            conv_blocks,
            wide_grad.reshape((dp,) + wide_shard.shape),
            down_grad.reshape((dp,) + down_weight.shape),
            gain_blocks,
        ),
        gain_chunk + down_chunk + wide_chunks[::-1] + conv_chunks,
        dp,
    )
    conv_sum = (
        conv_sum.reshape(COARSE, group_width, FINE, columns)
        .transpose(0, 2, 1, 3)
        .reshape(conv_weight.shape)
    )
    outputs = lax.all_to_all(output[None], "seq", split_axis=1, concat_axis=0, tiled=True)
    frame_grads = lax.all_to_all(frame_grad[None], "seq", split_axis=1, concat_axis=0, tiled=True)
    return (
        outputs,
        frame_grads,
        conv_sum,
        gain_sum[0, :gain_width],
        wide_sum[:, : 3 * width],
        wide_sum[:, 3 * width : 4 * width],
        gain_sum[1, :gain_width],
        wide_sum[:, 4 * width :],
        down_sum,
        gain_sum[2, :gain_width],
    )


def solution(mesh):
    frames_spec = P(None, ("dp", "seq"), None)
    row, matrix, columns = P("dp"), P("dp", None), P(None, None, "dp")
    return jax.shard_map(
        shards,
        mesh=mesh,
        in_specs=(
            frames_spec,
            P(None, "dp", None),
            columns,
            row,
            matrix,
            matrix,
            row,
            matrix,
            matrix,
            row,
            frames_spec,
        ),
        out_specs=(
            frames_spec,
            frames_spec,
            columns,
            row,
            matrix,
            matrix,
            row,
            matrix,
            matrix,
            row,
        ),
        check_vma=False,
    )
```

```python
import functools

import jax
import jax.numpy as jnp
from jax import lax
from jax.experimental import pallas as pl
from jax.experimental.pallas import tpu as pltpu
from jax.sharding import PartitionSpec as P

MESH = pl.DeviceIdType.MESH


def dp_factors(size):
    return {16: (4, 2, 2), 128: (4, 4, 8)}.get(size, (size, 1, 1))


def offsets_of(dims):
    return [(i, j, k) for i in range(dims[0]) for j in range(dims[1]) for k in range(dims[2])]


def place(dims, order, position, offsets):
    coords = list(position)
    for axis, offset in zip(order, offsets):
        if offset:
            coords[axis] = lax.rem(coords[axis] + offset, dims[axis])
    return (coords[0] * dims[1] + coords[1]) * dims[2] + coords[2]


def position_of(dims):
    me = lax.axis_index("dp")
    return (me // (dims[1] * dims[2]), lax.rem(me // dims[2], dims[1]), lax.rem(me, dims[2]))


def greet(dims, position, core):
    barrier = pltpu.get_barrier_semaphore()
    count = 1
    pl.semaphore_signal(barrier, inc=1, device_id={"seq": 1 - core}, device_id_type=MESH)
    for axis in range(3):
        for offset in range(1, dims[axis]):
            other = place(dims, (axis,), position, (offset,))
            pl.semaphore_signal(barrier, inc=1, device_id={"dp": other}, device_id_type=MESH)
            count += 1
    pl.semaphore_wait(barrier, count)


ORDERS = ((0, 1, 2), (0, 2, 1))


def by_core(core_index, body):
    for core in range(2):
        pl.when(core_index == core)(functools.partial(body, core))


class Gather:
    def __init__(self, dims, chunks, ins, outs, sems):
        self.dims, self.chunks, self.ins, self.outs = dims, chunks, ins, outs
        self.send_sems, self.recv_sems, self.push_send, self.push_recv = sems
        self.position = position_of(dims)
        self.count = dims[0] * dims[1] * dims[2]
        self.sent = {}

    def part(self, which, chunk, side):
        array, rows, lanes = self.chunks[chunk][side]
        out = self.outs[array]
        if len(out.shape) == 3:
            return out.at[which, pl.ds(*rows), pl.ds(*lanes)]
        first = pl.multiple_of(which * self.ins[array].shape[0] + rows[0], 16)
        return out.at[pl.ds(first, rows[1]), pl.ds(*lanes)]

    def whole(self, which, array):
        out, height = self.outs[array], self.ins[array].shape[0]
        if len(out.shape) == 3:
            return out.at[which]
        return out.at[pl.ds(pl.multiple_of(which * height, 16), height)]

    def send(self, core, chunk, offsets, level, distance):
        order = ORDERS[core]
        gid = place(self.dims, order, self.position, offsets)
        array, rows, lanes = self.chunks[chunk][core]
        mine = self.ins[array].at[pl.ds(*rows), pl.ds(*lanes)]
        number = self.sent.get((core, chunk), 0)
        self.sent[core, chunk] = number + 1
        pltpu.make_async_remote_copy(
            src_ref=mine if offsets == (0, 0, 0) else self.part(gid, chunk, core),
            dst_ref=self.part(gid, chunk, core),
            send_sem=self.send_sems.at[chunk, number],
            recv_sem=self.recv_sems.at[chunk, gid],
            device_id={"dp": place(self.dims, (order[level],), self.position, (distance,))},
            device_id_type=MESH,
        ).start()

    def spread(self, core, chunk, offsets, first):
        for level in range(first, 3):
            for distance in range(1, self.dims[ORDERS[core][level]]):
                self.send(core, chunk, offsets, level, distance)

    def forward(self, core, chunk, offsets, first):
        gid = place(self.dims, ORDERS[core], self.position, offsets)
        ref = self.part(gid, chunk, core)
        pltpu.make_async_copy(ref, ref, self.recv_sems.at[chunk, gid]).wait()
        self.spread(core, chunk, offsets, first)
        pltpu.make_async_remote_copy(
            src_ref=ref,
            dst_ref=ref,
            send_sem=self.push_send.at[chunk, gid],
            recv_sem=self.push_recv.at[chunk, gid],
            device_id={"seq": 1 - core},
            device_id_type=MESH,
        ).start()

    def tasks(self, core, chunk, stage):
        sizes = [self.dims[axis] for axis in ORDERS[core]]
        if stage == 0:
            return [functools.partial(self.spread, core, chunk, (0, 0, 0), 0)]
        if stage == 1:
            places = [(i, 0, 0) for i in range(1, sizes[0])]
        elif stage == 2:
            places = [(i, j, 0) for i in range(sizes[0]) for j in range(1, sizes[1])]
        else:
            places = [o for o in offsets_of(sizes) if o[2]]
        return [functools.partial(self.forward, core, chunk, offsets, stage) for offsets in places]

    def steps(self, core, step):
        done = []
        for stage in range(4):
            if 0 <= step - stage < len(self.chunks):
                done += self.tasks(core, step - stage, stage)
        return done

    def others(self, body):
        me = lax.axis_index("dp")

        @pl.loop(1, self.count)
        def _(offset):
            body(lax.rem(me + offset, self.count), offset)

    def arrived(self, core, chunk):
        def body(gid, _):
            ref = self.part(gid, chunk, 1 - core)
            pltpu.make_async_copy(ref, ref, self.push_recv.at[chunk, gid]).wait()

        self.others(body)

    def finish(self, core):
        for chunk in range(len(self.chunks)):

            def body(gid, number, chunk=chunk):
                ref = self.part(gid, chunk, core)
                pltpu.make_async_copy(ref, ref, self.push_send.at[chunk, gid]).wait()
                pltpu.make_async_copy(ref, ref, self.send_sems.at[chunk, number - 1]).wait()

            self.others(body)


def gather_kernel(dims, chunks, *refs):
    n_arr = len(refs[:-5]) // 2
    ins, outs = refs[:n_arr], refs[n_arr : 2 * n_arr]
    gather = Gather(dims, chunks, ins, outs, refs[2 * n_arr : 2 * n_arr + 4])
    local_sems = refs[-1]
    core_index = lax.axis_index("seq")
    greet(dims, gather.position, core_index)
    own = [
        pltpu.make_async_copy(ins[i], outs[i].at[lax.axis_index("dp")], local_sems.at[i])
        for i in range(n_arr)
    ]
    for copy in own:
        copy.start()

    def run(core):
        for step in range(len(chunks) + 3):
            for task in gather.steps(core, step):
                task()
        for chunk in range(len(chunks)):
            gather.arrived(core, chunk)
        gather.finish(core)

    by_core(core_index, run)
    for copy in own:
        copy.wait()


def all_gather(arrays, chunks, dp, collective_id=0):
    dims = dp_factors(dp)
    n = len(chunks)
    any_ = pl.BlockSpec(memory_space=pl.ANY)
    return pl.pallas_call(
        functools.partial(gather_kernel, dims, chunks),
        out_shape=[jax.ShapeDtypeStruct((dp,) + a.shape, a.dtype) for a in arrays],
        in_specs=[any_] * len(arrays),
        out_specs=[any_] * len(arrays),
        scratch_shapes=[
            pltpu.SemaphoreType.DMA((n, dp)),
            pltpu.SemaphoreType.DMA((n, dp)),
            pltpu.SemaphoreType.DMA((n, dp)),
            pltpu.SemaphoreType.DMA((n, dp)),
            pltpu.SemaphoreType.DMA((len(arrays),)),
        ],
        compiler_params=pltpu.CompilerParams(collective_id=collective_id, has_side_effects=True),
    )(*arrays)


def scatter_kernel(dims, chunks, n_arr, *refs):
    ins, outs = refs[:n_arr], refs[n_arr : 2 * n_arr]
    scratch = list(refs[2 * n_arr :])
    n = len(chunks)
    stage_refs, pair_refs = scratch[:n], scratch[n : 2 * n]
    hop_refs = [scratch[(2 + level) * n : (3 + level) * n] for level in range(3)]
    (load_sems, pair_send, pair_recv, hop_send, hop_recv, last_send, last_recv) = scratch[5 * n :]
    position = position_of(dims)
    core_index = lax.axis_index("seq")
    greet(dims, position, core_index)

    def run(core):
        order = ORDERS[core]
        sizes = [dims[axis] for axis in order]
        started = []
        other_order = ORDERS[1 - core]
        other_sizes = [dims[axis] for axis in other_order]

        def part(array_refs, which, chunk, side):
            array, rows, lanes = chunks[chunk][side]
            return array_refs[array].at[which, pl.ds(*rows), pl.ds(*lanes)]

        def slot(level, offsets, distance):
            index = distance - 1
            for i in range(level):
                index = index * sizes[i] + offsets[i]
            return index

        def semaphore(level, index):
            return (1, sizes[0], sizes[0] * sizes[1])[level] + index - 1

        def begin(chunk):
            array = chunks[chunk][core][0]
            theirs = sorted(offsets_of(other_sizes), key=lambda o: (o[2] == 0, o[1] == 0, o[0] == 0))
            mine = sorted(offsets_of(sizes), key=lambda o: (o[2] == 0, o[1] == 0, o[0] == 0))
            for given, kept in zip(theirs, mine):
                gid = place(dims, other_order, position, given)
                copy = pltpu.make_async_remote_copy(
                    src_ref=part(ins, gid, chunk, 1 - core),
                    dst_ref=pair_refs[chunk].at[gid],
                    send_sem=pair_send.at[chunk],
                    recv_sem=pair_recv.at[chunk, gid],
                    device_id={"seq": 1 - core},
                    device_id_type=MESH,
                )
                copy.start()
                gid = place(dims, order, position, kept)
                pltpu.make_async_copy(
                    part(ins, gid, chunk, core), stage_refs[chunk].at[gid], load_sems.at[chunk, gid]
                ).start()

        def combine(chunk, offsets, target):
            gid = place(dims, order, position, offsets)
            own = stage_refs[chunk].at[gid]
            pair = pair_refs[chunk].at[gid]
            pltpu.make_async_copy(own, own, load_sems.at[chunk, gid]).wait()
            pltpu.make_async_copy(pair, pair, pair_recv.at[chunk, gid]).wait()
            terms = [own, pair]
            for level in (2, 1, 0):
                if offsets[level]:
                    break
                for distance in range(1, sizes[level]):
                    index = slot(level, offsets, distance)
                    ref = hop_refs[level][chunk].at[index]
                    pltpu.make_async_copy(ref, ref, hop_recv.at[chunk, semaphore(level, index)]).wait()
                    terms.append(ref)
            height = own.shape[0]

            tall = 16 if height % 16 == 0 else height

            @pl.loop(0, height // tall)
            def _(tile):
                rows = pl.ds(pl.multiple_of(tile * tall, tall), tall)
                total = terms[0][rows, :].astype(jnp.float32)
                for term in terms[1:]:
                    total = total + term[rows, :].astype(jnp.float32)
                if target is None:
                    own[rows, :] = total.astype(own.dtype)
                else:
                    target[rows, :] = total

            return gid

        def send(chunk, offsets):
            level = max(i for i in range(3) if offsets[i])
            gid = combine(chunk, offsets, None)
            index = slot(level, offsets, offsets[level])
            target = place(dims, (order[level],), position, (offsets[level],))
            copy = pltpu.make_async_remote_copy(
                src_ref=stage_refs[chunk].at[gid],
                dst_ref=hop_refs[level][chunk].at[index],
                send_sem=hop_send.at[chunk, semaphore(level, index)],
                recv_sem=hop_recv.at[chunk, semaphore(level, index)],
                device_id={"dp": target},
                device_id_type=MESH,
            )
            copy.start()
            started.append(copy)

        def final(chunk):
            array, rows, lanes = chunks[chunk][core]
            half = outs[array].at[pl.ds(*rows), pl.ds(*lanes)]
            combine(chunk, (0, 0, 0), half)
            copy = pltpu.make_async_remote_copy(
                src_ref=half,
                dst_ref=half,
                send_sem=last_send.at[chunk],
                recv_sem=last_recv.at[chunk],
                device_id={"seq": 1 - core},
                device_id_type=MESH,
            )
            copy.start()
            started.append(copy)

        for chunk in range(n):
            begin(chunk)

        def stage(chunk, number):
            if number == 0:
                for d in range(1, sizes[2]):
                    for i in range(sizes[0]):
                        for j in range(sizes[1]):
                            send(chunk, (i, (j + 1) % sizes[1], d))
            if number == 1:
                for d in range(1, sizes[1]):
                    for i in range(sizes[0]):
                        send(chunk, ((i + 1) % sizes[0], d, 0))
            if number == 2:
                for d in range(1, sizes[0]):
                    send(chunk, (d, 0, 0))
            if number == 3:
                final(chunk)

        for step in range(n + 3):
            for number in range(4):
                if 0 <= step - number < n:
                    stage(step - number, number)
        for chunk in range(n):
            array, rows, lanes = chunks[chunk][1 - core]
            half = outs[array].at[pl.ds(*rows), pl.ds(*lanes)]
            pltpu.make_async_copy(half, half, last_recv.at[chunk]).wait()
            sent = pair_refs[chunk]
            pltpu.make_async_copy(sent, sent, pair_send.at[chunk]).wait()
        for copy in started:
            copy.wait_send()

    for core in range(2):
        pl.when(core_index == core)(functools.partial(run, core))


def hop_slots(dims, core):
    a, b, c = [dims[axis] for axis in ORDERS[core]]
    return (a - 1, a * (b - 1), a * b * (c - 1))


def reduce_scatter(arrays, chunks, dp, collective_id=1):
    dims = dp_factors(dp)
    n = len(chunks)
    any_ = pl.BlockSpec(memory_space=pl.ANY)
    shapes = [(chunk[0][1][1], chunk[0][2][1]) for chunk in chunks]
    slots = [max(pair) for pair in zip(hop_slots(dims, 0), hop_slots(dims, 1))]
    low = jnp.bfloat16
    scratch = [pltpu.VMEM((dp,) + s, low) for s in shapes] * 2
    for level in range(3):
        scratch += [pltpu.VMEM((slots[level],) + s, low) for s in shapes]
    return pl.pallas_call(
        functools.partial(scatter_kernel, dims, chunks, len(arrays)),
        out_shape=[jax.ShapeDtypeStruct(a.shape[1:], jnp.float32) for a in arrays],
        in_specs=[any_] * len(arrays),
        out_specs=[pl.BlockSpec(memory_space=pltpu.VMEM)] * len(arrays),
        scratch_shapes=scratch
        + [
            pltpu.SemaphoreType.DMA((n, dp)),
            pltpu.SemaphoreType.DMA((n,)),
            pltpu.SemaphoreType.DMA((n, dp)),
            pltpu.SemaphoreType.DMA((n, dp)),
            pltpu.SemaphoreType.DMA((n, dp)),
            pltpu.SemaphoreType.DMA((n,)),
            pltpu.SemaphoreType.DMA((n,)),
        ],
        compiler_params=pltpu.CompilerParams(
            collective_id=collective_id, has_side_effects=True, vmem_limit_bytes=58 << 20
        ),
    )(*arrays)


GROUPS = 16
KERNEL = 128
FINE = 16
COARSE = KERNEL // FINE
LANES = 128


def lane_numbers(rows):
    return lax.broadcasted_iota(jnp.int32, (rows, LANES), 1)


def take_group(ref, rows, group, width):
    start = group * width
    base = pl.multiple_of(start // LANES * LANES, LANES)
    window = ref[rows, pl.ds(base, 2 * LANES)]
    turned = pltpu.roll(window, lax.rem(2 * LANES - (start - base), 2 * LANES), 1)[:, :LANES]
    return jnp.where(lane_numbers(turned.shape[0]) < width, turned, 0.0)


def add_group(ref, values, group, width):
    start = group * width
    base = pl.multiple_of(start // LANES * LANES, LANES)
    wide = jnp.concatenate([values, jnp.zeros_like(values)], axis=1)
    ref[:, pl.ds(base, 2 * LANES)] += pltpu.roll(wide, start - base, 1)


def double_96(pair, moved):
    lane = lane_numbers(pair.shape[0])
    turned = pltpu.roll(moved, 96, 1)
    return jnp.where(lane < 96, pair, turned), jnp.where(lane < 64, turned, 0.0)


def double_192(first, second, moved_first, moved_second):
    lane = lane_numbers(first.shape[0])
    a, b = pltpu.roll(moved_first, 64, 1), pltpu.roll(moved_second, 64, 1)
    return first, jnp.where(lane < 64, second, a), jnp.where(lane < 64, a, b)


def fold_lanes(tiles, shift):
    a, b, c = tiles
    lane = lane_numbers(a.shape[0])
    tb, tc = pltpu.roll(b, 64, 1), pltpu.roll(c, 64, 1)
    a, b = shift(a, jnp.where(lane < 64, tb, tc), 4), shift(b, tc, 4)
    lane = lane_numbers(a.shape[0])
    far = jnp.where(lane < 32, pltpu.roll(a, 32, 1), pltpu.roll(b, 32, 1))
    a = shift(a, far, 2)
    a = shift(a, pltpu.roll(a, 80, 1), 1)
    return jnp.where(lane_numbers(a.shape[0]) < 48, a, 0.0)


def make_patch(padded, group, pack):
    reach = pack + FINE
    one = take_group(padded, slice(0, reach + KERNEL - FINE), group, 48)
    rows = one.shape[0] - FINE
    two = one[:rows] + pltpu.roll(one[FINE:], 48, 1)
    low, high = double_96(two[: rows - 2 * FINE], two[2 * FINE :])
    tiles = double_192(low[:reach], high[:reach], low[4 * FINE :], high[4 * FINE :])
    return jnp.concatenate(tiles, axis=1).astype(jnp.bfloat16)


def add_forward(total, patch, weight, group, pack):
    product = jnp.dot(patch, weight, preferred_element_type=jnp.float32)
    size = pack + 8
    near = product[:size, :384] + product[8 : 8 + size, 384:]

    def shift(base, moved, amount):
        return base + pltpu.roll(moved, size - amount, 0)

    tiles = [near[:, i * LANES : (i + 1) * LANES] for i in range(3)]
    add_group(total, fold_lanes(tiles, shift)[:pack], group, 48)


def fill_padded(padded, frames):
    half = KERNEL // 2
    padded[...] = jnp.zeros_like(padded)
    padded[half : half + frames.shape[0], 0 : frames.shape[1]] = frames[...].astype(jnp.float32)


def forward_kernel(pack, frames, weight, out, patches, padded, total):
    group = pl.program_id(0)

    @pl.when(group == 0)
    def _():
        fill_padded(padded, frames)
        total[...] = jnp.zeros_like(total)

    patch = make_patch(padded, group, pack)
    patches[0] = patch
    add_forward(total, patch, weight[0], group, pack)

    @pl.when(group == GROUPS - 1)
    def _():
        out[...] = total[:, : frames.shape[1]]


def conv_forward(frames, weight):
    pack, width = frames.shape
    reach = pack + FINE
    return pl.pallas_call(
        functools.partial(forward_kernel, pack),
        grid=(GROUPS,),
        out_shape=[
            jax.ShapeDtypeStruct((pack, width), jnp.float32),
            jax.ShapeDtypeStruct((GROUPS, reach, 384), jnp.bfloat16),
        ],
        in_specs=[
            pl.BlockSpec((pack, width), lambda g: (0, 0)),
            pl.BlockSpec((1, 384, 768), lambda g: (g, 0, 0)),
        ],
        out_specs=[
            pl.BlockSpec((pack, width), lambda g: (0, 0)),
            pl.BlockSpec((1, reach, 384), lambda g: (g, 0, 0)),
        ],
        scratch_shapes=[
            pltpu.VMEM((pack + KERNEL, width + LANES), jnp.float32),
            pltpu.VMEM((pack, width + LANES), jnp.float32),
        ],
        compiler_params=pltpu.CompilerParams(vmem_limit_bytes=40 << 20),
    )(frames, weight)


def backward_kernel(pack, grads, direct, weight, patches, out, weight_grad, padded, tall, total):
    group = pl.program_id(0)
    reach = pack + FINE
    edge = KERNEL // 2 - FINE

    @pl.when(group == 0)
    def _():
        padded[...] = jnp.zeros_like(padded)
        padded[:pack, : grads.shape[1]] = grads[...].astype(jnp.float32)
        tall[...] = jnp.zeros_like(tall)
        total[...] = jnp.zeros_like(total)
        total[:, : direct.shape[1]] = direct[...]

    def later(values, amount):
        return pltpu.roll(values, amount, 0)

    one = take_group(padded, slice(0, reach), group, 48)
    two = one + pltpu.roll(later(one, 1), 48, 1)
    low, high = double_96(two, later(two, 2))
    tiles = double_192(low, high, later(low, 4), later(high, 4))
    near = jnp.concatenate(tiles, axis=1)
    spread = jnp.concatenate([near, later(near, 8)], axis=1).astype(jnp.bfloat16)
    weight_grad[0] = lax.dot_general(
        patches[0], spread, (((0,), (0,)), ((), ())), preferred_element_type=jnp.float32
    ).astype(jnp.bfloat16)
    tall[edge : edge + reach] = lax.dot_general(
        spread, weight[0], (((1,), (1,)), ((), ())), preferred_element_type=jnp.float32
    )

    def shift(base, moved, amount):
        return base[amount * FINE :] + moved[: base.shape[0] - amount * FINE]

    tiles = [tall[:, i * LANES : (i + 1) * LANES] for i in range(3)]
    add_group(total, fold_lanes(tiles, shift), group, 48)

    @pl.when(group == GROUPS - 1)
    def _():
        out[...] = total[:, : grads.shape[1]]


def conv_backward(grads, direct, weight, patches):
    pack, width = grads.shape
    reach = pack + FINE
    whole = lambda g: (0, 0)
    each = lambda g: (g, 0, 0)
    return pl.pallas_call(
        functools.partial(backward_kernel, pack),
        grid=(GROUPS,),
        out_shape=[
            jax.ShapeDtypeStruct((pack, width), jnp.float32),
            jax.ShapeDtypeStruct(weight.shape, jnp.bfloat16),
        ],
        in_specs=[
            pl.BlockSpec((pack, width), whole),
            pl.BlockSpec((pack, width), whole),
            pl.BlockSpec((1, 384, 768), each),
            pl.BlockSpec((1, reach, 384), each),
        ],
        out_specs=[
            pl.BlockSpec((pack, width), whole),
            pl.BlockSpec((1, 384, 768), each),
        ],
        scratch_shapes=[
            pltpu.VMEM((reach, width + LANES), jnp.float32),
            pltpu.VMEM((pack + KERNEL - FINE, 384), jnp.float32),
            pltpu.VMEM((pack, width + LANES), jnp.float32),
        ],
        compiler_params=pltpu.CompilerParams(vmem_limit_bytes=40 << 20),
    )(grads, direct, weight, patches)


HEAD_DIM = 64
EPSILON = 1e-05
ROWS = 32
TILE = 256


def dot(a, b, contract=(1, 0)):
    return lax.dot_general(
        a, b, ((contract[:1], contract[1:]), ((), ())), preferred_element_type=jnp.float32
    )


def gelu(values):
    return values * (0.5 * (1.0 + lax.erf(values * 0.7071067811865476)))


def gelu_slope(values):
    cumulative = 0.5 * (1.0 + lax.erf(values * 0.7071067811865476))
    density = jnp.exp(-0.5 * values * values) * 0.3989422804014327
    return cumulative + values * density


def unit_norm(values):
    centered = values - jnp.mean(values, axis=-1, keepdims=True)
    inverse = lax.rsqrt(jnp.mean(centered * centered, axis=-1, keepdims=True) + EPSILON)
    return centered * inverse, inverse


def norm_back(grad, unit, inverse, gain):
    scaled = grad * gain
    inner = jnp.mean(scaled, axis=-1, keepdims=True)
    along = jnp.mean(scaled * unit, axis=-1, keepdims=True)
    return inverse * (scaled - inner - unit * along)


def row_tiles(pack, body):
    @pl.loop(0, pack // ROWS)
    def _(tile):
        body(pl.ds(pl.multiple_of(tile * ROWS, ROWS), ROWS))


def lane_tiles(count, body, first=0):
    @pl.loop(first, count)
    def _(tile):
        body(tile, pl.ds(pl.multiple_of(tile * TILE, TILE), TILE))


def clip_mask(lengths, micro, pack):
    row = lax.broadcasted_iota(jnp.int32, (pack, pack), 0)
    column = lax.broadcasted_iota(jnp.int32, (pack, pack), 1)
    row_clip, column_clip = jnp.zeros_like(row), jnp.zeros_like(column)
    end = 0
    for clip in range(lengths.shape[1]):
        end = end + lengths[micro, clip]
        row_clip += (row >= end).astype(jnp.int32)
        column_clip += (column >= end).astype(jnp.int32)
    return row_clip == column_clip


def front_norm(frames, convolved, gains, normed, normed_low, unit, inverse):
    def body(rows):
        mixed = frames[rows, :].astype(jnp.float32) + gelu(convolved[rows, :])
        units, inv = unit_norm(mixed)
        unit[rows, :] = units
        inverse[rows, :] = jnp.broadcast_to(inv, (ROWS, LANES))
        total = units * gains[0:1, :]
        normed[rows, :] = total
        normed_low[rows, :] = total.astype(normed_low.dtype)

    row_tiles(frames.shape[0], body)


def project(normed_low, weight, projected):
    def body(tile, lanes):
        projected[:, lanes] = dot(normed_low[...], weight[:, lanes]).astype(projected.dtype)

    lane_tiles(projected.shape[1] // TILE, body)


def pair_parts(projected, pair, width):
    return [
        projected[:, pl.ds(pl.multiple_of(part * width + pair * LANES, LANES), LANES)] for part in range(3)
    ]


def attend(projected, lengths, micro, probs, attended, first=0, last=None):
    pack, width = attended.shape
    low = projected.dtype
    scale = HEAD_DIM ** (-0.5)

    @pl.loop(first, last or width // LANES)
    def _(pair):
        same = clip_mask(lengths, micro, pack)
        queries, keys, values = pair_parts(projected, pair, width)
        lane = lax.broadcasted_iota(jnp.int32, (pack, LANES), 1)
        sides = []
        for side in range(2):
            own = (lane < HEAD_DIM) == (side == 0)
            scores = dot(jnp.where(own, queries, jnp.zeros_like(queries)), keys, (1, 1)) * scale
            scores = jnp.where(same, scores, -1e30)
            shifted = jnp.exp(scores - jnp.max(scores, axis=-1, keepdims=True))
            weights = shifted / jnp.sum(shifted, axis=-1, keepdims=True)
            probs[2 * pair + side] = weights
            sides.append(dot(weights.astype(low), values))
        lanes = pl.ds(pl.multiple_of(pair * LANES, LANES), LANES)
        attended[:, lanes] = jnp.where(lane < HEAD_DIM, *sides).astype(low)


def middle_norm(attended, weight, normed, gains, middle, middle_low, unit, inverse):
    def body(tile, lanes):
        middle[:, lanes] = normed[:, lanes] + dot(attended[...], weight[:, lanes])

    lane_tiles(normed.shape[1] // TILE, body)

    def finish(rows):
        units, inv = unit_norm(middle[rows, :])
        unit[rows, :] = units
        inverse[rows, :] = jnp.broadcast_to(inv, (ROWS, LANES))
        total = units * gains[1:2, :]
        middle[rows, :] = total
        middle_low[rows, :] = total.astype(middle_low.dtype)

    row_tiles(normed.shape[0], finish)


def feed_up(middle_low, weight, hidden, activated, first=0, last=None):
    def body(tile, lanes):
        values = dot(middle_low[...], weight[:, lanes])
        hidden[:, lanes] = values
        activated[:, lanes] = gelu(values).astype(activated.dtype)

    lane_tiles(last or hidden.shape[1] // TILE, body, first)


def feed_down(activated, weight, middle, gains, cotangent, output, grad_final, gain_grads):
    def body(tile, lanes):
        middle[...] += dot(activated[:, lanes], weight[lanes, :])

    lane_tiles(activated.shape[1] // TILE, body)
    gain_grads[2:3, :] = jnp.zeros((1, middle.shape[1]), jnp.float32)

    def finish(rows):
        units, inv = unit_norm(middle[rows, :])
        gain = gains[2:3, :]
        output[rows, :] = (units * gain).astype(output.dtype)
        grad = cotangent[rows, :].astype(jnp.float32)
        gain_grads[2:3, :] += jnp.sum(grad * units, axis=0, keepdims=True)
        grad_final[rows, :] = norm_back(grad, units, inv, gain)

    row_tiles(middle.shape[0], finish)


def feed_back(grad, hidden, activated, middle_low, up, down, up_grad, down_grad):
    low = activated.dtype
    grad_feed = grad[...].astype(low)
    turned = jnp.transpose(middle_low[...].astype(jnp.float32)).astype(low)

    def body(tile, lanes):
        down_grad[lanes, :] = dot(activated[:, lanes], grad_feed, (0, 0)).astype(low)
        slope = gelu_slope(hidden[:, lanes])
        grad_hidden = (dot(grad_feed, down[lanes, :], (1, 1)) * slope).astype(low)
        up_grad[:, lanes] = dot(turned, grad_hidden).astype(low)
        grad[...] += dot(grad_hidden, up[:, lanes], (1, 1))

    lane_tiles(hidden.shape[1] // TILE, body)


def norm_back_rows(grad, unit, inverse, gains, which, gain_grads):
    gain_grads[which : which + 1, :] = jnp.zeros((1, grad.shape[1]), jnp.float32)

    def body(rows):
        incoming, units = grad[rows, :], unit[rows, :]
        gain_grads[which : which + 1, :] += jnp.sum(incoming * units, axis=0, keepdims=True)
        grad[rows, :] = norm_back(incoming, units, inverse[rows, 0:1], gains[which : which + 1, :])

    row_tiles(grad.shape[0], body)


def branch_back(grad, attended, weight, grad_attended, out_grad):
    low = attended.dtype
    grad_branch = grad[...].astype(low)

    def body(tile, lanes):
        out_grad[lanes, :] = dot(attended[:, lanes], grad_branch, (0, 0)).astype(low)
        grad_attended[:, lanes] = dot(grad_branch, weight[lanes, :], (1, 1)).astype(low)

    lane_tiles(attended.shape[1] // TILE, body)


def attend_back(projected, grad_attended, probs, grad_projected):
    pack, width = grad_attended.shape
    low = projected.dtype
    scale = HEAD_DIM ** (-0.5)

    @pl.loop(0, width // LANES)
    def _(pair):
        queries, keys, values = pair_parts(projected, pair, width)
        grad = grad_attended[:, pl.ds(pl.multiple_of(pair * LANES, LANES), LANES)]
        lane = lax.broadcasted_iota(jnp.int32, (pack, LANES), 1)
        sides = []
        for side in range(2):
            own = (lane < HEAD_DIM) == (side == 0)
            weights = probs[2 * pair + side]
            grad_values = dot(weights.astype(low), grad, (0, 0))
            grad_probs = dot(jnp.where(own, grad, jnp.zeros_like(grad)), values, (1, 1))
            along = jnp.sum(weights * grad_probs, axis=-1, keepdims=True)
            grad_scores = (weights * (grad_probs - along)).astype(low)
            grad_queries = dot(grad_scores, keys) * scale
            grad_keys = dot(grad_scores, queries, (0, 0)) * scale
            sides.append((grad_queries, grad_keys, grad_values))
        for part in range(3):
            lanes = pl.ds(pl.multiple_of(part * width + pair * LANES, LANES), LANES)
            grad_projected[:, lanes] = jnp.where(lane < HEAD_DIM, sides[0][part], sides[1][part]).astype(low)


def project_back(grad, grad_projected, unit, gains, weight, qkv_grad):
    low = grad_projected.dtype
    turned = jnp.transpose(unit[...] * gains[0:1, :]).astype(low)

    def body(tile, lanes):
        qkv_grad[:, lanes] = dot(turned, grad_projected[:, lanes]).astype(low)
        grad[...] += dot(grad_projected[:, lanes], weight[:, lanes], (1, 1))

    lane_tiles(grad_projected.shape[1] // TILE, body)


def slope_rows(grad, convolved, grad_convolved):
    def body(rows):
        grad_convolved[rows, :] = (grad[rows, :] * gelu_slope(convolved[rows, :])).astype(grad_convolved.dtype)

    row_tiles(grad.shape[0], body)


def middle_forward_kernel(
    lengths, frames, convolved, gains, wide, down, cotangent,
    output, grad_final, unit_front, inverse_front, projected, probs, attended,
    unit_middle, inverse_middle, middle_low, hidden, activated, gain_grads,
    normed, normed_low, middle,
):
    width = frames.shape[1]
    gain_grads[...] = jnp.zeros_like(gain_grads)
    front_norm(frames, convolved, gains, normed, normed_low, unit_front, inverse_front)
    project(normed_low, wide.at[:, 0 : 3 * width], projected)
    attend(projected, lengths, 0, probs, attended)
    middle_norm(
        attended, wide.at[:, 3 * width : 4 * width], normed, gains, middle, middle_low, unit_middle,
        inverse_middle,
    )
    feed_up(middle_low, wide.at[:, 4 * width :], hidden, activated)
    feed_down(activated, down, middle, gains, cotangent, output, grad_final, gain_grads)


def middle_backward_kernel(
    gains, wide, down, convolved, grad_final, unit_front, inverse_front, projected, probs, attended,
    unit_middle, inverse_middle, middle_low, hidden, activated, last_gain_grad,
    grad, grad_convolved, wide_grad, down_grad, gain_grads,
    grad_attended, grad_projected,
):
    width = grad.shape[1]
    gain_grads[...] = last_gain_grad[...]
    grad[...] = grad_final[...]
    feed_back(
        grad, hidden, activated, middle_low, wide.at[:, 4 * width :], down, wide_grad.at[:, 4 * width :],
        down_grad,
    )
    norm_back_rows(grad, unit_middle, inverse_middle, gains, 1, gain_grads)
    branch_back(
        grad, attended, wide.at[:, 3 * width : 4 * width], grad_attended,
        wide_grad.at[:, 3 * width : 4 * width],
    )
    attend_back(projected, grad_attended, probs, grad_projected)
    project_back(
        grad, grad_projected, unit_front, gains, wide.at[:, 0 : 3 * width], wide_grad.at[:, 0 : 3 * width]
    )
    norm_back_rows(grad, unit_front, inverse_front, gains, 0, gain_grads)
    slope_rows(grad, convolved, grad_convolved)


def middle_forward(frames, convolved, lengths, gains, wide, down, cotangent):
    pack, width = frames.shape
    inner = down.shape[0]
    heads = width // HEAD_DIM
    low, full = jnp.bfloat16, jnp.float32
    shape = jax.ShapeDtypeStruct
    vmem = pl.BlockSpec(memory_space=pltpu.VMEM)
    saved = [
        shape((pack, width), low),
        shape((pack, width), full),
        shape((pack, width), full),
        shape((pack, LANES), full),
        shape((pack, 3 * width), low),
        shape((heads, pack, pack), full),
        shape((pack, width), low),
        shape((pack, width), full),
        shape((pack, LANES), full),
        shape((pack, width), low),
        shape((pack, inner), full),
        shape((pack, inner), low),
        shape((8, width), full),
    ]
    return pl.pallas_call(
        middle_forward_kernel,
        out_shape=saved,
        in_specs=[pl.BlockSpec(memory_space=pltpu.SMEM)] + [vmem] * 6,
        out_specs=[vmem] * len(saved),
        scratch_shapes=[
            pltpu.VMEM((pack, width), full),
            pltpu.VMEM((pack, width), low),
            pltpu.VMEM((pack, width), full),
        ],
        compiler_params=pltpu.CompilerParams(vmem_limit_bytes=58 << 20),
    )(lengths, frames, convolved, gains, wide, down, cotangent)


def middle_backward(gains, wide, down, convolved, kept):
    pack, width = convolved.shape
    low, full = jnp.bfloat16, jnp.float32
    shape = jax.ShapeDtypeStruct
    vmem = pl.BlockSpec(memory_space=pltpu.VMEM)
    grads = [
        shape((pack, width), full),
        shape((pack, width), low),
        shape(wide.shape, low),
        shape(down.shape, low),
        shape((8, width), full),
    ]
    return pl.pallas_call(
        middle_backward_kernel,
        out_shape=grads,
        in_specs=[vmem] * (4 + len(kept)),
        out_specs=[vmem] * len(grads),
        scratch_shapes=[pltpu.VMEM((pack, width), low), pltpu.VMEM((pack, 3 * width), low)],
        compiler_params=pltpu.CompilerParams(vmem_limit_bytes=58 << 20),
    )(gains, wide, down, convolved, *kept)


def weave(tasks, pieces):
    core_index = lax.axis_index("seq")
    count, done = len(tasks[0]), 0
    for number, piece in enumerate(pieces + [None]):
        until = count if piece is None else (number + 1) * count // (len(pieces) + 1)

        def some(core, first=done, last=until):
            for task in tasks[core][first:last]:
                task()

        if until > done:
            by_core(core_index, some)
        done = until
        if piece is not None:
            piece()


def fused_forward_kernel(
    dims, chunks,
    lengths, frames, cotangent, conv_shard, wide_shard, down_shard, gain_shard,
    conv_out, wide_out, down_out, both_output, patches, gains, convolved,
    grad_final, unit_front, inverse_front, projected, probs, attended, unit_middle, inverse_middle,
    middle_low, hidden, activated, gain_grads,
    conv_all, wide_all, down_all, gain_all, pack_frames, pack_cotangent, output, padded, total,
    gains_wide, normed, normed_low, middle,
    send_sems, recv_sems, push_send, push_recv, local_sems, pair_sems,
):
    ins = (conv_shard, wide_shard, down_shard, gain_shard)
    outs = (conv_all, wide_all, down_all, gain_all)
    gather = Gather(dims, chunks, ins, outs, (send_sems, recv_sems, push_send, push_recv))
    core_index = lax.axis_index("seq")
    me = lax.axis_index("dp")
    pack, width = pack_frames.shape
    half = pack // 2
    greet(dims, gather.position, core_index)

    here = pl.ds(pl.multiple_of(core_index * half, half), half)
    there = pl.ds(pl.multiple_of((1 - core_index) * half, half), half)

    def to_partner(source, target, number):
        return pltpu.make_async_remote_copy(
            src_ref=source,
            dst_ref=target,
            send_sem=pair_sems.at[0, number],
            recv_sem=pair_sems.at[1, number],
            device_id={"seq": 1 - core_index},
            device_id_type=MESH,
        )

    moves = []
    for number, (source, target) in enumerate(((frames, pack_frames), (cotangent, pack_cotangent))):
        moves.append(to_partner(source.at[1 - core_index], target.at[here], number))
        moves.append(pltpu.make_async_copy(source.at[core_index], target.at[here], local_sems.at[number]))
    for copy in moves:
        copy.start()
    own = [
        pltpu.make_async_copy(ins[i], gather.whole(me, i), local_sems.at[2 + i]) for i in range(len(ins))
    ]
    for copy in own:
        copy.start()

    def early(core):
        for chunk in range(3):
            for task in gather.tasks(core, chunk, 0):
                task()

    by_core(core_index, early)
    steps = []
    for step in range(1, len(chunks) + 3):
        both = []
        for core in range(2):
            tasks = []
            if 3 <= step + 2 < len(chunks):
                tasks += gather.tasks(core, step + 2, 0)
            for stage in (1, 2, 3):
                if 0 <= step - stage < len(chunks):
                    tasks += gather.tasks(core, step - stage, stage)
            both.append(tasks)
        steps.append(both)

    def gate(*numbers):
        def body(core):
            for number in numbers:
                gather.arrived(core, number)

        by_core(core_index, body)

    for copy in moves[:2]:
        copy.wait()
    fill_padded(padded, pack_frames)
    total[...] = jnp.zeros_like(total)

    def patch_piece(first, last):
        def piece():
            @pl.loop(first, last)
            def _(group):
                patches[group] = make_patch(padded, group, pack)

        return piece

    def conv_piece(first, last):
        def piece():
            @pl.loop(first, last)
            def _(group):
                add_forward(total, patches[group], conv_all[group], group, pack)

        return piece

    quarter = GROUPS // 4
    early_pieces = [patch_piece(i * quarter, (i + 1) * quarter) for i in range(4)]
    weave(steps[0], early_pieces[:1])
    weave(steps[1], early_pieces[1:3])
    weave(steps[2], early_pieces[3:])
    weave(steps[3], [])
    weave(steps[4], [])
    for copy in own:
        copy.wait()
    gate(0, 1, 2)
    saves = [pltpu.make_async_copy(a, b, local_sems.at[6 + i]) for i, (a, b) in enumerate(
        ((conv_all, conv_out), (wide_all, wide_out), (down_all, down_out)))]
    saves[0].start()
    gains_wide[...] = jnp.zeros_like(gains_wide)

    @pl.loop(0, gather.count)
    def _(shard):
        add_group(gains_wide, gain_all[shard, 0:16, :].astype(jnp.float32), shard, width // gather.count)

    gains[...] = gains_wide[0:8, 0:width]
    weave(steps[5], [conv_piece(i, i + 2) for i in range(0, GROUPS, 2)])

    def front_piece():
        convolved[...] = total[:, :width]
        front_norm(pack_frames, convolved, gains, normed, normed_low, unit_front, inverse_front)

    def project_piece():
        gate(3)
        project(normed_low, wide_all.at[:, 0 : 3 * width], projected)

    def attend_piece(first, last):
        return lambda: attend(projected, lengths, core_index, probs, attended, first, last)

    def middle_piece():
        middle_norm(
            attended, wide_all.at[:, 3 * width : 4 * width], normed, gains, middle, middle_low, unit_middle,
            inverse_middle,
        )

    pairs = width // LANES
    weave(
        steps[6],
        [front_piece, project_piece]
        + [attend_piece(i, i + 2) for i in range(0, pairs, 2)]
        + [middle_piece],
    )
    up = wide_all.at[:, 4 * width :]
    count = hidden.shape[1] // TILE
    third = count // 3

    def up_piece(first):
        def piece():
            if first == 0:
                gate(4)
                saves[1].start()
            feed_up(middle_low, up, hidden, activated, first, first + third)

        return piece

    weave(steps[7], [up_piece(i) for i in range(0, count, third)])
    gate(5)
    saves[2].start()
    for copy in moves[2:]:
        copy.wait()
    gain_grads[...] = jnp.zeros_like(gain_grads)
    feed_down(activated, down_all, middle, gains, pack_cotangent, output, grad_final, gain_grads)
    last = to_partner(output.at[there], both_output.at[core_index], 2)
    last.start()
    stay = pltpu.make_async_copy(output.at[here], both_output.at[core_index], local_sems.at[9])
    stay.start()
    by_core(core_index, gather.finish)
    for copy in saves + [stay, last]:
        copy.wait()


def fused_forward(frames, cotangent, lengths, shards_in, chunks, dp):
    dims = dp_factors(dp)
    n = len(chunks)
    conv_shard, wide_shard, down_shard, gain_shard = shards_in
    pack, width = 2 * frames.shape[1], frames.shape[2]
    inner = down_shard.shape[0] * dp
    heads = width // HEAD_DIM
    low, full = jnp.bfloat16, jnp.float32
    shape = jax.ShapeDtypeStruct
    vmem = pl.BlockSpec(memory_space=pltpu.VMEM)
    any_ = pl.BlockSpec(memory_space=pl.ANY)
    conv_shape = (dp,) + conv_shard.shape
    wide_shape = (width, wide_shard.shape[1])
    down_shape = (inner, width)
    tall = pack + FINE
    saved = [
        shape(frames.shape, low),
        shape((GROUPS, tall, 384), low),
        shape((8, width), full),
        shape((pack, width), full),
        shape((pack, width), full),
        shape((pack, width), full),
        shape((pack, LANES), full),
        shape((pack, 3 * width), low),
        shape((heads, pack, pack), full),
        shape((pack, width), low),
        shape((pack, width), full),
        shape((pack, LANES), full),
        shape((pack, width), low),
        shape((pack, inner), full),
        shape((pack, inner), low),
        shape((8, width), full),
    ]
    return pl.pallas_call(
        functools.partial(fused_forward_kernel, dims, chunks),
        out_shape=[shape(conv_shape, low), shape(wide_shape, low), shape(down_shape, low)] + saved,
        in_specs=[pl.BlockSpec(memory_space=pltpu.SMEM)] + [any_] * 6,
        out_specs=[any_] * 3 + [vmem] * len(saved),
        scratch_shapes=[
            pltpu.VMEM(conv_shape, low),
            pltpu.VMEM(wide_shape, low),
            pltpu.VMEM(down_shape, low),
            pltpu.VMEM((dp,) + gain_shard.shape, low),
            pltpu.VMEM((pack, width), low),
            pltpu.VMEM((pack, width), low),
            pltpu.VMEM((pack, width), low),
            pltpu.VMEM((pack + KERNEL, width + LANES), full),
            pltpu.VMEM((pack, width + LANES), full),
            pltpu.VMEM((16, width + LANES), full),
            pltpu.VMEM((pack, width), full),
            pltpu.VMEM((pack, width), low),
            pltpu.VMEM((pack, width), full),
            pltpu.SemaphoreType.DMA((n, dp)),
            pltpu.SemaphoreType.DMA((n, dp)),
            pltpu.SemaphoreType.DMA((n, dp)),
            pltpu.SemaphoreType.DMA((n, dp)),
            pltpu.SemaphoreType.DMA((10,)),
            pltpu.SemaphoreType.DMA((2, 3)),
        ],
        compiler_params=pltpu.CompilerParams(
            collective_id=2, has_side_effects=True, vmem_limit_bytes=60 << 20
        ),
    )(lengths, frames, cotangent, *shards_in)


GAIN_ROWS = 16


def chunks_of(conv_rows, conv_lanes, wide_rows, width, down_rows):
    both = range(2)
    quarter, half = conv_rows // 4, width // 2
    conv = [
        [(0, ((2 * part + core) * quarter, quarter), (0, conv_lanes)) for core in both] for part in both
    ]
    wide = [
        [(1, (0, wide_rows), ((2 * part + core) * 2 * width, 2 * width)) for core in both] for part in both
    ]
    down = [[(2, (0, down_rows), (core * half, half)) for core in both]]
    gain = [[(3, (core * GAIN_ROWS, GAIN_ROWS), (0, LANES)) for core in both]]
    return gain, conv, wide, down


def shards(
    frames,
    clip_lengths,
    conv_weight,
    front_gain,
    qkv_weight,
    out_weight,
    middle_gain,
    up_weight,
    down_weight,
    final_gain,
    cotangent,
):
    dp = lax.axis_size("dp")
    low = jnp.bfloat16
    width = frames.shape[2]
    columns = conv_weight.shape[2]
    group_width = conv_weight.shape[1]
    gain_width = front_gain.shape[0]
    conv_shard = (
        conv_weight.reshape(COARSE, FINE, group_width, columns)
        .transpose(0, 2, 1, 3)
        .reshape(COARSE * group_width, FINE * columns)
    )
    wide_shard = jnp.concatenate([qkv_weight, out_weight, up_weight], axis=1)
    gain_shard = jnp.pad(
        jnp.stack([front_gain, middle_gain, final_gain]),
        ((0, 2 * GAIN_ROWS - 3), (0, LANES - gain_width)),
    )
    parts = (conv_shard, wide_shard, down_weight, gain_shard)
    gain_chunk, conv_chunks, wide_chunks, down_chunk = chunks_of(
        *conv_shard.shape, wide_shard.shape[0], width, down_weight.shape[0]
    )
    chunks = gain_chunk + conv_chunks + wide_chunks + down_chunk
    split = group_width // columns
    if split == 1:
        (weight, wide, down, outputs, patches, gains, convolved, *kept) = fused_forward(
            frames, cotangent, clip_lengths[:, 0], parts, chunks, dp
        )
    else:
        conv_all, wide_all, down_all, gain_all = all_gather(parts, chunks, dp)
        weight = (
            conv_all.reshape(GROUPS, split, COARSE * group_width, FINE, columns)
            .transpose(0, 2, 3, 1, 4)
            .reshape(GROUPS, COARSE * group_width, FINE * group_width)
        )
        wide = wide_all.reshape(width, wide_shard.shape[1])
        down = down_all.reshape(-1, width)
        gains = gain_all[:, :3, :gain_width].transpose(1, 0, 2).reshape(3, width).astype(jnp.float32)
        gains = jnp.pad(gains, ((0, 5), (0, 0)))
        both = lax.all_to_all(
            jnp.stack([frames, cotangent], axis=1), "seq", split_axis=0, concat_axis=2, tiled=True
        )
        pack_frames, pack_cotangent = both[0, 0], both[0, 1]
        lengths = lax.dynamic_index_in_dim(clip_lengths[:, 0], lax.axis_index("seq"), 0)
        convolved, patches = conv_forward(pack_frames, weight)
        output, *kept = middle_forward(
            pack_frames, convolved, lengths, gains, wide, down, pack_cotangent
        )
        outputs = lax.all_to_all(output[None], "seq", split_axis=1, concat_axis=0, tiled=True)

    grad_mixed, grad_convolved, wide_grad, down_grad, gain_grads = middle_backward(
        gains, wide, down, convolved, kept
    )
    frame_grad, conv_grad = conv_backward(grad_convolved, grad_mixed, weight, patches)

    conv_blocks = (
        conv_grad.reshape(GROUPS, COARSE * group_width, FINE, split, columns)
        .transpose(0, 3, 1, 2, 4)
        .reshape((dp,) + conv_shard.shape)
    )
    gain_blocks = jnp.pad(
        gain_grads[:3].astype(low).reshape(3, dp, gain_width).transpose(1, 0, 2),
        ((0, 0), (0, 2 * GAIN_ROWS - 3), (0, LANES - gain_width)),
    )
    conv_sum, wide_sum, down_sum, gain_sum = reduce_scatter(
        (
            conv_blocks,
            wide_grad.reshape((dp,) + wide_shard.shape),
            down_grad.reshape((dp,) + down_weight.shape),
            gain_blocks,
        ),
        gain_chunk + down_chunk + wide_chunks[::-1] + conv_chunks,
        dp,
    )
    conv_sum = (
        conv_sum.reshape(COARSE, group_width, FINE, columns)
        .transpose(0, 2, 1, 3)
        .reshape(conv_weight.shape)
    )
    frame_grads = lax.all_to_all(frame_grad[None], "seq", split_axis=1, concat_axis=0, tiled=True)
    return (
        outputs,
        frame_grads,
        conv_sum,
        gain_sum[0, :gain_width],
        wide_sum[:, : 3 * width],
        wide_sum[:, 3 * width : 4 * width],
        gain_sum[1, :gain_width],
        wide_sum[:, 4 * width :],
        down_sum,
        gain_sum[2, :gain_width],
    )


def solution(mesh):
    frames_spec = P(None, ("dp", "seq"), None)
    row, matrix, columns = P("dp"), P("dp", None), P(None, None, "dp")
    return jax.shard_map(
        shards,
        mesh=mesh,
        in_specs=(
            frames_spec,
            P(None, "dp", None),
            columns,
            row,
            matrix,
            matrix,
            row,
            matrix,
            matrix,
            row,
            frames_spec,
        ),
        out_specs=(
            frames_spec,
            frames_spec,
            columns,
            row,
            matrix,
            matrix,
            row,
            matrix,
            matrix,
            row,
        ),
        check_vma=False,
    )
```

```python
import functools

import jax
import jax.numpy as jnp
from jax import lax
from jax.experimental import pallas as pl
from jax.experimental.pallas import tpu as pltpu
from jax.sharding import PartitionSpec as P

MESH = pl.DeviceIdType.MESH


def dp_factors(size):
    return {16: (4, 2, 2), 128: (4, 4, 8)}.get(size, (size, 1, 1))


def offsets_of(dims):
    return [(i, j, k) for i in range(dims[0]) for j in range(dims[1]) for k in range(dims[2])]


def place(dims, order, position, offsets):
    coords = list(position)
    for axis, offset in zip(order, offsets):
        if offset:
            coords[axis] = lax.rem(coords[axis] + offset, dims[axis])
    return (coords[0] * dims[1] + coords[1]) * dims[2] + coords[2]


def position_of(dims):
    me = lax.axis_index("dp")
    return (me // (dims[1] * dims[2]), lax.rem(me // dims[2], dims[1]), lax.rem(me, dims[2]))


def greet(dims, position, core):
    barrier = pltpu.get_barrier_semaphore()
    count = 1
    pl.semaphore_signal(barrier, inc=1, device_id={"seq": 1 - core}, device_id_type=MESH)
    for axis in range(3):
        for offset in range(1, dims[axis]):
            other = place(dims, (axis,), position, (offset,))
            pl.semaphore_signal(barrier, inc=1, device_id={"dp": other}, device_id_type=MESH)
            count += 1
    pl.semaphore_wait(barrier, count)


ORDERS = ((0, 1, 2), (0, 2, 1))


def by_core(core_index, body):
    for core in range(2):
        pl.when(core_index == core)(functools.partial(body, core))


class Gather:
    def __init__(self, dims, chunks, ins, outs, sems):
        self.dims, self.chunks, self.ins, self.outs = dims, chunks, ins, outs
        self.send_sems, self.recv_sems, self.push_send, self.push_recv = sems
        self.position = position_of(dims)
        self.count = dims[0] * dims[1] * dims[2]
        self.sent = {}

    def part(self, which, chunk, side):
        array, rows, lanes = self.chunks[chunk][side]
        out = self.outs[array]
        if len(out.shape) == 3:
            return out.at[which, pl.ds(*rows), pl.ds(*lanes)]
        first = pl.multiple_of(which * self.ins[array].shape[0] + rows[0], 16)
        return out.at[pl.ds(first, rows[1]), pl.ds(*lanes)]

    def whole(self, which, array):
        out, height = self.outs[array], self.ins[array].shape[0]
        if len(out.shape) == 3:
            return out.at[which]
        return out.at[pl.ds(pl.multiple_of(which * height, 16), height)]

    def send(self, core, chunk, offsets, level, distance):
        order = ORDERS[core]
        gid = place(self.dims, order, self.position, offsets)
        array, rows, lanes = self.chunks[chunk][core]
        mine = self.ins[array].at[pl.ds(*rows), pl.ds(*lanes)]
        number = self.sent.get((core, chunk), 0)
        self.sent[core, chunk] = number + 1
        pltpu.make_async_remote_copy(
            src_ref=mine if offsets == (0, 0, 0) else self.part(gid, chunk, core),
            dst_ref=self.part(gid, chunk, core),
            send_sem=self.send_sems.at[chunk, number],
            recv_sem=self.recv_sems.at[chunk, gid],
            device_id={"dp": place(self.dims, (order[level],), self.position, (distance,))},
            device_id_type=MESH,
        ).start()

    def spread(self, core, chunk, offsets, first):
        for level in range(first, 3):
            for distance in range(1, self.dims[ORDERS[core][level]]):
                self.send(core, chunk, offsets, level, distance)

    def forward(self, core, chunk, offsets, first):
        gid = place(self.dims, ORDERS[core], self.position, offsets)
        ref = self.part(gid, chunk, core)
        pltpu.make_async_copy(ref, ref, self.recv_sems.at[chunk, gid]).wait()
        self.spread(core, chunk, offsets, first)
        pltpu.make_async_remote_copy(
            src_ref=ref,
            dst_ref=ref,
            send_sem=self.push_send.at[chunk, gid],
            recv_sem=self.push_recv.at[chunk, gid],
            device_id={"seq": 1 - core},
            device_id_type=MESH,
        ).start()

    def tasks(self, core, chunk, stage):
        sizes = [self.dims[axis] for axis in ORDERS[core]]
        if stage == 0:
            return [functools.partial(self.spread, core, chunk, (0, 0, 0), 0)]
        if stage == 1:
            places = [(i, 0, 0) for i in range(1, sizes[0])]
        elif stage == 2:
            places = [(i, j, 0) for i in range(sizes[0]) for j in range(1, sizes[1])]
        else:
            places = [o for o in offsets_of(sizes) if o[2]]
        return [functools.partial(self.forward, core, chunk, offsets, stage) for offsets in places]

    def steps(self, core, step):
        done = []
        for stage in range(4):
            if 0 <= step - stage < len(self.chunks):
                done += self.tasks(core, step - stage, stage)
        return done

    def others(self, body):
        me = lax.axis_index("dp")

        @pl.loop(1, self.count)
        def _(offset):
            body(lax.rem(me + offset, self.count), offset)

    def arrived(self, core, chunk):
        def body(gid, _):
            ref = self.part(gid, chunk, 1 - core)
            pltpu.make_async_copy(ref, ref, self.push_recv.at[chunk, gid]).wait()

        self.others(body)

    def finish(self, core):
        for chunk in range(len(self.chunks)):

            def body(gid, number, chunk=chunk):
                ref = self.part(gid, chunk, core)
                pltpu.make_async_copy(ref, ref, self.push_send.at[chunk, gid]).wait()
                pltpu.make_async_copy(ref, ref, self.send_sems.at[chunk, number - 1]).wait()

            self.others(body)


def gather_kernel(dims, chunks, *refs):
    n_arr = len(refs[:-5]) // 2
    ins, outs = refs[:n_arr], refs[n_arr : 2 * n_arr]
    gather = Gather(dims, chunks, ins, outs, refs[2 * n_arr : 2 * n_arr + 4])
    local_sems = refs[-1]
    core_index = lax.axis_index("seq")
    greet(dims, gather.position, core_index)
    own = [
        pltpu.make_async_copy(ins[i], outs[i].at[lax.axis_index("dp")], local_sems.at[i])
        for i in range(n_arr)
    ]
    for copy in own:
        copy.start()

    def run(core):
        for step in range(len(chunks) + 3):
            for task in gather.steps(core, step):
                task()
        for chunk in range(len(chunks)):
            gather.arrived(core, chunk)
        gather.finish(core)

    by_core(core_index, run)
    for copy in own:
        copy.wait()


def all_gather(arrays, chunks, dp, collective_id=0):
    dims = dp_factors(dp)
    n = len(chunks)
    any_ = pl.BlockSpec(memory_space=pl.ANY)
    return pl.pallas_call(
        functools.partial(gather_kernel, dims, chunks),
        out_shape=[jax.ShapeDtypeStruct((dp,) + a.shape, a.dtype) for a in arrays],
        in_specs=[any_] * len(arrays),
        out_specs=[any_] * len(arrays),
        scratch_shapes=[
            pltpu.SemaphoreType.DMA((n, dp)),
            pltpu.SemaphoreType.DMA((n, dp)),
            pltpu.SemaphoreType.DMA((n, dp)),
            pltpu.SemaphoreType.DMA((n, dp)),
            pltpu.SemaphoreType.DMA((len(arrays),)),
        ],
        compiler_params=pltpu.CompilerParams(collective_id=collective_id, has_side_effects=True),
    )(*arrays)


def scatter_kernel(dims, chunks, n_arr, *refs):
    ins, outs = refs[:n_arr], refs[n_arr : 2 * n_arr]
    scratch = list(refs[2 * n_arr :])
    n = len(chunks)
    stage_refs, pair_refs = scratch[:n], scratch[n : 2 * n]
    hop_refs = [scratch[(2 + level) * n : (3 + level) * n] for level in range(3)]
    (load_sems, pair_send, pair_recv, hop_send, hop_recv, last_send, last_recv) = scratch[5 * n :]
    position = position_of(dims)
    core_index = lax.axis_index("seq")
    greet(dims, position, core_index)

    def run(core):
        order = ORDERS[core]
        sizes = [dims[axis] for axis in order]
        started = []
        other_order = ORDERS[1 - core]
        other_sizes = [dims[axis] for axis in other_order]

        def part(array_refs, which, chunk, side):
            array, rows, lanes = chunks[chunk][side]
            return array_refs[array].at[which, pl.ds(*rows), pl.ds(*lanes)]

        def slot(level, offsets, distance):
            index = distance - 1
            for i in range(level):
                index = index * sizes[i] + offsets[i]
            return index

        def semaphore(level, index):
            return (1, sizes[0], sizes[0] * sizes[1])[level] + index - 1

        def begin(chunk):
            array = chunks[chunk][core][0]
            theirs = sorted(offsets_of(other_sizes), key=lambda o: (o[2] == 0, o[1] == 0, o[0] == 0))
            mine = sorted(offsets_of(sizes), key=lambda o: (o[2] == 0, o[1] == 0, o[0] == 0))
            for given, kept in zip(theirs, mine):
                gid = place(dims, other_order, position, given)
                copy = pltpu.make_async_remote_copy(
                    src_ref=part(ins, gid, chunk, 1 - core),
                    dst_ref=pair_refs[chunk].at[gid],
                    send_sem=pair_send.at[chunk],
                    recv_sem=pair_recv.at[chunk, gid],
                    device_id={"seq": 1 - core},
                    device_id_type=MESH,
                )
                copy.start()
                gid = place(dims, order, position, kept)
                pltpu.make_async_copy(
                    part(ins, gid, chunk, core), stage_refs[chunk].at[gid], load_sems.at[chunk, gid]
                ).start()

        def combine(chunk, offsets, target):
            gid = place(dims, order, position, offsets)
            own = stage_refs[chunk].at[gid]
            pair = pair_refs[chunk].at[gid]
            pltpu.make_async_copy(own, own, load_sems.at[chunk, gid]).wait()
            pltpu.make_async_copy(pair, pair, pair_recv.at[chunk, gid]).wait()
            terms = [own, pair]
            for level in (2, 1, 0):
                if offsets[level]:
                    break
                for distance in range(1, sizes[level]):
                    index = slot(level, offsets, distance)
                    ref = hop_refs[level][chunk].at[index]
                    pltpu.make_async_copy(ref, ref, hop_recv.at[chunk, semaphore(level, index)]).wait()
                    terms.append(ref)
            height = own.shape[0]

            tall = 16 if height % 16 == 0 else height

            @pl.loop(0, height // tall)
            def _(tile):
                rows = pl.ds(pl.multiple_of(tile * tall, tall), tall)
                total = terms[0][rows, :].astype(jnp.float32)
                for term in terms[1:]:
                    total = total + term[rows, :].astype(jnp.float32)
                if target is None:
                    own[rows, :] = total.astype(own.dtype)
                else:
                    target[rows, :] = total

            return gid

        def send(chunk, offsets):
            level = max(i for i in range(3) if offsets[i])
            gid = combine(chunk, offsets, None)
            index = slot(level, offsets, offsets[level])
            target = place(dims, (order[level],), position, (offsets[level],))
            copy = pltpu.make_async_remote_copy(
                src_ref=stage_refs[chunk].at[gid],
                dst_ref=hop_refs[level][chunk].at[index],
                send_sem=hop_send.at[chunk, semaphore(level, index)],
                recv_sem=hop_recv.at[chunk, semaphore(level, index)],
                device_id={"dp": target},
                device_id_type=MESH,
            )
            copy.start()
            started.append(copy)

        def final(chunk):
            array, rows, lanes = chunks[chunk][core]
            half = outs[array].at[pl.ds(*rows), pl.ds(*lanes)]
            combine(chunk, (0, 0, 0), half)
            copy = pltpu.make_async_remote_copy(
                src_ref=half,
                dst_ref=half,
                send_sem=last_send.at[chunk],
                recv_sem=last_recv.at[chunk],
                device_id={"seq": 1 - core},
                device_id_type=MESH,
            )
            copy.start()
            started.append(copy)

        for chunk in range(n):
            begin(chunk)

        def stage(chunk, number):
            if number == 0:
                for d in range(1, sizes[2]):
                    for i in range(sizes[0]):
                        for j in range(sizes[1]):
                            send(chunk, (i, (j + 1) % sizes[1], d))
            if number == 1:
                for d in range(1, sizes[1]):
                    for i in range(sizes[0]):
                        send(chunk, ((i + 1) % sizes[0], d, 0))
            if number == 2:
                for d in range(1, sizes[0]):
                    send(chunk, (d, 0, 0))
            if number == 3:
                final(chunk)

        for step in range(n + 3):
            for number in range(4):
                if 0 <= step - number < n:
                    stage(step - number, number)
        for chunk in range(n):
            array, rows, lanes = chunks[chunk][1 - core]
            half = outs[array].at[pl.ds(*rows), pl.ds(*lanes)]
            pltpu.make_async_copy(half, half, last_recv.at[chunk]).wait()
            sent = pair_refs[chunk]
            pltpu.make_async_copy(sent, sent, pair_send.at[chunk]).wait()
        for copy in started:
            copy.wait_send()

    for core in range(2):
        pl.when(core_index == core)(functools.partial(run, core))


def hop_slots(dims, core):
    a, b, c = [dims[axis] for axis in ORDERS[core]]
    return (a - 1, a * (b - 1), a * b * (c - 1))


def reduce_scatter(arrays, chunks, dp, collective_id=1):
    dims = dp_factors(dp)
    n = len(chunks)
    any_ = pl.BlockSpec(memory_space=pl.ANY)
    shapes = [(chunk[0][1][1], chunk[0][2][1]) for chunk in chunks]
    slots = [max(pair) for pair in zip(hop_slots(dims, 0), hop_slots(dims, 1))]
    low = jnp.bfloat16
    scratch = [pltpu.VMEM((dp,) + s, low) for s in shapes] * 2
    for level in range(3):
        scratch += [pltpu.VMEM((slots[level],) + s, low) for s in shapes]
    return pl.pallas_call(
        functools.partial(scatter_kernel, dims, chunks, len(arrays)),
        out_shape=[jax.ShapeDtypeStruct(a.shape[1:], jnp.float32) for a in arrays],
        in_specs=[any_] * len(arrays),
        out_specs=[pl.BlockSpec(memory_space=pltpu.VMEM)] * len(arrays),
        scratch_shapes=scratch
        + [
            pltpu.SemaphoreType.DMA((n, dp)),
            pltpu.SemaphoreType.DMA((n,)),
            pltpu.SemaphoreType.DMA((n, dp)),
            pltpu.SemaphoreType.DMA((n, dp)),
            pltpu.SemaphoreType.DMA((n, dp)),
            pltpu.SemaphoreType.DMA((n,)),
            pltpu.SemaphoreType.DMA((n,)),
        ],
        compiler_params=pltpu.CompilerParams(
            collective_id=collective_id, has_side_effects=True, vmem_limit_bytes=58 << 20
        ),
    )(*arrays)


GROUPS = 16
KERNEL = 128
FINE = 16
COARSE = KERNEL // FINE
LANES = 128


def lane_numbers(rows):
    return lax.broadcasted_iota(jnp.int32, (rows, LANES), 1)


def take_group(ref, rows, group, width):
    start = group * width
    base = pl.multiple_of(start // LANES * LANES, LANES)
    window = ref[rows, pl.ds(base, 2 * LANES)]
    turned = pltpu.roll(window, lax.rem(2 * LANES - (start - base), 2 * LANES), 1)[:, :LANES]
    return jnp.where(lane_numbers(turned.shape[0]) < width, turned, 0.0)


def add_group(ref, values, group, width):
    start = group * width
    base = pl.multiple_of(start // LANES * LANES, LANES)
    wide = jnp.concatenate([values, jnp.zeros_like(values)], axis=1)
    ref[:, pl.ds(base, 2 * LANES)] += pltpu.roll(wide, start - base, 1)


def double_96(pair, moved):
    lane = lane_numbers(pair.shape[0])
    turned = pltpu.roll(moved, 96, 1)
    return jnp.where(lane < 96, pair, turned), jnp.where(lane < 64, turned, 0.0)


def double_192(first, second, moved_first, moved_second):
    lane = lane_numbers(first.shape[0])
    a, b = pltpu.roll(moved_first, 64, 1), pltpu.roll(moved_second, 64, 1)
    return first, jnp.where(lane < 64, second, a), jnp.where(lane < 64, a, b)


def fold_lanes(tiles, shift):
    a, b, c = tiles
    lane = lane_numbers(a.shape[0])
    tb, tc = pltpu.roll(b, 64, 1), pltpu.roll(c, 64, 1)
    a, b = shift(a, jnp.where(lane < 64, tb, tc), 4), shift(b, tc, 4)
    lane = lane_numbers(a.shape[0])
    far = jnp.where(lane < 32, pltpu.roll(a, 32, 1), pltpu.roll(b, 32, 1))
    a = shift(a, far, 2)
    a = shift(a, pltpu.roll(a, 80, 1), 1)
    return jnp.where(lane_numbers(a.shape[0]) < 48, a, 0.0)


def make_patch(padded, group, pack):
    reach = pack + FINE
    one = take_group(padded, slice(0, reach + KERNEL - FINE), group, 48)
    rows = one.shape[0] - FINE
    two = one[:rows] + pltpu.roll(one[FINE:], 48, 1)
    low, high = double_96(two[: rows - 2 * FINE], two[2 * FINE :])
    tiles = double_192(low[:reach], high[:reach], low[4 * FINE :], high[4 * FINE :])
    return jnp.concatenate(tiles, axis=1).astype(jnp.bfloat16)


def add_forward(total, patch, weight, group, pack):
    product = jnp.dot(patch, weight, preferred_element_type=jnp.float32)
    size = pack + 8
    near = product[:size, :384] + product[8 : 8 + size, 384:]

    def shift(base, moved, amount):
        return base + pltpu.roll(moved, size - amount, 0)

    tiles = [near[:, i * LANES : (i + 1) * LANES] for i in range(3)]
    add_group(total, fold_lanes(tiles, shift)[:pack], group, 48)


def fill_padded(padded, frames):
    half = KERNEL // 2
    padded[...] = jnp.zeros_like(padded)
    padded[half : half + frames.shape[0], 0 : frames.shape[1]] = frames[...].astype(jnp.float32)


def forward_kernel(pack, frames, weight, out, patches, padded, total):
    group = pl.program_id(0)

    @pl.when(group == 0)
    def _():
        fill_padded(padded, frames)
        total[...] = jnp.zeros_like(total)

    patch = make_patch(padded, group, pack)
    patches[0] = patch
    add_forward(total, patch, weight[0], group, pack)

    @pl.when(group == GROUPS - 1)
    def _():
        out[...] = total[:, : frames.shape[1]]


def conv_forward(frames, weight):
    pack, width = frames.shape
    reach = pack + FINE
    return pl.pallas_call(
        functools.partial(forward_kernel, pack),
        grid=(GROUPS,),
        out_shape=[
            jax.ShapeDtypeStruct((pack, width), jnp.float32),
            jax.ShapeDtypeStruct((GROUPS, reach, 384), jnp.bfloat16),
        ],
        in_specs=[
            pl.BlockSpec((pack, width), lambda g: (0, 0)),
            pl.BlockSpec((1, 384, 768), lambda g: (g, 0, 0)),
        ],
        out_specs=[
            pl.BlockSpec((pack, width), lambda g: (0, 0)),
            pl.BlockSpec((1, reach, 384), lambda g: (g, 0, 0)),
        ],
        scratch_shapes=[
            pltpu.VMEM((pack + KERNEL, width + LANES), jnp.float32),
            pltpu.VMEM((pack, width + LANES), jnp.float32),
        ],
        compiler_params=pltpu.CompilerParams(vmem_limit_bytes=40 << 20),
    )(frames, weight)


def backward_kernel(pack, grads, direct, weight, patches, out, weight_grad, padded, tall, total):
    group = pl.program_id(0)
    reach = pack + FINE
    edge = KERNEL // 2 - FINE

    @pl.when(group == 0)
    def _():
        padded[...] = jnp.zeros_like(padded)
        padded[:pack, : grads.shape[1]] = grads[...].astype(jnp.float32)
        tall[...] = jnp.zeros_like(tall)
        total[...] = jnp.zeros_like(total)
        total[:, : direct.shape[1]] = direct[...]

    def later(values, amount):
        return pltpu.roll(values, amount, 0)

    one = take_group(padded, slice(0, reach), group, 48)
    two = one + pltpu.roll(later(one, 1), 48, 1)
    low, high = double_96(two, later(two, 2))
    tiles = double_192(low, high, later(low, 4), later(high, 4))
    near = jnp.concatenate(tiles, axis=1)
    spread = jnp.concatenate([near, later(near, 8)], axis=1).astype(jnp.bfloat16)
    weight_grad[0] = lax.dot_general(
        patches[0], spread, (((0,), (0,)), ((), ())), preferred_element_type=jnp.float32
    ).astype(jnp.bfloat16)
    tall[edge : edge + reach] = lax.dot_general(
        spread, weight[0], (((1,), (1,)), ((), ())), preferred_element_type=jnp.float32
    )

    def shift(base, moved, amount):
        return base[amount * FINE :] + moved[: base.shape[0] - amount * FINE]

    tiles = [tall[:, i * LANES : (i + 1) * LANES] for i in range(3)]
    add_group(total, fold_lanes(tiles, shift), group, 48)

    @pl.when(group == GROUPS - 1)
    def _():
        out[...] = total[:, : grads.shape[1]]


def conv_backward(grads, direct, weight, patches):
    pack, width = grads.shape
    reach = pack + FINE
    whole = lambda g: (0, 0)
    each = lambda g: (g, 0, 0)
    return pl.pallas_call(
        functools.partial(backward_kernel, pack),
        grid=(GROUPS,),
        out_shape=[
            jax.ShapeDtypeStruct((pack, width), jnp.float32),
            jax.ShapeDtypeStruct(weight.shape, jnp.bfloat16),
        ],
        in_specs=[
            pl.BlockSpec((pack, width), whole),
            pl.BlockSpec((pack, width), whole),
            pl.BlockSpec((1, 384, 768), each),
            pl.BlockSpec((1, reach, 384), each),
        ],
        out_specs=[
            pl.BlockSpec((pack, width), whole),
            pl.BlockSpec((1, 384, 768), each),
        ],
        scratch_shapes=[
            pltpu.VMEM((reach, width + LANES), jnp.float32),
            pltpu.VMEM((pack + KERNEL - FINE, 384), jnp.float32),
            pltpu.VMEM((pack, width + LANES), jnp.float32),
        ],
        compiler_params=pltpu.CompilerParams(vmem_limit_bytes=40 << 20),
    )(grads, direct, weight, patches)


HEAD_DIM = 64
EPSILON = 1e-05
ROWS = 32
TILE = 256


def dot(a, b, contract=(1, 0)):
    return lax.dot_general(
        a, b, ((contract[:1], contract[1:]), ((), ())), preferred_element_type=jnp.float32
    )


def below_normal(values):
    return 0.5 * (1.0 + lax.erf(values * 0.7071067811865476))


def density(values):
    return jnp.exp(-0.5 * values * values) * 0.3989422804014327


def unit_norm(values):
    centered = values - jnp.mean(values, axis=-1, keepdims=True)
    inverse = lax.rsqrt(jnp.mean(centered * centered, axis=-1, keepdims=True) + EPSILON)
    return centered * inverse, inverse


def norm_back(grad, unit, inverse, gain):
    scaled = grad * gain
    inner = jnp.mean(scaled, axis=-1, keepdims=True)
    along = jnp.mean(scaled * unit, axis=-1, keepdims=True)
    return inverse * (scaled - inner - unit * along)


def row_tiles(pack, body):
    @pl.loop(0, pack // ROWS)
    def _(tile):
        body(pl.ds(pl.multiple_of(tile * ROWS, ROWS), ROWS))


def lane_tiles(count, body, first=0):
    @pl.loop(first, count)
    def _(tile):
        body(tile, pl.ds(pl.multiple_of(tile * TILE, TILE), TILE))


def clip_mask(lengths, micro, pack):
    row = lax.broadcasted_iota(jnp.int32, (pack, pack), 0)
    column = lax.broadcasted_iota(jnp.int32, (pack, pack), 1)
    row_clip, column_clip = jnp.zeros_like(row), jnp.zeros_like(column)
    end = 0
    for clip in range(lengths.shape[1]):
        end = end + lengths[micro, clip]
        row_clip += (row >= end).astype(jnp.int32)
        column_clip += (column >= end).astype(jnp.int32)
    return row_clip == column_clip


def front_norm(frames, convolved, gains, normed, normed_low, unit, inverse, front_slope):
    def body(rows):
        values = convolved[rows, 0 : frames.shape[1]]
        below = below_normal(values)
        front_slope[rows, :] = below + values * density(values)
        mixed = frames[rows, :].astype(jnp.float32) + values * below
        units, inv = unit_norm(mixed)
        unit[rows, :] = units
        inverse[rows, :] = jnp.broadcast_to(inv, (ROWS, LANES))
        total = units * gains[0:1, :]
        normed[rows, :] = total
        normed_low[rows, :] = total.astype(normed_low.dtype)

    row_tiles(frames.shape[0], body)


def project(normed_low, weight, projected):
    def body(tile, lanes):
        projected[:, lanes] = dot(normed_low[...], weight[:, lanes]).astype(projected.dtype)

    lane_tiles(projected.shape[1] // TILE, body)


def pair_parts(projected, pair, width):
    return [
        projected[:, pl.ds(pl.multiple_of(part * width + pair * LANES, LANES), LANES)] for part in range(3)
    ]


def attend(projected, lengths, micro, probs, attended, first=0, last=None):
    pack, width = attended.shape
    low = projected.dtype
    scale = HEAD_DIM ** (-0.5)

    @pl.loop(first, last or width // LANES)
    def _(pair):
        same = clip_mask(lengths, micro, pack)
        queries, keys, values = pair_parts(projected, pair, width)
        lane = lax.broadcasted_iota(jnp.int32, (pack, LANES), 1)
        sides = []
        for side in range(2):
            own = (lane < HEAD_DIM) == (side == 0)
            scores = dot(jnp.where(own, queries, jnp.zeros_like(queries)), keys, (1, 1)) * scale
            scores = jnp.where(same, scores, -1e30)
            shifted = jnp.exp(scores - jnp.max(scores, axis=-1, keepdims=True))
            weights = shifted / jnp.sum(shifted, axis=-1, keepdims=True)
            probs[2 * pair + side] = weights
            sides.append(dot(weights.astype(low), values))
        lanes = pl.ds(pl.multiple_of(pair * LANES, LANES), LANES)
        attended[:, lanes] = jnp.where(lane < HEAD_DIM, *sides).astype(low)


def middle_norm(attended, weight, normed, gains, middle, middle_low, unit, inverse):
    def body(tile, lanes):
        middle[:, lanes] = normed[:, lanes] + dot(attended[...], weight[:, lanes])

    lane_tiles(normed.shape[1] // TILE, body)

    def finish(rows):
        units, inv = unit_norm(middle[rows, :])
        unit[rows, :] = units
        inverse[rows, :] = jnp.broadcast_to(inv, (ROWS, LANES))
        total = units * gains[1:2, :]
        middle[rows, :] = total
        middle_low[rows, :] = total.astype(middle_low.dtype)

    row_tiles(normed.shape[0], finish)


def feed_up(middle_low, weight, slope, activated, first=0, last=None):
    def body(tile, lanes):
        values = dot(middle_low[...], weight[:, lanes])
        below = below_normal(values)
        slope[:, lanes] = (below + values * density(values)).astype(slope.dtype)
        activated[:, lanes] = (values * below).astype(activated.dtype)

    lane_tiles(last or slope.shape[1] // TILE, body, first)


def feed_down(activated, weight, middle, gains, cotangent, output, grad_final, gain_grads):
    def body(tile, lanes):
        middle[...] += dot(activated[:, lanes], weight[lanes, :])

    lane_tiles(activated.shape[1] // TILE, body)
    gain_grads[2:3, :] = jnp.zeros((1, middle.shape[1]), jnp.float32)

    def finish(rows):
        units, inv = unit_norm(middle[rows, :])
        gain = gains[2:3, :]
        output[rows, :] = (units * gain).astype(output.dtype)
        grad = cotangent[rows, :].astype(jnp.float32)
        gain_grads[2:3, :] += jnp.sum(grad * units, axis=0, keepdims=True)
        grad_final[rows, :] = norm_back(grad, units, inv, gain)

    row_tiles(middle.shape[0], finish)


def feed_back(grad, slope, activated, middle_low, up, down, up_grad, down_grad):
    low = activated.dtype
    grad_feed = grad[...].astype(low)
    turned = jnp.transpose(middle_low[...].astype(jnp.float32)).astype(low)

    def body(tile, lanes):
        down_grad[lanes, :] = dot(activated[:, lanes], grad_feed, (0, 0)).astype(low)
        grad_hidden = (dot(grad_feed, down[lanes, :], (1, 1)) * slope[:, lanes].astype(jnp.float32)).astype(low)
        up_grad[:, lanes] = dot(turned, grad_hidden).astype(low)
        grad[...] += dot(grad_hidden, up[:, lanes], (1, 1))

    lane_tiles(slope.shape[1] // TILE, body)


def norm_back_rows(grad, unit, inverse, gains, which, gain_grads):
    gain_grads[which : which + 1, :] = jnp.zeros((1, grad.shape[1]), jnp.float32)

    def body(rows):
        incoming, units = grad[rows, :], unit[rows, :]
        gain_grads[which : which + 1, :] += jnp.sum(incoming * units, axis=0, keepdims=True)
        grad[rows, :] = norm_back(incoming, units, inverse[rows, 0:1], gains[which : which + 1, :])

    row_tiles(grad.shape[0], body)


def branch_back(grad, attended, weight, grad_attended, out_grad):
    low = attended.dtype
    grad_branch = grad[...].astype(low)

    def body(tile, lanes):
        out_grad[lanes, :] = dot(attended[:, lanes], grad_branch, (0, 0)).astype(low)
        grad_attended[:, lanes] = dot(grad_branch, weight[lanes, :], (1, 1)).astype(low)

    lane_tiles(attended.shape[1] // TILE, body)


def attend_back_pair(projected, grad_attended, weights_of, grad_projected, pair):
    pack, width = grad_attended.shape
    low = projected.dtype
    scale = HEAD_DIM ** (-0.5)

    def lanes_of(part):
        start = part * width + pair * LANES
        return pl.ds(start if isinstance(pair, int) else pl.multiple_of(start, LANES), LANES)

    queries, keys, values = [projected[:, lanes_of(part)] for part in range(3)]
    grad = grad_attended[:, lanes_of(0)]
    lane = lax.broadcasted_iota(jnp.int32, (pack, LANES), 1)
    sides = []
    for side in range(2):
        own = (lane < HEAD_DIM) == (side == 0)
        weights = weights_of[side]
        grad_values = dot(weights.astype(low), grad, (0, 0))
        grad_probs = dot(jnp.where(own, grad, jnp.zeros_like(grad)), values, (1, 1))
        along = jnp.sum(weights * grad_probs, axis=-1, keepdims=True)
        grad_scores = (weights * (grad_probs - along)).astype(low)
        grad_queries = dot(grad_scores, keys) * scale
        grad_keys = dot(grad_scores, queries, (0, 0)) * scale
        sides.append((grad_queries, grad_keys, grad_values))
    for part in range(3):
        grad_projected[:, lanes_of(part)] = jnp.where(lane < HEAD_DIM, sides[0][part], sides[1][part]).astype(low)


def attend_back(projected, grad_attended, probs, grad_projected):
    @pl.loop(0, grad_attended.shape[1] // LANES)
    def _(pair):
        attend_back_pair(projected, grad_attended, probs.at[pl.ds(2 * pair, 2)], grad_projected, pair)


def project_back(grad, grad_projected, unit, gains, weight, qkv_grad):
    low = grad_projected.dtype
    turned = jnp.transpose(unit[...] * gains[0:1, :]).astype(low)

    def body(tile, lanes):
        qkv_grad[:, lanes] = dot(turned, grad_projected[:, lanes]).astype(low)
        grad[...] += dot(grad_projected[:, lanes], weight[:, lanes], (1, 1))

    lane_tiles(grad_projected.shape[1] // TILE, body)


def slope_rows(grad, front_slope, grad_convolved):
    def body(rows):
        grad_convolved[rows, :] = (grad[rows, :] * front_slope[rows, :]).astype(grad_convolved.dtype)

    row_tiles(grad.shape[0], body)


def middle_forward_kernel(
    lengths, frames, convolved, gains, wide, down, cotangent,
    output, front_slope, grad_final, unit_front, inverse_front, projected, probs, attended,
    unit_middle, inverse_middle, middle_low, slope, activated, gain_grads,
    normed, normed_low, middle,
):
    width = frames.shape[1]
    gain_grads[...] = jnp.zeros_like(gain_grads)
    front_norm(frames, convolved, gains, normed, normed_low, unit_front, inverse_front, front_slope)
    project(normed_low, wide.at[:, 0 : 3 * width], projected)
    attend(projected, lengths, 0, probs, attended)
    middle_norm(
        attended, wide.at[:, 3 * width : 4 * width], normed, gains, middle, middle_low, unit_middle,
        inverse_middle,
    )
    feed_up(middle_low, wide.at[:, 4 * width :], slope, activated)
    feed_down(activated, down, middle, gains, cotangent, output, grad_final, gain_grads)


def middle_backward_kernel(
    gains, wide, down, front_slope, grad_final, unit_front, inverse_front, projected, probs, attended,
    unit_middle, inverse_middle, middle_low, slope, activated, last_gain_grad,
    grad, grad_convolved, wide_grad, down_grad, gain_grads,
    grad_attended, grad_projected,
):
    width = grad.shape[1]
    gain_grads[...] = last_gain_grad[...]
    grad[...] = grad_final[...]
    feed_back(
        grad, slope, activated, middle_low, wide.at[:, 4 * width :], down, wide_grad.at[:, 4 * width :],
        down_grad,
    )
    norm_back_rows(grad, unit_middle, inverse_middle, gains, 1, gain_grads)
    branch_back(
        grad, attended, wide.at[:, 3 * width : 4 * width], grad_attended,
        wide_grad.at[:, 3 * width : 4 * width],
    )
    attend_back(projected, grad_attended, probs, grad_projected)
    project_back(
        grad, grad_projected, unit_front, gains, wide.at[:, 0 : 3 * width], wide_grad.at[:, 0 : 3 * width]
    )
    norm_back_rows(grad, unit_front, inverse_front, gains, 0, gain_grads)
    slope_rows(grad, front_slope, grad_convolved)


def middle_forward(frames, convolved, lengths, gains, wide, down, cotangent):
    pack, width = frames.shape
    inner = down.shape[0]
    heads = width // HEAD_DIM
    low, full = jnp.bfloat16, jnp.float32
    shape = jax.ShapeDtypeStruct
    vmem = pl.BlockSpec(memory_space=pltpu.VMEM)
    saved = [
        shape((pack, width), low),
        shape((pack, width), full),
        shape((pack, width), full),
        shape((pack, width), full),
        shape((pack, LANES), full),
        shape((pack, 3 * width), low),
        shape((heads, pack, pack), full),
        shape((pack, width), low),
        shape((pack, width), full),
        shape((pack, LANES), full),
        shape((pack, width), low),
        shape((pack, inner), low),
        shape((pack, inner), low),
        shape((8, width), full),
    ]
    return pl.pallas_call(
        middle_forward_kernel,
        out_shape=saved,
        in_specs=[pl.BlockSpec(memory_space=pltpu.SMEM)] + [vmem] * 6,
        out_specs=[vmem] * len(saved),
        scratch_shapes=[
            pltpu.VMEM((pack, width), full),
            pltpu.VMEM((pack, width), low),
            pltpu.VMEM((pack, width), full),
        ],
        compiler_params=pltpu.CompilerParams(vmem_limit_bytes=58 << 20),
    )(lengths, frames, convolved, gains, wide, down, cotangent)


def middle_backward(gains, wide, down, kept):
    pack, width = kept[0].shape
    low, full = jnp.bfloat16, jnp.float32
    shape = jax.ShapeDtypeStruct
    vmem = pl.BlockSpec(memory_space=pltpu.VMEM)
    grads = [
        shape((pack, width), full),
        shape((pack, width), low),
        shape(wide.shape, low),
        shape(down.shape, low),
        shape((8, width), full),
    ]
    return pl.pallas_call(
        middle_backward_kernel,
        out_shape=grads,
        in_specs=[vmem] * (3 + len(kept)),
        out_specs=[vmem] * len(grads),
        scratch_shapes=[pltpu.VMEM((pack, width), low), pltpu.VMEM((pack, 3 * width), low)],
        compiler_params=pltpu.CompilerParams(vmem_limit_bytes=58 << 20),
    )(gains, wide, down, *kept)


def weave(tasks, pieces):
    core_index = lax.axis_index("seq")
    count, done = len(tasks[0]), 0
    for number, piece in enumerate(pieces + [None]):
        until = count if piece is None else (number + 1) * count // (len(pieces) + 1)

        def some(core, first=done, last=until):
            for task in tasks[core][first:last]:
                task()

        if until > done:
            by_core(core_index, some)
        done = until
        if piece is not None:
            piece()


def fused_forward_kernel(
    dims, chunks,
    lengths, frames, cotangent, conv_shard, wide_shard, down_shard, gain_shard,
    conv_out, wide_out, down_out, both_output, patches, gains, front_slope, grad_final, unit_front, inverse_front, projected, probs, attended, unit_middle, inverse_middle,
    middle_low, slope, activated, gain_grads,
    conv_all, wide_all, down_all, gain_all, pack_frames, pack_cotangent, output, padded, total,
    gains_wide, normed, normed_low, middle,
    send_sems, recv_sems, push_send, push_recv, local_sems, pair_sems,
):
    ins = (conv_shard, wide_shard, down_shard, gain_shard)
    outs = (conv_all, wide_all, down_all, gain_all)
    gather = Gather(dims, chunks, ins, outs, (send_sems, recv_sems, push_send, push_recv))
    core_index = lax.axis_index("seq")
    me = lax.axis_index("dp")
    pack, width = pack_frames.shape
    half = pack // 2
    greet(dims, gather.position, core_index)

    here = pl.ds(pl.multiple_of(core_index * half, half), half)
    there = pl.ds(pl.multiple_of((1 - core_index) * half, half), half)

    def to_partner(source, target, number):
        return pltpu.make_async_remote_copy(
            src_ref=source,
            dst_ref=target,
            send_sem=pair_sems.at[0, number],
            recv_sem=pair_sems.at[1, number],
            device_id={"seq": 1 - core_index},
            device_id_type=MESH,
        )

    moves = []
    for number, (source, target) in enumerate(((frames, pack_frames), (cotangent, pack_cotangent))):
        moves.append(to_partner(source.at[1 - core_index], target.at[here], number))
        moves.append(pltpu.make_async_copy(source.at[core_index], target.at[here], local_sems.at[number]))
    for copy in moves:
        copy.start()
    own = [
        pltpu.make_async_copy(ins[i], gather.whole(me, i), local_sems.at[2 + i]) for i in range(len(ins))
    ]
    for copy in own:
        copy.start()

    def early(core):
        for chunk in range(3):
            for task in gather.tasks(core, chunk, 0):
                task()

    by_core(core_index, early)
    steps = []
    for step in range(1, len(chunks) + 3):
        both = []
        for core in range(2):
            tasks = []
            if 3 <= step + 2 < len(chunks):
                tasks += gather.tasks(core, step + 2, 0)
            for stage in (1, 2, 3):
                if 0 <= step - stage < len(chunks):
                    tasks += gather.tasks(core, step - stage, stage)
            both.append(tasks)
        steps.append(both)

    def gate(*numbers):
        def body(core):
            for number in numbers:
                gather.arrived(core, number)

        by_core(core_index, body)

    for copy in moves[:2]:
        copy.wait()
    fill_padded(padded, pack_frames)
    total[...] = jnp.zeros_like(total)

    def patch_piece(first, last):
        def piece():
            @pl.loop(first, last)
            def _(group):
                patches[group] = make_patch(padded, group, pack)

        return piece

    def conv_piece(first, last):
        def piece():
            @pl.loop(first, last)
            def _(group):
                add_forward(total, patches[group], conv_all[group], group, pack)

        return piece

    quarter = GROUPS // 4
    early_pieces = [patch_piece(i * quarter, (i + 1) * quarter) for i in range(4)]
    weave(steps[0], early_pieces[:1])
    weave(steps[1], early_pieces[1:3])
    weave(steps[2], early_pieces[3:])
    weave(steps[3], [])
    weave(steps[4], [])
    for copy in own:
        copy.wait()
    gate(0, 1, 2)
    saves = [pltpu.make_async_copy(a, b, local_sems.at[6 + i]) for i, (a, b) in enumerate(
        ((conv_all, conv_out), (wide_all, wide_out), (down_all, down_out)))]
    saves[0].start()
    gains_wide[...] = jnp.zeros_like(gains_wide)

    @pl.loop(0, gather.count)
    def _(shard):
        add_group(gains_wide, gain_all[shard, 0:16, :].astype(jnp.float32), shard, width // gather.count)

    gains[...] = gains_wide[0:8, 0:width]
    weave(steps[5], [conv_piece(i, i + 2) for i in range(0, GROUPS, 2)])

    def front_piece():
        front_norm(pack_frames, total, gains, normed, normed_low, unit_front, inverse_front, front_slope)

    def project_piece():
        gate(3)
        project(normed_low, wide_all.at[:, 0 : 3 * width], projected)

    def attend_piece(first, last):
        return lambda: attend(projected, lengths, core_index, probs, attended, first, last)

    def middle_piece():
        middle_norm(
            attended, wide_all.at[:, 3 * width : 4 * width], normed, gains, middle, middle_low, unit_middle,
            inverse_middle,
        )

    pairs = width // LANES
    weave(
        steps[6],
        [front_piece, project_piece]
        + [attend_piece(i, i + 2) for i in range(0, pairs, 2)]
        + [middle_piece],
    )
    up = wide_all.at[:, 4 * width :]
    count = slope.shape[1] // TILE
    third = count // 3

    def up_piece(first):
        def piece():
            if first == 0:
                gate(4)
                saves[1].start()
            feed_up(middle_low, up, slope, activated, first, first + third)

        return piece

    weave(steps[7], [up_piece(i) for i in range(0, count, third)])
    gate(5)
    saves[2].start()
    for copy in moves[2:]:
        copy.wait()
    gain_grads[...] = jnp.zeros_like(gain_grads)
    feed_down(activated, down_all, middle, gains, pack_cotangent, output, grad_final, gain_grads)
    last = to_partner(output.at[there], both_output.at[core_index], 2)
    last.start()
    stay = pltpu.make_async_copy(output.at[here], both_output.at[core_index], local_sems.at[9])
    stay.start()
    by_core(core_index, gather.finish)
    for copy in saves + [stay, last]:
        copy.wait()


def fused_forward(frames, cotangent, lengths, shards_in, chunks, dp):
    dims = dp_factors(dp)
    n = len(chunks)
    conv_shard, wide_shard, down_shard, gain_shard = shards_in
    pack, width = 2 * frames.shape[1], frames.shape[2]
    inner = down_shard.shape[0] * dp
    heads = width // HEAD_DIM
    low, full = jnp.bfloat16, jnp.float32
    shape = jax.ShapeDtypeStruct
    vmem = pl.BlockSpec(memory_space=pltpu.VMEM)
    any_ = pl.BlockSpec(memory_space=pl.ANY)
    conv_shape = (dp,) + conv_shard.shape
    wide_shape = (width, wide_shard.shape[1])
    down_shape = (inner, width)
    tall = pack + FINE
    saved = [
        shape(frames.shape, low),
        shape((GROUPS, tall, 384), low),
        shape((8, width), full),
        shape((pack, width), full),
        shape((pack, width), full),
        shape((pack, width), full),
        shape((pack, LANES), full),
        shape((pack, 3 * width), low),
        shape((heads, pack, pack), full),
        shape((pack, width), low),
        shape((pack, width), full),
        shape((pack, LANES), full),
        shape((pack, width), low),
        shape((pack, inner), low),
        shape((pack, inner), low),
        shape((8, width), full),
    ]
    return pl.pallas_call(
        functools.partial(fused_forward_kernel, dims, chunks),
        out_shape=[shape(conv_shape, low), shape(wide_shape, low), shape(down_shape, low)] + saved,
        in_specs=[pl.BlockSpec(memory_space=pltpu.SMEM)] + [any_] * 6,
        out_specs=[any_] * 3 + [vmem] * len(saved),
        scratch_shapes=[
            pltpu.VMEM(conv_shape, low),
            pltpu.VMEM(wide_shape, low),
            pltpu.VMEM(down_shape, low),
            pltpu.VMEM((dp,) + gain_shard.shape, low),
            pltpu.VMEM((pack, width), low),
            pltpu.VMEM((pack, width), low),
            pltpu.VMEM((pack, width), low),
            pltpu.VMEM((pack + KERNEL, width + LANES), full),
            pltpu.VMEM((pack, width + LANES), full),
            pltpu.VMEM((16, width + LANES), full),
            pltpu.VMEM((pack, width), full),
            pltpu.VMEM((pack, width), low),
            pltpu.VMEM((pack, width), full),
            pltpu.SemaphoreType.DMA((n, dp)),
            pltpu.SemaphoreType.DMA((n, dp)),
            pltpu.SemaphoreType.DMA((n, dp)),
            pltpu.SemaphoreType.DMA((n, dp)),
            pltpu.SemaphoreType.DMA((10,)),
            pltpu.SemaphoreType.DMA((2, 3)),
        ],
        compiler_params=pltpu.CompilerParams(
            collective_id=2, has_side_effects=True, vmem_limit_bytes=60 << 20
        ),
    )(lengths, frames, cotangent, *shards_in)


STRIP = 384
DOWN, UP, OUT, QKV, CONV, GAIN = range(6)


class Scatter:
    def __init__(self, dims, heights, stages, pairs, hops, outs, by_block, sems):
        self.dims, self.heights = dims, heights
        self.stages, self.pairs, self.hops, self.outs, self.by_block = stages, pairs, hops, outs, by_block
        self.pair_recv, self.hop_send, self.hop_recv, self.last_send, self.last_recv = sems
        self.position = position_of(dims)
        self.count = dims[0] * dims[1] * dims[2]

    def block(self, ref, chunk, gid):
        if len(ref.shape) == 3:
            return ref.at[gid]
        height = self.heights[chunk]
        return ref.at[pl.ds(pl.multiple_of(gid * height, 16), height)]

    def sizes(self, core):
        return [self.dims[axis] for axis in ORDERS[core]]

    def slot(self, core, level, offsets, distance):
        index = distance - 1
        for i in range(level):
            index = index * self.sizes(core)[i] + offsets[i]
        return index

    def semaphore(self, core, level, index):
        sizes = self.sizes(core)
        return (1, sizes[0], sizes[0] * sizes[1])[level] + index - 1

    def combine(self, core, chunk, offsets, target):
        gid = place(self.dims, ORDERS[core], self.position, offsets)
        own, pair = self.block(self.stages[chunk], chunk, gid), self.block(self.pairs[chunk], chunk, gid)
        if chunk in self.by_block:
            pltpu.make_async_copy(pair, pair, self.pair_recv.at[chunk, gid]).wait()
        terms = [own, pair]
        for level in (2, 1, 0):
            if offsets[level]:
                break
            for distance in range(1, self.sizes(core)[level]):
                index = self.slot(core, level, offsets, distance)
                ref = self.hops[level][chunk].at[index]
                number = self.semaphore(core, level, index)
                pltpu.make_async_copy(ref, ref, self.hop_recv.at[chunk, number]).wait()
                terms.append(ref)

        @pl.loop(0, own.shape[0] // 16)
        def _(tile):
            rows = pl.ds(pl.multiple_of(tile * 16, 16), 16)
            total = terms[0][rows, :].astype(jnp.float32)
            for term in terms[1:]:
                total = total + term[rows, :].astype(jnp.float32)
            if target is None:
                own[rows, :] = total.astype(own.dtype)
            else:
                target[rows, :] = total

        return own

    def send(self, core, chunk, offsets):
        level = max(i for i in range(3) if offsets[i])
        own = self.combine(core, chunk, offsets, None)
        index = self.slot(core, level, offsets, offsets[level])
        number = self.semaphore(core, level, index)
        pltpu.make_async_remote_copy(
            src_ref=own,
            dst_ref=self.hops[level][chunk].at[index],
            send_sem=self.hop_send.at[chunk, number],
            recv_sem=self.hop_recv.at[chunk, number],
            device_id={"dp": place(self.dims, (ORDERS[core][level],), self.position, (offsets[level],))},
            device_id_type=MESH,
        ).start()

    def half(self, chunk, core):
        out = self.outs[chunk]
        lanes = out.shape[1] // 2
        return out.at[:, pl.ds(core * lanes, lanes)]

    def final(self, core, chunk):
        half = self.half(chunk, core)
        self.combine(core, chunk, (0, 0, 0), half)
        pltpu.make_async_remote_copy(
            src_ref=half,
            dst_ref=half,
            send_sem=self.last_send.at[chunk],
            recv_sem=self.last_recv.at[chunk],
            device_id={"seq": 1 - core},
            device_id_type=MESH,
        ).start()

    def tasks(self, core, chunk, stage):
        sizes = self.sizes(core)
        if stage == 3:
            return [functools.partial(self.final, core, chunk)]
        if stage == 2:
            places = [(i, 0, 0) for i in range(1, sizes[0])]
        elif stage == 1:
            places = [(i % sizes[0], d, 0) for d in range(1, sizes[1]) for i in range(1, sizes[0] + 1)]
        else:
            places = [
                (i, j % sizes[1], d)
                for d in range(1, sizes[2])
                for j in range(1, sizes[1] + 1)
                for i in range(sizes[0])
            ]
        return [functools.partial(self.send, core, chunk, offsets) for offsets in places]

    def finish(self, core):
        for chunk in range(len(self.outs)):
            half = self.half(chunk, 1 - core)
            pltpu.make_async_copy(half, half, self.last_recv.at[chunk]).wait()
            pltpu.make_async_copy(half, half, self.last_send.at[chunk]).wait()

            @pl.loop(0, self.count - 1)
            def _(number, chunk=chunk):
                ref = self.block(self.stages[chunk], chunk, 0)
                pltpu.make_async_copy(ref, ref, self.hop_send.at[chunk, number]).wait()


class Stream:
    def __init__(self, buffer, sems):
        self.buffer, self.sems = buffer, sems

    def start(self, source, number):
        pltpu.make_async_copy(source, self.buffer.at[number % 2], self.sems.at[number % 2]).start()

    def take(self, number):
        ref = self.buffer.at[number % 2]
        pltpu.make_async_copy(ref, ref, self.sems.at[number % 2]).wait()
        return ref


class Outbox:
    def __init__(self, buffer, sems):
        self.buffer, self.sems, self.busy, self.number = buffer, sems, [None, None], 0

    def free(self):
        slot = self.number % 2
        self.number += 1
        if self.busy[slot] is not None:
            self.busy[slot].wait_send()
            self.busy[slot] = None
        return slot, self.buffer.at[slot]

    def send(self, slot, source, target, recv_sem):
        copy = pltpu.make_async_remote_copy(
            src_ref=source,
            dst_ref=target,
            send_sem=self.sems.at[slot],
            recv_sem=recv_sem,
            device_id={"seq": 1 - lax.axis_index("seq")},
            device_id_type=MESH,
        )
        copy.start()
        self.busy[slot] = copy

    def drain(self):
        for copy in self.busy:
            if copy is not None:
                copy.wait_send()
        self.busy = [None, None]


def spread_grads(padded, group, pack):
    def later(values, amount):
        return pltpu.roll(values, amount, 0)

    one = take_group(padded, slice(0, pack + FINE), group, 48)
    two = one + pltpu.roll(later(one, 1), 48, 1)
    low, high = double_96(two, later(two, 2))
    near = jnp.concatenate(double_192(low, high, later(low, 4), later(high, 4)), axis=1)
    return jnp.concatenate([near, later(near, 8)], axis=1).astype(jnp.bfloat16)


def add_backward(total, tall, spread, weight, group, pack):
    edge = KERNEL // 2 - FINE
    tall[edge : edge + pack + FINE] = dot(spread, weight, (1, 1))

    def shift(base, moved, amount):
        return base[amount * FINE :] + moved[: base.shape[0] - amount * FINE]

    tiles = [tall[:, i * LANES : (i + 1) * LANES] for i in range(3)]
    add_group(total, fold_lanes(tiles, shift), group, 48)


def fused_backward_kernel(
    dims,
    weight, wide, down, patches, probs, grad_final,
    gains, front_slope, unit_front, inverse_front, projected, attended, unit_middle, inverse_middle,
    middle_low, slope, activated, last_gain_grad,
    conv_out, qkv_out, out_out, up_out, down_out, gain_out, both_grads, *scratch,
):
    outs = (down_out, up_out, out_out, qkv_out, conv_out, gain_out)
    n = len(outs)
    stages, pairs = scratch[:n], scratch[n : 2 * n]
    hops = [scratch[(2 + level) * n : (3 + level) * n] for level in range(3)]
    (
        grad, turned, grad_attended, grad_projected, padded, spread, tall, total, gain_grads, gain_wide,
        gain_box, tall_box, wide_box, tall_tiles, wide_tiles, prob_tiles, patch_tiles,
        pair_recv, hop_send, hop_recv, last_send, last_recv, box_sems, tile_sems, load_sems,
    ) = scratch[5 * n :]
    core_index = lax.axis_index("seq")
    other = 1 - core_index
    pack, width = grad.shape
    inner = activated.shape[1]
    low = jnp.bfloat16
    heights = [out.shape[0] for out in outs]
    scatter = Scatter(
        dims, heights, stages, pairs, hops, outs, (CONV,), (pair_recv, hop_send, hop_recv, last_send, last_recv)
    )
    tall_stream, wide_stream = Stream(tall_tiles, tile_sems.at[0]), Stream(wide_tiles, tile_sems.at[1])
    prob_stream, patch_stream = Stream(prob_tiles, tile_sems.at[2]), Stream(patch_tiles, tile_sems.at[3])
    tall_out, wide_out_box = Outbox(tall_box, box_sems.at[0]), Outbox(wide_box, box_sems.at[1])

    def strip(index, base=0):
        return pl.ds(pl.multiple_of(base + index * STRIP, LANES), STRIP)

    up_base, out_base = 4 * width, 3 * width
    load = pltpu.make_async_copy(grad_final, grad, load_sems.at[0])
    load.start()
    up_half, qkv_half, out_half = inner // 2, 3 * width // 2, width // 2
    up_strips, qkv_strips = up_half // STRIP, qkv_half // STRIP
    down_strips = inner // STRIP

    def ordered(index, strips):
        return jnp.where(index < strips, other * strips + index, core_index * strips + index - strips)

    def up_start(index):
        which = ordered(index, up_strips)
        wide_stream.start(wide.at[:, strip(which, up_base)], index)
        tall_stream.start(down.at[strip(which)], index)

    up_start(0)
    greet(dims, scatter.position, core_index)
    load.wait()

    def all_tasks(*wanted):
        return [[task for chunk, stage in wanted for task in scatter.tasks(core, chunk, stage)] for core in range(2)]

    def gate(chunk, count, height, lanes):
        for index in range(count):
            ref = pairs[chunk].at[pl.ds(0, height), pl.ds(0, lanes)]
            pltpu.make_async_copy(ref, ref, pair_recv.at[chunk, index]).wait()

    own_lanes = pl.ds(pl.multiple_of(core_index * out_half, LANES), out_half)
    other_lanes = pl.ds(pl.multiple_of(other * out_half, LANES), out_half)
    grad_feed = grad[...].astype(low)
    for index in range(down_strips):
        slot, box = tall_out.free()
        box[...] = dot(activated[:, index * STRIP : (index + 1) * STRIP], grad_feed, (0, 0)).astype(low)
        rows = pl.ds(index * STRIP, STRIP)
        tall_out.send(slot, box.at[:, other_lanes], pairs[DOWN].at[rows], pair_recv.at[DOWN, index])
        stages[DOWN][rows, :] = box[:, own_lanes]
    turned[...] = jnp.transpose(middle_low[...].astype(jnp.float32)).astype(low)
    gate(DOWN, down_strips, STRIP, out_half)
    spread[0:pack, :] = grad_feed

    def give(chunk, index, strips, values):
        if index < strips:
            slot, box = wide_out_box.free()
            box[...] = values
            lanes = pl.ds(index * STRIP, STRIP)
            wide_out_box.send(slot, box, pairs[chunk].at[:, lanes], pair_recv.at[chunk, index])
        else:
            stages[chunk][:, (index - strips) * STRIP : (index - strips + 1) * STRIP] = values

    def up_piece(index):
        def piece():
            if index + 1 < 2 * up_strips:
                up_start(index + 1)
            up_tile, down_tile = wide_stream.take(index), tall_stream.take(index)
            lanes = strip(ordered(index, up_strips))
            slopes = slope[:, lanes].astype(jnp.float32)
            grad_hidden = (dot(spread[0:pack, :], down_tile[...], (1, 1)) * slopes).astype(low)
            give(UP, index, up_strips, dot(turned[...], grad_hidden).astype(low))
            grad[...] += dot(grad_hidden, up_tile[...], (1, 1))

        return piece

    weave(all_tasks((DOWN, 0)), [up_piece(i) for i in range(2 * up_strips)])

    def prob_start(pair):
        prob_stream.start(probs.at[pl.ds(2 * pair, 2)], pair)

    for index in range(2):
        tall_stream.start(wide.at[strip(index), out_base : out_base + width], index)
    prob_start(0)
    gain_grads[...] = last_gain_grad[...]

    def middle_piece():
        gate(UP, up_strips, width, STRIP)
        norm_back_rows(grad, unit_middle, inverse_middle, gains, 1, gain_grads)

    def out_piece():
        grad_branch = grad[...].astype(low)
        spread[0:pack, :] = grad_branch
        turned[...] = jnp.transpose(attended[...].astype(jnp.float32)).astype(low)
        for index, half in enumerate((other, core_index)):
            give(OUT, index, 1, dot(turned[...], spread[0:pack, strip(half)]).astype(low))
            tile = tall_stream.take(index)
            lanes = slice(index * STRIP, (index + 1) * STRIP)
            grad_attended[:, lanes] = dot(grad_branch, tile[...], (1, 1)).astype(low)

    pairs_of_heads = width // LANES

    def attend_piece(pair):
        def piece():
            if pair + 1 < pairs_of_heads:
                prob_start(pair + 1)
            attend_back_pair(projected, grad_attended, prob_stream.take(pair), grad_projected, pair)

        return piece

    def qkv_start(index):
        wide_stream.start(wide.at[:, strip(ordered(index, qkv_strips))], index)

    middle_piece()
    weave(all_tasks((UP, 0), (DOWN, 1)), [out_piece] + [attend_piece(i) for i in range(pairs_of_heads)])

    def qkv_piece(index):
        def piece():
            if index == 0:
                qkv_start(0)
                turned[...] = jnp.transpose(unit_front[...] * gains[0:1, :]).astype(low)
            if index + 1 < 2 * qkv_strips:
                qkv_start(index + 1)
            tile = wide_stream.take(index)
            values = grad_projected[:, strip(ordered(index, qkv_strips))]
            give(QKV, index, qkv_strips, dot(turned[...], values).astype(low))
            grad[...] += dot(values, tile[...], (1, 1))

        return piece

    gate(OUT, 1, width, STRIP)
    weave(all_tasks((OUT, 0), (UP, 1), (DOWN, 2)), [qkv_piece(i) for i in range(2 * qkv_strips)])

    places = sorted(offsets_of(dims), key=lambda o: (o[1] == 0) + (o[2] == 0))
    groups = [place(dims, (0, 1, 2), scatter.position, offsets) for offsets in places]

    def conv_start(number):
        tall_stream.start(weight.at[groups[number]], number)
        patch_stream.start(patches.at[groups[number]], number)

    def front_piece():
        conv_start(0)
        norm_back_rows(grad, unit_front, inverse_front, gains, 0, gain_grads)
        padded[...] = jnp.zeros_like(padded)
        tall[...] = jnp.zeros_like(tall)
        total[...] = jnp.zeros_like(total)
        total[:, :width] = grad[...]

        def body(rows):
            padded[rows, 0:width] = (grad[rows, :] * front_slope[rows, :]).astype(low).astype(jnp.float32)

        row_tiles(pack, body)
        gain_wide[...] = jnp.zeros_like(gain_wide)
        gain_wide[0:8, 0:width] = gain_grads[...]

        @pl.loop(0, scatter.count)
        def _(shard):
            one = take_group(gain_wide, slice(0, 16), shard, width // scatter.count)
            gain_box[shard] = one.astype(low)
            stages[GAIN][shard] = one.astype(low)

        gain_copy.start()

    gain_copy = pltpu.make_async_remote_copy(
        src_ref=gain_box,
        dst_ref=pairs[GAIN],
        send_sem=load_sems.at[1],
        recv_sem=load_sems.at[2],
        device_id={"seq": other},
        device_id_type=MESH,
    )

    def conv_piece(number):
        def piece():
            if number + 1 < len(groups):
                conv_start(number + 1)
            group = groups[number]
            tile, patch = tall_stream.take(number), patch_stream.take(number)
            spread[...] = spread_grads(padded, group, pack)
            slot, box = tall_out.free()
            box[...] = dot(patch[...], spread[...], (0, 0)).astype(low)
            tall_out.send(slot, box.at[:, other_lanes], pairs[CONV].at[group], pair_recv.at[CONV, group])
            stages[CONV][group] = box[:, own_lanes]
            add_backward(total, tall, spread[...], tile[...], group, pack)

        return piece

    gate(QKV, qkv_strips, width, STRIP)
    pieces = [conv_piece(i) for i in range(len(groups))]
    weave(all_tasks((QKV, 0)), [front_piece] + pieces[:4])
    weave(all_tasks((OUT, 1), (UP, 2), (DOWN, 3)), pieces[4:8])
    weave(all_tasks((QKV, 1)), pieces[8:12])
    weave(all_tasks((CONV, 0), (OUT, 2), (UP, 3)), pieces[12:])
    half = pack // 2
    here = pl.ds(pl.multiple_of(core_index * half, half), half)
    there = pl.ds(pl.multiple_of(other * half, half), half)
    frames_copy = pltpu.make_async_remote_copy(
        src_ref=total.at[there, pl.ds(0, width)],
        dst_ref=both_grads.at[core_index],
        send_sem=load_sems.at[3],
        recv_sem=load_sems.at[4],
        device_id={"seq": other},
        device_id_type=MESH,
    )
    frames_copy.start()
    both_grads[core_index] = total[here, 0:width]
    gain_copy.wait()
    weave(all_tasks((GAIN, 0), (QKV, 2), (CONV, 1), (GAIN, 1), (OUT, 3), (QKV, 3), (CONV, 2), (GAIN, 2), (GAIN, 3), (CONV, 3)), [])
    by_core(core_index, scatter.finish)
    tall_out.drain()
    wide_out_box.drain()
    frames_copy.wait()


def fused_backward(weight, wide, down, patches, gains, kept, dp):
    dims = dp_factors(dp)
    (front_slope, grad_final, unit_front, inverse_front, projected, probs, attended, unit_middle,
     inverse_middle, middle_low, slope, activated, gain_grads) = kept
    pack, width = front_slope.shape
    inner = activated.shape[1]
    low, full = jnp.bfloat16, jnp.float32
    shape = jax.ShapeDtypeStruct
    vmem = pl.BlockSpec(memory_space=pltpu.VMEM)
    any_ = pl.BlockSpec(memory_space=pl.ANY)
    rows = width // dp
    slots = [max(pair) for pair in zip(hop_slots(dims, 0), hop_slots(dims, 1))]
    flat = [(inner, width // 2), (width, inner // 2), (width, width // 2), (width, 3 * width // 2)]
    wholes = flat + [(dp, 384, 384), (dp, 16, LANES)]
    blocks = [(s[0] // dp, s[1]) for s in flat] + [(384, 384), (16, LANES)]
    scratch = [pltpu.VMEM(s, low) for s in wholes] * 2
    for level in range(3):
        scratch += [pltpu.VMEM((slots[level],) + s, low) for s in blocks]
    tall_rows = pack + FINE
    scratch += [
        pltpu.VMEM((pack, width), full),
        pltpu.VMEM((width, pack), low),
        pltpu.VMEM((pack, width), low),
        pltpu.VMEM((pack, 3 * width), low),
        pltpu.VMEM((tall_rows, width + LANES), full),
        pltpu.VMEM((tall_rows, width), low),
        pltpu.VMEM((pack + KERNEL - FINE, 384), full),
        pltpu.VMEM((pack, width + LANES), full),
        pltpu.VMEM((8, width), full),
        pltpu.VMEM((16, width + LANES), full),
        pltpu.VMEM((dp, 16, LANES), low),
        pltpu.VMEM((2, STRIP, width), low),
        pltpu.VMEM((2, width, STRIP), low),
        pltpu.VMEM((2, STRIP, width), low),
        pltpu.VMEM((2, width, STRIP), low),
        pltpu.VMEM((2, 2, pack, pack), full),
        pltpu.VMEM((2, tall_rows, 384), low),
        pltpu.SemaphoreType.DMA((6, dp)),
        pltpu.SemaphoreType.DMA((6, dp)),
        pltpu.SemaphoreType.DMA((6, dp)),
        pltpu.SemaphoreType.DMA((6,)),
        pltpu.SemaphoreType.DMA((6,)),
        pltpu.SemaphoreType.DMA((2, 2)),
        pltpu.SemaphoreType.DMA((4, 2)),
        pltpu.SemaphoreType.DMA((5,)),
    ]
    return pl.pallas_call(
        functools.partial(fused_backward_kernel, dims),
        out_shape=[
            shape((384, width), full),
            shape((rows, 3 * width), full),
            shape((rows, width), full),
            shape((rows, inner), full),
            shape((inner // dp, width), full),
            shape((16, 2 * LANES), full),
            shape((2, pack // 2, width), full),
        ],
        in_specs=[any_] * 6 + [vmem] * 12,
        out_specs=[vmem] * 7,
        scratch_shapes=scratch,
        compiler_params=pltpu.CompilerParams(
            collective_id=3, has_side_effects=True, vmem_limit_bytes=63 << 20
        ),
    )(weight, wide, down, patches, probs, grad_final, gains, front_slope, unit_front, inverse_front,
      projected, attended, unit_middle, inverse_middle, middle_low, slope, activated, gain_grads)


GAIN_ROWS = 16


def chunks_of(conv_rows, conv_lanes, wide_rows, width, down_rows):
    both = range(2)
    quarter, half = conv_rows // 4, width // 2
    conv = [
        [(0, ((2 * part + core) * quarter, quarter), (0, conv_lanes)) for core in both] for part in both
    ]
    wide = [
        [(1, (0, wide_rows), ((2 * part + core) * 2 * width, 2 * width)) for core in both] for part in both
    ]
    down = [[(2, (0, down_rows), (core * half, half)) for core in both]]
    gain = [[(3, (core * GAIN_ROWS, GAIN_ROWS), (0, LANES)) for core in both]]
    return gain, conv, wide, down


def shards(
    frames,
    clip_lengths,
    conv_weight,
    front_gain,
    qkv_weight,
    out_weight,
    middle_gain,
    up_weight,
    down_weight,
    final_gain,
    cotangent,
):
    dp = lax.axis_size("dp")
    low = jnp.bfloat16
    width = frames.shape[2]
    columns = conv_weight.shape[2]
    group_width = conv_weight.shape[1]
    gain_width = front_gain.shape[0]
    conv_shard = (
        conv_weight.reshape(COARSE, FINE, group_width, columns)
        .transpose(0, 2, 1, 3)
        .reshape(COARSE * group_width, FINE * columns)
    )
    wide_shard = jnp.concatenate([qkv_weight, out_weight, up_weight], axis=1)
    gain_shard = jnp.pad(
        jnp.stack([front_gain, middle_gain, final_gain]),
        ((0, 2 * GAIN_ROWS - 3), (0, LANES - gain_width)),
    )
    parts = (conv_shard, wide_shard, down_weight, gain_shard)
    gain_chunk, conv_chunks, wide_chunks, down_chunk = chunks_of(
        *conv_shard.shape, wide_shard.shape[0], width, down_weight.shape[0]
    )
    chunks = gain_chunk + conv_chunks + wide_chunks + down_chunk
    split = group_width // columns
    if split == 1:
        (weight, wide, down, outputs, patches, gains, *kept) = fused_forward(
            frames, cotangent, clip_lengths[:, 0], parts, chunks, dp
        )
    else:
        conv_all, wide_all, down_all, gain_all = all_gather(parts, chunks, dp)
        weight = (
            conv_all.reshape(GROUPS, split, COARSE * group_width, FINE, columns)
            .transpose(0, 2, 3, 1, 4)
            .reshape(GROUPS, COARSE * group_width, FINE * group_width)
        )
        wide = wide_all.reshape(width, wide_shard.shape[1])
        down = down_all.reshape(-1, width)
        gains = gain_all[:, :3, :gain_width].transpose(1, 0, 2).reshape(3, width).astype(jnp.float32)
        gains = jnp.pad(gains, ((0, 5), (0, 0)))
        both = lax.all_to_all(
            jnp.stack([frames, cotangent], axis=1), "seq", split_axis=0, concat_axis=2, tiled=True
        )
        pack_frames, pack_cotangent = both[0, 0], both[0, 1]
        lengths = lax.dynamic_index_in_dim(clip_lengths[:, 0], lax.axis_index("seq"), 0)
        convolved, patches = conv_forward(pack_frames, weight)
        output, *kept = middle_forward(
            pack_frames, convolved, lengths, gains, wide, down, pack_cotangent
        )
        outputs = lax.all_to_all(output[None], "seq", split_axis=1, concat_axis=0, tiled=True)

    if split == 1:
        conv_sum, qkv_sum, out_sum, up_sum, down_sum, gain_sum, frame_grads = fused_backward(
            weight, wide, down, patches, gains, kept, dp
        )
    else:
        grad_mixed, grad_convolved, wide_grad, down_grad, gain_grads = middle_backward(
            gains, wide, down, kept
        )
        frame_grad, conv_grad = conv_backward(grad_convolved, grad_mixed, weight, patches)

        conv_blocks = (
            conv_grad.reshape(GROUPS, COARSE * group_width, FINE, split, columns)
            .transpose(0, 3, 1, 2, 4)
            .reshape((dp,) + conv_shard.shape)
        )
        gain_blocks = jnp.pad(
            gain_grads[:3].astype(low).reshape(3, dp, gain_width).transpose(1, 0, 2),
            ((0, 0), (0, 2 * GAIN_ROWS - 3), (0, LANES - gain_width)),
        )
        conv_sum, wide_sum, down_sum, gain_sum = reduce_scatter(
            (
                conv_blocks,
                wide_grad.reshape((dp,) + wide_shard.shape),
                down_grad.reshape((dp,) + down_weight.shape),
                gain_blocks,
            ),
            gain_chunk + down_chunk + wide_chunks[::-1] + conv_chunks,
            dp,
        )
        qkv_sum, out_sum, up_sum = (
            wide_sum[:, : 3 * width],
            wide_sum[:, 3 * width : 4 * width],
            wide_sum[:, 4 * width :],
        )
        frame_grads = lax.all_to_all(frame_grad[None], "seq", split_axis=1, concat_axis=0, tiled=True)

    conv_sum = (
        conv_sum.reshape(COARSE, group_width, FINE, columns)
        .transpose(0, 2, 1, 3)
        .reshape(conv_weight.shape)
    )
    return (
        outputs,
        frame_grads,
        conv_sum,
        gain_sum[0, :gain_width],
        qkv_sum,
        out_sum,
        gain_sum[1, :gain_width],
        up_sum,
        down_sum,
        gain_sum[2, :gain_width],
    )


def solution(mesh):
    frames_spec = P(None, ("dp", "seq"), None)
    row, matrix, columns = P("dp"), P("dp", None), P(None, None, "dp")
    return jax.shard_map(
        shards,
        mesh=mesh,
        in_specs=(
            frames_spec,
            P(None, "dp", None),
            columns,
            row,
            matrix,
            matrix,
            row,
            matrix,
            matrix,
            row,
            frames_spec,
        ),
        out_specs=(
            frames_spec,
            frames_spec,
            columns,
            row,
            matrix,
            matrix,
            row,
            matrix,
            matrix,
            row,
        ),
        check_vma=False,
    )
```

```python
import functools

import jax
import jax.numpy as jnp
from jax import lax
from jax.experimental import pallas as pl
from jax.experimental.pallas import tpu as pltpu
from jax.sharding import PartitionSpec as P

MESH = pl.DeviceIdType.MESH


def dp_factors(size):
    return {16: (4, 2, 2), 128: (4, 4, 8)}.get(size, (size, 1, 1))


def near_first(size):
    return [1, 3, 2] if size == 4 else list(range(1, size))


def offsets_of(dims):
    return [(i, j, k) for i in range(dims[0]) for j in range(dims[1]) for k in range(dims[2])]


def partner(coordinate, offset):
    bit = 1
    while bit <= offset:
        if offset & bit:
            coordinate = coordinate + bit - 2 * bit * lax.rem(coordinate // bit, 2)
        bit *= 2
    return coordinate


def place(dims, order, position, offsets):
    coords = list(position)
    for axis, offset in zip(order, offsets):
        if offset:
            coords[axis] = partner(coords[axis], offset)
    return (coords[0] * dims[1] + coords[1]) * dims[2] + coords[2]


def position_of(dims):
    me = lax.axis_index("dp")
    return (me // (dims[1] * dims[2]), lax.rem(me // dims[2], dims[1]), lax.rem(me, dims[2]))


def greet(dims, position, core):
    barrier = pltpu.get_barrier_semaphore()
    count = 1
    pl.semaphore_signal(barrier, inc=1, device_id={"seq": 1 - core}, device_id_type=MESH)
    for axis in range(3):
        for offset in range(1, dims[axis]):
            other = place(dims, (axis,), position, (offset,))
            pl.semaphore_signal(barrier, inc=1, device_id={"dp": other}, device_id_type=MESH)
            count += 1
    pl.semaphore_wait(barrier, count)


FIRST = ((0, 1, 2), (0, 2, 1))
SECOND = ((1, 0, 2), (2, 0, 1))
ORDERS = FIRST


def by_core(core_index, body):
    for core in range(2):
        pl.when(core_index == core)(functools.partial(body, core))


class Gather:
    def __init__(self, dims, chunks, ins, outs, sems):
        self.dims, self.chunks, self.ins, self.outs = dims, chunks, ins, outs
        self.send_sems, self.recv_sems, self.push_send, self.push_recv = sems
        self.position = position_of(dims)
        self.count = dims[0] * dims[1] * dims[2]
        self.sent = {}

    def part(self, which, chunk, side):
        source, array, rows, _, lane, lanes = self.chunks[chunk][1 + side]
        out = self.outs[array]
        if len(out.shape) == 3:
            return out.at[which, pl.ds(*rows), pl.ds(lane, lanes)]
        first = pl.multiple_of(which * self.ins[source].shape[0] + rows[0], 16)
        return out.at[pl.ds(first, rows[1]), pl.ds(lane, lanes)]

    def mine(self, chunk, side):
        source, _, rows, lane, _, lanes = self.chunks[chunk][1 + side]
        return self.ins[source].at[pl.ds(*rows), pl.ds(lane, lanes)]

    def own_copies(self, sems):
        me = lax.axis_index("dp")
        return [
            pltpu.make_async_copy(self.mine(chunk, side), self.part(me, chunk, side), sems.at[chunk, side])
            for chunk in range(len(self.chunks))
            for side in range(2)
        ]

    def send(self, core, chunk, offsets, level, distance):
        order = self.chunks[chunk][0][core]
        gid = place(self.dims, order, self.position, offsets)
        number = self.sent.get((core, chunk), 0)
        self.sent[core, chunk] = number + 1
        pltpu.make_async_remote_copy(
            src_ref=self.mine(chunk, core) if offsets == (0, 0, 0) else self.part(gid, chunk, core),
            dst_ref=self.part(gid, chunk, core),
            send_sem=self.send_sems.at[chunk, number],
            recv_sem=self.recv_sems.at[chunk, gid],
            device_id={"dp": place(self.dims, (order[level],), self.position, (distance,))},
            device_id_type=MESH,
        ).start()

    def spread(self, core, chunk, offsets, first):
        for level in range(first, 3):
            for distance in near_first(self.dims[self.chunks[chunk][0][core][level]]):
                self.send(core, chunk, offsets, level, distance)

    def forward(self, core, chunk, offsets, first):
        gid = place(self.dims, self.chunks[chunk][0][core], self.position, offsets)
        ref = self.part(gid, chunk, core)
        pltpu.make_async_copy(ref, ref, self.recv_sems.at[chunk, gid]).wait()
        self.spread(core, chunk, offsets, first)
        pltpu.make_async_remote_copy(
            src_ref=ref,
            dst_ref=ref,
            send_sem=self.push_send.at[chunk, gid],
            recv_sem=self.push_recv.at[chunk, gid],
            device_id={"seq": 1 - core},
            device_id_type=MESH,
        ).start()

    def tasks(self, core, chunk, stage):
        sizes = [self.dims[axis] for axis in self.chunks[chunk][0][core]]
        if stage == 0:
            return [functools.partial(self.spread, core, chunk, (0, 0, 0), 0)]
        if stage == 1:
            places = [(i, 0, 0) for i in near_first(sizes[0])]
        elif stage == 2:
            places = [(i, j, 0) for i in [0] + near_first(sizes[0]) for j in near_first(sizes[1])]
        else:
            places = [
                (i, j, k)
                for j in [0] + near_first(sizes[1])
                for i in [0] + near_first(sizes[0])
                for k in near_first(sizes[2])
            ]
        return [functools.partial(self.forward, core, chunk, offsets, stage) for offsets in places]

    def steps(self, core, step):
        done = []
        for stage in range(4):
            if 0 <= step - stage < len(self.chunks):
                done += self.tasks(core, step - stage, stage)
        return done

    def others(self, body):
        me = lax.axis_index("dp")

        @pl.loop(1, self.count)
        def _(offset):
            body(lax.rem(me + offset, self.count), offset)

    def arrived_block(self, core, chunk, gid):
        ref = self.part(gid, chunk, 1 - core)
        pltpu.make_async_copy(ref, ref, self.push_recv.at[chunk, gid]).wait()

    def arrived(self, core, chunk):
        def body(gid, _):
            ref = self.part(gid, chunk, 1 - core)
            pltpu.make_async_copy(ref, ref, self.push_recv.at[chunk, gid]).wait()

        self.others(body)

    def finish(self, core):
        for chunk in range(len(self.chunks)):

            def body(gid, number, chunk=chunk):
                ref = self.part(gid, chunk, core)
                pltpu.make_async_copy(ref, ref, self.push_send.at[chunk, gid]).wait()
                pltpu.make_async_copy(ref, ref, self.send_sems.at[chunk, number - 1]).wait()

            self.others(body)


def gather_kernel(dims, chunks, *refs):
    n_arr = len(refs[:-5]) // 2
    ins, outs = refs[:n_arr], refs[n_arr : 2 * n_arr]
    gather = Gather(dims, chunks, ins, outs, refs[2 * n_arr : 2 * n_arr + 4])
    local_sems = refs[-1]
    core_index = lax.axis_index("seq")
    greet(dims, gather.position, core_index)
    own = gather.own_copies(local_sems)
    for copy in own:
        copy.start()

    def run(core):
        for step in range(len(chunks) + 3):
            for task in gather.steps(core, step):
                task()
        for chunk in range(len(chunks)):
            gather.arrived(core, chunk)
        gather.finish(core)

    by_core(core_index, run)
    for copy in own:
        copy.wait()


def all_gather(arrays, chunks, dp, collective_id=0):
    dims = dp_factors(dp)
    n = len(chunks)
    any_ = pl.BlockSpec(memory_space=pl.ANY)
    return pl.pallas_call(
        functools.partial(gather_kernel, dims, chunks),
        out_shape=[jax.ShapeDtypeStruct((dp,) + a.shape, a.dtype) for a in arrays],
        in_specs=[any_] * len(arrays),
        out_specs=[any_] * len(arrays),
        scratch_shapes=[
            pltpu.SemaphoreType.DMA((n, dp)),
            pltpu.SemaphoreType.DMA((n, dp)),
            pltpu.SemaphoreType.DMA((n, dp)),
            pltpu.SemaphoreType.DMA((n, dp)),
            pltpu.SemaphoreType.DMA((n, 2)),
        ],
        compiler_params=pltpu.CompilerParams(collective_id=collective_id, has_side_effects=True),
    )(*arrays)


def scatter_kernel(dims, chunks, n_arr, *refs):
    ins, outs = refs[:n_arr], refs[n_arr : 2 * n_arr]
    scratch = list(refs[2 * n_arr :])
    n = len(chunks)
    stage_refs, pair_refs = scratch[:n], scratch[n : 2 * n]
    hop_refs = [scratch[(2 + level) * n : (3 + level) * n] for level in range(3)]
    (load_sems, pair_send, pair_recv, hop_send, hop_recv, last_send, last_recv) = scratch[5 * n :]
    position = position_of(dims)
    core_index = lax.axis_index("seq")
    greet(dims, position, core_index)

    def run(core):
        order = ORDERS[core]
        sizes = [dims[axis] for axis in order]
        started = []
        other_order = ORDERS[1 - core]
        other_sizes = [dims[axis] for axis in other_order]

        def part(array_refs, which, chunk, side):
            array, rows, lanes = chunks[chunk][side]
            return array_refs[array].at[which, pl.ds(*rows), pl.ds(*lanes)]

        def slot(level, offsets, distance):
            index = distance - 1
            for i in range(level):
                index = index * sizes[i] + offsets[i]
            return index

        def semaphore(level, index):
            return (1, sizes[0], sizes[0] * sizes[1])[level] + index - 1

        def begin(chunk):
            array = chunks[chunk][core][0]
            theirs = sorted(offsets_of(other_sizes), key=lambda o: (o[2] == 0, o[1] == 0, o[0] == 0))
            mine = sorted(offsets_of(sizes), key=lambda o: (o[2] == 0, o[1] == 0, o[0] == 0))
            for given, kept in zip(theirs, mine):
                gid = place(dims, other_order, position, given)
                copy = pltpu.make_async_remote_copy(
                    src_ref=part(ins, gid, chunk, 1 - core),
                    dst_ref=pair_refs[chunk].at[gid],
                    send_sem=pair_send.at[chunk],
                    recv_sem=pair_recv.at[chunk, gid],
                    device_id={"seq": 1 - core},
                    device_id_type=MESH,
                )
                copy.start()
                gid = place(dims, order, position, kept)
                pltpu.make_async_copy(
                    part(ins, gid, chunk, core), stage_refs[chunk].at[gid], load_sems.at[chunk, gid]
                ).start()

        def combine(chunk, offsets, target):
            gid = place(dims, order, position, offsets)
            own = stage_refs[chunk].at[gid]
            pair = pair_refs[chunk].at[gid]
            pltpu.make_async_copy(own, own, load_sems.at[chunk, gid]).wait()
            pltpu.make_async_copy(pair, pair, pair_recv.at[chunk, gid]).wait()
            terms = [own, pair]
            for level in (2, 1, 0):
                if offsets[level]:
                    break
                for distance in range(1, sizes[level]):
                    index = slot(level, offsets, distance)
                    ref = hop_refs[level][chunk].at[index]
                    pltpu.make_async_copy(ref, ref, hop_recv.at[chunk, semaphore(level, index)]).wait()
                    terms.append(ref)
            height = own.shape[0]

            tall = 16 if height % 16 == 0 else height

            @pl.loop(0, height // tall)
            def _(tile):
                rows = pl.ds(pl.multiple_of(tile * tall, tall), tall)
                total = terms[0][rows, :].astype(jnp.float32)
                for term in terms[1:]:
                    total = total + term[rows, :].astype(jnp.float32)
                if target is None:
                    own[rows, :] = total.astype(own.dtype)
                else:
                    target[rows, :] = total

            return gid

        def send(chunk, offsets):
            level = max(i for i in range(3) if offsets[i])
            gid = combine(chunk, offsets, None)
            index = slot(level, offsets, offsets[level])
            target = place(dims, (order[level],), position, (offsets[level],))
            copy = pltpu.make_async_remote_copy(
                src_ref=stage_refs[chunk].at[gid],
                dst_ref=hop_refs[level][chunk].at[index],
                send_sem=hop_send.at[chunk, semaphore(level, index)],
                recv_sem=hop_recv.at[chunk, semaphore(level, index)],
                device_id={"dp": target},
                device_id_type=MESH,
            )
            copy.start()
            started.append(copy)

        def final(chunk):
            array, rows, lanes = chunks[chunk][core]
            half = outs[array].at[pl.ds(*rows), pl.ds(*lanes)]
            combine(chunk, (0, 0, 0), half)
            copy = pltpu.make_async_remote_copy(
                src_ref=half,
                dst_ref=half,
                send_sem=last_send.at[chunk],
                recv_sem=last_recv.at[chunk],
                device_id={"seq": 1 - core},
                device_id_type=MESH,
            )
            copy.start()
            started.append(copy)

        for chunk in range(n):
            begin(chunk)

        def stage(chunk, number):
            if number == 0:
                for d in range(1, sizes[2]):
                    for i in range(sizes[0]):
                        for j in range(sizes[1]):
                            send(chunk, (i, (j + 1) % sizes[1], d))
            if number == 1:
                for d in range(1, sizes[1]):
                    for i in range(sizes[0]):
                        send(chunk, ((i + 1) % sizes[0], d, 0))
            if number == 2:
                for d in range(1, sizes[0]):
                    send(chunk, (d, 0, 0))
            if number == 3:
                final(chunk)

        for step in range(n + 3):
            for number in range(4):
                if 0 <= step - number < n:
                    stage(step - number, number)
        for chunk in range(n):
            array, rows, lanes = chunks[chunk][1 - core]
            half = outs[array].at[pl.ds(*rows), pl.ds(*lanes)]
            pltpu.make_async_copy(half, half, last_recv.at[chunk]).wait()
            sent = pair_refs[chunk]
            pltpu.make_async_copy(sent, sent, pair_send.at[chunk]).wait()
        for copy in started:
            copy.wait_send()

    for core in range(2):
        pl.when(core_index == core)(functools.partial(run, core))


def hop_slots(dims, order):
    a, b, c = [dims[axis] for axis in order]
    return (a - 1, a * (b - 1), a * b * (c - 1))


def reduce_scatter(arrays, chunks, dp, collective_id=1):
    dims = dp_factors(dp)
    n = len(chunks)
    any_ = pl.BlockSpec(memory_space=pl.ANY)
    shapes = [(chunk[0][1][1], chunk[0][2][1]) for chunk in chunks]
    slots = [max(pair) for pair in zip(hop_slots(dims, ORDERS[0]), hop_slots(dims, ORDERS[1]))]
    low = jnp.bfloat16
    scratch = [pltpu.VMEM((dp,) + s, low) for s in shapes] * 2
    for level in range(3):
        scratch += [pltpu.VMEM((slots[level],) + s, low) for s in shapes]
    return pl.pallas_call(
        functools.partial(scatter_kernel, dims, chunks, len(arrays)),
        out_shape=[jax.ShapeDtypeStruct(a.shape[1:], jnp.float32) for a in arrays],
        in_specs=[any_] * len(arrays),
        out_specs=[pl.BlockSpec(memory_space=pltpu.VMEM)] * len(arrays),
        scratch_shapes=scratch
        + [
            pltpu.SemaphoreType.DMA((n, dp)),
            pltpu.SemaphoreType.DMA((n,)),
            pltpu.SemaphoreType.DMA((n, dp)),
            pltpu.SemaphoreType.DMA((n, dp)),
            pltpu.SemaphoreType.DMA((n, dp)),
            pltpu.SemaphoreType.DMA((n,)),
            pltpu.SemaphoreType.DMA((n,)),
        ],
        compiler_params=pltpu.CompilerParams(
            collective_id=collective_id, has_side_effects=True, vmem_limit_bytes=58 << 20
        ),
    )(*arrays)


GROUPS = 16
KERNEL = 128
FINE = 16
COARSE = KERNEL // FINE
LANES = 128


def lane_numbers(rows):
    return lax.broadcasted_iota(jnp.int32, (rows, LANES), 1)


def take_group(ref, rows, group, width):
    start = group * width
    base = pl.multiple_of(start // LANES * LANES, LANES)
    window = ref[rows, pl.ds(base, 2 * LANES)]
    turned = pltpu.roll(window, lax.rem(2 * LANES - (start - base), 2 * LANES), 1)[:, :LANES]
    return jnp.where(lane_numbers(turned.shape[0]) < width, turned, 0.0)


def add_group(ref, values, group, width):
    start = group * width
    base = pl.multiple_of(start // LANES * LANES, LANES)
    wide = jnp.concatenate([values, jnp.zeros_like(values)], axis=1)
    ref[:, pl.ds(base, 2 * LANES)] += pltpu.roll(wide, start - base, 1)


def double_96(pair, moved):
    lane = lane_numbers(pair.shape[0])
    turned = pltpu.roll(moved, 96, 1)
    return jnp.where(lane < 96, pair, turned), jnp.where(lane < 64, turned, 0.0)


def double_192(first, second, moved_first, moved_second):
    lane = lane_numbers(first.shape[0])
    a, b = pltpu.roll(moved_first, 64, 1), pltpu.roll(moved_second, 64, 1)
    return first, jnp.where(lane < 64, second, a), jnp.where(lane < 64, a, b)


def fold_lanes(tiles, shift):
    a, b, c = tiles
    lane = lane_numbers(a.shape[0])
    tb, tc = pltpu.roll(b, 64, 1), pltpu.roll(c, 64, 1)
    a, b = shift(a, jnp.where(lane < 64, tb, tc), 4), shift(b, tc, 4)
    lane = lane_numbers(a.shape[0])
    far = jnp.where(lane < 32, pltpu.roll(a, 32, 1), pltpu.roll(b, 32, 1))
    a = shift(a, far, 2)
    a = shift(a, pltpu.roll(a, 80, 1), 1)
    return jnp.where(lane_numbers(a.shape[0]) < 48, a, 0.0)


def make_patch(padded, group, pack):
    reach = pack + FINE
    one = take_group(padded, slice(0, reach + KERNEL - FINE), group, 48)
    rows = one.shape[0] - FINE
    two = one[:rows] + pltpu.roll(one[FINE:], 48, 1)
    low, high = double_96(two[: rows - 2 * FINE], two[2 * FINE :])
    tiles = double_192(low[:reach], high[:reach], low[4 * FINE :], high[4 * FINE :])
    return jnp.concatenate(tiles, axis=1).astype(jnp.bfloat16)


def add_forward(total, patch, weight, group, pack):
    product = jnp.dot(patch, weight, preferred_element_type=jnp.float32)
    size = pack + 8
    near = product[:size, :384] + product[8 : 8 + size, 384:]

    def shift(base, moved, amount):
        return base + pltpu.roll(moved, size - amount, 0)

    tiles = [near[:, i * LANES : (i + 1) * LANES] for i in range(3)]
    add_group(total, fold_lanes(tiles, shift)[:pack], group, 48)


def fill_padded(padded, frames):
    half = KERNEL // 2
    padded[...] = jnp.zeros_like(padded)
    padded[half : half + frames.shape[0], 0 : frames.shape[1]] = frames[...].astype(jnp.float32)


def forward_kernel(pack, frames, weight, out, patches, padded, total):
    group = pl.program_id(0)

    @pl.when(group == 0)
    def _():
        fill_padded(padded, frames)
        total[...] = jnp.zeros_like(total)

    patch = make_patch(padded, group, pack)
    patches[0] = patch
    add_forward(total, patch, weight[0], group, pack)

    @pl.when(group == GROUPS - 1)
    def _():
        out[...] = total[:, : frames.shape[1]]


def conv_forward(frames, weight):
    pack, width = frames.shape
    reach = pack + FINE
    return pl.pallas_call(
        functools.partial(forward_kernel, pack),
        grid=(GROUPS,),
        out_shape=[
            jax.ShapeDtypeStruct((pack, width), jnp.float32),
            jax.ShapeDtypeStruct((GROUPS, reach, 384), jnp.bfloat16),
        ],
        in_specs=[
            pl.BlockSpec((pack, width), lambda g: (0, 0)),
            pl.BlockSpec((1, 384, 768), lambda g: (g, 0, 0)),
        ],
        out_specs=[
            pl.BlockSpec((pack, width), lambda g: (0, 0)),
            pl.BlockSpec((1, reach, 384), lambda g: (g, 0, 0)),
        ],
        scratch_shapes=[
            pltpu.VMEM((pack + KERNEL, width + LANES), jnp.float32),
            pltpu.VMEM((pack, width + LANES), jnp.float32),
        ],
        compiler_params=pltpu.CompilerParams(vmem_limit_bytes=40 << 20),
    )(frames, weight)


def backward_kernel(pack, grads, direct, weight, patches, out, weight_grad, padded, tall, total):
    group = pl.program_id(0)
    reach = pack + FINE
    edge = KERNEL // 2 - FINE

    @pl.when(group == 0)
    def _():
        padded[...] = jnp.zeros_like(padded)
        padded[:pack, : grads.shape[1]] = grads[...].astype(jnp.float32)
        tall[...] = jnp.zeros_like(tall)
        total[...] = jnp.zeros_like(total)
        total[:, : direct.shape[1]] = direct[...]

    def later(values, amount):
        return pltpu.roll(values, amount, 0)

    one = take_group(padded, slice(0, reach), group, 48)
    two = one + pltpu.roll(later(one, 1), 48, 1)
    low, high = double_96(two, later(two, 2))
    tiles = double_192(low, high, later(low, 4), later(high, 4))
    near = jnp.concatenate(tiles, axis=1)
    spread = jnp.concatenate([near, later(near, 8)], axis=1).astype(jnp.bfloat16)
    weight_grad[0] = lax.dot_general(
        patches[0], spread, (((0,), (0,)), ((), ())), preferred_element_type=jnp.float32
    ).astype(jnp.bfloat16)
    tall[edge : edge + reach] = lax.dot_general(
        spread, weight[0], (((1,), (1,)), ((), ())), preferred_element_type=jnp.float32
    )

    def shift(base, moved, amount):
        return base[amount * FINE :] + moved[: base.shape[0] - amount * FINE]

    tiles = [tall[:, i * LANES : (i + 1) * LANES] for i in range(3)]
    add_group(total, fold_lanes(tiles, shift), group, 48)

    @pl.when(group == GROUPS - 1)
    def _():
        out[...] = total[:, : grads.shape[1]]


def conv_backward(grads, direct, weight, patches):
    pack, width = grads.shape
    reach = pack + FINE
    whole = lambda g: (0, 0)
    each = lambda g: (g, 0, 0)
    return pl.pallas_call(
        functools.partial(backward_kernel, pack),
        grid=(GROUPS,),
        out_shape=[
            jax.ShapeDtypeStruct((pack, width), jnp.float32),
            jax.ShapeDtypeStruct(weight.shape, jnp.bfloat16),
        ],
        in_specs=[
            pl.BlockSpec((pack, width), whole),
            pl.BlockSpec((pack, width), whole),
            pl.BlockSpec((1, 384, 768), each),
            pl.BlockSpec((1, reach, 384), each),
        ],
        out_specs=[
            pl.BlockSpec((pack, width), whole),
            pl.BlockSpec((1, 384, 768), each),
        ],
        scratch_shapes=[
            pltpu.VMEM((reach, width + LANES), jnp.float32),
            pltpu.VMEM((pack + KERNEL - FINE, 384), jnp.float32),
            pltpu.VMEM((pack, width + LANES), jnp.float32),
        ],
        compiler_params=pltpu.CompilerParams(vmem_limit_bytes=40 << 20),
    )(grads, direct, weight, patches)


HEAD_DIM = 64
EPSILON = 1e-05
ROWS = 32
TILE = 256


def dot(a, b, contract=(1, 0)):
    return lax.dot_general(
        a, b, ((contract[:1], contract[1:]), ((), ())), preferred_element_type=jnp.float32
    )


def below_normal(values):
    return 0.5 * (1.0 + lax.erf(values * 0.7071067811865476))


def density(values):
    return jnp.exp(-0.5 * values * values) * 0.3989422804014327


def unit_norm(values):
    centered = values - jnp.mean(values, axis=-1, keepdims=True)
    inverse = lax.rsqrt(jnp.mean(centered * centered, axis=-1, keepdims=True) + EPSILON)
    return centered * inverse, inverse


def norm_back(grad, unit, inverse, gain):
    scaled = grad * gain
    inner = jnp.mean(scaled, axis=-1, keepdims=True)
    along = jnp.mean(scaled * unit, axis=-1, keepdims=True)
    return inverse * (scaled - inner - unit * along)


def row_tiles(pack, body):
    @pl.loop(0, pack // ROWS)
    def _(tile):
        body(pl.ds(pl.multiple_of(tile * ROWS, ROWS), ROWS))


def lane_tiles(count, body, first=0):
    @pl.loop(first, count)
    def _(tile):
        body(tile, pl.ds(pl.multiple_of(tile * TILE, TILE), TILE))


def clip_mask(lengths, micro, pack):
    row = lax.broadcasted_iota(jnp.int32, (pack, pack), 0)
    column = lax.broadcasted_iota(jnp.int32, (pack, pack), 1)
    row_clip, column_clip = jnp.zeros_like(row), jnp.zeros_like(column)
    end = 0
    for clip in range(lengths.shape[1]):
        end = end + lengths[micro, clip]
        row_clip += (row >= end).astype(jnp.int32)
        column_clip += (column >= end).astype(jnp.int32)
    return row_clip == column_clip


def front_norm(frames, convolved, gains, normed, normed_low, unit, inverse, front_slope):
    def body(rows):
        values = convolved[rows, 0 : frames.shape[1]]
        below = below_normal(values)
        front_slope[rows, :] = below + values * density(values)
        mixed = frames[rows, :].astype(jnp.float32) + values * below
        units, inv = unit_norm(mixed)
        unit[rows, :] = units
        inverse[rows, :] = jnp.broadcast_to(inv, (ROWS, LANES))
        total = units * gains[0:1, :]
        normed[rows, :] = total
        normed_low[rows, :] = total.astype(normed_low.dtype)

    row_tiles(frames.shape[0], body)


def project(normed_low, weight, projected):
    def body(tile, lanes):
        projected[:, lanes] = dot(normed_low[...], weight[:, lanes]).astype(projected.dtype)

    lane_tiles(projected.shape[1] // TILE, body)


def pair_parts(projected, pair, width):
    return [
        projected[:, pl.ds(pl.multiple_of(part * width + pair * LANES, LANES), LANES)] for part in range(3)
    ]


def attend(projected, lengths, micro, probs, attended, first=0, last=None):
    pack, width = attended.shape
    low = projected.dtype
    scale = HEAD_DIM ** (-0.5)

    @pl.loop(first, last or width // LANES)
    def _(pair):
        same = clip_mask(lengths, micro, pack)
        queries, keys, values = pair_parts(projected, pair, width)
        lane = lax.broadcasted_iota(jnp.int32, (pack, LANES), 1)
        sides = []
        for side in range(2):
            own = (lane < HEAD_DIM) == (side == 0)
            scores = dot(jnp.where(own, queries, jnp.zeros_like(queries)), keys, (1, 1)) * scale
            scores = jnp.where(same, scores, -1e30)
            shifted = jnp.exp(scores - jnp.max(scores, axis=-1, keepdims=True))
            weights = shifted / jnp.sum(shifted, axis=-1, keepdims=True)
            probs[2 * pair + side] = weights
            sides.append(dot(weights.astype(low), values))
        lanes = pl.ds(pl.multiple_of(pair * LANES, LANES), LANES)
        attended[:, lanes] = jnp.where(lane < HEAD_DIM, *sides).astype(low)


def middle_norm(attended, weight, normed, gains, middle, middle_low, unit, inverse):
    def body(tile, lanes):
        middle[:, lanes] = normed[:, lanes] + dot(attended[...], weight[:, lanes])

    lane_tiles(normed.shape[1] // TILE, body)

    def finish(rows):
        units, inv = unit_norm(middle[rows, :])
        unit[rows, :] = units
        inverse[rows, :] = jnp.broadcast_to(inv, (ROWS, LANES))
        total = units * gains[1:2, :]
        middle[rows, :] = total
        middle_low[rows, :] = total.astype(middle_low.dtype)

    row_tiles(normed.shape[0], finish)


def feed_up(middle_low, weight, slope, activated, first=0, last=None):
    def body(tile, lanes):
        values = dot(middle_low[...], weight[:, lanes])
        below = below_normal(values)
        slope[:, lanes] = (below + values * density(values)).astype(slope.dtype)
        activated[:, lanes] = (values * below).astype(activated.dtype)

    lane_tiles(last or slope.shape[1] // TILE, body, first)


def feed_down(activated, weight, middle, gains, cotangent, output, grad_final, gain_grads):
    def body(tile, lanes):
        middle[...] += dot(activated[:, lanes], weight[lanes, :])

    lane_tiles(activated.shape[1] // TILE, body)
    gain_grads[2:3, :] = jnp.zeros((1, middle.shape[1]), jnp.float32)

    def finish(rows):
        units, inv = unit_norm(middle[rows, :])
        gain = gains[2:3, :]
        output[rows, :] = (units * gain).astype(output.dtype)
        grad = cotangent[rows, :].astype(jnp.float32)
        gain_grads[2:3, :] += jnp.sum(grad * units, axis=0, keepdims=True)
        grad_final[rows, :] = norm_back(grad, units, inv, gain)

    row_tiles(middle.shape[0], finish)


def feed_back(grad, slope, activated, middle_low, up, down, up_grad, down_grad):
    low = activated.dtype
    grad_feed = grad[...].astype(low)
    turned = jnp.transpose(middle_low[...].astype(jnp.float32)).astype(low)

    def body(tile, lanes):
        down_grad[lanes, :] = dot(activated[:, lanes], grad_feed, (0, 0)).astype(low)
        grad_hidden = (dot(grad_feed, down[lanes, :], (1, 1)) * slope[:, lanes].astype(jnp.float32)).astype(low)
        up_grad[:, lanes] = dot(turned, grad_hidden).astype(low)
        grad[...] += dot(grad_hidden, up[:, lanes], (1, 1))

    lane_tiles(slope.shape[1] // TILE, body)


def norm_back_rows(grad, unit, inverse, gains, which, gain_grads):
    gain_grads[which : which + 1, :] = jnp.zeros((1, grad.shape[1]), jnp.float32)

    def body(rows):
        incoming, units = grad[rows, :], unit[rows, :]
        gain_grads[which : which + 1, :] += jnp.sum(incoming * units, axis=0, keepdims=True)
        grad[rows, :] = norm_back(incoming, units, inverse[rows, 0:1], gains[which : which + 1, :])

    row_tiles(grad.shape[0], body)


def branch_back(grad, attended, weight, grad_attended, out_grad):
    low = attended.dtype
    grad_branch = grad[...].astype(low)

    def body(tile, lanes):
        out_grad[lanes, :] = dot(attended[:, lanes], grad_branch, (0, 0)).astype(low)
        grad_attended[:, lanes] = dot(grad_branch, weight[lanes, :], (1, 1)).astype(low)

    lane_tiles(attended.shape[1] // TILE, body)


def attend_back_pair(projected, grad_attended, weights_of, grad_projected, pair):
    pack, width = grad_attended.shape
    low = projected.dtype
    scale = HEAD_DIM ** (-0.5)

    def lanes_of(part):
        start = part * width + pair * LANES
        return pl.ds(start if isinstance(pair, int) else pl.multiple_of(start, LANES), LANES)

    queries, keys, values = [projected[:, lanes_of(part)] for part in range(3)]
    grad = grad_attended[:, lanes_of(0)]
    lane = lax.broadcasted_iota(jnp.int32, (pack, LANES), 1)
    sides = []
    for side in range(2):
        own = (lane < HEAD_DIM) == (side == 0)
        weights = weights_of[side]
        grad_values = dot(weights.astype(low), grad, (0, 0))
        grad_probs = dot(jnp.where(own, grad, jnp.zeros_like(grad)), values, (1, 1))
        along = jnp.sum(weights * grad_probs, axis=-1, keepdims=True)
        grad_scores = (weights * (grad_probs - along)).astype(low)
        grad_queries = dot(grad_scores, keys) * scale
        grad_keys = dot(grad_scores, queries, (0, 0)) * scale
        sides.append((grad_queries, grad_keys, grad_values))
    for part in range(3):
        grad_projected[:, lanes_of(part)] = jnp.where(lane < HEAD_DIM, sides[0][part], sides[1][part]).astype(low)


def attend_back(projected, grad_attended, probs, grad_projected):
    @pl.loop(0, grad_attended.shape[1] // LANES)
    def _(pair):
        attend_back_pair(projected, grad_attended, probs.at[pl.ds(2 * pair, 2)], grad_projected, pair)


def project_back(grad, grad_projected, unit, gains, weight, qkv_grad):
    low = grad_projected.dtype
    turned = jnp.transpose(unit[...] * gains[0:1, :]).astype(low)

    def body(tile, lanes):
        qkv_grad[:, lanes] = dot(turned, grad_projected[:, lanes]).astype(low)
        grad[...] += dot(grad_projected[:, lanes], weight[:, lanes], (1, 1))

    lane_tiles(grad_projected.shape[1] // TILE, body)


def slope_rows(grad, front_slope, grad_convolved):
    def body(rows):
        grad_convolved[rows, :] = (grad[rows, :] * front_slope[rows, :]).astype(grad_convolved.dtype)

    row_tiles(grad.shape[0], body)


def middle_forward_kernel(
    lengths, frames, convolved, gains, wide, down, cotangent,
    output, front_slope, grad_final, unit_front, inverse_front, projected, probs, attended,
    unit_middle, inverse_middle, middle_low, slope, activated, gain_grads,
    normed, normed_low, middle,
):
    width = frames.shape[1]
    gain_grads[...] = jnp.zeros_like(gain_grads)
    front_norm(frames, convolved, gains, normed, normed_low, unit_front, inverse_front, front_slope)
    project(normed_low, wide.at[:, 0 : 3 * width], projected)
    attend(projected, lengths, 0, probs, attended)
    middle_norm(
        attended, wide.at[:, 3 * width : 4 * width], normed, gains, middle, middle_low, unit_middle,
        inverse_middle,
    )
    feed_up(middle_low, wide.at[:, 4 * width :], slope, activated)
    feed_down(activated, down, middle, gains, cotangent, output, grad_final, gain_grads)


def middle_backward_kernel(
    gains, wide, down, front_slope, grad_final, unit_front, inverse_front, projected, probs, attended,
    unit_middle, inverse_middle, middle_low, slope, activated, last_gain_grad,
    grad, grad_convolved, wide_grad, down_grad, gain_grads,
    grad_attended, grad_projected,
):
    width = grad.shape[1]
    gain_grads[...] = last_gain_grad[...]
    grad[...] = grad_final[...]
    feed_back(
        grad, slope, activated, middle_low, wide.at[:, 4 * width :], down, wide_grad.at[:, 4 * width :],
        down_grad,
    )
    norm_back_rows(grad, unit_middle, inverse_middle, gains, 1, gain_grads)
    branch_back(
        grad, attended, wide.at[:, 3 * width : 4 * width], grad_attended,
        wide_grad.at[:, 3 * width : 4 * width],
    )
    attend_back(projected, grad_attended, probs, grad_projected)
    project_back(
        grad, grad_projected, unit_front, gains, wide.at[:, 0 : 3 * width], wide_grad.at[:, 0 : 3 * width]
    )
    norm_back_rows(grad, unit_front, inverse_front, gains, 0, gain_grads)
    slope_rows(grad, front_slope, grad_convolved)


def middle_forward(frames, convolved, lengths, gains, wide, down, cotangent):
    pack, width = frames.shape
    inner = down.shape[0]
    heads = width // HEAD_DIM
    low, full = jnp.bfloat16, jnp.float32
    shape = jax.ShapeDtypeStruct
    vmem = pl.BlockSpec(memory_space=pltpu.VMEM)
    saved = [
        shape((pack, width), low),
        shape((pack, width), full),
        shape((pack, width), full),
        shape((pack, width), full),
        shape((pack, LANES), full),
        shape((pack, 3 * width), low),
        shape((heads, pack, pack), full),
        shape((pack, width), low),
        shape((pack, width), full),
        shape((pack, LANES), full),
        shape((pack, width), low),
        shape((pack, inner), low),
        shape((pack, inner), low),
        shape((8, width), full),
    ]
    return pl.pallas_call(
        middle_forward_kernel,
        out_shape=saved,
        in_specs=[pl.BlockSpec(memory_space=pltpu.SMEM)] + [vmem] * 6,
        out_specs=[vmem] * len(saved),
        scratch_shapes=[
            pltpu.VMEM((pack, width), full),
            pltpu.VMEM((pack, width), low),
            pltpu.VMEM((pack, width), full),
        ],
        compiler_params=pltpu.CompilerParams(vmem_limit_bytes=58 << 20),
    )(lengths, frames, convolved, gains, wide, down, cotangent)


def middle_backward(gains, wide, down, kept):
    pack, width = kept[0].shape
    low, full = jnp.bfloat16, jnp.float32
    shape = jax.ShapeDtypeStruct
    vmem = pl.BlockSpec(memory_space=pltpu.VMEM)
    grads = [
        shape((pack, width), full),
        shape((pack, width), low),
        shape(wide.shape, low),
        shape(down.shape, low),
        shape((8, width), full),
    ]
    return pl.pallas_call(
        middle_backward_kernel,
        out_shape=grads,
        in_specs=[vmem] * (3 + len(kept)),
        out_specs=[vmem] * len(grads),
        scratch_shapes=[pltpu.VMEM((pack, width), low), pltpu.VMEM((pack, 3 * width), low)],
        compiler_params=pltpu.CompilerParams(vmem_limit_bytes=58 << 20),
    )(gains, wide, down, *kept)


def weave(tasks, pieces):
    core_index = lax.axis_index("seq")
    count, done = len(tasks[0]), 0
    for number, piece in enumerate(pieces + [None]):
        until = count if piece is None else (number + 1) * count // (len(pieces) + 1)

        def some(core, first=done, last=until):
            for task in tasks[core][first:last]:
                task()

        if until > done:
            by_core(core_index, some)
        done = until
        if piece is not None:
            piece()


def fused_forward_kernel(
    dims, chunks,
    lengths, frames, cotangent, conv_shard, qkv_shard, out_shard, up_shard, down_shard, front_gain, middle_gain,
    final_gain,
    conv_out, wide_out, down_out, patches_out, front_slope_out, unit_front_out, projected_out, probs_out,
    attended_out, unit_middle_out, middle_low_out, both_output, gains, grad_final, inverse_front, inverse_middle,
    slope, activated, gain_grads,
    patches, front_slope, unit_front, projected, probs, attended, unit_middle, middle_low, gain_shard,
    conv_all, wide_all, down_all, gain_all, pack_frames, pack_cotangent, output, padded, total,
    gains_wide, normed, normed_low, middle,
    send_sems, recv_sems, push_send, push_recv, own_sems, local_sems, save_sems, pair_sems,
):
    ins = (conv_shard, qkv_shard, out_shard, up_shard, down_shard, gain_shard)
    outs = (conv_all, wide_all, down_all, gain_all)
    gather = Gather(dims, chunks, ins, outs, (send_sems, recv_sems, push_send, push_recv))
    core_index = lax.axis_index("seq")
    pack, width = pack_frames.shape
    half = pack // 2
    row = lax.broadcasted_iota(jnp.int32, (GAIN_ROWS, LANES), 0)
    rows = jnp.zeros((GAIN_ROWS, LANES), jnp.float32)
    for index, gain in enumerate((front_gain, middle_gain, final_gain)):
        one = gain[...].astype(jnp.float32)
        one = jnp.concatenate([one, jnp.zeros((1, LANES - one.shape[1]), jnp.float32)], axis=1)
        rows = jnp.where(row == index, one, rows)
    gain_shard[...] = jnp.concatenate([rows, rows], axis=0).astype(gain_shard.dtype)
    greet(dims, gather.position, core_index)

    here = pl.ds(pl.multiple_of(core_index * half, half), half)
    there = pl.ds(pl.multiple_of((1 - core_index) * half, half), half)

    def to_partner(source, target, number):
        return pltpu.make_async_remote_copy(
            src_ref=source,
            dst_ref=target,
            send_sem=pair_sems.at[0, number],
            recv_sem=pair_sems.at[1, number],
            device_id={"seq": 1 - core_index},
            device_id_type=MESH,
        )

    moves = []
    for number, (source, target) in enumerate(((frames, pack_frames), (cotangent, pack_cotangent))):
        moves.append(to_partner(source.at[1 - core_index], target.at[here], number))
        moves.append(pltpu.make_async_copy(source.at[core_index], target.at[here], local_sems.at[number]))
    for copy in moves:
        copy.start()
    own = gather.own_copies(own_sems)
    for copy in own:
        copy.start()

    def early(core):
        for chunk in range(3):
            for task in gather.tasks(core, chunk, 0):
                task()

    by_core(core_index, early)
    steps = []
    for step in range(1, len(chunks) + 3):
        both = []
        for core in range(2):
            tasks = []
            if 3 <= step + 2 < len(chunks):
                tasks += gather.tasks(core, step + 2, 0)
            for stage in (1, 2, 3):
                if 0 <= step - stage < len(chunks):
                    tasks += gather.tasks(core, step - stage, stage)
            both.append(tasks)
        steps.append(both)

    def gate(*numbers):
        def body(core):
            for number in numbers:
                gather.arrived(core, number)

        by_core(core_index, body)

    for copy in moves[:2]:
        copy.wait()
    fill_padded(padded, pack_frames)
    total[...] = jnp.zeros_like(total)

    def patch_piece(first, last):
        def piece():
            @pl.loop(first, last)
            def _(group):
                patches[group] = make_patch(padded, group, pack)

        return piece

    rank = [0] + near_first(dims[0])
    places = sorted(offsets_of(dims), key=lambda o: ((o[1] != 0) + (o[2] != 0), rank.index(o[0])))

    def conv_piece(offsets):
        group = place(dims, (0, 1, 2), gather.position, offsets)

        def wait(core):
            for chunk in (1, 2):
                gather.arrived_block(core, chunk, group)

        def piece():
            if offsets != (0, 0, 0):
                by_core(core_index, wait)
            add_forward(total, patches[group], conv_all[group], group, pack)

        return piece

    quarter = GROUPS // 4
    early_pieces = [patch_piece(i * quarter, (i + 1) * quarter) for i in range(4)]
    weave(steps[0], early_pieces[:1])
    weave(steps[1], early_pieces[1:3])
    weave(steps[2], early_pieces[3:])
    for copy in own:
        copy.wait()
    conv_pieces = [conv_piece(offsets) for offsets in places]
    alone = sum(1 for offsets in places if not (offsets[1] or offsets[2]))
    pairs = sum(1 for offsets in places if offsets[1] and offsets[2])
    weave(steps[3], conv_pieces[:alone])
    last = len(gather.tasks(0, 2, 3))
    weave([tasks[:-last] for tasks in steps[4]], [])
    taken = alone
    for number in range(last):
        many = 1 if number >= last - pairs else (len(places) - alone - pairs) // (last - pairs)
        weave([tasks[number - last :][:1] for tasks in steps[4]], [])
        for piece in conv_pieces[taken : taken + many]:
            piece()
        taken += many
    gate(0)
    saves = []

    def save(source, target):
        copy = pltpu.make_async_copy(source, target, save_sems.at[len(saves)])
        copy.start()
        saves.append(copy)

    save(patches, patches_out)
    save(conv_all, conv_out)
    gains_wide[...] = jnp.zeros_like(gains_wide)

    @pl.loop(0, gather.count)
    def _(shard):
        add_group(gains_wide, gain_all[shard, 0:16, :].astype(jnp.float32), shard, width // gather.count)

    gains[...] = gains_wide[0:8, 0:width]
    def front_piece():
        front_norm(pack_frames, total, gains, normed, normed_low, unit_front, inverse_front, front_slope)
        save(front_slope, front_slope_out)
        save(unit_front, unit_front_out)

    def project_piece():
        gate(3)
        project(normed_low, wide_all.at[:, 0 : 3 * width], projected)
        save(projected, projected_out)

    def attend_piece(first, last):
        return lambda: attend(projected, lengths, core_index, probs, attended, first, last)

    def middle_piece():
        gate(4)
        save(probs, probs_out)
        save(attended, attended_out)
        middle_norm(
            attended, wide_all.at[:, 3 * width : 4 * width], normed, gains, middle, middle_low, unit_middle,
            inverse_middle,
        )
        save(unit_middle, unit_middle_out)
        save(middle_low, middle_low_out)

    head_pairs = width // LANES
    weave(steps[5], [front_piece])
    weave(steps[6], [project_piece] + [attend_piece(i, i + 2) for i in range(0, head_pairs, 2)])
    weave(steps[7], [middle_piece])
    up = wide_all.at[:, 4 * width :]
    count = slope.shape[1] // TILE
    third = count // 3

    def up_piece(first):
        def piece():
            if first == 0:
                gate(5)
                save(wide_all, wide_out)
            feed_up(middle_low, up, slope, activated, first, first + third)

        return piece

    weave(steps[8], [up_piece(i) for i in range(0, count, third)])
    gate(6)
    save(down_all, down_out)
    for copy in moves[2:]:
        copy.wait()
    gain_grads[...] = jnp.zeros_like(gain_grads)
    feed_down(activated, down_all, middle, gains, pack_cotangent, output, grad_final, gain_grads)
    last = to_partner(output.at[there], both_output.at[core_index], 2)
    last.start()
    stay = pltpu.make_async_copy(output.at[here], both_output.at[core_index], local_sems.at[2])
    stay.start()
    by_core(core_index, gather.finish)
    for copy in saves + [stay, last]:
        copy.wait()


def fused_forward(frames, cotangent, lengths, shards_in, chunks, dp):
    dims = dp_factors(dp)
    n = len(chunks)
    conv_shard, qkv_shard, out_shard, up_shard, down_shard = shards_in[:5]
    pack, width = 2 * frames.shape[1], frames.shape[2]
    inner = down_shard.shape[0] * dp
    heads = width // HEAD_DIM
    low, full = jnp.bfloat16, jnp.float32
    shape = jax.ShapeDtypeStruct
    vmem = pl.BlockSpec(memory_space=pltpu.VMEM)
    any_ = pl.BlockSpec(memory_space=pl.ANY)
    conv_shape = (dp,) + conv_shard.shape
    wide_shape = (width, 4 * width + up_shard.shape[1])
    down_shape = (inner, width)
    kept = [
        shape((GROUPS, pack + FINE, 384), low),
        shape((pack, width), full),
        shape((pack, width), full),
        shape((pack, 3 * width), low),
        shape((heads, pack, pack), full),
        shape((pack, width), low),
        shape((pack, width), full),
        shape((pack, width), low),
    ]
    saved = [
        shape(frames.shape, low),
        shape((8, width), full),
        shape((pack, width), full),
        shape((pack, LANES), full),
        shape((pack, LANES), full),
        shape((pack, inner), low),
        shape((pack, inner), low),
        shape((8, width), full),
    ]
    return pl.pallas_call(
        functools.partial(fused_forward_kernel, dims, chunks),
        out_shape=[shape(conv_shape, low), shape(wide_shape, low), shape(down_shape, low)] + kept + saved,
        in_specs=[pl.BlockSpec(memory_space=pltpu.SMEM)] + [any_] * 7 + [vmem] * 3,
        out_specs=[any_] * 11 + [vmem] * len(saved),
        scratch_shapes=[pltpu.VMEM(one.shape, one.dtype) for one in kept]
        + [
            pltpu.VMEM((2 * GAIN_ROWS, LANES), low),
            pltpu.VMEM(conv_shape, low),
            pltpu.VMEM(wide_shape, low),
            pltpu.VMEM(down_shape, low),
            pltpu.VMEM((dp, 2 * GAIN_ROWS, LANES), low),
            pltpu.VMEM((pack, width), low),
            pltpu.VMEM((pack, width), low),
            pltpu.VMEM((pack, width), low),
            pltpu.VMEM((pack + KERNEL, width + LANES), full),
            pltpu.VMEM((pack, width + LANES), full),
            pltpu.VMEM((16, width + LANES), full),
            pltpu.VMEM((pack, width), full),
            pltpu.VMEM((pack, width), low),
            pltpu.VMEM((pack, width), full),
            pltpu.SemaphoreType.DMA((n, dp)),
            pltpu.SemaphoreType.DMA((n, dp)),
            pltpu.SemaphoreType.DMA((n, dp)),
            pltpu.SemaphoreType.DMA((n, dp)),
            pltpu.SemaphoreType.DMA((n, 2)),
            pltpu.SemaphoreType.DMA((3,)),
            pltpu.SemaphoreType.DMA((11,)),
            pltpu.SemaphoreType.DMA((2, 3)),
        ],
        compiler_params=pltpu.CompilerParams(
            collective_id=2, has_side_effects=True, vmem_limit_bytes=60 << 20
        ),
    )(lengths, frames, cotangent, *shards_in)


STRIP = 384
DOWN, UP, OUT, QKV, GAIN, CONV = range(6)
CONV_PARTS = 4
SCATTER_ORDERS = (FIRST, FIRST, FIRST, FIRST, FIRST) + (FIRST,) * CONV_PARTS


class Scatter:
    def __init__(self, dims, heights, stages, pairs, hops, outs, conv_pair, sems):
        self.dims, self.heights = dims, heights
        self.stages, self.pairs, self.hops, self.outs, self.conv_pair = stages, pairs, hops, outs, conv_pair
        self.waited = set()
        self.pair_recv, self.hop_send, self.hop_recv, self.last_send, self.last_recv = sems
        self.position = position_of(dims)
        self.count = dims[0] * dims[1] * dims[2]

    def block(self, ref, chunk, gid):
        if len(ref.shape) == 3:
            return ref.at[gid]
        height = self.heights[chunk]
        return ref.at[pl.ds(pl.multiple_of(gid * height, 16), height)]

    def sizes(self, core, chunk):
        return [self.dims[axis] for axis in SCATTER_ORDERS[chunk][core]]

    def slot(self, core, chunk, level, offsets, distance):
        index = distance - 1
        for i in range(level):
            index = index * self.sizes(core, chunk)[i] + offsets[i]
        return index

    def semaphore(self, core, chunk, level, index):
        sizes = self.sizes(core, chunk)
        return (1, sizes[0], sizes[0] * sizes[1])[level] + index - 1

    def combine(self, core, chunk, offsets, target):
        order = SCATTER_ORDERS[chunk][core]
        gid = place(self.dims, order, self.position, offsets)
        own, pair = self.block(self.stages[chunk], chunk, gid), self.block(self.pairs[chunk], chunk, gid)
        natural = (core,) + tuple(offset for _, offset in sorted(zip(order, offsets)))
        if chunk >= CONV and natural not in self.waited:
            self.waited.add(natural)
            whole = self.conv_pair.at[gid]
            pltpu.make_async_copy(whole, whole, self.pair_recv.at[CONV, gid]).wait()
        terms = [own, pair]
        for level in (2, 1, 0):
            if offsets[level]:
                break
            for distance in range(1, self.sizes(core, chunk)[level]):
                index = self.slot(core, chunk, level, offsets, distance)
                ref = self.hops[level][chunk].at[index]
                number = self.semaphore(core, chunk, level, index)
                pltpu.make_async_copy(ref, ref, self.hop_recv.at[chunk, number]).wait()
                terms.append(ref)

        tall = 48 if own.shape[0] % 48 == 0 else 16

        @pl.loop(0, own.shape[0] // tall)
        def _(tile):
            rows = pl.ds(pl.multiple_of(tile * tall, 16), tall)
            if target is None and len(terms) == 2:
                own[rows, :] = own[rows, :] + pair[rows, :]
                return
            total = terms[0][rows, :].astype(jnp.float32)
            for term in terms[1:]:
                total = total + term[rows, :].astype(jnp.float32)
            if target is None:
                own[rows, :] = total.astype(own.dtype)
            else:
                target[rows, :] = total

        return own

    def send(self, core, chunk, offsets):
        level = max(i for i in range(3) if offsets[i])
        own = self.combine(core, chunk, offsets, None)
        index = self.slot(core, chunk, level, offsets, offsets[level])
        number = self.semaphore(core, chunk, level, index)
        pltpu.make_async_remote_copy(
            src_ref=own,
            dst_ref=self.hops[level][chunk].at[index],
            send_sem=self.hop_send.at[chunk, number],
            recv_sem=self.hop_recv.at[chunk, number],
            device_id={"dp": place(self.dims, (SCATTER_ORDERS[chunk][core][level],), self.position, (offsets[level],))},
            device_id_type=MESH,
        ).start()

    def half(self, chunk, core):
        out = self.outs[chunk]
        lanes = out.shape[1] // 2
        return out.at[:, pl.ds(core * lanes, lanes)]

    def final(self, core, chunk):
        half = self.half(chunk, core)
        self.combine(core, chunk, (0, 0, 0), half)
        pltpu.make_async_remote_copy(
            src_ref=half,
            dst_ref=half,
            send_sem=self.last_send.at[chunk],
            recv_sem=self.last_recv.at[chunk],
            device_id={"seq": 1 - core},
            device_id_type=MESH,
        ).start()

    def tasks(self, core, chunk, stage):
        sizes = self.sizes(core, chunk)
        if stage == 3:
            return [functools.partial(self.final, core, chunk)]
        if stage == 2:
            places = [(i, 0, 0) for i in near_first(sizes[0])[::-1]]
        elif stage == 1:
            places = [(i, d, 0) for d in near_first(sizes[1]) for i in near_first(sizes[0])[::-1] + [0]]
        else:
            places = [
                (i, j, d)
                for d in near_first(sizes[2])
                for j in near_first(sizes[1]) + [0]
                for i in near_first(sizes[0])[::-1] + [0]
            ]
        return [functools.partial(self.send, core, chunk, offsets) for offsets in places]

    def finish(self, core):
        for chunk in range(len(self.outs)):
            half = self.half(chunk, 1 - core)
            pltpu.make_async_copy(half, half, self.last_recv.at[chunk]).wait()
            pltpu.make_async_copy(half, half, self.last_send.at[chunk]).wait()

            @pl.loop(0, self.count - 1)
            def _(number, chunk=chunk):
                ref = self.block(self.stages[chunk], chunk, 0)
                pltpu.make_async_copy(ref, ref, self.hop_send.at[chunk, number]).wait()


class Stream:
    def __init__(self, buffer, sems):
        self.buffer, self.sems = buffer, sems

    def start(self, source, number):
        pltpu.make_async_copy(source, self.buffer.at[number % 2], self.sems.at[number % 2]).start()

    def take(self, number):
        ref = self.buffer.at[number % 2]
        pltpu.make_async_copy(ref, ref, self.sems.at[number % 2]).wait()
        return ref


class Outbox:
    def __init__(self, buffer, sems):
        self.buffer, self.sems, self.busy, self.number = buffer, sems, [None, None], 0

    def free(self):
        slot = self.number % 2
        self.number += 1
        if self.busy[slot] is not None:
            self.busy[slot].wait_send()
            self.busy[slot] = None
        return slot, self.buffer.at[slot]

    def send(self, slot, source, target, recv_sem):
        copy = pltpu.make_async_remote_copy(
            src_ref=source,
            dst_ref=target,
            send_sem=self.sems.at[slot],
            recv_sem=recv_sem,
            device_id={"seq": 1 - lax.axis_index("seq")},
            device_id_type=MESH,
        )
        copy.start()
        self.busy[slot] = copy

    def drain(self):
        for copy in self.busy:
            if copy is not None:
                copy.wait_send()
        self.busy = [None, None]


def spread_grads(padded, group, pack):
    def later(values, amount):
        return pltpu.roll(values, amount, 0)

    one = take_group(padded, slice(0, pack + FINE), group, 48)
    two = one + pltpu.roll(later(one, 1), 48, 1)
    low, high = double_96(two, later(two, 2))
    near = jnp.concatenate(double_192(low, high, later(low, 4), later(high, 4)), axis=1)
    return jnp.concatenate([near, later(near, 8)], axis=1).astype(jnp.bfloat16)


def add_backward(total, tall, spread, weight, group, pack):
    edge = KERNEL // 2 - FINE
    tall[edge : edge + pack + FINE] = dot(spread, weight, (1, 1))

    def shift(base, moved, amount):
        return base[amount * FINE :] + moved[: base.shape[0] - amount * FINE]

    tiles = [tall[:, i * LANES : (i + 1) * LANES] for i in range(3)]
    add_group(total, fold_lanes(tiles, shift), group, 48)


def fused_backward_kernel(
    dims,
    weight, wide, down, patches, probs, grad_final,
    gains, front_slope, unit_front, inverse_front, projected, attended, unit_middle, inverse_middle,
    middle_low, slope, activated, last_gain_grad,
    conv_out, qkv_out, out_out, up_out, down_out, gain_out, both_grads, *scratch,
):
    arrays = CONV + 1
    n = CONV + CONV_PARTS
    stages, pairs = scratch[:arrays], scratch[arrays : 2 * arrays]
    hops = [scratch[2 * arrays + level * n : 2 * arrays + (level + 1) * n] for level in range(3)]
    conv_rows = [pl.ds(i * (384 // CONV_PARTS), 384 // CONV_PARTS) for i in range(CONV_PARTS)]

    def in_parts(refs):
        return list(refs[:CONV]) + [refs[CONV].at[:, rows] for rows in conv_rows]

    outs = [down_out, up_out, out_out, qkv_out, gain_out] + [conv_out.at[rows] for rows in conv_rows]
    (
        grad, turned, grad_attended, grad_projected, padded, spread, tall, total, gain_grads, gain_wide,
        gain_box, tall_box, wide_box, tall_tiles, wide_tiles, prob_tiles, patch_tiles,
        pair_recv, hop_send, hop_recv, last_send, last_recv, box_sems, tile_sems, load_sems,
    ) = scratch[2 * arrays + 3 * n :]
    core_index = lax.axis_index("seq")
    other = 1 - core_index
    pack, width = grad.shape
    inner = activated.shape[1]
    low = jnp.bfloat16
    heights = [out.shape[0] for out in outs]
    scatter = Scatter(
        dims, heights, in_parts(stages), in_parts(pairs), hops, outs, pairs[CONV],
        (pair_recv, hop_send, hop_recv, last_send, last_recv),
    )
    tall_stream, wide_stream = Stream(tall_tiles, tile_sems.at[0]), Stream(wide_tiles, tile_sems.at[1])
    prob_stream, patch_stream = Stream(prob_tiles, tile_sems.at[2]), Stream(patch_tiles, tile_sems.at[3])
    tall_out, wide_out_box = Outbox(tall_box, box_sems.at[0]), Outbox(wide_box, box_sems.at[1])

    def strip(index, base=0):
        return pl.ds(pl.multiple_of(base + index * STRIP, LANES), STRIP)

    up_base, out_base = 4 * width, 3 * width
    load = pltpu.make_async_copy(grad_final, grad, load_sems.at[0])
    load.start()
    up_half, qkv_half, out_half = inner // 2, 3 * width // 2, width // 2
    up_strips, qkv_strips = up_half // STRIP, qkv_half // STRIP
    down_strips = inner // STRIP

    def ordered(index, strips):
        return jnp.where(index < strips, other * strips + index, core_index * strips + index - strips)

    def up_start(index):
        which = ordered(index, up_strips)
        wide_stream.start(wide.at[:, strip(which, up_base)], index)
        tall_stream.start(down.at[strip(which)], index)

    up_start(0)
    greet(dims, scatter.position, core_index)
    load.wait()

    def all_tasks(*wanted):
        return [[task for chunk, stage in wanted for task in scatter.tasks(core, chunk, stage)] for core in range(2)]

    def step(number):
        wanted = [(number - stage, stage) for stage in range(4) if 0 <= number - stage < n]
        return all_tasks(*wanted)

    def gate(chunk, count, height, lanes):
        for index in range(count):
            ref = pairs[chunk].at[pl.ds(0, height), pl.ds(0, lanes)]
            pltpu.make_async_copy(ref, ref, pair_recv.at[chunk, index]).wait()

    own_lanes = pl.ds(pl.multiple_of(core_index * out_half, LANES), out_half)
    other_lanes = pl.ds(pl.multiple_of(other * out_half, LANES), out_half)
    grad_feed = grad[...].astype(low)
    for index in range(down_strips):
        slot, box = tall_out.free()
        box[...] = dot(activated[:, index * STRIP : (index + 1) * STRIP], grad_feed, (0, 0)).astype(low)
        rows = pl.ds(index * STRIP, STRIP)
        tall_out.send(slot, box.at[:, other_lanes], pairs[DOWN].at[rows], pair_recv.at[DOWN, index])
        stages[DOWN][rows, :] = box[:, own_lanes]
    turned[...] = jnp.transpose(middle_low[...].astype(jnp.float32)).astype(low)
    gate(DOWN, down_strips, STRIP, out_half)
    spread[0:pack, :] = grad_feed

    def give(chunk, index, strips, values):
        if index < strips:
            slot, box = wide_out_box.free()
            box[...] = values
            lanes = pl.ds(index * STRIP, STRIP)
            wide_out_box.send(slot, box, pairs[chunk].at[:, lanes], pair_recv.at[chunk, index])
        else:
            stages[chunk][:, (index - strips) * STRIP : (index - strips + 1) * STRIP] = values

    def up_piece(index):
        def piece():
            if index + 1 < 2 * up_strips:
                up_start(index + 1)
            up_tile, down_tile = wide_stream.take(index), tall_stream.take(index)
            lanes = strip(ordered(index, up_strips))
            slopes = slope[:, lanes].astype(jnp.float32)
            grad_hidden = (dot(spread[0:pack, :], down_tile[...], (1, 1)) * slopes).astype(low)
            give(UP, index, up_strips, dot(turned[...], grad_hidden).astype(low))
            grad[...] += dot(grad_hidden, up_tile[...], (1, 1))

        return piece

    weave(step(0), [up_piece(i) for i in range(2 * up_strips)])

    def prob_start(pair):
        prob_stream.start(probs.at[pl.ds(2 * pair, 2)], pair)

    for index in range(2):
        tall_stream.start(wide.at[strip(index), out_base : out_base + width], index)
    prob_start(0)
    gain_grads[...] = last_gain_grad[...]

    def middle_piece():
        gate(UP, up_strips, width, STRIP)
        norm_back_rows(grad, unit_middle, inverse_middle, gains, 1, gain_grads)

    def out_piece():
        grad_branch = grad[...].astype(low)
        spread[0:pack, :] = grad_branch
        turned[...] = jnp.transpose(attended[...].astype(jnp.float32)).astype(low)
        for index, half in enumerate((other, core_index)):
            give(OUT, index, 1, dot(turned[...], spread[0:pack, strip(half)]).astype(low))
            tile = tall_stream.take(index)
            lanes = slice(index * STRIP, (index + 1) * STRIP)
            grad_attended[:, lanes] = dot(grad_branch, tile[...], (1, 1)).astype(low)

    pairs_of_heads = width // LANES

    def attend_piece(pair):
        def piece():
            if pair + 1 < pairs_of_heads:
                prob_start(pair + 1)
            attend_back_pair(projected, grad_attended, prob_stream.take(pair), grad_projected, pair)

        return piece

    def qkv_start(index):
        wide_stream.start(wide.at[:, strip(ordered(index, qkv_strips))], index)

    def qkv_piece(index):
        def piece():
            if index == 0:
                qkv_start(0)
                turned[...] = jnp.transpose(unit_front[...] * gains[0:1, :]).astype(low)
            if index + 1 < 2 * qkv_strips:
                qkv_start(index + 1)
            tile = wide_stream.take(index)
            values = grad_projected[:, strip(ordered(index, qkv_strips))]
            give(QKV, index, qkv_strips, dot(turned[...], values).astype(low))
            grad[...] += dot(values, tile[...], (1, 1))

        return piece

    places = sorted(offsets_of(dims), key=lambda o: (o[1] == 0) + (o[2] == 0))
    groups = [place(dims, (0, 1, 2), scatter.position, offsets) for offsets in places]

    def conv_start(number):
        tall_stream.start(weight.at[groups[number]], number)
        patch_stream.start(patches.at[groups[number]], number)

    def front_piece():
        conv_start(0)
        norm_back_rows(grad, unit_front, inverse_front, gains, 0, gain_grads)
        padded[...] = jnp.zeros_like(padded)
        tall[...] = jnp.zeros_like(tall)
        total[...] = jnp.zeros_like(total)
        total[:, :width] = grad[...]

        def body(rows):
            padded[rows, 0:width] = (grad[rows, :] * front_slope[rows, :]).astype(low).astype(jnp.float32)

        row_tiles(pack, body)
        gain_wide[...] = jnp.zeros_like(gain_wide)
        gain_wide[0:8, 0:width] = gain_grads[...]

        @pl.loop(0, scatter.count)
        def _(shard):
            one = take_group(gain_wide, slice(0, 16), shard, width // scatter.count)
            gain_box[shard] = one.astype(low)
            stages[GAIN][shard] = one.astype(low)

        gain_copy.start()

    gain_copy = pltpu.make_async_remote_copy(
        src_ref=gain_box,
        dst_ref=pairs[GAIN],
        send_sem=load_sems.at[1],
        recv_sem=load_sems.at[2],
        device_id={"seq": other},
        device_id_type=MESH,
    )

    def conv_piece(number):
        def piece():
            if number + 1 < len(groups):
                conv_start(number + 1)
            group = groups[number]
            tile, patch = tall_stream.take(number), patch_stream.take(number)
            spread[...] = spread_grads(padded, group, pack)
            slot, box = tall_out.free()
            box[...] = dot(patch[...], spread[...], (0, 0)).astype(low)
            tall_out.send(slot, box.at[:, other_lanes], pairs[CONV].at[group], pair_recv.at[CONV, group])
            stages[CONV][group] = box[:, own_lanes]
            add_backward(total, tall, spread[...], tile[...], group, pack)

        return piece

    middle_piece()
    weave(
        step(1),
        [out_piece]
        + [attend_piece(i) for i in range(pairs_of_heads)]
        + [qkv_piece(i) for i in range(2 * qkv_strips)]
        + [front_piece],
    )
    pieces = [conv_piece(i) for i in range(len(groups))]
    gate(OUT, 1, width, STRIP)
    weave(step(2), pieces[:7])
    gate(QKV, qkv_strips, width, STRIP)
    weave(step(3), pieces[7:14])
    gain_copy.wait()
    weave(step(4), pieces[14:])
    half = pack // 2
    here = pl.ds(pl.multiple_of(core_index * half, half), half)
    there = pl.ds(pl.multiple_of(other * half, half), half)
    frames_copy = pltpu.make_async_remote_copy(
        src_ref=total.at[there, pl.ds(0, width)],
        dst_ref=both_grads.at[core_index],
        send_sem=load_sems.at[3],
        recv_sem=load_sems.at[4],
        device_id={"seq": other},
        device_id_type=MESH,
    )
    frames_copy.start()
    both_grads[core_index] = total[here, 0:width]
    for number in range(5, n + 3):
        weave(step(number), [])
    by_core(core_index, scatter.finish)
    tall_out.drain()
    wide_out_box.drain()
    frames_copy.wait()


def fused_backward(weight, wide, down, patches, gains, kept, dp):
    dims = dp_factors(dp)
    (front_slope, grad_final, unit_front, inverse_front, projected, probs, attended, unit_middle,
     inverse_middle, middle_low, slope, activated, gain_grads) = kept
    pack, width = front_slope.shape
    inner = activated.shape[1]
    low, full = jnp.bfloat16, jnp.float32
    shape = jax.ShapeDtypeStruct
    vmem = pl.BlockSpec(memory_space=pltpu.VMEM)
    any_ = pl.BlockSpec(memory_space=pl.ANY)
    rows = width // dp
    flat = [(inner, width // 2), (width, inner // 2), (width, width // 2), (width, 3 * width // 2)]
    wholes = flat + [(dp, 16, LANES), (dp, 384, 384)]
    blocks = [(s[0] // dp, s[1]) for s in flat] + [(16, LANES)] + [(384 // CONV_PARTS, 384)] * CONV_PARTS
    n = len(blocks)
    scratch = [pltpu.VMEM(s, low) for s in wholes] * 2
    for level in range(3):
        for block, orders in zip(blocks, SCATTER_ORDERS):
            slots = max(hop_slots(dims, order)[level] for order in orders)
            scratch.append(pltpu.VMEM((slots,) + block, low))
    tall_rows = pack + FINE
    scratch += [
        pltpu.VMEM((pack, width), full),
        pltpu.VMEM((width, pack), low),
        pltpu.VMEM((pack, width), low),
        pltpu.VMEM((pack, 3 * width), low),
        pltpu.VMEM((tall_rows, width + LANES), full),
        pltpu.VMEM((tall_rows, width), low),
        pltpu.VMEM((pack + KERNEL - FINE, 384), full),
        pltpu.VMEM((pack, width + LANES), full),
        pltpu.VMEM((8, width), full),
        pltpu.VMEM((16, width + LANES), full),
        pltpu.VMEM((dp, 16, LANES), low),
        pltpu.VMEM((2, STRIP, width), low),
        pltpu.VMEM((2, width, STRIP), low),
        pltpu.VMEM((2, STRIP, width), low),
        pltpu.VMEM((2, width, STRIP), low),
        pltpu.VMEM((2, 2, pack, pack), full),
        pltpu.VMEM((2, tall_rows, 384), low),
        pltpu.SemaphoreType.DMA((n, dp)),
        pltpu.SemaphoreType.DMA((n, dp)),
        pltpu.SemaphoreType.DMA((n, dp)),
        pltpu.SemaphoreType.DMA((n,)),
        pltpu.SemaphoreType.DMA((n,)),
        pltpu.SemaphoreType.DMA((2, 2)),
        pltpu.SemaphoreType.DMA((4, 2)),
        pltpu.SemaphoreType.DMA((5,)),
    ]
    return pl.pallas_call(
        functools.partial(fused_backward_kernel, dims),
        out_shape=[
            shape((384, width), full),
            shape((rows, 3 * width), full),
            shape((rows, width), full),
            shape((rows, inner), full),
            shape((inner // dp, width), full),
            shape((16, 2 * LANES), full),
            shape((2, pack // 2, width), full),
        ],
        in_specs=[any_] * 6 + [vmem] * 12,
        out_specs=[vmem] * 7,
        scratch_shapes=scratch,
        compiler_params=pltpu.CompilerParams(
            collective_id=3, has_side_effects=True, vmem_limit_bytes=63 << 20
        ),
    )(weight, wide, down, patches, probs, grad_final, gains, front_slope, unit_front, inverse_front,
      projected, attended, unit_middle, inverse_middle, middle_low, slope, activated, gain_grads)


GAIN_ROWS = 16


def chunks_of(conv_rows, conv_lanes, wide_rows, width, down_rows):
    both = range(2)
    quarter, half = conv_rows // 4, width // 2
    conv = [
        [(0, ((2 * part + core) * quarter, quarter), (0, conv_lanes)) for core in both] for part in both
    ]
    wide = [
        [(1, (0, wide_rows), ((2 * part + core) * 2 * width, 2 * width)) for core in both] for part in both
    ]
    down = [[(2, (0, down_rows), (core * half, half)) for core in both]]
    gain = [[(3, (core * GAIN_ROWS, GAIN_ROWS), (0, LANES)) for core in both]]
    return gain, conv, wide, down


def gather_chunks(chunks):
    return [
        (FIRST,) + tuple((array, array, rows, lanes[0], lanes[0], lanes[1]) for array, rows, lanes in chunk)
        for chunk in chunks
    ]


def fused_chunks(conv_rows, width, wide_rows, inner, down_rows):
    quarter = conv_rows // 4
    chunks = [(FIRST,) + tuple((5, 3, (core * GAIN_ROWS, GAIN_ROWS), 0, 0, LANES) for core in range(2))]
    for part, orders in enumerate((FIRST, FIRST)):
        chunks.append(
            (orders,) + tuple((0, 0, ((2 * part + core) * quarter, quarter), 0, 0, width) for core in range(2))
        )
    begin = 0
    for source, lanes, orders in ((1, 3 * width, FIRST), (2, width, FIRST), (3, inner, SECOND)):
        half = lanes // 2
        chunks.append(
            (orders,)
            + tuple((source, 1, (0, wide_rows), core * half, begin + core * half, half) for core in range(2))
        )
        begin += lanes
    half = width // 2
    chunks.append(
        (FIRST,) + tuple((4, 2, (0, down_rows), core * half, core * half, half) for core in range(2))
    )
    return chunks


def shards(
    frames,
    clip_lengths,
    conv_weight,
    front_gain,
    qkv_weight,
    out_weight,
    middle_gain,
    up_weight,
    down_weight,
    final_gain,
    cotangent,
):
    dp = lax.axis_size("dp")
    low = jnp.bfloat16
    width = frames.shape[2]
    columns = conv_weight.shape[2]
    group_width = conv_weight.shape[1]
    gain_width = front_gain.shape[0]
    conv_shard = (
        conv_weight.reshape(COARSE, FINE, group_width, columns)
        .transpose(0, 2, 1, 3)
        .reshape(COARSE * group_width, FINE * columns)
    )
    split = group_width // columns
    if split == 1:
        shards_in = (conv_shard, qkv_weight, out_weight, up_weight, down_weight) + tuple(
            gain[None] for gain in (front_gain, middle_gain, final_gain)
        )
        chunks = fused_chunks(conv_shard.shape[0], width, qkv_weight.shape[0], up_weight.shape[1], down_weight.shape[0])
        (weight, wide, down, patches, front_slope, unit_front, projected, probs, attended, unit_middle, middle_low,
         outputs, gains, grad_final, inverse_front, inverse_middle, slope, activated, last_gain_grad) = fused_forward(
            frames, cotangent, clip_lengths[:, 0], shards_in, chunks, dp
        )
        kept = (front_slope, grad_final, unit_front, inverse_front, projected, probs, attended, unit_middle,
                inverse_middle, middle_low, slope, activated, last_gain_grad)
    else:
        wide_shard = jnp.concatenate([qkv_weight, out_weight, up_weight], axis=1)
        gain_shard = jnp.pad(
            jnp.stack([front_gain, middle_gain, final_gain]),
            ((0, 2 * GAIN_ROWS - 3), (0, LANES - gain_width)),
        )
        parts = (conv_shard, wide_shard, down_weight, gain_shard)
        gain_chunk, conv_chunks, wide_chunks, down_chunk = chunks_of(
            *conv_shard.shape, wide_shard.shape[0], width, down_weight.shape[0]
        )
        chunks = gather_chunks(gain_chunk + conv_chunks + wide_chunks + down_chunk)
        conv_all, wide_all, down_all, gain_all = all_gather(parts, chunks, dp)
        weight = (
            conv_all.reshape(GROUPS, split, COARSE * group_width, FINE, columns)
            .transpose(0, 2, 3, 1, 4)
            .reshape(GROUPS, COARSE * group_width, FINE * group_width)
        )
        wide = wide_all.reshape(width, wide_shard.shape[1])
        down = down_all.reshape(-1, width)
        gains = gain_all[:, :3, :gain_width].transpose(1, 0, 2).reshape(3, width).astype(jnp.float32)
        gains = jnp.pad(gains, ((0, 5), (0, 0)))
        both = lax.all_to_all(
            jnp.stack([frames, cotangent], axis=1), "seq", split_axis=0, concat_axis=2, tiled=True
        )
        pack_frames, pack_cotangent = both[0, 0], both[0, 1]
        lengths = lax.dynamic_index_in_dim(clip_lengths[:, 0], lax.axis_index("seq"), 0)
        convolved, patches = conv_forward(pack_frames, weight)
        output, *kept = middle_forward(
            pack_frames, convolved, lengths, gains, wide, down, pack_cotangent
        )
        outputs = lax.all_to_all(output[None], "seq", split_axis=1, concat_axis=0, tiled=True)

    if split == 1:
        conv_sum, qkv_sum, out_sum, up_sum, down_sum, gain_sum, frame_grads = fused_backward(
            weight, wide, down, patches, gains, kept, dp
        )
    else:
        grad_mixed, grad_convolved, wide_grad, down_grad, gain_grads = middle_backward(
            gains, wide, down, kept
        )
        frame_grad, conv_grad = conv_backward(grad_convolved, grad_mixed, weight, patches)

        conv_blocks = (
            conv_grad.reshape(GROUPS, COARSE * group_width, FINE, split, columns)
            .transpose(0, 3, 1, 2, 4)
            .reshape((dp,) + conv_shard.shape)
        )
        gain_blocks = jnp.pad(
            gain_grads[:3].astype(low).reshape(3, dp, gain_width).transpose(1, 0, 2),
            ((0, 0), (0, 2 * GAIN_ROWS - 3), (0, LANES - gain_width)),
        )
        conv_sum, wide_sum, down_sum, gain_sum = reduce_scatter(
            (
                conv_blocks,
                wide_grad.reshape((dp,) + wide_shard.shape),
                down_grad.reshape((dp,) + down_weight.shape),
                gain_blocks,
            ),
            gain_chunk + down_chunk + wide_chunks[::-1] + conv_chunks,
            dp,
        )
        qkv_sum, out_sum, up_sum = (
            wide_sum[:, : 3 * width],
            wide_sum[:, 3 * width : 4 * width],
            wide_sum[:, 4 * width :],
        )
        frame_grads = lax.all_to_all(frame_grad[None], "seq", split_axis=1, concat_axis=0, tiled=True)

    conv_sum = (
        conv_sum.reshape(COARSE, group_width, FINE, columns)
        .transpose(0, 2, 1, 3)
        .reshape(conv_weight.shape)
    )
    return (
        outputs,
        frame_grads,
        conv_sum,
        gain_sum[0, :gain_width],
        qkv_sum,
        out_sum,
        gain_sum[1, :gain_width],
        up_sum,
        down_sum,
        gain_sum[2, :gain_width],
    )


def solution(mesh):
    frames_spec = P(None, ("dp", "seq"), None)
    row, matrix, columns = P("dp"), P("dp", None), P(None, None, "dp")
    return jax.shard_map(
        shards,
        mesh=mesh,
        in_specs=(
            frames_spec,
            P(None, "dp", None),
            columns,
            row,
            matrix,
            matrix,
            row,
            matrix,
            matrix,
            row,
            frames_spec,
        ),
        out_specs=(
            frames_spec,
            frames_spec,
            columns,
            row,
            matrix,
            matrix,
            row,
            matrix,
            matrix,
            row,
        ),
        check_vma=False,
    )
```

```python
import functools

import jax
import jax.numpy as jnp
from jax import lax
from jax.experimental import pallas as pl
from jax.experimental.pallas import tpu as pltpu
from jax.sharding import PartitionSpec as P

MESH = pl.DeviceIdType.MESH


def dp_factors(size):
    return {16: (4, 2, 2), 128: (4, 4, 8)}.get(size, (size, 1, 1))


def near_first(size):
    return [1, 3, 2] if size == 4 else list(range(1, size))


def offsets_of(dims):
    return [(i, j, k) for i in range(dims[0]) for j in range(dims[1]) for k in range(dims[2])]


def partner(coordinate, offset):
    bit = 1
    while bit <= offset:
        if offset & bit:
            coordinate = coordinate + bit - 2 * bit * lax.rem(coordinate // bit, 2)
        bit *= 2
    return coordinate


def place(dims, order, position, offsets):
    coords = list(position)
    for axis, offset in zip(order, offsets):
        if offset:
            coords[axis] = partner(coords[axis], offset)
    return (coords[0] * dims[1] + coords[1]) * dims[2] + coords[2]


def position_of(dims):
    me = lax.axis_index("dp")
    return (me // (dims[1] * dims[2]), lax.rem(me // dims[2], dims[1]), lax.rem(me, dims[2]))


def greet(dims, position, core):
    barrier = pltpu.get_barrier_semaphore()
    count = 1
    pl.semaphore_signal(barrier, inc=1, device_id={"seq": 1 - core}, device_id_type=MESH)
    for axis in range(3):
        for offset in range(1, dims[axis]):
            other = place(dims, (axis,), position, (offset,))
            pl.semaphore_signal(barrier, inc=1, device_id={"dp": other}, device_id_type=MESH)
            count += 1
    pl.semaphore_wait(barrier, count)


FIRST = ((0, 1, 2), (0, 2, 1))
SECOND = ((1, 0, 2), (2, 0, 1))
ORDERS = FIRST


def by_core(core_index, body):
    for core in range(2):
        pl.when(core_index == core)(functools.partial(body, core))


class Gather:
    def __init__(self, dims, chunks, ins, outs, sems):
        self.dims, self.chunks, self.ins, self.outs = dims, chunks, ins, outs
        self.send_sems, self.recv_sems, self.push_send, self.push_recv = sems
        self.position = position_of(dims)
        self.count = dims[0] * dims[1] * dims[2]
        self.sent = {}

    def part(self, which, chunk, side):
        source, array, rows, _, lane, lanes = self.chunks[chunk][1 + side]
        out = self.outs[array]
        if len(out.shape) == 3:
            return out.at[which, pl.ds(*rows), pl.ds(lane, lanes)]
        first = pl.multiple_of(which * self.ins[source].shape[0] + rows[0], 16)
        return out.at[pl.ds(first, rows[1]), pl.ds(lane, lanes)]

    def mine(self, chunk, side):
        source, _, rows, lane, _, lanes = self.chunks[chunk][1 + side]
        return self.ins[source].at[pl.ds(*rows), pl.ds(lane, lanes)]

    def own_copies(self, sems):
        me = lax.axis_index("dp")
        return [
            pltpu.make_async_copy(self.mine(chunk, side), self.part(me, chunk, side), sems.at[chunk, side])
            for chunk in range(len(self.chunks))
            for side in range(2)
        ]

    def send(self, core, chunk, offsets, level, distance):
        order = self.chunks[chunk][0][core]
        gid = place(self.dims, order, self.position, offsets)
        number = self.sent.get((core, chunk), 0)
        self.sent[core, chunk] = number + 1
        pltpu.make_async_remote_copy(
            src_ref=self.mine(chunk, core) if offsets == (0, 0, 0) else self.part(gid, chunk, core),
            dst_ref=self.part(gid, chunk, core),
            send_sem=self.send_sems.at[chunk, number],
            recv_sem=self.recv_sems.at[chunk, gid],
            device_id={"dp": place(self.dims, (order[level],), self.position, (distance,))},
            device_id_type=MESH,
        ).start()

    def spread(self, core, chunk, offsets, first):
        for level in range(first, 3):
            for distance in near_first(self.dims[self.chunks[chunk][0][core][level]]):
                self.send(core, chunk, offsets, level, distance)

    def forward(self, core, chunk, offsets, first):
        gid = place(self.dims, self.chunks[chunk][0][core], self.position, offsets)
        ref = self.part(gid, chunk, core)
        pltpu.make_async_copy(ref, ref, self.recv_sems.at[chunk, gid]).wait()
        self.spread(core, chunk, offsets, first)
        pltpu.make_async_remote_copy(
            src_ref=ref,
            dst_ref=ref,
            send_sem=self.push_send.at[chunk, gid],
            recv_sem=self.push_recv.at[chunk, gid],
            device_id={"seq": 1 - core},
            device_id_type=MESH,
        ).start()

    def tasks(self, core, chunk, stage):
        sizes = [self.dims[axis] for axis in self.chunks[chunk][0][core]]
        if stage == 0:
            return [functools.partial(self.spread, core, chunk, (0, 0, 0), 0)]
        if stage == 1:
            places = [(i, 0, 0) for i in near_first(sizes[0])]
        elif stage == 2:
            places = [(i, j, 0) for i in [0] + near_first(sizes[0]) for j in near_first(sizes[1])]
        else:
            places = [
                (i, j, k)
                for j in [0] + near_first(sizes[1])
                for i in [0] + near_first(sizes[0])
                for k in near_first(sizes[2])
            ]
        return [functools.partial(self.forward, core, chunk, offsets, stage) for offsets in places]

    def steps(self, core, step):
        done = []
        for stage in range(4):
            if 0 <= step - stage < len(self.chunks):
                done += self.tasks(core, step - stage, stage)
        return done

    def others(self, body):
        me = lax.axis_index("dp")

        @pl.loop(1, self.count)
        def _(offset):
            body(lax.rem(me + offset, self.count), offset)

    def arrived_block(self, core, chunk, gid):
        ref = self.part(gid, chunk, 1 - core)
        pltpu.make_async_copy(ref, ref, self.push_recv.at[chunk, gid]).wait()

    def arrived(self, core, chunk):
        def body(gid, _):
            ref = self.part(gid, chunk, 1 - core)
            pltpu.make_async_copy(ref, ref, self.push_recv.at[chunk, gid]).wait()

        self.others(body)

    def finish(self, core):
        for chunk in range(len(self.chunks)):

            def body(gid, number, chunk=chunk):
                ref = self.part(gid, chunk, core)
                pltpu.make_async_copy(ref, ref, self.push_send.at[chunk, gid]).wait()
                pltpu.make_async_copy(ref, ref, self.send_sems.at[chunk, number - 1]).wait()

            self.others(body)


def gather_kernel(dims, chunks, *refs):
    n_arr = len(refs[:-5]) // 2
    ins, outs = refs[:n_arr], refs[n_arr : 2 * n_arr]
    gather = Gather(dims, chunks, ins, outs, refs[2 * n_arr : 2 * n_arr + 4])
    local_sems = refs[-1]
    core_index = lax.axis_index("seq")
    greet(dims, gather.position, core_index)
    own = gather.own_copies(local_sems)
    for copy in own:
        copy.start()

    def run(core):
        for step in range(len(chunks) + 3):
            for task in gather.steps(core, step):
                task()
        for chunk in range(len(chunks)):
            gather.arrived(core, chunk)
        gather.finish(core)

    by_core(core_index, run)
    for copy in own:
        copy.wait()


def all_gather(arrays, chunks, dp, collective_id=0):
    dims = dp_factors(dp)
    n = len(chunks)
    any_ = pl.BlockSpec(memory_space=pl.ANY)
    return pl.pallas_call(
        functools.partial(gather_kernel, dims, chunks),
        out_shape=[jax.ShapeDtypeStruct((dp,) + a.shape, a.dtype) for a in arrays],
        in_specs=[any_] * len(arrays),
        out_specs=[any_] * len(arrays),
        scratch_shapes=[
            pltpu.SemaphoreType.DMA((n, dp)),
            pltpu.SemaphoreType.DMA((n, dp)),
            pltpu.SemaphoreType.DMA((n, dp)),
            pltpu.SemaphoreType.DMA((n, dp)),
            pltpu.SemaphoreType.DMA((n, 2)),
        ],
        compiler_params=pltpu.CompilerParams(collective_id=collective_id, has_side_effects=True),
    )(*arrays)


def scatter_kernel(dims, chunks, n_arr, *refs):
    ins, outs = refs[:n_arr], refs[n_arr : 2 * n_arr]
    scratch = list(refs[2 * n_arr :])
    n = len(chunks)
    stage_refs, pair_refs = scratch[:n], scratch[n : 2 * n]
    hop_refs = [scratch[(2 + level) * n : (3 + level) * n] for level in range(3)]
    (load_sems, pair_send, pair_recv, hop_send, hop_recv, last_send, last_recv) = scratch[5 * n :]
    position = position_of(dims)
    core_index = lax.axis_index("seq")
    greet(dims, position, core_index)

    def run(core):
        order = ORDERS[core]
        sizes = [dims[axis] for axis in order]
        started = []
        other_order = ORDERS[1 - core]
        other_sizes = [dims[axis] for axis in other_order]

        def part(array_refs, which, chunk, side):
            array, rows, lanes = chunks[chunk][side]
            return array_refs[array].at[which, pl.ds(*rows), pl.ds(*lanes)]

        def slot(level, offsets, distance):
            index = distance - 1
            for i in range(level):
                index = index * sizes[i] + offsets[i]
            return index

        def semaphore(level, index):
            return (1, sizes[0], sizes[0] * sizes[1])[level] + index - 1

        def begin(chunk):
            array = chunks[chunk][core][0]
            theirs = sorted(offsets_of(other_sizes), key=lambda o: (o[2] == 0, o[1] == 0, o[0] == 0))
            mine = sorted(offsets_of(sizes), key=lambda o: (o[2] == 0, o[1] == 0, o[0] == 0))
            for given, kept in zip(theirs, mine):
                gid = place(dims, other_order, position, given)
                copy = pltpu.make_async_remote_copy(
                    src_ref=part(ins, gid, chunk, 1 - core),
                    dst_ref=pair_refs[chunk].at[gid],
                    send_sem=pair_send.at[chunk],
                    recv_sem=pair_recv.at[chunk, gid],
                    device_id={"seq": 1 - core},
                    device_id_type=MESH,
                )
                copy.start()
                gid = place(dims, order, position, kept)
                pltpu.make_async_copy(
                    part(ins, gid, chunk, core), stage_refs[chunk].at[gid], load_sems.at[chunk, gid]
                ).start()

        def combine(chunk, offsets, target):
            gid = place(dims, order, position, offsets)
            own = stage_refs[chunk].at[gid]
            pair = pair_refs[chunk].at[gid]
            pltpu.make_async_copy(own, own, load_sems.at[chunk, gid]).wait()
            pltpu.make_async_copy(pair, pair, pair_recv.at[chunk, gid]).wait()
            terms = [own, pair]
            for level in (2, 1, 0):
                if offsets[level]:
                    break
                for distance in range(1, sizes[level]):
                    index = slot(level, offsets, distance)
                    ref = hop_refs[level][chunk].at[index]
                    pltpu.make_async_copy(ref, ref, hop_recv.at[chunk, semaphore(level, index)]).wait()
                    terms.append(ref)
            height = own.shape[0]

            tall = 16 if height % 16 == 0 else height

            @pl.loop(0, height // tall)
            def _(tile):
                rows = pl.ds(pl.multiple_of(tile * tall, tall), tall)
                total = terms[0][rows, :].astype(jnp.float32)
                for term in terms[1:]:
                    total = total + term[rows, :].astype(jnp.float32)
                if target is None:
                    own[rows, :] = total.astype(own.dtype)
                else:
                    target[rows, :] = total

            return gid

        def send(chunk, offsets):
            level = max(i for i in range(3) if offsets[i])
            gid = combine(chunk, offsets, None)
            index = slot(level, offsets, offsets[level])
            target = place(dims, (order[level],), position, (offsets[level],))
            copy = pltpu.make_async_remote_copy(
                src_ref=stage_refs[chunk].at[gid],
                dst_ref=hop_refs[level][chunk].at[index],
                send_sem=hop_send.at[chunk, semaphore(level, index)],
                recv_sem=hop_recv.at[chunk, semaphore(level, index)],
                device_id={"dp": target},
                device_id_type=MESH,
            )
            copy.start()
            started.append(copy)

        def final(chunk):
            array, rows, lanes = chunks[chunk][core]
            half = outs[array].at[pl.ds(*rows), pl.ds(*lanes)]
            combine(chunk, (0, 0, 0), half)
            copy = pltpu.make_async_remote_copy(
                src_ref=half,
                dst_ref=half,
                send_sem=last_send.at[chunk],
                recv_sem=last_recv.at[chunk],
                device_id={"seq": 1 - core},
                device_id_type=MESH,
            )
            copy.start()
            started.append(copy)

        for chunk in range(n):
            begin(chunk)

        def stage(chunk, number):
            if number == 0:
                for d in range(1, sizes[2]):
                    for i in range(sizes[0]):
                        for j in range(sizes[1]):
                            send(chunk, (i, (j + 1) % sizes[1], d))
            if number == 1:
                for d in range(1, sizes[1]):
                    for i in range(sizes[0]):
                        send(chunk, ((i + 1) % sizes[0], d, 0))
            if number == 2:
                for d in range(1, sizes[0]):
                    send(chunk, (d, 0, 0))
            if number == 3:
                final(chunk)

        for step in range(n + 3):
            for number in range(4):
                if 0 <= step - number < n:
                    stage(step - number, number)
        for chunk in range(n):
            array, rows, lanes = chunks[chunk][1 - core]
            half = outs[array].at[pl.ds(*rows), pl.ds(*lanes)]
            pltpu.make_async_copy(half, half, last_recv.at[chunk]).wait()
            sent = pair_refs[chunk]
            pltpu.make_async_copy(sent, sent, pair_send.at[chunk]).wait()
        for copy in started:
            copy.wait_send()

    for core in range(2):
        pl.when(core_index == core)(functools.partial(run, core))


def hop_slots(dims, order):
    a, b, c = [dims[axis] for axis in order]
    return (a - 1, a * (b - 1), a * b * (c - 1))


def reduce_scatter(arrays, chunks, dp, collective_id=1):
    dims = dp_factors(dp)
    n = len(chunks)
    any_ = pl.BlockSpec(memory_space=pl.ANY)
    shapes = [(chunk[0][1][1], chunk[0][2][1]) for chunk in chunks]
    slots = [max(pair) for pair in zip(hop_slots(dims, ORDERS[0]), hop_slots(dims, ORDERS[1]))]
    low = jnp.bfloat16
    scratch = [pltpu.VMEM((dp,) + s, low) for s in shapes] * 2
    for level in range(3):
        scratch += [pltpu.VMEM((slots[level],) + s, low) for s in shapes]
    return pl.pallas_call(
        functools.partial(scatter_kernel, dims, chunks, len(arrays)),
        out_shape=[jax.ShapeDtypeStruct(a.shape[1:], jnp.float32) for a in arrays],
        in_specs=[any_] * len(arrays),
        out_specs=[pl.BlockSpec(memory_space=pltpu.VMEM)] * len(arrays),
        scratch_shapes=scratch
        + [
            pltpu.SemaphoreType.DMA((n, dp)),
            pltpu.SemaphoreType.DMA((n,)),
            pltpu.SemaphoreType.DMA((n, dp)),
            pltpu.SemaphoreType.DMA((n, dp)),
            pltpu.SemaphoreType.DMA((n, dp)),
            pltpu.SemaphoreType.DMA((n,)),
            pltpu.SemaphoreType.DMA((n,)),
        ],
        compiler_params=pltpu.CompilerParams(
            collective_id=collective_id, has_side_effects=True, vmem_limit_bytes=58 << 20
        ),
    )(*arrays)


GROUPS = 16
KERNEL = 128
FINE = 16
COARSE = KERNEL // FINE
LANES = 128


def lane_numbers(rows):
    return lax.broadcasted_iota(jnp.int32, (rows, LANES), 1)


def take_group(ref, rows, group, width):
    start = group * width
    base = pl.multiple_of(start // LANES * LANES, LANES)
    window = ref[rows, pl.ds(base, 2 * LANES)]
    turned = pltpu.roll(window, lax.rem(2 * LANES - (start - base), 2 * LANES), 1)[:, :LANES]
    return jnp.where(lane_numbers(turned.shape[0]) < width, turned, 0.0)


def add_group(ref, values, group, width):
    start = group * width
    base = pl.multiple_of(start // LANES * LANES, LANES)
    wide = jnp.concatenate([values, jnp.zeros_like(values)], axis=1)
    ref[:, pl.ds(base, 2 * LANES)] += pltpu.roll(wide, start - base, 1)


def double_96(pair, moved):
    lane = lane_numbers(pair.shape[0])
    turned = pltpu.roll(moved, 96, 1)
    return jnp.where(lane < 96, pair, turned), jnp.where(lane < 64, turned, 0.0)


def double_192(first, second, moved_first, moved_second):
    lane = lane_numbers(first.shape[0])
    a, b = pltpu.roll(moved_first, 64, 1), pltpu.roll(moved_second, 64, 1)
    return first, jnp.where(lane < 64, second, a), jnp.where(lane < 64, a, b)


def fold_lanes(tiles, shift):
    a, b, c = tiles
    lane = lane_numbers(a.shape[0])
    tb, tc = pltpu.roll(b, 64, 1), pltpu.roll(c, 64, 1)
    a, b = shift(a, jnp.where(lane < 64, tb, tc), 4), shift(b, tc, 4)
    lane = lane_numbers(a.shape[0])
    far = jnp.where(lane < 32, pltpu.roll(a, 32, 1), pltpu.roll(b, 32, 1))
    a = shift(a, far, 2)
    a = shift(a, pltpu.roll(a, 80, 1), 1)
    return jnp.where(lane_numbers(a.shape[0]) < 48, a, 0.0)


def make_patch(padded, group, pack):
    reach = pack + FINE
    one = take_group(padded, slice(0, reach + KERNEL - FINE), group, 48)
    rows = one.shape[0] - FINE
    two = one[:rows] + pltpu.roll(one[FINE:], 48, 1)
    low, high = double_96(two[: rows - 2 * FINE], two[2 * FINE :])
    tiles = double_192(low[:reach], high[:reach], low[4 * FINE :], high[4 * FINE :])
    return jnp.concatenate(tiles, axis=1).astype(jnp.bfloat16)


def add_forward(total, patch, weight, group, pack):
    product = jnp.dot(patch, weight, preferred_element_type=jnp.float32)
    size = pack + 8
    near = product[:size, :384] + product[8 : 8 + size, 384:]

    def shift(base, moved, amount):
        return base + pltpu.roll(moved, size - amount, 0)

    tiles = [near[:, i * LANES : (i + 1) * LANES] for i in range(3)]
    add_group(total, fold_lanes(tiles, shift)[:pack], group, 48)


def fill_padded(padded, frames):
    half = KERNEL // 2
    padded[...] = jnp.zeros_like(padded)
    padded[half : half + frames.shape[0], 0 : frames.shape[1]] = frames[...].astype(jnp.float32)


def forward_kernel(pack, frames, weight, out, patches, padded, total):
    group = pl.program_id(0)

    @pl.when(group == 0)
    def _():
        fill_padded(padded, frames)
        total[...] = jnp.zeros_like(total)

    patch = make_patch(padded, group, pack)
    patches[0] = patch
    add_forward(total, patch, weight[0], group, pack)

    @pl.when(group == GROUPS - 1)
    def _():
        out[...] = total[:, : frames.shape[1]]


def conv_forward(frames, weight):
    pack, width = frames.shape
    reach = pack + FINE
    return pl.pallas_call(
        functools.partial(forward_kernel, pack),
        grid=(GROUPS,),
        out_shape=[
            jax.ShapeDtypeStruct((pack, width), jnp.float32),
            jax.ShapeDtypeStruct((GROUPS, reach, 384), jnp.bfloat16),
        ],
        in_specs=[
            pl.BlockSpec((pack, width), lambda g: (0, 0)),
            pl.BlockSpec((1, 384, 768), lambda g: (g, 0, 0)),
        ],
        out_specs=[
            pl.BlockSpec((pack, width), lambda g: (0, 0)),
            pl.BlockSpec((1, reach, 384), lambda g: (g, 0, 0)),
        ],
        scratch_shapes=[
            pltpu.VMEM((pack + KERNEL, width + LANES), jnp.float32),
            pltpu.VMEM((pack, width + LANES), jnp.float32),
        ],
        compiler_params=pltpu.CompilerParams(vmem_limit_bytes=40 << 20),
    )(frames, weight)


def backward_kernel(pack, grads, direct, weight, patches, out, weight_grad, padded, tall, total):
    group = pl.program_id(0)
    reach = pack + FINE
    edge = KERNEL // 2 - FINE

    @pl.when(group == 0)
    def _():
        padded[...] = jnp.zeros_like(padded)
        padded[:pack, : grads.shape[1]] = grads[...].astype(jnp.float32)
        tall[...] = jnp.zeros_like(tall)
        total[...] = jnp.zeros_like(total)
        total[:, : direct.shape[1]] = direct[...]

    def later(values, amount):
        return pltpu.roll(values, amount, 0)

    one = take_group(padded, slice(0, reach), group, 48)
    two = one + pltpu.roll(later(one, 1), 48, 1)
    low, high = double_96(two, later(two, 2))
    tiles = double_192(low, high, later(low, 4), later(high, 4))
    near = jnp.concatenate(tiles, axis=1)
    spread = jnp.concatenate([near, later(near, 8)], axis=1).astype(jnp.bfloat16)
    weight_grad[0] = lax.dot_general(
        patches[0], spread, (((0,), (0,)), ((), ())), preferred_element_type=jnp.float32
    ).astype(jnp.bfloat16)
    tall[edge : edge + reach] = lax.dot_general(
        spread, weight[0], (((1,), (1,)), ((), ())), preferred_element_type=jnp.float32
    )

    def shift(base, moved, amount):
        return base[amount * FINE :] + moved[: base.shape[0] - amount * FINE]

    tiles = [tall[:, i * LANES : (i + 1) * LANES] for i in range(3)]
    add_group(total, fold_lanes(tiles, shift), group, 48)

    @pl.when(group == GROUPS - 1)
    def _():
        out[...] = total[:, : grads.shape[1]]


def conv_backward(grads, direct, weight, patches):
    pack, width = grads.shape
    reach = pack + FINE
    whole = lambda g: (0, 0)
    each = lambda g: (g, 0, 0)
    return pl.pallas_call(
        functools.partial(backward_kernel, pack),
        grid=(GROUPS,),
        out_shape=[
            jax.ShapeDtypeStruct((pack, width), jnp.float32),
            jax.ShapeDtypeStruct(weight.shape, jnp.bfloat16),
        ],
        in_specs=[
            pl.BlockSpec((pack, width), whole),
            pl.BlockSpec((pack, width), whole),
            pl.BlockSpec((1, 384, 768), each),
            pl.BlockSpec((1, reach, 384), each),
        ],
        out_specs=[
            pl.BlockSpec((pack, width), whole),
            pl.BlockSpec((1, 384, 768), each),
        ],
        scratch_shapes=[
            pltpu.VMEM((reach, width + LANES), jnp.float32),
            pltpu.VMEM((pack + KERNEL - FINE, 384), jnp.float32),
            pltpu.VMEM((pack, width + LANES), jnp.float32),
        ],
        compiler_params=pltpu.CompilerParams(vmem_limit_bytes=40 << 20),
    )(grads, direct, weight, patches)


HEAD_DIM = 64
EPSILON = 1e-05
ROWS = 32
TILE = 256


def dot(a, b, contract=(1, 0)):
    return lax.dot_general(
        a, b, ((contract[:1], contract[1:]), ((), ())), preferred_element_type=jnp.float32
    )


def below_normal(values):
    return 0.5 * (1.0 + lax.erf(values * 0.7071067811865476))


def density(values):
    return jnp.exp(-0.5 * values * values) * 0.3989422804014327


def unit_norm(values):
    centered = values - jnp.mean(values, axis=-1, keepdims=True)
    inverse = lax.rsqrt(jnp.mean(centered * centered, axis=-1, keepdims=True) + EPSILON)
    return centered * inverse, inverse


def norm_back(grad, unit, inverse, gain):
    scaled = grad * gain
    inner = jnp.mean(scaled, axis=-1, keepdims=True)
    along = jnp.mean(scaled * unit, axis=-1, keepdims=True)
    return inverse * (scaled - inner - unit * along)


def row_tiles(pack, body):
    @pl.loop(0, pack // ROWS)
    def _(tile):
        body(pl.ds(pl.multiple_of(tile * ROWS, ROWS), ROWS))


def lane_tiles(count, body, first=0):
    @pl.loop(first, count)
    def _(tile):
        body(tile, pl.ds(pl.multiple_of(tile * TILE, TILE), TILE))


def clip_mask(lengths, micro, pack):
    row = lax.broadcasted_iota(jnp.int32, (pack, pack), 0)
    column = lax.broadcasted_iota(jnp.int32, (pack, pack), 1)
    row_clip, column_clip = jnp.zeros_like(row), jnp.zeros_like(column)
    end = 0
    for clip in range(lengths.shape[1]):
        end = end + lengths[micro, clip]
        row_clip += (row >= end).astype(jnp.int32)
        column_clip += (column >= end).astype(jnp.int32)
    return row_clip == column_clip


def front_norm(frames, convolved, gains, normed, normed_low, unit, inverse, front_slope):
    def body(rows):
        values = convolved[rows, 0 : frames.shape[1]]
        below = below_normal(values)
        front_slope[rows, :] = below + values * density(values)
        mixed = frames[rows, :].astype(jnp.float32) + values * below
        units, inv = unit_norm(mixed)
        unit[rows, :] = units
        inverse[rows, :] = jnp.broadcast_to(inv, (ROWS, LANES))
        total = units * gains[0:1, :]
        normed[rows, :] = total
        normed_low[rows, :] = total.astype(normed_low.dtype)

    row_tiles(frames.shape[0], body)


def project(normed_low, weight, projected):
    def body(tile, lanes):
        projected[:, lanes] = dot(normed_low[...], weight[:, lanes]).astype(projected.dtype)

    lane_tiles(projected.shape[1] // TILE, body)


def pair_parts(projected, pair, width):
    return [
        projected[:, pl.ds(pl.multiple_of(part * width + pair * LANES, LANES), LANES)] for part in range(3)
    ]


def attend(projected, lengths, micro, probs, attended, first=0, last=None):
    pack, width = attended.shape
    low = projected.dtype
    scale = HEAD_DIM ** (-0.5)

    @pl.loop(first, last or width // LANES)
    def _(pair):
        same = clip_mask(lengths, micro, pack)
        queries, keys, values = pair_parts(projected, pair, width)
        lane = lax.broadcasted_iota(jnp.int32, (pack, LANES), 1)
        sides = []
        for side in range(2):
            own = (lane < HEAD_DIM) == (side == 0)
            scores = dot(jnp.where(own, queries, jnp.zeros_like(queries)), keys, (1, 1)) * scale
            scores = jnp.where(same, scores, -1e30)
            shifted = jnp.exp(scores - jnp.max(scores, axis=-1, keepdims=True))
            weights = shifted / jnp.sum(shifted, axis=-1, keepdims=True)
            probs[2 * pair + side] = weights
            sides.append(dot(weights.astype(low), values))
        lanes = pl.ds(pl.multiple_of(pair * LANES, LANES), LANES)
        attended[:, lanes] = jnp.where(lane < HEAD_DIM, *sides).astype(low)


def middle_norm(attended, weight, normed, gains, middle, middle_low, unit, inverse):
    def body(tile, lanes):
        middle[:, lanes] = normed[:, lanes] + dot(attended[...], weight[:, lanes])

    lane_tiles(normed.shape[1] // TILE, body)

    def finish(rows):
        units, inv = unit_norm(middle[rows, :])
        unit[rows, :] = units
        inverse[rows, :] = jnp.broadcast_to(inv, (ROWS, LANES))
        total = units * gains[1:2, :]
        middle[rows, :] = total
        middle_low[rows, :] = total.astype(middle_low.dtype)

    row_tiles(normed.shape[0], finish)


def feed_up(middle_low, weight, slope, activated, first=0, last=None):
    def body(tile, lanes):
        values = dot(middle_low[...], weight[:, lanes])
        below = below_normal(values)
        slope[:, lanes] = (below + values * density(values)).astype(slope.dtype)
        activated[:, lanes] = (values * below).astype(activated.dtype)

    lane_tiles(last or slope.shape[1] // TILE, body, first)


def feed_down(activated, weight, middle, gains, cotangent, output, grad_final, gain_grads):
    def body(tile, lanes):
        middle[...] += dot(activated[:, lanes], weight[lanes, :])

    lane_tiles(activated.shape[1] // TILE, body)
    last_norm(middle, gains, cotangent, output, grad_final, gain_grads)


def last_norm(middle, gains, cotangent, output, grad_final, gain_grads):
    gain_grads[2:3, :] = jnp.zeros((1, middle.shape[1]), jnp.float32)

    def finish(rows):
        units, inv = unit_norm(middle[rows, :])
        gain = gains[2:3, :]
        output[rows, :] = (units * gain).astype(output.dtype)
        grad = cotangent[rows, :].astype(jnp.float32)
        gain_grads[2:3, :] += jnp.sum(grad * units, axis=0, keepdims=True)
        grad_final[rows, :] = norm_back(grad, units, inv, gain)

    row_tiles(middle.shape[0], finish)


def feed_back(grad, slope, activated, middle_low, up, down, up_grad, down_grad):
    low = activated.dtype
    grad_feed = grad[...].astype(low)
    turned = jnp.transpose(middle_low[...].astype(jnp.float32)).astype(low)

    def body(tile, lanes):
        down_grad[lanes, :] = dot(activated[:, lanes], grad_feed, (0, 0)).astype(low)
        grad_hidden = (dot(grad_feed, down[lanes, :], (1, 1)) * slope[:, lanes].astype(jnp.float32)).astype(low)
        up_grad[:, lanes] = dot(turned, grad_hidden).astype(low)
        grad[...] += dot(grad_hidden, up[:, lanes], (1, 1))

    lane_tiles(slope.shape[1] // TILE, body)


def norm_back_rows(grad, unit, inverse, gains, which, gain_grads):
    gain_grads[which : which + 1, :] = jnp.zeros((1, grad.shape[1]), jnp.float32)

    def body(rows):
        incoming, units = grad[rows, :], unit[rows, :]
        gain_grads[which : which + 1, :] += jnp.sum(incoming * units, axis=0, keepdims=True)
        grad[rows, :] = norm_back(incoming, units, inverse[rows, 0:1], gains[which : which + 1, :])

    row_tiles(grad.shape[0], body)


def branch_back(grad, attended, weight, grad_attended, out_grad):
    low = attended.dtype
    grad_branch = grad[...].astype(low)

    def body(tile, lanes):
        out_grad[lanes, :] = dot(attended[:, lanes], grad_branch, (0, 0)).astype(low)
        grad_attended[:, lanes] = dot(grad_branch, weight[lanes, :], (1, 1)).astype(low)

    lane_tiles(attended.shape[1] // TILE, body)


def attend_back_pair(projected, grad_attended, weights_of, grad_projected, pair):
    pack, width = grad_attended.shape
    low = projected.dtype
    scale = HEAD_DIM ** (-0.5)

    def lanes_of(part):
        start = part * width + pair * LANES
        return pl.ds(start if isinstance(pair, int) else pl.multiple_of(start, LANES), LANES)

    queries, keys, values = [projected[:, lanes_of(part)] for part in range(3)]
    grad = grad_attended[:, lanes_of(0)]
    lane = lax.broadcasted_iota(jnp.int32, (pack, LANES), 1)
    sides = []
    for side in range(2):
        own = (lane < HEAD_DIM) == (side == 0)
        weights = weights_of[side]
        grad_values = dot(weights.astype(low), grad, (0, 0))
        grad_probs = dot(jnp.where(own, grad, jnp.zeros_like(grad)), values, (1, 1))
        along = jnp.sum(weights * grad_probs, axis=-1, keepdims=True)
        grad_scores = (weights * (grad_probs - along)).astype(low)
        grad_queries = dot(grad_scores, keys) * scale
        grad_keys = dot(grad_scores, queries, (0, 0)) * scale
        sides.append((grad_queries, grad_keys, grad_values))
    for part in range(3):
        grad_projected[:, lanes_of(part)] = jnp.where(lane < HEAD_DIM, sides[0][part], sides[1][part]).astype(low)


def attend_back(projected, grad_attended, probs, grad_projected):
    @pl.loop(0, grad_attended.shape[1] // LANES)
    def _(pair):
        attend_back_pair(projected, grad_attended, probs.at[pl.ds(2 * pair, 2)], grad_projected, pair)


def project_back(grad, grad_projected, unit, gains, weight, qkv_grad):
    low = grad_projected.dtype
    turned = jnp.transpose(unit[...] * gains[0:1, :]).astype(low)

    def body(tile, lanes):
        qkv_grad[:, lanes] = dot(turned, grad_projected[:, lanes]).astype(low)
        grad[...] += dot(grad_projected[:, lanes], weight[:, lanes], (1, 1))

    lane_tiles(grad_projected.shape[1] // TILE, body)


def slope_rows(grad, front_slope, grad_convolved):
    def body(rows):
        grad_convolved[rows, :] = (grad[rows, :] * front_slope[rows, :]).astype(grad_convolved.dtype)

    row_tiles(grad.shape[0], body)


def middle_forward_kernel(
    lengths, frames, convolved, gains, wide, down, cotangent,
    output, front_slope, grad_final, unit_front, inverse_front, projected, probs, attended,
    unit_middle, inverse_middle, middle_low, slope, activated, gain_grads,
    normed, normed_low, middle,
):
    width = frames.shape[1]
    gain_grads[...] = jnp.zeros_like(gain_grads)
    front_norm(frames, convolved, gains, normed, normed_low, unit_front, inverse_front, front_slope)
    project(normed_low, wide.at[:, 0 : 3 * width], projected)
    attend(projected, lengths, 0, probs, attended)
    middle_norm(
        attended, wide.at[:, 3 * width : 4 * width], normed, gains, middle, middle_low, unit_middle,
        inverse_middle,
    )
    feed_up(middle_low, wide.at[:, 4 * width :], slope, activated)
    feed_down(activated, down, middle, gains, cotangent, output, grad_final, gain_grads)


def middle_backward_kernel(
    gains, wide, down, front_slope, grad_final, unit_front, inverse_front, projected, probs, attended,
    unit_middle, inverse_middle, middle_low, slope, activated, last_gain_grad,
    grad, grad_convolved, wide_grad, down_grad, gain_grads,
    grad_attended, grad_projected,
):
    width = grad.shape[1]
    gain_grads[...] = last_gain_grad[...]
    grad[...] = grad_final[...]
    feed_back(
        grad, slope, activated, middle_low, wide.at[:, 4 * width :], down, wide_grad.at[:, 4 * width :],
        down_grad,
    )
    norm_back_rows(grad, unit_middle, inverse_middle, gains, 1, gain_grads)
    branch_back(
        grad, attended, wide.at[:, 3 * width : 4 * width], grad_attended,
        wide_grad.at[:, 3 * width : 4 * width],
    )
    attend_back(projected, grad_attended, probs, grad_projected)
    project_back(
        grad, grad_projected, unit_front, gains, wide.at[:, 0 : 3 * width], wide_grad.at[:, 0 : 3 * width]
    )
    norm_back_rows(grad, unit_front, inverse_front, gains, 0, gain_grads)
    slope_rows(grad, front_slope, grad_convolved)


def middle_forward(frames, convolved, lengths, gains, wide, down, cotangent):
    pack, width = frames.shape
    inner = down.shape[0]
    heads = width // HEAD_DIM
    low, full = jnp.bfloat16, jnp.float32
    shape = jax.ShapeDtypeStruct
    vmem = pl.BlockSpec(memory_space=pltpu.VMEM)
    saved = [
        shape((pack, width), low),
        shape((pack, width), full),
        shape((pack, width), full),
        shape((pack, width), full),
        shape((pack, LANES), full),
        shape((pack, 3 * width), low),
        shape((heads, pack, pack), full),
        shape((pack, width), low),
        shape((pack, width), full),
        shape((pack, LANES), full),
        shape((pack, width), low),
        shape((pack, inner), low),
        shape((pack, inner), low),
        shape((8, width), full),
    ]
    return pl.pallas_call(
        middle_forward_kernel,
        out_shape=saved,
        in_specs=[pl.BlockSpec(memory_space=pltpu.SMEM)] + [vmem] * 6,
        out_specs=[vmem] * len(saved),
        scratch_shapes=[
            pltpu.VMEM((pack, width), full),
            pltpu.VMEM((pack, width), low),
            pltpu.VMEM((pack, width), full),
        ],
        compiler_params=pltpu.CompilerParams(vmem_limit_bytes=58 << 20),
    )(lengths, frames, convolved, gains, wide, down, cotangent)


def middle_backward(gains, wide, down, kept):
    pack, width = kept[0].shape
    low, full = jnp.bfloat16, jnp.float32
    shape = jax.ShapeDtypeStruct
    vmem = pl.BlockSpec(memory_space=pltpu.VMEM)
    grads = [
        shape((pack, width), full),
        shape((pack, width), low),
        shape(wide.shape, low),
        shape(down.shape, low),
        shape((8, width), full),
    ]
    return pl.pallas_call(
        middle_backward_kernel,
        out_shape=grads,
        in_specs=[vmem] * (3 + len(kept)),
        out_specs=[vmem] * len(grads),
        scratch_shapes=[pltpu.VMEM((pack, width), low), pltpu.VMEM((pack, 3 * width), low)],
        compiler_params=pltpu.CompilerParams(vmem_limit_bytes=58 << 20),
    )(gains, wide, down, *kept)


def weave(tasks, pieces):
    core_index = lax.axis_index("seq")
    count, done = len(tasks[0]), 0
    for number, piece in enumerate(pieces + [None]):
        until = count if piece is None else (number + 1) * count // (len(pieces) + 1)

        def some(core, first=done, last=until):
            for task in tasks[core][first:last]:
                task()

        if until > done:
            by_core(core_index, some)
        done = until
        if piece is not None:
            piece()


def fused_forward_kernel(
    dims, chunks,
    lengths, frames, cotangent, conv_shard, qkv_shard, out_shard, up_shard, down_shard, front_gain, middle_gain,
    final_gain,
    conv_out, wide_out, down_out, patches_out, front_slope_out, unit_front_out, projected_out, probs_out,
    attended_out, unit_middle_out, middle_low_out, slope_out, activated_out, both_output, gains, grad_final,
    inverse_front, inverse_middle, gain_grads,
    patches, front_slope, unit_front, projected, probs, attended, unit_middle, middle_low, slope, activated,
    gain_shard,
    conv_all, wide_all, down_all, gain_all, pack_frames, pack_cotangent, output, padded, total,
    gains_wide, normed, normed_low, middle,
    send_sems, recv_sems, push_send, push_recv, own_sems, local_sems, save_sems, pair_sems,
):
    ins = (conv_shard, qkv_shard, out_shard, up_shard, down_shard, gain_shard)
    outs = (conv_all, wide_all, down_all, gain_all)
    gather = Gather(dims, chunks, ins, outs, (send_sems, recv_sems, push_send, push_recv))
    core_index = lax.axis_index("seq")
    pack, width = pack_frames.shape
    half = pack // 2
    row = lax.broadcasted_iota(jnp.int32, (GAIN_ROWS, LANES), 0)
    rows = jnp.zeros((GAIN_ROWS, LANES), jnp.float32)
    for index, gain in enumerate((front_gain, middle_gain, final_gain)):
        one = gain[...].astype(jnp.float32)
        one = jnp.concatenate([one, jnp.zeros((1, LANES - one.shape[1]), jnp.float32)], axis=1)
        rows = jnp.where(row == index, one, rows)
    gain_shard[...] = jnp.concatenate([rows, rows], axis=0).astype(gain_shard.dtype)
    greet(dims, gather.position, core_index)

    here = pl.ds(pl.multiple_of(core_index * half, half), half)
    there = pl.ds(pl.multiple_of((1 - core_index) * half, half), half)

    def to_partner(source, target, number):
        return pltpu.make_async_remote_copy(
            src_ref=source,
            dst_ref=target,
            send_sem=pair_sems.at[0, number],
            recv_sem=pair_sems.at[1, number],
            device_id={"seq": 1 - core_index},
            device_id_type=MESH,
        )

    moves = []
    for number, (source, target) in enumerate(((frames, pack_frames), (cotangent, pack_cotangent))):
        moves.append(to_partner(source.at[1 - core_index], target.at[here], number))
        moves.append(pltpu.make_async_copy(source.at[core_index], target.at[here], local_sems.at[number]))
    for copy in moves:
        copy.start()
    own = gather.own_copies(own_sems)
    for copy in own:
        copy.start()

    def early(core):
        for chunk in range(3):
            for task in gather.tasks(core, chunk, 0):
                task()

    by_core(core_index, early)
    steps = []
    for step in range(1, len(chunks) + 3):
        both = []
        for core in range(2):
            tasks = []
            for stage in (3, 2, 1):
                if 0 <= step - stage < len(chunks):
                    tasks += gather.tasks(core, step - stage, stage)
            if 3 <= step + 2 < len(chunks):
                tasks += gather.tasks(core, step + 2, 0)
            both.append(tasks)
        steps.append(both)

    def gate(*numbers):
        def body(core):
            for number in numbers:
                gather.arrived(core, number)

        by_core(core_index, body)

    for copy in moves[:2]:
        copy.wait()
    fill_padded(padded, pack_frames)
    total[...] = jnp.zeros_like(total)

    def patch_piece(first, last):
        def piece():
            @pl.loop(first, last)
            def _(group):
                patches[group] = make_patch(padded, group, pack)

        return piece

    rank = [0] + near_first(dims[0])
    places = sorted(offsets_of(dims), key=lambda o: ((o[1] != 0) + (o[2] != 0), rank.index(o[0])))

    def conv_piece(offsets):
        group = place(dims, (0, 1, 2), gather.position, offsets)

        def wait(core):
            for chunk in (1, 2):
                gather.arrived_block(core, chunk, group)

        def piece():
            if offsets != (0, 0, 0):
                by_core(core_index, wait)
            add_forward(total, patches[group], conv_all[group], group, pack)

        return piece

    quarter = GROUPS // 4
    early_pieces = [patch_piece(i * quarter, (i + 1) * quarter) for i in range(4)]
    weave(steps[0], early_pieces[:1])
    weave(steps[1], early_pieces[1:3])
    weave(steps[2], early_pieces[3:])
    for copy in own:
        copy.wait()
    conv_pieces = [conv_piece(offsets) for offsets in places]
    alone = sum(1 for offsets in places if not (offsets[1] or offsets[2]))
    weave(steps[3], [])
    weave(steps[4], conv_pieces[:alone])
    gate(0)
    saves = []

    def save(source, target):
        copy = pltpu.make_async_copy(source, target, save_sems.at[len(saves)])
        copy.start()
        saves.append(copy)

    save(patches, patches_out)
    gains_wide[...] = jnp.zeros_like(gains_wide)

    @pl.loop(0, gather.count)
    def _(shard):
        add_group(gains_wide, gain_all[shard, 0:16, :].astype(jnp.float32), shard, width // gather.count)

    gains[...] = gains_wide[0:8, 0:width]
    def front_piece():
        save(conv_all, conv_out)
        front_norm(pack_frames, total, gains, normed, normed_low, unit_front, inverse_front, front_slope)
        save(front_slope, front_slope_out)
        save(unit_front, unit_front_out)

    def project_piece():
        gate(3)
        project(normed_low, wide_all.at[:, 0 : 3 * width], projected)
        save(projected, projected_out)

    def attend_piece(first, last):
        return lambda: attend(projected, lengths, core_index, probs, attended, first, last)

    def middle_piece():
        gate(4)
        save(probs, probs_out)
        save(attended, attended_out)
        middle_norm(
            attended, wide_all.at[:, 3 * width : 4 * width], normed, gains, middle, middle_low, unit_middle,
            inverse_middle,
        )
        save(unit_middle, unit_middle_out)
        save(middle_low, middle_low_out)

    head_pairs = width // LANES
    weave(steps[5], conv_pieces[alone : 3 * alone])
    weave(
        steps[6],
        conv_pieces[3 * alone :]
        + [front_piece, project_piece]
        + [attend_piece(i, i + 2) for i in range(0, head_pairs, 2)],
    )
    weave(steps[7], [middle_piece])
    up = wide_all.at[:, 4 * width :]
    count = slope.shape[1] // TILE
    third = count // 3

    def up_piece(first):
        def piece():
            if first == 0:
                gate(5)
                save(wide_all, wide_out)
            feed_up(middle_low, up, slope, activated, first, first + third)

        return piece

    arrivals = [(i, j) for j in [0] + near_first(dims[1]) for i in rank]
    down_tasks = steps[8]
    near = len(rank)

    def strip_piece(offsets):
        gids = [place(dims, (0, 1, 2), gather.position, offsets + (k,)) for k in range(2)]

        def wait(core):
            for k, gid in enumerate(gids):
                if offsets + (k,) != (0, 0, 0):
                    gather.arrived_block(core, 6, gid)

        by_core(core_index, wait)
        rows = pl.ds(pl.multiple_of(gids[0] // 2 * STRIP, STRIP), STRIP)
        save(down_all.at[rows], down_out.at[rows])
        middle[...] += dot(activated[:, rows], down_all[rows, :])

    weave([tasks[:near] for tasks in down_tasks], [up_piece(i) for i in range(0, count, third)])
    save(slope, slope_out)
    save(activated, activated_out)
    for copy in moves[2:]:
        copy.wait()
    gain_grads[...] = jnp.zeros_like(gain_grads)
    for number, offsets in enumerate(arrivals):
        if number >= near:
            weave([tasks[number : number + 1] for tasks in down_tasks], [])
        strip_piece(offsets)
    last_norm(middle, gains, pack_cotangent, output, grad_final, gain_grads)
    last = to_partner(output.at[there], both_output.at[core_index], 2)
    last.start()
    stay = pltpu.make_async_copy(output.at[here], both_output.at[core_index], local_sems.at[2])
    stay.start()
    by_core(core_index, gather.finish)
    for copy in saves + [stay, last]:
        copy.wait()


def fused_forward(frames, cotangent, lengths, shards_in, chunks, dp):
    dims = dp_factors(dp)
    n = len(chunks)
    conv_shard, qkv_shard, out_shard, up_shard, down_shard = shards_in[:5]
    pack, width = 2 * frames.shape[1], frames.shape[2]
    inner = down_shard.shape[0] * dp
    heads = width // HEAD_DIM
    low, full = jnp.bfloat16, jnp.float32
    shape = jax.ShapeDtypeStruct
    vmem = pl.BlockSpec(memory_space=pltpu.VMEM)
    any_ = pl.BlockSpec(memory_space=pl.ANY)
    conv_shape = (dp,) + conv_shard.shape
    wide_shape = (width, 4 * width + up_shard.shape[1])
    down_shape = (inner, width)
    kept = [
        shape((GROUPS, pack + FINE, 384), low),
        shape((pack, width), full),
        shape((pack, width), full),
        shape((pack, 3 * width), low),
        shape((heads, pack, pack), full),
        shape((pack, width), low),
        shape((pack, width), full),
        shape((pack, width), low),
        shape((pack, inner), low),
        shape((pack, inner), low),
    ]
    saved = [
        shape(frames.shape, low),
        shape((8, width), full),
        shape((pack, width), full),
        shape((pack, LANES), full),
        shape((pack, LANES), full),
        shape((8, width), full),
    ]
    return pl.pallas_call(
        functools.partial(fused_forward_kernel, dims, chunks),
        out_shape=[shape(conv_shape, low), shape(wide_shape, low), shape(down_shape, low)] + kept + saved,
        in_specs=[pl.BlockSpec(memory_space=pltpu.SMEM)] + [any_] * 7 + [vmem] * 3,
        out_specs=[any_] * 13 + [vmem] * len(saved),
        scratch_shapes=[pltpu.VMEM(one.shape, one.dtype) for one in kept]
        + [
            pltpu.VMEM((2 * GAIN_ROWS, LANES), low),
            pltpu.VMEM(conv_shape, low),
            pltpu.VMEM(wide_shape, low),
            pltpu.VMEM(down_shape, low),
            pltpu.VMEM((dp, 2 * GAIN_ROWS, LANES), low),
            pltpu.VMEM((pack, width), low),
            pltpu.VMEM((pack, width), low),
            pltpu.VMEM((pack, width), low),
            pltpu.VMEM((pack + KERNEL, width + LANES), full),
            pltpu.VMEM((pack, width + LANES), full),
            pltpu.VMEM((16, width + LANES), full),
            pltpu.VMEM((pack, width), full),
            pltpu.VMEM((pack, width), low),
            pltpu.VMEM((pack, width), full),
            pltpu.SemaphoreType.DMA((n, dp)),
            pltpu.SemaphoreType.DMA((n, dp)),
            pltpu.SemaphoreType.DMA((n, dp)),
            pltpu.SemaphoreType.DMA((n, dp)),
            pltpu.SemaphoreType.DMA((n, 2)),
            pltpu.SemaphoreType.DMA((3,)),
            pltpu.SemaphoreType.DMA((20,)),
            pltpu.SemaphoreType.DMA((2, 3)),
        ],
        compiler_params=pltpu.CompilerParams(
            collective_id=2, has_side_effects=True, vmem_limit_bytes=60 << 20
        ),
    )(lengths, frames, cotangent, *shards_in)


STRIP = 384
DOWN, UP, OUT, QKV, GAIN, CONV = range(6)
CONV_PARTS = 4
SCATTER_ORDERS = (FIRST, FIRST, FIRST, FIRST, FIRST) + (FIRST,) * CONV_PARTS


class Scatter:
    def __init__(self, dims, heights, stages, pairs, hops, outs, conv_pair, sems):
        self.dims, self.heights = dims, heights
        self.stages, self.pairs, self.hops, self.outs, self.conv_pair = stages, pairs, hops, outs, conv_pair
        self.waited = set()
        self.pair_recv, self.hop_send, self.hop_recv, self.last_send, self.last_recv = sems
        self.position = position_of(dims)
        self.count = dims[0] * dims[1] * dims[2]

    def block(self, ref, chunk, gid):
        if len(ref.shape) == 3:
            return ref.at[gid]
        height = self.heights[chunk]
        return ref.at[pl.ds(pl.multiple_of(gid * height, 16), height)]

    def sizes(self, core, chunk):
        return [self.dims[axis] for axis in SCATTER_ORDERS[chunk][core]]

    def slot(self, core, chunk, level, offsets, distance):
        index = distance - 1
        for i in range(level):
            index = index * self.sizes(core, chunk)[i] + offsets[i]
        return index

    def semaphore(self, core, chunk, level, index):
        sizes = self.sizes(core, chunk)
        return (1, sizes[0], sizes[0] * sizes[1])[level] + index - 1

    def combine(self, core, chunk, offsets, target):
        order = SCATTER_ORDERS[chunk][core]
        gid = place(self.dims, order, self.position, offsets)
        own, pair = self.block(self.stages[chunk], chunk, gid), self.block(self.pairs[chunk], chunk, gid)
        natural = (core,) + tuple(offset for _, offset in sorted(zip(order, offsets)))
        if chunk >= CONV and natural not in self.waited:
            self.waited.add(natural)
            whole = self.conv_pair.at[gid]
            pltpu.make_async_copy(whole, whole, self.pair_recv.at[CONV, gid]).wait()
        terms = [own, pair]
        for level in (2, 1, 0):
            if offsets[level]:
                break
            for distance in range(1, self.sizes(core, chunk)[level]):
                index = self.slot(core, chunk, level, offsets, distance)
                ref = self.hops[level][chunk].at[index]
                number = self.semaphore(core, chunk, level, index)
                pltpu.make_async_copy(ref, ref, self.hop_recv.at[chunk, number]).wait()
                terms.append(ref)

        tall = 48 if own.shape[0] % 48 == 0 else 16

        @pl.loop(0, own.shape[0] // tall)
        def _(tile):
            rows = pl.ds(pl.multiple_of(tile * tall, 16), tall)
            if target is None and len(terms) == 2:
                own[rows, :] = own[rows, :] + pair[rows, :]
                return
            total = terms[0][rows, :].astype(jnp.float32)
            for term in terms[1:]:
                total = total + term[rows, :].astype(jnp.float32)
            if target is None:
                own[rows, :] = total.astype(own.dtype)
            else:
                target[rows, :] = total

        return own

    def send(self, core, chunk, offsets):
        level = max(i for i in range(3) if offsets[i])
        own = self.combine(core, chunk, offsets, None)
        index = self.slot(core, chunk, level, offsets, offsets[level])
        number = self.semaphore(core, chunk, level, index)
        pltpu.make_async_remote_copy(
            src_ref=own,
            dst_ref=self.hops[level][chunk].at[index],
            send_sem=self.hop_send.at[chunk, number],
            recv_sem=self.hop_recv.at[chunk, number],
            device_id={"dp": place(self.dims, (SCATTER_ORDERS[chunk][core][level],), self.position, (offsets[level],))},
            device_id_type=MESH,
        ).start()

    def half(self, chunk, core):
        out = self.outs[chunk]
        lanes = out.shape[1] // 2
        return out.at[:, pl.ds(core * lanes, lanes)]

    def final(self, core, chunk):
        half = self.half(chunk, core)
        self.combine(core, chunk, (0, 0, 0), half)
        pltpu.make_async_remote_copy(
            src_ref=half,
            dst_ref=half,
            send_sem=self.last_send.at[chunk],
            recv_sem=self.last_recv.at[chunk],
            device_id={"seq": 1 - core},
            device_id_type=MESH,
        ).start()

    def tasks(self, core, chunk, stage):
        sizes = self.sizes(core, chunk)
        if stage == 3:
            return [functools.partial(self.final, core, chunk)]
        if stage == 2:
            places = [(i, 0, 0) for i in near_first(sizes[0])[::-1]]
        elif stage == 1:
            places = [(i, d, 0) for d in near_first(sizes[1]) for i in near_first(sizes[0])[::-1] + [0]]
        else:
            places = [
                (i, j, d)
                for d in near_first(sizes[2])
                for j in near_first(sizes[1]) + [0]
                for i in near_first(sizes[0])[::-1] + [0]
            ]
        return [functools.partial(self.send, core, chunk, offsets) for offsets in places]

    def finish(self, core):
        for chunk in range(len(self.outs)):
            half = self.half(chunk, 1 - core)
            pltpu.make_async_copy(half, half, self.last_recv.at[chunk]).wait()
            pltpu.make_async_copy(half, half, self.last_send.at[chunk]).wait()

            @pl.loop(0, self.count - 1)
            def _(number, chunk=chunk):
                ref = self.block(self.stages[chunk], chunk, 0)
                pltpu.make_async_copy(ref, ref, self.hop_send.at[chunk, number]).wait()


class Stream:
    def __init__(self, buffer, sems):
        self.buffer, self.sems = buffer, sems

    def start(self, source, number):
        pltpu.make_async_copy(source, self.buffer.at[number % 2], self.sems.at[number % 2]).start()

    def take(self, number):
        ref = self.buffer.at[number % 2]
        pltpu.make_async_copy(ref, ref, self.sems.at[number % 2]).wait()
        return ref


class Outbox:
    def __init__(self, buffer, sems):
        self.buffer, self.sems, self.busy, self.number = buffer, sems, [None, None], 0

    def free(self):
        slot = self.number % 2
        self.number += 1
        if self.busy[slot] is not None:
            self.busy[slot].wait_send()
            self.busy[slot] = None
        return slot, self.buffer.at[slot]

    def send(self, slot, source, target, recv_sem):
        copy = pltpu.make_async_remote_copy(
            src_ref=source,
            dst_ref=target,
            send_sem=self.sems.at[slot],
            recv_sem=recv_sem,
            device_id={"seq": 1 - lax.axis_index("seq")},
            device_id_type=MESH,
        )
        copy.start()
        self.busy[slot] = copy

    def drain(self):
        for copy in self.busy:
            if copy is not None:
                copy.wait_send()
        self.busy = [None, None]


def spread_grads(padded, group, pack):
    def later(values, amount):
        return pltpu.roll(values, amount, 0)

    one = take_group(padded, slice(0, pack + FINE), group, 48)
    two = one + pltpu.roll(later(one, 1), 48, 1)
    low, high = double_96(two, later(two, 2))
    near = jnp.concatenate(double_192(low, high, later(low, 4), later(high, 4)), axis=1)
    return jnp.concatenate([near, later(near, 8)], axis=1).astype(jnp.bfloat16)


def add_backward(total, tall, spread, weight, group, pack):
    edge = KERNEL // 2 - FINE
    tall[edge : edge + pack + FINE] = dot(spread, weight, (1, 1))

    def shift(base, moved, amount):
        return base[amount * FINE :] + moved[: base.shape[0] - amount * FINE]

    tiles = [tall[:, i * LANES : (i + 1) * LANES] for i in range(3)]
    add_group(total, fold_lanes(tiles, shift), group, 48)


def fused_backward_kernel(
    dims,
    weight, wide, down, patches, probs, grad_in, activated_in, middle_low_in, slope_in, unit_middle_in, attended_in,
    projected_in, unit_front_in, front_slope_in,
    gains, inverse_front, inverse_middle, last_gain_grad,
    conv_out, qkv_out, out_out, up_out, down_out, gain_out, both_grads, *scratch,
):
    arrays = CONV + 1
    n = CONV + CONV_PARTS
    stages, pairs = scratch[:arrays], scratch[arrays : 2 * arrays]
    hops = [scratch[2 * arrays + level * n : 2 * arrays + (level + 1) * n] for level in range(3)]
    conv_rows = [pl.ds(i * (384 // CONV_PARTS), 384 // CONV_PARTS) for i in range(CONV_PARTS)]

    def in_parts(refs):
        return list(refs[:CONV]) + [refs[CONV].at[:, rows] for rows in conv_rows]

    outs = [down_out, up_out, out_out, qkv_out, gain_out] + [conv_out.at[rows] for rows in conv_rows]
    (
        grad, activated, middle_low, slope, unit_middle, attended, projected, unit_front, front_slope,
        turned, grad_attended, grad_projected, padded, spread, tall, total, gain_grads, gain_wide,
        gain_box, tall_box, wide_box, tall_tiles, wide_tiles, prob_tiles, patch_tiles,
        pair_recv, hop_send, hop_recv, last_send, last_recv, box_sems, tile_sems, load_sems, input_sems,
    ) = scratch[2 * arrays + 3 * n :]
    core_index = lax.axis_index("seq")
    other = 1 - core_index
    pack, width = grad.shape
    inner = activated.shape[1]
    low = jnp.bfloat16
    heights = [out.shape[0] for out in outs]
    scatter = Scatter(
        dims, heights, in_parts(stages), in_parts(pairs), hops, outs, pairs[CONV],
        (pair_recv, hop_send, hop_recv, last_send, last_recv),
    )
    tall_stream, wide_stream = Stream(tall_tiles, tile_sems.at[0]), Stream(wide_tiles, tile_sems.at[1])
    prob_stream, patch_stream = Stream(prob_tiles, tile_sems.at[2]), Stream(patch_tiles, tile_sems.at[3])
    tall_out, wide_out_box = Outbox(tall_box, box_sems.at[0]), Outbox(wide_box, box_sems.at[1])

    def strip(index, base=0):
        return pl.ds(pl.multiple_of(base + index * STRIP, LANES), STRIP)

    up_base, out_base = 4 * width, 3 * width
    sources = (grad_in, activated_in, middle_low_in, slope_in, unit_middle_in, attended_in, projected_in,
               unit_front_in, front_slope_in)
    targets = (grad, activated, middle_low, slope, unit_middle, attended, projected, unit_front, front_slope)
    loads = [
        pltpu.make_async_copy(source, target, input_sems.at[i])
        for i, (source, target) in enumerate(zip(sources, targets))
    ]
    for load in loads:
        load.start()
    up_half, qkv_half, out_half = inner // 2, 3 * width // 2, width // 2
    up_strips, qkv_strips = up_half // STRIP, qkv_half // STRIP
    down_strips = inner // STRIP

    def ordered(index, strips):
        return (core_index if index % 2 else other) * strips + index // 2

    def up_start(index):
        which = ordered(index, up_strips)
        wide_stream.start(wide.at[:, strip(which, up_base)], index)
        tall_stream.start(down.at[strip(which)], index)

    up_start(0)
    greet(dims, scatter.position, core_index)

    def all_tasks(*wanted):
        return [[task for chunk, stage in wanted for task in scatter.tasks(core, chunk, stage)] for core in range(2)]

    def step(number):
        wanted = [(number - stage, stage) for stage in (3, 2, 1, 0) if 0 < number - stage < n]
        if number < 3:
            wanted.insert(0, (DOWN, number + 1))
        return all_tasks(*wanted)

    def gate(chunk, count, height, lanes):
        for index in range(count):
            ref = pairs[chunk].at[pl.ds(0, height), pl.ds(0, lanes)]
            pltpu.make_async_copy(ref, ref, pair_recv.at[chunk, index]).wait()

    own_lanes = pl.ds(pl.multiple_of(core_index * out_half, LANES), out_half)
    other_lanes = pl.ds(pl.multiple_of(other * out_half, LANES), out_half)
    loads[0].wait()
    loads[1].wait()
    grad_feed = grad[...].astype(low)
    spread[0:pack, :] = grad_feed
    first = [(i, j, 0) for j in near_first(dims[1]) + [0] for i in near_first(dims[0])[::-1] + [0]]
    strips = [place(dims, (0, 1, 2), scatter.position, offsets) // 2 for offsets in first]
    sends = [scatter.tasks(core, DOWN, 0) for core in range(2)]
    ahead = len(strips) // 2
    for index in range(down_strips + 1):
        if index < down_strips:
            slot, box = tall_out.free()
            rows = strip(strips[index])
            box[...] = dot(activated[:, rows], spread[0:pack, :], (0, 0)).astype(low)
            tall_out.send(slot, box.at[:, other_lanes], pairs[DOWN].at[rows], pair_recv.at[DOWN, index])
            stages[DOWN][rows, :] = box[:, own_lanes]
        if index > 0:
            came = pairs[DOWN].at[strip(strips[index - 1])]
            pltpu.make_async_copy(came, came, pair_recv.at[DOWN, index - 1]).wait()

            def early(core, index=index - 1):
                if core == 0:
                    sends[0][index]()
                elif index < ahead:
                    sends[1][index]()
                    sends[1][index + ahead]()

            by_core(core_index, early)
    loads[2].wait()
    loads[3].wait()
    turned[...] = jnp.transpose(middle_low[...].astype(jnp.float32)).astype(low)

    def give(chunk, index, values):
        lanes = pl.ds(index // 2 * STRIP, STRIP)
        if index % 2 == 0:
            slot, box = wide_out_box.free()
            box[...] = values
            wide_out_box.send(slot, box, pairs[chunk].at[:, lanes], pair_recv.at[chunk, index // 2])
        else:
            stages[chunk][:, lanes] = values

    def up_piece(index):
        def piece():
            if index + 1 < 2 * up_strips:
                up_start(index + 1)
            up_tile, down_tile = wide_stream.take(index), tall_stream.take(index)
            lanes = strip(ordered(index, up_strips))
            slopes = slope[:, lanes].astype(jnp.float32)
            grad_hidden = (dot(spread[0:pack, :], down_tile[...], (1, 1)) * slopes).astype(low)
            give(UP, index, dot(turned[...], grad_hidden).astype(low))
            grad[...] += dot(grad_hidden, up_tile[...], (1, 1))

        return piece

    weave(step(0), [up_piece(i) for i in range(2 * up_strips)])

    def prob_start(pair):
        prob_stream.start(probs.at[pl.ds(2 * pair, 2)], pair)

    for index in range(2):
        tall_stream.start(wide.at[strip(index), out_base : out_base + width], index)
    prob_start(0)
    gain_grads[...] = last_gain_grad[...]

    def middle_piece():
        for load in loads[4:]:
            load.wait()
        gate(UP, up_strips, width, STRIP)
        norm_back_rows(grad, unit_middle, inverse_middle, gains, 1, gain_grads)

    def out_piece():
        grad_branch = grad[...].astype(low)
        spread[0:pack, :] = grad_branch
        turned[...] = jnp.transpose(attended[...].astype(jnp.float32)).astype(low)
        for index, half in enumerate((other, core_index)):
            give(OUT, index, dot(turned[...], spread[0:pack, strip(half)]).astype(low))
            tile = tall_stream.take(index)
            lanes = slice(index * STRIP, (index + 1) * STRIP)
            grad_attended[:, lanes] = dot(grad_branch, tile[...], (1, 1)).astype(low)

    pairs_of_heads = width // LANES

    def attend_piece(pair):
        def piece():
            if pair + 1 < pairs_of_heads:
                prob_start(pair + 1)
            attend_back_pair(projected, grad_attended, prob_stream.take(pair), grad_projected, pair)

        return piece

    def qkv_start(index):
        wide_stream.start(wide.at[:, strip(ordered(index, qkv_strips))], index)

    def qkv_piece(index):
        def piece():
            if index == 0:
                qkv_start(0)
                turned[...] = jnp.transpose(unit_front[...] * gains[0:1, :]).astype(low)
            if index + 1 < 2 * qkv_strips:
                qkv_start(index + 1)
            tile = wide_stream.take(index)
            values = grad_projected[:, strip(ordered(index, qkv_strips))]
            give(QKV, index, dot(turned[...], values).astype(low))
            grad[...] += dot(values, tile[...], (1, 1))

        return piece

    places = sorted(offsets_of(dims), key=lambda o: (o[1] == 0) + (o[2] == 0))
    groups = [place(dims, (0, 1, 2), scatter.position, offsets) for offsets in places]

    def conv_start(number):
        tall_stream.start(weight.at[groups[number]], number)
        patch_stream.start(patches.at[groups[number]], number)

    def front_piece():
        conv_start(0)
        norm_back_rows(grad, unit_front, inverse_front, gains, 0, gain_grads)
        padded[...] = jnp.zeros_like(padded)
        tall[...] = jnp.zeros_like(tall)
        total[...] = jnp.zeros_like(total)
        total[:, :width] = grad[...]

        def body(rows):
            padded[rows, 0:width] = (grad[rows, :] * front_slope[rows, :]).astype(low).astype(jnp.float32)

        row_tiles(pack, body)
        gain_wide[...] = jnp.zeros_like(gain_wide)
        gain_wide[0:8, 0:width] = gain_grads[...]

        @pl.loop(0, scatter.count)
        def _(shard):
            one = take_group(gain_wide, slice(0, 16), shard, width // scatter.count)
            gain_box[shard] = one.astype(low)
            stages[GAIN][shard] = one.astype(low)

        gain_copy.start()

    gain_copy = pltpu.make_async_remote_copy(
        src_ref=gain_box,
        dst_ref=pairs[GAIN],
        send_sem=load_sems.at[1],
        recv_sem=load_sems.at[2],
        device_id={"seq": other},
        device_id_type=MESH,
    )

    def conv_piece(number):
        def piece():
            if number + 1 < len(groups):
                conv_start(number + 1)
            group = groups[number]
            tile, patch = tall_stream.take(number), patch_stream.take(number)
            spread[...] = spread_grads(padded, group, pack)
            slot, box = tall_out.free()
            box[...] = dot(patch[...], spread[...], (0, 0)).astype(low)
            tall_out.send(slot, box.at[:, other_lanes], pairs[CONV].at[group], pair_recv.at[CONV, group])
            stages[CONV][group] = box[:, own_lanes]
            add_backward(total, tall, spread[...], tile[...], group, pack)

        return piece

    middle_piece()
    weave(
        step(1),
        [out_piece]
        + [attend_piece(i) for i in range(pairs_of_heads)]
        + [qkv_piece(i) for i in range(2 * qkv_strips)]
        + [front_piece],
    )
    pieces = [conv_piece(i) for i in range(len(groups))]
    gate(OUT, 1, width, STRIP)
    weave(step(2), pieces[:5])
    gate(QKV, qkv_strips, width, STRIP)
    weave(step(3), pieces[5:11])
    gain_copy.wait()
    weave(step(4), pieces[11:])
    half = pack // 2
    here = pl.ds(pl.multiple_of(core_index * half, half), half)
    there = pl.ds(pl.multiple_of(other * half, half), half)
    frames_copy = pltpu.make_async_remote_copy(
        src_ref=total.at[there, pl.ds(0, width)],
        dst_ref=both_grads.at[core_index],
        send_sem=load_sems.at[3],
        recv_sem=load_sems.at[4],
        device_id={"seq": other},
        device_id_type=MESH,
    )
    frames_copy.start()
    both_grads[core_index] = total[here, 0:width]
    for number in range(5, n + 3):
        weave(step(number), [])
    by_core(core_index, scatter.finish)
    tall_out.drain()
    wide_out_box.drain()
    frames_copy.wait()


def fused_backward(weight, wide, down, patches, gains, kept, dp):
    dims = dp_factors(dp)
    (front_slope, grad_final, unit_front, inverse_front, projected, probs, attended, unit_middle,
     inverse_middle, middle_low, slope, activated, gain_grads) = kept
    pack, width = front_slope.shape
    inner = activated.shape[1]
    low, full = jnp.bfloat16, jnp.float32
    shape = jax.ShapeDtypeStruct
    vmem = pl.BlockSpec(memory_space=pltpu.VMEM)
    any_ = pl.BlockSpec(memory_space=pl.ANY)
    rows = width // dp
    flat = [(inner, width // 2), (width, inner // 2), (width, width // 2), (width, 3 * width // 2)]
    wholes = flat + [(dp, 16, LANES), (dp, 384, 384)]
    blocks = [(s[0] // dp, s[1]) for s in flat] + [(16, LANES)] + [(384 // CONV_PARTS, 384)] * CONV_PARTS
    n = len(blocks)
    scratch = [pltpu.VMEM(s, low) for s in wholes] * 2
    for level in range(3):
        for block, orders in zip(blocks, SCATTER_ORDERS):
            slots = max(hop_slots(dims, order)[level] for order in orders)
            scratch.append(pltpu.VMEM((slots,) + block, low))
    tall_rows = pack + FINE
    given = (grad_final, activated, middle_low, slope, unit_middle, attended, projected, unit_front, front_slope)
    scratch += [pltpu.VMEM(one.shape, one.dtype) for one in given]
    scratch += [
        pltpu.VMEM((width, pack), low),
        pltpu.VMEM((pack, width), low),
        pltpu.VMEM((pack, 3 * width), low),
        pltpu.VMEM((tall_rows, width + LANES), full),
        pltpu.VMEM((tall_rows, width), low),
        pltpu.VMEM((pack + KERNEL - FINE, 384), full),
        pltpu.VMEM((pack, width + LANES), full),
        pltpu.VMEM((8, width), full),
        pltpu.VMEM((16, width + LANES), full),
        pltpu.VMEM((dp, 16, LANES), low),
        pltpu.VMEM((2, STRIP, width), low),
        pltpu.VMEM((2, width, STRIP), low),
        pltpu.VMEM((2, STRIP, width), low),
        pltpu.VMEM((2, width, STRIP), low),
        pltpu.VMEM((2, 2, pack, pack), full),
        pltpu.VMEM((2, tall_rows, 384), low),
        pltpu.SemaphoreType.DMA((n, dp)),
        pltpu.SemaphoreType.DMA((n, dp)),
        pltpu.SemaphoreType.DMA((n, dp)),
        pltpu.SemaphoreType.DMA((n,)),
        pltpu.SemaphoreType.DMA((n,)),
        pltpu.SemaphoreType.DMA((2, 2)),
        pltpu.SemaphoreType.DMA((4, 2)),
        pltpu.SemaphoreType.DMA((5,)),
        pltpu.SemaphoreType.DMA((len(given),)),
    ]
    return pl.pallas_call(
        functools.partial(fused_backward_kernel, dims),
        out_shape=[
            shape((384, width), full),
            shape((rows, 3 * width), full),
            shape((rows, width), full),
            shape((rows, inner), full),
            shape((inner // dp, width), full),
            shape((16, 2 * LANES), full),
            shape((2, pack // 2, width), full),
        ],
        in_specs=[any_] * (5 + len(given)) + [vmem] * 4,
        out_specs=[vmem] * 7,
        scratch_shapes=scratch,
        compiler_params=pltpu.CompilerParams(
            collective_id=3, has_side_effects=True, vmem_limit_bytes=63 << 20
        ),
    )(weight, wide, down, patches, probs, *given, gains, inverse_front, inverse_middle, gain_grads)


GAIN_ROWS = 16


def chunks_of(conv_rows, conv_lanes, wide_rows, width, down_rows):
    both = range(2)
    quarter, half = conv_rows // 4, width // 2
    conv = [
        [(0, ((2 * part + core) * quarter, quarter), (0, conv_lanes)) for core in both] for part in both
    ]
    wide = [
        [(1, (0, wide_rows), ((2 * part + core) * 2 * width, 2 * width)) for core in both] for part in both
    ]
    down = [[(2, (0, down_rows), (core * half, half)) for core in both]]
    gain = [[(3, (core * GAIN_ROWS, GAIN_ROWS), (0, LANES)) for core in both]]
    return gain, conv, wide, down


def gather_chunks(chunks):
    return [
        (FIRST,) + tuple((array, array, rows, lanes[0], lanes[0], lanes[1]) for array, rows, lanes in chunk)
        for chunk in chunks
    ]


def fused_chunks(conv_rows, width, wide_rows, inner, down_rows):
    quarter = conv_rows // 4
    chunks = [(FIRST,) + tuple((5, 3, (core * GAIN_ROWS, GAIN_ROWS), 0, 0, LANES) for core in range(2))]
    for part, orders in enumerate((FIRST, FIRST)):
        chunks.append(
            (orders,) + tuple((0, 0, ((2 * part + core) * quarter, quarter), 0, 0, width) for core in range(2))
        )
    begin = 0
    for source, lanes, orders in ((1, 3 * width, FIRST), (2, width, FIRST), (3, inner, SECOND)):
        half = lanes // 2
        chunks.append(
            (orders,)
            + tuple((source, 1, (0, wide_rows), core * half, begin + core * half, half) for core in range(2))
        )
        begin += lanes
    half = width // 2
    chunks.append(
        (FIRST,) + tuple((4, 2, (0, down_rows), core * half, core * half, half) for core in range(2))
    )
    return chunks


def shards(
    frames,
    clip_lengths,
    conv_weight,
    front_gain,
    qkv_weight,
    out_weight,
    middle_gain,
    up_weight,
    down_weight,
    final_gain,
    cotangent,
):
    dp = lax.axis_size("dp")
    low = jnp.bfloat16
    width = frames.shape[2]
    columns = conv_weight.shape[2]
    group_width = conv_weight.shape[1]
    gain_width = front_gain.shape[0]
    conv_shard = (
        conv_weight.reshape(COARSE, FINE, group_width, columns)
        .transpose(0, 2, 1, 3)
        .reshape(COARSE * group_width, FINE * columns)
    )
    split = group_width // columns
    if split == 1:
        shards_in = (conv_shard, qkv_weight, out_weight, up_weight, down_weight) + tuple(
            gain[None] for gain in (front_gain, middle_gain, final_gain)
        )
        chunks = fused_chunks(conv_shard.shape[0], width, qkv_weight.shape[0], up_weight.shape[1], down_weight.shape[0])
        (weight, wide, down, patches, front_slope, unit_front, projected, probs, attended, unit_middle, middle_low,
         slope, activated, outputs, gains, grad_final, inverse_front, inverse_middle, last_gain_grad) = fused_forward(
            frames, cotangent, clip_lengths[:, 0], shards_in, chunks, dp
        )
        kept = (front_slope, grad_final, unit_front, inverse_front, projected, probs, attended, unit_middle,
                inverse_middle, middle_low, slope, activated, last_gain_grad)
    else:
        wide_shard = jnp.concatenate([qkv_weight, out_weight, up_weight], axis=1)
        gain_shard = jnp.pad(
            jnp.stack([front_gain, middle_gain, final_gain]),
            ((0, 2 * GAIN_ROWS - 3), (0, LANES - gain_width)),
        )
        parts = (conv_shard, wide_shard, down_weight, gain_shard)
        gain_chunk, conv_chunks, wide_chunks, down_chunk = chunks_of(
            *conv_shard.shape, wide_shard.shape[0], width, down_weight.shape[0]
        )
        chunks = gather_chunks(gain_chunk + conv_chunks + wide_chunks + down_chunk)
        conv_all, wide_all, down_all, gain_all = all_gather(parts, chunks, dp)
        weight = (
            conv_all.reshape(GROUPS, split, COARSE * group_width, FINE, columns)
            .transpose(0, 2, 3, 1, 4)
            .reshape(GROUPS, COARSE * group_width, FINE * group_width)
        )
        wide = wide_all.reshape(width, wide_shard.shape[1])
        down = down_all.reshape(-1, width)
        gains = gain_all[:, :3, :gain_width].transpose(1, 0, 2).reshape(3, width).astype(jnp.float32)
        gains = jnp.pad(gains, ((0, 5), (0, 0)))
        both = lax.all_to_all(
            jnp.stack([frames, cotangent], axis=1), "seq", split_axis=0, concat_axis=2, tiled=True
        )
        pack_frames, pack_cotangent = both[0, 0], both[0, 1]
        lengths = lax.dynamic_index_in_dim(clip_lengths[:, 0], lax.axis_index("seq"), 0)
        convolved, patches = conv_forward(pack_frames, weight)
        output, *kept = middle_forward(
            pack_frames, convolved, lengths, gains, wide, down, pack_cotangent
        )
        outputs = lax.all_to_all(output[None], "seq", split_axis=1, concat_axis=0, tiled=True)

    if split == 1:
        conv_sum, qkv_sum, out_sum, up_sum, down_sum, gain_sum, frame_grads = fused_backward(
            weight, wide, down, patches, gains, kept, dp
        )
    else:
        grad_mixed, grad_convolved, wide_grad, down_grad, gain_grads = middle_backward(
            gains, wide, down, kept
        )
        frame_grad, conv_grad = conv_backward(grad_convolved, grad_mixed, weight, patches)

        conv_blocks = (
            conv_grad.reshape(GROUPS, COARSE * group_width, FINE, split, columns)
            .transpose(0, 3, 1, 2, 4)
            .reshape((dp,) + conv_shard.shape)
        )
        gain_blocks = jnp.pad(
            gain_grads[:3].astype(low).reshape(3, dp, gain_width).transpose(1, 0, 2),
            ((0, 0), (0, 2 * GAIN_ROWS - 3), (0, LANES - gain_width)),
        )
        conv_sum, wide_sum, down_sum, gain_sum = reduce_scatter(
            (
                conv_blocks,
                wide_grad.reshape((dp,) + wide_shard.shape),
                down_grad.reshape((dp,) + down_weight.shape),
                gain_blocks,
            ),
            gain_chunk + down_chunk + wide_chunks[::-1] + conv_chunks,
            dp,
        )
        qkv_sum, out_sum, up_sum = (
            wide_sum[:, : 3 * width],
            wide_sum[:, 3 * width : 4 * width],
            wide_sum[:, 4 * width :],
        )
        frame_grads = lax.all_to_all(frame_grad[None], "seq", split_axis=1, concat_axis=0, tiled=True)

    conv_sum = (
        conv_sum.reshape(COARSE, group_width, FINE, columns)
        .transpose(0, 2, 1, 3)
        .reshape(conv_weight.shape)
    )
    return (
        outputs,
        frame_grads,
        conv_sum,
        gain_sum[0, :gain_width],
        qkv_sum,
        out_sum,
        gain_sum[1, :gain_width],
        up_sum,
        down_sum,
        gain_sum[2, :gain_width],
    )


def solution(mesh):
    frames_spec = P(None, ("dp", "seq"), None)
    row, matrix, columns = P("dp"), P("dp", None), P(None, None, "dp")
    return jax.shard_map(
        shards,
        mesh=mesh,
        in_specs=(
            frames_spec,
            P(None, "dp", None),
            columns,
            row,
            matrix,
            matrix,
            row,
            matrix,
            matrix,
            row,
            frames_spec,
        ),
        out_specs=(
            frames_spec,
            frames_spec,
            columns,
            row,
            matrix,
            matrix,
            row,
            matrix,
            matrix,
            row,
        ),
        check_vma=False,
    )
```

```python
import functools

import jax
import jax.numpy as jnp
from jax import lax
from jax.experimental import pallas as pl
from jax.experimental.pallas import tpu as pltpu
from jax.sharding import PartitionSpec as P

MESH = pl.DeviceIdType.MESH


def dp_factors(size):
    return {16: (4, 2, 2), 128: (4, 4, 8)}.get(size, (size, 1, 1))


def near_first(size):
    return [1, 3, 2] if size == 4 else list(range(1, size))


def offsets_of(dims):
    return [(i, j, k) for i in range(dims[0]) for j in range(dims[1]) for k in range(dims[2])]


def partner(coordinate, offset):
    bit = 1
    while bit <= offset:
        if offset & bit:
            coordinate = coordinate + bit - 2 * bit * lax.rem(coordinate // bit, 2)
        bit *= 2
    return coordinate


def place(dims, order, position, offsets):
    coords = list(position)
    for axis, offset in zip(order, offsets):
        if offset:
            coords[axis] = partner(coords[axis], offset)
    return (coords[0] * dims[1] + coords[1]) * dims[2] + coords[2]


def position_of(dims):
    me = lax.axis_index("dp")
    return (me // (dims[1] * dims[2]), lax.rem(me // dims[2], dims[1]), lax.rem(me, dims[2]))


def greet(dims, position, core):
    barrier = pltpu.get_barrier_semaphore()
    count = 1
    pl.semaphore_signal(barrier, inc=1, device_id={"seq": 1 - core}, device_id_type=MESH)
    for axis in range(3):
        for offset in range(1, dims[axis]):
            other = place(dims, (axis,), position, (offset,))
            pl.semaphore_signal(barrier, inc=1, device_id={"dp": other}, device_id_type=MESH)
            count += 1
    pl.semaphore_wait(barrier, count)


FIRST = ((0, 1, 2), (0, 2, 1))
SECOND = ((1, 0, 2), (2, 0, 1))
ORDERS = FIRST


def by_core(core_index, body):
    for core in range(2):
        pl.when(core_index == core)(functools.partial(body, core))


class Gather:
    def __init__(self, dims, chunks, ins, outs, sems):
        self.dims, self.chunks, self.ins, self.outs = dims, chunks, ins, outs
        self.send_sems, self.recv_sems, self.push_send, self.push_recv = sems
        self.position = position_of(dims)
        self.count = dims[0] * dims[1] * dims[2]
        self.sent = {}

    def part(self, which, chunk, side):
        source, array, rows, _, lane, lanes = self.chunks[chunk][1 + side]
        out = self.outs[array]
        if len(out.shape) == 3:
            return out.at[which, pl.ds(*rows), pl.ds(lane, lanes)]
        first = pl.multiple_of(which * self.ins[source].shape[0] + rows[0], 16)
        return out.at[pl.ds(first, rows[1]), pl.ds(lane, lanes)]

    def mine(self, chunk, side):
        source, _, rows, lane, _, lanes = self.chunks[chunk][1 + side]
        return self.ins[source].at[pl.ds(*rows), pl.ds(lane, lanes)]

    def own_copies(self, sems):
        me = lax.axis_index("dp")
        return [
            pltpu.make_async_copy(self.mine(chunk, side), self.part(me, chunk, side), sems.at[chunk, side])
            for chunk in range(len(self.chunks))
            for side in range(2)
        ]

    def send(self, core, chunk, offsets, level, distance):
        order = self.chunks[chunk][0][core]
        gid = place(self.dims, order, self.position, offsets)
        number = self.sent.get((core, chunk), 0)
        self.sent[core, chunk] = number + 1
        pltpu.make_async_remote_copy(
            src_ref=self.mine(chunk, core) if offsets == (0, 0, 0) else self.part(gid, chunk, core),
            dst_ref=self.part(gid, chunk, core),
            send_sem=self.send_sems.at[chunk, number],
            recv_sem=self.recv_sems.at[chunk, gid],
            device_id={"dp": place(self.dims, (order[level],), self.position, (distance,))},
            device_id_type=MESH,
        ).start()

    def spread(self, core, chunk, offsets, first):
        for level in range(first, 3):
            for distance in near_first(self.dims[self.chunks[chunk][0][core][level]]):
                self.send(core, chunk, offsets, level, distance)

    def forward(self, core, chunk, offsets, first):
        gid = place(self.dims, self.chunks[chunk][0][core], self.position, offsets)
        ref = self.part(gid, chunk, core)
        pltpu.make_async_copy(ref, ref, self.recv_sems.at[chunk, gid]).wait()
        self.spread(core, chunk, offsets, first)
        pltpu.make_async_remote_copy(
            src_ref=ref,
            dst_ref=ref,
            send_sem=self.push_send.at[chunk, gid],
            recv_sem=self.push_recv.at[chunk, gid],
            device_id={"seq": 1 - core},
            device_id_type=MESH,
        ).start()

    def tasks(self, core, chunk, stage):
        sizes = [self.dims[axis] for axis in self.chunks[chunk][0][core]]
        if stage == 0:
            return [functools.partial(self.spread, core, chunk, (0, 0, 0), 0)]
        if stage == 1:
            places = [(i, 0, 0) for i in near_first(sizes[0])]
        elif stage == 2:
            places = [(i, j, 0) for i in [0] + near_first(sizes[0]) for j in near_first(sizes[1])]
        else:
            places = [
                (i, j, k)
                for j in [0] + near_first(sizes[1])
                for i in [0] + near_first(sizes[0])
                for k in near_first(sizes[2])
            ]
        return [functools.partial(self.forward, core, chunk, offsets, stage) for offsets in places]

    def steps(self, core, step):
        done = []
        for stage in range(4):
            if 0 <= step - stage < len(self.chunks):
                done += self.tasks(core, step - stage, stage)
        return done

    def others(self, body):
        me = lax.axis_index("dp")

        @pl.loop(1, self.count)
        def _(offset):
            body(lax.rem(me + offset, self.count), offset)

    def arrived_block(self, core, chunk, gid):
        ref = self.part(gid, chunk, 1 - core)
        pltpu.make_async_copy(ref, ref, self.push_recv.at[chunk, gid]).wait()

    def arrived(self, core, chunk):
        def body(gid, _):
            ref = self.part(gid, chunk, 1 - core)
            pltpu.make_async_copy(ref, ref, self.push_recv.at[chunk, gid]).wait()

        self.others(body)

    def finish(self, core):
        for chunk in range(len(self.chunks)):

            def body(gid, number, chunk=chunk):
                ref = self.part(gid, chunk, core)
                pltpu.make_async_copy(ref, ref, self.push_send.at[chunk, gid]).wait()
                pltpu.make_async_copy(ref, ref, self.send_sems.at[chunk, number - 1]).wait()

            self.others(body)


def gather_kernel(dims, chunks, *refs):
    n_arr = len(refs[:-5]) // 2
    ins, outs = refs[:n_arr], refs[n_arr : 2 * n_arr]
    gather = Gather(dims, chunks, ins, outs, refs[2 * n_arr : 2 * n_arr + 4])
    local_sems = refs[-1]
    core_index = lax.axis_index("seq")
    greet(dims, gather.position, core_index)
    own = gather.own_copies(local_sems)
    for copy in own:
        copy.start()

    def run(core):
        for step in range(len(chunks) + 3):
            for task in gather.steps(core, step):
                task()
        for chunk in range(len(chunks)):
            gather.arrived(core, chunk)
        gather.finish(core)

    by_core(core_index, run)
    for copy in own:
        copy.wait()


def all_gather(arrays, chunks, dp, collective_id=0):
    dims = dp_factors(dp)
    n = len(chunks)
    any_ = pl.BlockSpec(memory_space=pl.ANY)
    return pl.pallas_call(
        functools.partial(gather_kernel, dims, chunks),
        out_shape=[jax.ShapeDtypeStruct((dp,) + a.shape, a.dtype) for a in arrays],
        in_specs=[any_] * len(arrays),
        out_specs=[any_] * len(arrays),
        scratch_shapes=[
            pltpu.SemaphoreType.DMA((n, dp)),
            pltpu.SemaphoreType.DMA((n, dp)),
            pltpu.SemaphoreType.DMA((n, dp)),
            pltpu.SemaphoreType.DMA((n, dp)),
            pltpu.SemaphoreType.DMA((n, 2)),
        ],
        compiler_params=pltpu.CompilerParams(collective_id=collective_id, has_side_effects=True),
    )(*arrays)


def scatter_kernel(dims, chunks, n_arr, *refs):
    ins, outs = refs[:n_arr], refs[n_arr : 2 * n_arr]
    scratch = list(refs[2 * n_arr :])
    n = len(chunks)
    stage_refs, pair_refs = scratch[:n], scratch[n : 2 * n]
    hop_refs = [scratch[(2 + level) * n : (3 + level) * n] for level in range(3)]
    (load_sems, pair_send, pair_recv, hop_send, hop_recv, last_send, last_recv) = scratch[5 * n :]
    position = position_of(dims)
    core_index = lax.axis_index("seq")
    greet(dims, position, core_index)

    def run(core):
        order = ORDERS[core]
        sizes = [dims[axis] for axis in order]
        started = []
        other_order = ORDERS[1 - core]
        other_sizes = [dims[axis] for axis in other_order]

        def part(array_refs, which, chunk, side):
            array, rows, lanes = chunks[chunk][side]
            return array_refs[array].at[which, pl.ds(*rows), pl.ds(*lanes)]

        def slot(level, offsets, distance):
            index = distance - 1
            for i in range(level):
                index = index * sizes[i] + offsets[i]
            return index

        def semaphore(level, index):
            return (1, sizes[0], sizes[0] * sizes[1])[level] + index - 1

        def begin(chunk):
            array = chunks[chunk][core][0]
            theirs = sorted(offsets_of(other_sizes), key=lambda o: (o[2] == 0, o[1] == 0, o[0] == 0))
            mine = sorted(offsets_of(sizes), key=lambda o: (o[2] == 0, o[1] == 0, o[0] == 0))
            for given, kept in zip(theirs, mine):
                gid = place(dims, other_order, position, given)
                copy = pltpu.make_async_remote_copy(
                    src_ref=part(ins, gid, chunk, 1 - core),
                    dst_ref=pair_refs[chunk].at[gid],
                    send_sem=pair_send.at[chunk],
                    recv_sem=pair_recv.at[chunk, gid],
                    device_id={"seq": 1 - core},
                    device_id_type=MESH,
                )
                copy.start()
                gid = place(dims, order, position, kept)
                pltpu.make_async_copy(
                    part(ins, gid, chunk, core), stage_refs[chunk].at[gid], load_sems.at[chunk, gid]
                ).start()

        def combine(chunk, offsets, target):
            gid = place(dims, order, position, offsets)
            own = stage_refs[chunk].at[gid]
            pair = pair_refs[chunk].at[gid]
            pltpu.make_async_copy(own, own, load_sems.at[chunk, gid]).wait()
            pltpu.make_async_copy(pair, pair, pair_recv.at[chunk, gid]).wait()
            terms = [own, pair]
            for level in (2, 1, 0):
                if offsets[level]:
                    break
                for distance in range(1, sizes[level]):
                    index = slot(level, offsets, distance)
                    ref = hop_refs[level][chunk].at[index]
                    pltpu.make_async_copy(ref, ref, hop_recv.at[chunk, semaphore(level, index)]).wait()
                    terms.append(ref)
            height = own.shape[0]

            tall = 16 if height % 16 == 0 else height

            @pl.loop(0, height // tall)
            def _(tile):
                rows = pl.ds(pl.multiple_of(tile * tall, tall), tall)
                total = terms[0][rows, :].astype(jnp.float32)
                for term in terms[1:]:
                    total = total + term[rows, :].astype(jnp.float32)
                if target is None:
                    own[rows, :] = total.astype(own.dtype)
                else:
                    target[rows, :] = total

            return gid

        def send(chunk, offsets):
            level = max(i for i in range(3) if offsets[i])
            gid = combine(chunk, offsets, None)
            index = slot(level, offsets, offsets[level])
            target = place(dims, (order[level],), position, (offsets[level],))
            copy = pltpu.make_async_remote_copy(
                src_ref=stage_refs[chunk].at[gid],
                dst_ref=hop_refs[level][chunk].at[index],
                send_sem=hop_send.at[chunk, semaphore(level, index)],
                recv_sem=hop_recv.at[chunk, semaphore(level, index)],
                device_id={"dp": target},
                device_id_type=MESH,
            )
            copy.start()
            started.append(copy)

        def final(chunk):
            array, rows, lanes = chunks[chunk][core]
            half = outs[array].at[pl.ds(*rows), pl.ds(*lanes)]
            combine(chunk, (0, 0, 0), half)
            copy = pltpu.make_async_remote_copy(
                src_ref=half,
                dst_ref=half,
                send_sem=last_send.at[chunk],
                recv_sem=last_recv.at[chunk],
                device_id={"seq": 1 - core},
                device_id_type=MESH,
            )
            copy.start()
            started.append(copy)

        for chunk in range(n):
            begin(chunk)

        def stage(chunk, number):
            if number == 0:
                for d in range(1, sizes[2]):
                    for i in range(sizes[0]):
                        for j in range(sizes[1]):
                            send(chunk, (i, (j + 1) % sizes[1], d))
            if number == 1:
                for d in range(1, sizes[1]):
                    for i in range(sizes[0]):
                        send(chunk, ((i + 1) % sizes[0], d, 0))
            if number == 2:
                for d in range(1, sizes[0]):
                    send(chunk, (d, 0, 0))
            if number == 3:
                final(chunk)

        for step in range(n + 3):
            for number in range(4):
                if 0 <= step - number < n:
                    stage(step - number, number)
        for chunk in range(n):
            array, rows, lanes = chunks[chunk][1 - core]
            half = outs[array].at[pl.ds(*rows), pl.ds(*lanes)]
            pltpu.make_async_copy(half, half, last_recv.at[chunk]).wait()
            sent = pair_refs[chunk]
            pltpu.make_async_copy(sent, sent, pair_send.at[chunk]).wait()
        for copy in started:
            copy.wait_send()

    for core in range(2):
        pl.when(core_index == core)(functools.partial(run, core))


def hop_slots(dims, order):
    a, b, c = [dims[axis] for axis in order]
    return (a - 1, a * (b - 1), a * b * (c - 1))


def reduce_scatter(arrays, chunks, dp, collective_id=1):
    dims = dp_factors(dp)
    n = len(chunks)
    any_ = pl.BlockSpec(memory_space=pl.ANY)
    shapes = [(chunk[0][1][1], chunk[0][2][1]) for chunk in chunks]
    slots = [max(pair) for pair in zip(hop_slots(dims, ORDERS[0]), hop_slots(dims, ORDERS[1]))]
    low = jnp.bfloat16
    scratch = [pltpu.VMEM((dp,) + s, low) for s in shapes] * 2
    for level in range(3):
        scratch += [pltpu.VMEM((slots[level],) + s, low) for s in shapes]
    return pl.pallas_call(
        functools.partial(scatter_kernel, dims, chunks, len(arrays)),
        out_shape=[jax.ShapeDtypeStruct(a.shape[1:], jnp.float32) for a in arrays],
        in_specs=[any_] * len(arrays),
        out_specs=[pl.BlockSpec(memory_space=pltpu.VMEM)] * len(arrays),
        scratch_shapes=scratch
        + [
            pltpu.SemaphoreType.DMA((n, dp)),
            pltpu.SemaphoreType.DMA((n,)),
            pltpu.SemaphoreType.DMA((n, dp)),
            pltpu.SemaphoreType.DMA((n, dp)),
            pltpu.SemaphoreType.DMA((n, dp)),
            pltpu.SemaphoreType.DMA((n,)),
            pltpu.SemaphoreType.DMA((n,)),
        ],
        compiler_params=pltpu.CompilerParams(
            collective_id=collective_id, has_side_effects=True, vmem_limit_bytes=58 << 20
        ),
    )(*arrays)


GROUPS = 16
KERNEL = 128
FINE = 16
COARSE = KERNEL // FINE
LANES = 128


def lane_numbers(rows):
    return lax.broadcasted_iota(jnp.int32, (rows, LANES), 1)


def take_group(ref, rows, group, width):
    start = group * width
    base = pl.multiple_of(start // LANES * LANES, LANES)
    window = ref[rows, pl.ds(base, 2 * LANES)]
    turned = pltpu.roll(window, lax.rem(2 * LANES - (start - base), 2 * LANES), 1)[:, :LANES]
    return jnp.where(lane_numbers(turned.shape[0]) < width, turned, 0.0)


def add_group(ref, values, group, width):
    start = group * width
    base = pl.multiple_of(start // LANES * LANES, LANES)
    wide = jnp.concatenate([values, jnp.zeros_like(values)], axis=1)
    ref[:, pl.ds(base, 2 * LANES)] += pltpu.roll(wide, start - base, 1)


def double_96(pair, moved):
    lane = lane_numbers(pair.shape[0])
    turned = pltpu.roll(moved, 96, 1)
    return jnp.where(lane < 96, pair, turned), jnp.where(lane < 64, turned, 0.0)


def double_192(first, second, moved_first, moved_second):
    lane = lane_numbers(first.shape[0])
    a, b = pltpu.roll(moved_first, 64, 1), pltpu.roll(moved_second, 64, 1)
    return first, jnp.where(lane < 64, second, a), jnp.where(lane < 64, a, b)


def fold_lanes(tiles, shift):
    a, b, c = tiles
    lane = lane_numbers(a.shape[0])
    tb, tc = pltpu.roll(b, 64, 1), pltpu.roll(c, 64, 1)
    a, b = shift(a, jnp.where(lane < 64, tb, tc), 4), shift(b, tc, 4)
    lane = lane_numbers(a.shape[0])
    far = jnp.where(lane < 32, pltpu.roll(a, 32, 1), pltpu.roll(b, 32, 1))
    a = shift(a, far, 2)
    a = shift(a, pltpu.roll(a, 80, 1), 1)
    return jnp.where(lane_numbers(a.shape[0]) < 48, a, 0.0)


def make_patch(padded, group, pack):
    reach = pack + FINE
    one = take_group(padded, slice(0, reach + KERNEL - FINE), group, 48)
    rows = one.shape[0] - FINE
    two = one[:rows] + pltpu.roll(one[FINE:], 48, 1)
    low, high = double_96(two[: rows - 2 * FINE], two[2 * FINE :])
    tiles = double_192(low[:reach], high[:reach], low[4 * FINE :], high[4 * FINE :])
    return jnp.concatenate(tiles, axis=1).astype(jnp.bfloat16)


def add_forward(total, patch, weight, group, pack):
    product = jnp.dot(patch, weight, preferred_element_type=jnp.float32)
    size = pack + 8
    near = product[:size, :384] + product[8 : 8 + size, 384:]

    def shift(base, moved, amount):
        return base + pltpu.roll(moved, size - amount, 0)

    tiles = [near[:, i * LANES : (i + 1) * LANES] for i in range(3)]
    add_group(total, fold_lanes(tiles, shift)[:pack], group, 48)


def fill_padded(padded, frames):
    half = KERNEL // 2
    padded[...] = jnp.zeros_like(padded)
    padded[half : half + frames.shape[0], 0 : frames.shape[1]] = frames[...].astype(jnp.float32)


def forward_kernel(pack, frames, weight, out, patches, padded, total):
    group = pl.program_id(0)

    @pl.when(group == 0)
    def _():
        fill_padded(padded, frames)
        total[...] = jnp.zeros_like(total)

    patch = make_patch(padded, group, pack)
    patches[0] = patch
    add_forward(total, patch, weight[0], group, pack)

    @pl.when(group == GROUPS - 1)
    def _():
        out[...] = total[:, : frames.shape[1]]


def conv_forward(frames, weight):
    pack, width = frames.shape
    reach = pack + FINE
    return pl.pallas_call(
        functools.partial(forward_kernel, pack),
        grid=(GROUPS,),
        out_shape=[
            jax.ShapeDtypeStruct((pack, width), jnp.float32),
            jax.ShapeDtypeStruct((GROUPS, reach, 384), jnp.bfloat16),
        ],
        in_specs=[
            pl.BlockSpec((pack, width), lambda g: (0, 0)),
            pl.BlockSpec((1, 384, 768), lambda g: (g, 0, 0)),
        ],
        out_specs=[
            pl.BlockSpec((pack, width), lambda g: (0, 0)),
            pl.BlockSpec((1, reach, 384), lambda g: (g, 0, 0)),
        ],
        scratch_shapes=[
            pltpu.VMEM((pack + KERNEL, width + LANES), jnp.float32),
            pltpu.VMEM((pack, width + LANES), jnp.float32),
        ],
        compiler_params=pltpu.CompilerParams(vmem_limit_bytes=40 << 20),
    )(frames, weight)


def backward_kernel(pack, grads, direct, weight, patches, out, weight_grad, padded, tall, total):
    group = pl.program_id(0)
    reach = pack + FINE
    edge = KERNEL // 2 - FINE

    @pl.when(group == 0)
    def _():
        padded[...] = jnp.zeros_like(padded)
        padded[:pack, : grads.shape[1]] = grads[...].astype(jnp.float32)
        tall[...] = jnp.zeros_like(tall)
        total[...] = jnp.zeros_like(total)
        total[:, : direct.shape[1]] = direct[...]

    def later(values, amount):
        return pltpu.roll(values, amount, 0)

    one = take_group(padded, slice(0, reach), group, 48)
    two = one + pltpu.roll(later(one, 1), 48, 1)
    low, high = double_96(two, later(two, 2))
    tiles = double_192(low, high, later(low, 4), later(high, 4))
    near = jnp.concatenate(tiles, axis=1)
    spread = jnp.concatenate([near, later(near, 8)], axis=1).astype(jnp.bfloat16)
    weight_grad[0] = lax.dot_general(
        patches[0], spread, (((0,), (0,)), ((), ())), preferred_element_type=jnp.float32
    ).astype(jnp.bfloat16)
    tall[edge : edge + reach] = lax.dot_general(
        spread, weight[0], (((1,), (1,)), ((), ())), preferred_element_type=jnp.float32
    )

    def shift(base, moved, amount):
        return base[amount * FINE :] + moved[: base.shape[0] - amount * FINE]

    tiles = [tall[:, i * LANES : (i + 1) * LANES] for i in range(3)]
    add_group(total, fold_lanes(tiles, shift), group, 48)

    @pl.when(group == GROUPS - 1)
    def _():
        out[...] = total[:, : grads.shape[1]]


def conv_backward(grads, direct, weight, patches):
    pack, width = grads.shape
    reach = pack + FINE
    whole = lambda g: (0, 0)
    each = lambda g: (g, 0, 0)
    return pl.pallas_call(
        functools.partial(backward_kernel, pack),
        grid=(GROUPS,),
        out_shape=[
            jax.ShapeDtypeStruct((pack, width), jnp.float32),
            jax.ShapeDtypeStruct(weight.shape, jnp.bfloat16),
        ],
        in_specs=[
            pl.BlockSpec((pack, width), whole),
            pl.BlockSpec((pack, width), whole),
            pl.BlockSpec((1, 384, 768), each),
            pl.BlockSpec((1, reach, 384), each),
        ],
        out_specs=[
            pl.BlockSpec((pack, width), whole),
            pl.BlockSpec((1, 384, 768), each),
        ],
        scratch_shapes=[
            pltpu.VMEM((reach, width + LANES), jnp.float32),
            pltpu.VMEM((pack + KERNEL - FINE, 384), jnp.float32),
            pltpu.VMEM((pack, width + LANES), jnp.float32),
        ],
        compiler_params=pltpu.CompilerParams(vmem_limit_bytes=40 << 20),
    )(grads, direct, weight, patches)


HEAD_DIM = 64
EPSILON = 1e-05
ROWS = 32
TILE = 256


def dot(a, b, contract=(1, 0)):
    return lax.dot_general(
        a, b, ((contract[:1], contract[1:]), ((), ())), preferred_element_type=jnp.float32
    )


def below_normal(values):
    return 0.5 * (1.0 + lax.erf(values * 0.7071067811865476))


def density(values):
    return jnp.exp(-0.5 * values * values) * 0.3989422804014327


def unit_norm(values):
    centered = values - jnp.mean(values, axis=-1, keepdims=True)
    inverse = lax.rsqrt(jnp.mean(centered * centered, axis=-1, keepdims=True) + EPSILON)
    return centered * inverse, inverse


def norm_back(grad, unit, inverse, gain):
    scaled = grad * gain
    inner = jnp.mean(scaled, axis=-1, keepdims=True)
    along = jnp.mean(scaled * unit, axis=-1, keepdims=True)
    return inverse * (scaled - inner - unit * along)


def row_tiles(pack, body):
    @pl.loop(0, pack // ROWS)
    def _(tile):
        body(pl.ds(pl.multiple_of(tile * ROWS, ROWS), ROWS))


def lane_tiles(count, body, first=0):
    @pl.loop(first, count)
    def _(tile):
        body(tile, pl.ds(pl.multiple_of(tile * TILE, TILE), TILE))


def clip_mask(lengths, micro, pack):
    row = lax.broadcasted_iota(jnp.int32, (pack, pack), 0)
    column = lax.broadcasted_iota(jnp.int32, (pack, pack), 1)
    row_clip, column_clip = jnp.zeros_like(row), jnp.zeros_like(column)
    end = 0
    for clip in range(lengths.shape[1]):
        end = end + lengths[micro, clip]
        row_clip += (row >= end).astype(jnp.int32)
        column_clip += (column >= end).astype(jnp.int32)
    return row_clip == column_clip


def front_norm(frames, convolved, gains, normed, normed_low, unit, inverse, front_slope):
    def body(rows):
        values = convolved[rows, 0 : frames.shape[1]]
        below = below_normal(values)
        front_slope[rows, :] = below + values * density(values)
        mixed = frames[rows, :].astype(jnp.float32) + values * below
        units, inv = unit_norm(mixed)
        unit[rows, :] = units
        inverse[rows, :] = jnp.broadcast_to(inv, (ROWS, LANES))
        total = units * gains[0:1, :]
        normed[rows, :] = total
        normed_low[rows, :] = total.astype(normed_low.dtype)

    row_tiles(frames.shape[0], body)


def project(normed_low, weight, projected):
    def body(tile, lanes):
        projected[:, lanes] = dot(normed_low[...], weight[:, lanes]).astype(projected.dtype)

    lane_tiles(projected.shape[1] // TILE, body)


def pair_parts(projected, pair, width):
    return [
        projected[:, pl.ds(pl.multiple_of(part * width + pair * LANES, LANES), LANES)] for part in range(3)
    ]


def attend(projected, lengths, micro, probs, attended, first=0, last=None):
    pack, width = attended.shape
    low = projected.dtype
    scale = HEAD_DIM ** (-0.5)

    @pl.loop(first, last or width // LANES)
    def _(pair):
        same = clip_mask(lengths, micro, pack)
        queries, keys, values = pair_parts(projected, pair, width)
        lane = lax.broadcasted_iota(jnp.int32, (pack, LANES), 1)
        sides = []
        for side in range(2):
            own = (lane < HEAD_DIM) == (side == 0)
            scores = dot(jnp.where(own, queries, jnp.zeros_like(queries)), keys, (1, 1)) * scale
            scores = jnp.where(same, scores, -1e30)
            shifted = jnp.exp(scores - jnp.max(scores, axis=-1, keepdims=True))
            weights = shifted / jnp.sum(shifted, axis=-1, keepdims=True)
            probs[2 * pair + side] = weights
            sides.append(dot(weights.astype(low), values))
        lanes = pl.ds(pl.multiple_of(pair * LANES, LANES), LANES)
        attended[:, lanes] = jnp.where(lane < HEAD_DIM, *sides).astype(low)


def middle_norm(attended, weight, normed, gains, middle, middle_low, unit, inverse):
    def body(tile, lanes):
        middle[:, lanes] = normed[:, lanes] + dot(attended[...], weight[:, lanes])

    lane_tiles(normed.shape[1] // TILE, body)

    def finish(rows):
        units, inv = unit_norm(middle[rows, :])
        unit[rows, :] = units
        inverse[rows, :] = jnp.broadcast_to(inv, (ROWS, LANES))
        total = units * gains[1:2, :]
        middle[rows, :] = total
        middle_low[rows, :] = total.astype(middle_low.dtype)

    row_tiles(normed.shape[0], finish)


def feed_up(middle_low, weight, slope, activated, first=0, last=None):
    def body(tile, lanes):
        values = dot(middle_low[...], weight[:, lanes])
        below = below_normal(values)
        slope[:, lanes] = (below + values * density(values)).astype(slope.dtype)
        activated[:, lanes] = (values * below).astype(activated.dtype)

    lane_tiles(last or slope.shape[1] // TILE, body, first)


def feed_down(activated, weight, middle, gains, cotangent, output, grad_final, gain_grads):
    def body(tile, lanes):
        middle[...] += dot(activated[:, lanes], weight[lanes, :])

    lane_tiles(activated.shape[1] // TILE, body)
    last_norm(middle, gains, cotangent, output, grad_final, gain_grads)


def last_norm(middle, gains, cotangent, output, grad_final, gain_grads):
    gain_grads[2:3, :] = jnp.zeros((1, middle.shape[1]), jnp.float32)

    def finish(rows):
        units, inv = unit_norm(middle[rows, :])
        gain = gains[2:3, :]
        output[rows, :] = (units * gain).astype(output.dtype)
        grad = cotangent[rows, :].astype(jnp.float32)
        gain_grads[2:3, :] += jnp.sum(grad * units, axis=0, keepdims=True)
        grad_final[rows, :] = norm_back(grad, units, inv, gain)

    row_tiles(middle.shape[0], finish)


def feed_back(grad, slope, activated, middle_low, up, down, up_grad, down_grad):
    low = activated.dtype
    grad_feed = grad[...].astype(low)
    turned = jnp.transpose(middle_low[...].astype(jnp.float32)).astype(low)

    def body(tile, lanes):
        down_grad[lanes, :] = dot(activated[:, lanes], grad_feed, (0, 0)).astype(low)
        grad_hidden = (dot(grad_feed, down[lanes, :], (1, 1)) * slope[:, lanes].astype(jnp.float32)).astype(low)
        up_grad[:, lanes] = dot(turned, grad_hidden).astype(low)
        grad[...] += dot(grad_hidden, up[:, lanes], (1, 1))

    lane_tiles(slope.shape[1] // TILE, body)


def norm_back_rows(grad, unit, inverse, gains, which, gain_grads):
    gain_grads[which : which + 1, :] = jnp.zeros((1, grad.shape[1]), jnp.float32)

    def body(rows):
        incoming, units = grad[rows, :], unit[rows, :]
        gain_grads[which : which + 1, :] += jnp.sum(incoming * units, axis=0, keepdims=True)
        grad[rows, :] = norm_back(incoming, units, inverse[rows, 0:1], gains[which : which + 1, :])

    row_tiles(grad.shape[0], body)


def branch_back(grad, attended, weight, grad_attended, out_grad):
    low = attended.dtype
    grad_branch = grad[...].astype(low)

    def body(tile, lanes):
        out_grad[lanes, :] = dot(attended[:, lanes], grad_branch, (0, 0)).astype(low)
        grad_attended[:, lanes] = dot(grad_branch, weight[lanes, :], (1, 1)).astype(low)

    lane_tiles(attended.shape[1] // TILE, body)


def attend_back_pair(projected, grad_attended, weights_of, grad_projected, pair):
    pack, width = grad_attended.shape
    low = projected.dtype
    scale = HEAD_DIM ** (-0.5)

    def lanes_of(part):
        start = part * width + pair * LANES
        return pl.ds(start if isinstance(pair, int) else pl.multiple_of(start, LANES), LANES)

    queries, keys, values = [projected[:, lanes_of(part)] for part in range(3)]
    grad = grad_attended[:, lanes_of(0)]
    lane = lax.broadcasted_iota(jnp.int32, (pack, LANES), 1)
    sides = []
    for side in range(2):
        own = (lane < HEAD_DIM) == (side == 0)
        weights = weights_of[side]
        grad_values = dot(weights.astype(low), grad, (0, 0))
        grad_probs = dot(jnp.where(own, grad, jnp.zeros_like(grad)), values, (1, 1))
        along = jnp.sum(weights * grad_probs, axis=-1, keepdims=True)
        grad_scores = (weights * (grad_probs - along)).astype(low)
        grad_queries = dot(grad_scores, keys) * scale
        grad_keys = dot(grad_scores, queries, (0, 0)) * scale
        sides.append((grad_queries, grad_keys, grad_values))
    for part in range(3):
        grad_projected[:, lanes_of(part)] = jnp.where(lane < HEAD_DIM, sides[0][part], sides[1][part]).astype(low)


def attend_back(projected, grad_attended, probs, grad_projected):
    @pl.loop(0, grad_attended.shape[1] // LANES)
    def _(pair):
        attend_back_pair(projected, grad_attended, probs.at[pl.ds(2 * pair, 2)], grad_projected, pair)


def project_back(grad, grad_projected, unit, gains, weight, qkv_grad):
    low = grad_projected.dtype
    turned = jnp.transpose(unit[...] * gains[0:1, :]).astype(low)

    def body(tile, lanes):
        qkv_grad[:, lanes] = dot(turned, grad_projected[:, lanes]).astype(low)
        grad[...] += dot(grad_projected[:, lanes], weight[:, lanes], (1, 1))

    lane_tiles(grad_projected.shape[1] // TILE, body)


def slope_rows(grad, front_slope, grad_convolved):
    def body(rows):
        grad_convolved[rows, :] = (grad[rows, :] * front_slope[rows, :]).astype(grad_convolved.dtype)

    row_tiles(grad.shape[0], body)


def middle_forward_kernel(
    lengths, frames, convolved, gains, wide, down, cotangent,
    output, front_slope, grad_final, unit_front, inverse_front, projected, probs, attended,
    unit_middle, inverse_middle, middle_low, slope, activated, gain_grads,
    normed, normed_low, middle,
):
    width = frames.shape[1]
    gain_grads[...] = jnp.zeros_like(gain_grads)
    front_norm(frames, convolved, gains, normed, normed_low, unit_front, inverse_front, front_slope)
    project(normed_low, wide.at[:, 0 : 3 * width], projected)
    attend(projected, lengths, 0, probs, attended)
    middle_norm(
        attended, wide.at[:, 3 * width : 4 * width], normed, gains, middle, middle_low, unit_middle,
        inverse_middle,
    )
    feed_up(middle_low, wide.at[:, 4 * width :], slope, activated)
    feed_down(activated, down, middle, gains, cotangent, output, grad_final, gain_grads)


def middle_backward_kernel(
    gains, wide, down, front_slope, grad_final, unit_front, inverse_front, projected, probs, attended,
    unit_middle, inverse_middle, middle_low, slope, activated, last_gain_grad,
    grad, grad_convolved, wide_grad, down_grad, gain_grads,
    grad_attended, grad_projected,
):
    width = grad.shape[1]
    gain_grads[...] = last_gain_grad[...]
    grad[...] = grad_final[...]
    feed_back(
        grad, slope, activated, middle_low, wide.at[:, 4 * width :], down, wide_grad.at[:, 4 * width :],
        down_grad,
    )
    norm_back_rows(grad, unit_middle, inverse_middle, gains, 1, gain_grads)
    branch_back(
        grad, attended, wide.at[:, 3 * width : 4 * width], grad_attended,
        wide_grad.at[:, 3 * width : 4 * width],
    )
    attend_back(projected, grad_attended, probs, grad_projected)
    project_back(
        grad, grad_projected, unit_front, gains, wide.at[:, 0 : 3 * width], wide_grad.at[:, 0 : 3 * width]
    )
    norm_back_rows(grad, unit_front, inverse_front, gains, 0, gain_grads)
    slope_rows(grad, front_slope, grad_convolved)


def middle_forward(frames, convolved, lengths, gains, wide, down, cotangent):
    pack, width = frames.shape
    inner = down.shape[0]
    heads = width // HEAD_DIM
    low, full = jnp.bfloat16, jnp.float32
    shape = jax.ShapeDtypeStruct
    vmem = pl.BlockSpec(memory_space=pltpu.VMEM)
    saved = [
        shape((pack, width), low),
        shape((pack, width), full),
        shape((pack, width), full),
        shape((pack, width), full),
        shape((pack, LANES), full),
        shape((pack, 3 * width), low),
        shape((heads, pack, pack), full),
        shape((pack, width), low),
        shape((pack, width), full),
        shape((pack, LANES), full),
        shape((pack, width), low),
        shape((pack, inner), low),
        shape((pack, inner), low),
        shape((8, width), full),
    ]
    return pl.pallas_call(
        middle_forward_kernel,
        out_shape=saved,
        in_specs=[pl.BlockSpec(memory_space=pltpu.SMEM)] + [vmem] * 6,
        out_specs=[vmem] * len(saved),
        scratch_shapes=[
            pltpu.VMEM((pack, width), full),
            pltpu.VMEM((pack, width), low),
            pltpu.VMEM((pack, width), full),
        ],
        compiler_params=pltpu.CompilerParams(vmem_limit_bytes=58 << 20),
    )(lengths, frames, convolved, gains, wide, down, cotangent)


def middle_backward(gains, wide, down, kept):
    pack, width = kept[0].shape
    low, full = jnp.bfloat16, jnp.float32
    shape = jax.ShapeDtypeStruct
    vmem = pl.BlockSpec(memory_space=pltpu.VMEM)
    grads = [
        shape((pack, width), full),
        shape((pack, width), low),
        shape(wide.shape, low),
        shape(down.shape, low),
        shape((8, width), full),
    ]
    return pl.pallas_call(
        middle_backward_kernel,
        out_shape=grads,
        in_specs=[vmem] * (3 + len(kept)),
        out_specs=[vmem] * len(grads),
        scratch_shapes=[pltpu.VMEM((pack, width), low), pltpu.VMEM((pack, 3 * width), low)],
        compiler_params=pltpu.CompilerParams(vmem_limit_bytes=58 << 20),
    )(gains, wide, down, *kept)


def weave(tasks, pieces):
    core_index = lax.axis_index("seq")
    count, done = len(tasks[0]), 0
    for number, piece in enumerate(pieces + [None]):
        until = count if piece is None else (number + 1) * count // (len(pieces) + 1)

        def some(core, first=done, last=until):
            for task in tasks[core][first:last]:
                task()

        if until > done:
            by_core(core_index, some)
        done = until
        if piece is not None:
            piece()


def fused_forward_kernel(
    dims, chunks,
    lengths, frames, cotangent, conv_shard, qkv_shard, out_shard, up_shard, down_shard, front_gain, middle_gain,
    final_gain,
    conv_out, wide_out, down_out, patches_out, front_slope_out, unit_front_out, projected_out, probs_out,
    attended_out, unit_middle_out, middle_low_out, slope_out, activated_out, both_output, gains, grad_final,
    inverse_front, inverse_middle, gain_grads,
    patches, front_slope, unit_front, projected, probs, attended, unit_middle, middle_low, slope, activated,
    gain_shard,
    conv_all, wide_all, down_all, gain_all, pack_frames, pack_cotangent, output, padded, total,
    gains_wide, normed, normed_low, middle,
    send_sems, recv_sems, push_send, push_recv, own_sems, local_sems, save_sems, pair_sems,
):
    ins = (conv_shard, qkv_shard, out_shard, up_shard, down_shard, gain_shard)
    outs = (conv_all, wide_all, down_all, gain_all)
    gather = Gather(dims, chunks, ins, outs, (send_sems, recv_sems, push_send, push_recv))
    core_index = lax.axis_index("seq")
    pack, width = pack_frames.shape
    half = pack // 2
    row = lax.broadcasted_iota(jnp.int32, (GAIN_ROWS, LANES), 0)
    rows = jnp.zeros((GAIN_ROWS, LANES), jnp.float32)
    for index, gain in enumerate((front_gain, middle_gain, final_gain)):
        one = gain[...].astype(jnp.float32)
        one = jnp.concatenate([one, jnp.zeros((1, LANES - one.shape[1]), jnp.float32)], axis=1)
        rows = jnp.where(row == index, one, rows)
    gain_shard[...] = jnp.concatenate([rows, rows], axis=0).astype(gain_shard.dtype)
    greet(dims, gather.position, core_index)

    here = pl.ds(pl.multiple_of(core_index * half, half), half)
    there = pl.ds(pl.multiple_of((1 - core_index) * half, half), half)

    def to_partner(source, target, number):
        return pltpu.make_async_remote_copy(
            src_ref=source,
            dst_ref=target,
            send_sem=pair_sems.at[0, number],
            recv_sem=pair_sems.at[1, number],
            device_id={"seq": 1 - core_index},
            device_id_type=MESH,
        )

    moves = []
    for number, (source, target) in enumerate(((frames, pack_frames), (cotangent, pack_cotangent))):
        moves.append(to_partner(source.at[1 - core_index], target.at[here], number))
        moves.append(pltpu.make_async_copy(source.at[core_index], target.at[here], local_sems.at[number]))
    for copy in moves:
        copy.start()
    own = gather.own_copies(own_sems)
    for copy in own:
        copy.start()

    def early(core):
        for chunk in range(3):
            for task in gather.tasks(core, chunk, 0):
                task()

    by_core(core_index, early)
    steps = []
    for step in range(1, len(chunks) + 3):
        both = []
        for core in range(2):
            tasks = []
            for stage in (3, 2, 1):
                if 0 <= step - stage < len(chunks):
                    tasks += gather.tasks(core, step - stage, stage)
            if 3 <= step + 2 < len(chunks):
                tasks += gather.tasks(core, step + 2, 0)
            both.append(tasks)
        steps.append(both)

    def gate(*numbers):
        def body(core):
            for number in numbers:
                gather.arrived(core, number)

        by_core(core_index, body)

    for copy in moves[:2]:
        copy.wait()
    fill_padded(padded, pack_frames)
    total[...] = jnp.zeros_like(total)

    def patch_piece(first, last):
        def piece():
            @pl.loop(first, last)
            def _(group):
                patches[group] = make_patch(padded, group, pack)

        return piece

    rank = [0] + near_first(dims[0])
    places = sorted(offsets_of(dims), key=lambda o: ((o[1] != 0) + (o[2] != 0), rank.index(o[0])))

    def conv_piece(offsets):
        group = place(dims, (0, 1, 2), gather.position, offsets)

        def wait(core):
            for chunk in (1, 2):
                gather.arrived_block(core, chunk, group)

        def piece():
            if offsets != (0, 0, 0):
                by_core(core_index, wait)
            add_forward(total, patches[group], conv_all[group], group, pack)

        return piece

    quarter = GROUPS // 4
    early_pieces = [patch_piece(i * quarter, (i + 1) * quarter) for i in range(4)]
    weave(steps[0], early_pieces[:1])
    weave(steps[1], early_pieces[1:3])
    weave(steps[2], early_pieces[3:])
    for copy in own:
        copy.wait()
    conv_pieces = [conv_piece(offsets) for offsets in places]
    alone = sum(1 for offsets in places if not (offsets[1] or offsets[2]))
    weave(steps[3], [])
    weave(steps[4], conv_pieces[:alone])
    gate(0)
    saves = []

    def save(source, target):
        copy = pltpu.make_async_copy(source, target, save_sems.at[len(saves)])
        copy.start()
        saves.append(copy)

    save(patches, patches_out)
    gains_wide[...] = jnp.zeros_like(gains_wide)

    @pl.loop(0, gather.count)
    def _(shard):
        add_group(gains_wide, gain_all[shard, 0:16, :].astype(jnp.float32), shard, width // gather.count)

    gains[...] = gains_wide[0:8, 0:width]
    def front_piece():
        save(conv_all, conv_out)
        front_norm(pack_frames, total, gains, normed, normed_low, unit_front, inverse_front, front_slope)
        save(front_slope, front_slope_out)
        save(unit_front, unit_front_out)

    def project_piece():
        gate(3)
        project(normed_low, wide_all.at[:, 0 : 3 * width], projected)
        save(projected, projected_out)

    def attend_piece(first, last):
        return lambda: attend(projected, lengths, core_index, probs, attended, first, last)

    def middle_piece():
        gate(4)
        save(probs, probs_out)
        save(attended, attended_out)
        middle_norm(
            attended, wide_all.at[:, 3 * width : 4 * width], normed, gains, middle, middle_low, unit_middle,
            inverse_middle,
        )
        save(unit_middle, unit_middle_out)
        save(middle_low, middle_low_out)

    head_pairs = width // LANES
    weave(steps[5], conv_pieces[alone : 3 * alone])
    weave(
        steps[6],
        conv_pieces[3 * alone :]
        + [front_piece, project_piece]
        + [attend_piece(i, i + 2) for i in range(0, head_pairs, 2)],
    )
    weave(steps[7], [middle_piece])
    up = wide_all.at[:, 4 * width :]
    count = slope.shape[1] // TILE
    third = count // 3

    def up_piece(first):
        def piece():
            if first == 0:
                gate(5)
                save(wide_all, wide_out)
            feed_up(middle_low, up, slope, activated, first, first + third)

        return piece

    arrivals = [(i, j) for j in [0] + near_first(dims[1]) for i in rank]
    down_tasks = steps[8]
    near = len(rank)

    def strip_piece(offsets):
        gids = [place(dims, (0, 1, 2), gather.position, offsets + (k,)) for k in range(2)]

        def wait(core):
            for k, gid in enumerate(gids):
                if offsets + (k,) != (0, 0, 0):
                    gather.arrived_block(core, 6, gid)

        by_core(core_index, wait)
        rows = pl.ds(pl.multiple_of(gids[0] // 2 * STRIP, STRIP), STRIP)
        save(down_all.at[rows], down_out.at[rows])
        middle[...] += dot(activated[:, rows], down_all[rows, :])

    weave([tasks[:near] for tasks in down_tasks], [up_piece(i) for i in range(0, count, third)])
    save(slope, slope_out)
    save(activated, activated_out)
    for copy in moves[2:]:
        copy.wait()
    gain_grads[...] = jnp.zeros_like(gain_grads)
    for number, offsets in enumerate(arrivals):
        if number >= near:
            weave([tasks[number : number + 1] for tasks in down_tasks], [])
        strip_piece(offsets)
    last_norm(middle, gains, pack_cotangent, output, grad_final, gain_grads)
    last = to_partner(output.at[there], both_output.at[core_index], 2)
    last.start()
    stay = pltpu.make_async_copy(output.at[here], both_output.at[core_index], local_sems.at[2])
    stay.start()
    by_core(core_index, gather.finish)
    for copy in saves + [stay, last]:
        copy.wait()


def fused_forward(frames, cotangent, lengths, shards_in, chunks, dp):
    dims = dp_factors(dp)
    n = len(chunks)
    conv_shard, qkv_shard, out_shard, up_shard, down_shard = shards_in[:5]
    pack, width = 2 * frames.shape[1], frames.shape[2]
    inner = down_shard.shape[0] * dp
    heads = width // HEAD_DIM
    low, full = jnp.bfloat16, jnp.float32
    shape = jax.ShapeDtypeStruct
    vmem = pl.BlockSpec(memory_space=pltpu.VMEM)
    any_ = pl.BlockSpec(memory_space=pl.ANY)
    conv_shape = (dp,) + conv_shard.shape
    wide_shape = (width, 4 * width + up_shard.shape[1])
    down_shape = (inner, width)
    kept = [
        shape((GROUPS, pack + FINE, 384), low),
        shape((pack, width), full),
        shape((pack, width), full),
        shape((pack, 3 * width), low),
        shape((heads, pack, pack), full),
        shape((pack, width), low),
        shape((pack, width), full),
        shape((pack, width), low),
        shape((pack, inner), low),
        shape((pack, inner), low),
    ]
    saved = [
        shape(frames.shape, low),
        shape((8, width), full),
        shape((pack, width), full),
        shape((pack, LANES), full),
        shape((pack, LANES), full),
        shape((8, width), full),
    ]
    return pl.pallas_call(
        functools.partial(fused_forward_kernel, dims, chunks),
        out_shape=[shape(conv_shape, low), shape(wide_shape, low), shape(down_shape, low)] + kept + saved,
        in_specs=[pl.BlockSpec(memory_space=pltpu.SMEM)] + [any_] * 7 + [vmem] * 3,
        out_specs=[any_] * 13 + [vmem] * len(saved),
        scratch_shapes=[pltpu.VMEM(one.shape, one.dtype) for one in kept]
        + [
            pltpu.VMEM((2 * GAIN_ROWS, LANES), low),
            pltpu.VMEM(conv_shape, low),
            pltpu.VMEM(wide_shape, low),
            pltpu.VMEM(down_shape, low),
            pltpu.VMEM((dp, 2 * GAIN_ROWS, LANES), low),
            pltpu.VMEM((pack, width), low),
            pltpu.VMEM((pack, width), low),
            pltpu.VMEM((pack, width), low),
            pltpu.VMEM((pack + KERNEL, width + LANES), full),
            pltpu.VMEM((pack, width + LANES), full),
            pltpu.VMEM((16, width + LANES), full),
            pltpu.VMEM((pack, width), full),
            pltpu.VMEM((pack, width), low),
            pltpu.VMEM((pack, width), full),
            pltpu.SemaphoreType.DMA((n, dp)),
            pltpu.SemaphoreType.DMA((n, dp)),
            pltpu.SemaphoreType.DMA((n, dp)),
            pltpu.SemaphoreType.DMA((n, dp)),
            pltpu.SemaphoreType.DMA((n, 2)),
            pltpu.SemaphoreType.DMA((3,)),
            pltpu.SemaphoreType.DMA((20,)),
            pltpu.SemaphoreType.DMA((2, 3)),
        ],
        compiler_params=pltpu.CompilerParams(
            collective_id=2, has_side_effects=True, vmem_limit_bytes=60 << 20
        ),
    )(lengths, frames, cotangent, *shards_in)


STRIP = 384
DOWN, UP, OUT, QKV, GAIN, CONV = range(6)
CONV_PARTS = 2
SCATTER_ORDERS = (FIRST, FIRST, FIRST, FIRST, FIRST) + (FIRST,) * CONV_PARTS


class Scatter:
    def __init__(self, dims, heights, stages, pairs, hops, outs, conv_pair, sems):
        self.dims, self.heights = dims, heights
        self.stages, self.pairs, self.hops, self.outs, self.conv_pair = stages, pairs, hops, outs, conv_pair
        self.waited = set()
        self.pair_recv, self.hop_send, self.hop_recv, self.last_send, self.last_recv = sems
        self.position = position_of(dims)
        self.count = dims[0] * dims[1] * dims[2]

    def block(self, ref, chunk, gid):
        if len(ref.shape) == 3:
            return ref.at[gid]
        height = self.heights[chunk]
        return ref.at[pl.ds(pl.multiple_of(gid * height, 16), height)]

    def sizes(self, core, chunk):
        return [self.dims[axis] for axis in SCATTER_ORDERS[chunk][core]]

    def slot(self, core, chunk, level, offsets, distance):
        index = distance - 1
        for i in range(level):
            index = index * self.sizes(core, chunk)[i] + offsets[i]
        return index

    def semaphore(self, core, chunk, level, index):
        sizes = self.sizes(core, chunk)
        return (1, sizes[0], sizes[0] * sizes[1])[level] + index - 1

    def combine(self, core, chunk, offsets, target):
        order = SCATTER_ORDERS[chunk][core]
        gid = place(self.dims, order, self.position, offsets)
        own, pair = self.block(self.stages[chunk], chunk, gid), self.block(self.pairs[chunk], chunk, gid)
        natural = (core,) + tuple(offset for _, offset in sorted(zip(order, offsets)))
        if chunk >= CONV and natural not in self.waited:
            self.waited.add(natural)
            whole = self.conv_pair.at[gid]
            pltpu.make_async_copy(whole, whole, self.pair_recv.at[CONV, gid]).wait()
        terms = [own, pair]
        for level in (2, 1, 0):
            if offsets[level]:
                break
            for distance in range(1, self.sizes(core, chunk)[level]):
                index = self.slot(core, chunk, level, offsets, distance)
                ref = self.hops[level][chunk].at[index]
                number = self.semaphore(core, chunk, level, index)
                pltpu.make_async_copy(ref, ref, self.hop_recv.at[chunk, number]).wait()
                terms.append(ref)

        tall = 48 if own.shape[0] % 48 == 0 else 16

        @pl.loop(0, own.shape[0] // tall)
        def _(tile):
            rows = pl.ds(pl.multiple_of(tile * tall, 16), tall)
            if target is None and len(terms) == 2:
                own[rows, :] = own[rows, :] + pair[rows, :]
                return
            total = terms[0][rows, :].astype(jnp.float32)
            for term in terms[1:]:
                total = total + term[rows, :].astype(jnp.float32)
            if target is None:
                own[rows, :] = total.astype(own.dtype)
            else:
                target[rows, :] = total

        return own

    def send(self, core, chunk, offsets):
        level = max(i for i in range(3) if offsets[i])
        own = self.combine(core, chunk, offsets, None)
        index = self.slot(core, chunk, level, offsets, offsets[level])
        number = self.semaphore(core, chunk, level, index)
        pltpu.make_async_remote_copy(
            src_ref=own,
            dst_ref=self.hops[level][chunk].at[index],
            send_sem=self.hop_send.at[chunk, number],
            recv_sem=self.hop_recv.at[chunk, number],
            device_id={"dp": place(self.dims, (SCATTER_ORDERS[chunk][core][level],), self.position, (offsets[level],))},
            device_id_type=MESH,
        ).start()

    def half(self, chunk, core):
        out = self.outs[chunk]
        lanes = out.shape[1] // 2
        return out.at[:, pl.ds(core * lanes, lanes)]

    def final(self, core, chunk):
        half = self.half(chunk, core)
        self.combine(core, chunk, (0, 0, 0), half)
        pltpu.make_async_remote_copy(
            src_ref=half,
            dst_ref=half,
            send_sem=self.last_send.at[chunk],
            recv_sem=self.last_recv.at[chunk],
            device_id={"seq": 1 - core},
            device_id_type=MESH,
        ).start()

    def tasks(self, core, chunk, stage):
        sizes = self.sizes(core, chunk)
        if stage == 3:
            return [functools.partial(self.final, core, chunk)]
        if stage == 2:
            places = [(i, 0, 0) for i in near_first(sizes[0])[::-1]]
        elif stage == 1:
            places = [(i, d, 0) for d in near_first(sizes[1]) for i in near_first(sizes[0])[::-1] + [0]]
        else:
            places = [
                (i, j, d)
                for d in near_first(sizes[2])
                for j in near_first(sizes[1]) + [0]
                for i in near_first(sizes[0])[::-1] + [0]
            ]
        return [functools.partial(self.send, core, chunk, offsets) for offsets in places]

    def finish(self, core):
        for chunk in range(len(self.outs)):
            half = self.half(chunk, 1 - core)
            pltpu.make_async_copy(half, half, self.last_recv.at[chunk]).wait()
            pltpu.make_async_copy(half, half, self.last_send.at[chunk]).wait()

            @pl.loop(0, self.count - 1)
            def _(number, chunk=chunk):
                ref = self.block(self.stages[chunk], chunk, 0)
                pltpu.make_async_copy(ref, ref, self.hop_send.at[chunk, number]).wait()


class Stream:
    def __init__(self, buffer, sems):
        self.buffer, self.sems = buffer, sems

    def start(self, source, number):
        pltpu.make_async_copy(source, self.buffer.at[number % 2], self.sems.at[number % 2]).start()

    def take(self, number):
        ref = self.buffer.at[number % 2]
        pltpu.make_async_copy(ref, ref, self.sems.at[number % 2]).wait()
        return ref


class Outbox:
    def __init__(self, buffer, sems):
        self.buffer, self.sems, self.busy, self.number = buffer, sems, [None, None], 0

    def free(self):
        slot = self.number % 2
        self.number += 1
        if self.busy[slot] is not None:
            self.busy[slot].wait_send()
            self.busy[slot] = None
        return slot, self.buffer.at[slot]

    def send(self, slot, source, target, recv_sem):
        copy = pltpu.make_async_remote_copy(
            src_ref=source,
            dst_ref=target,
            send_sem=self.sems.at[slot],
            recv_sem=recv_sem,
            device_id={"seq": 1 - lax.axis_index("seq")},
            device_id_type=MESH,
        )
        copy.start()
        self.busy[slot] = copy

    def drain(self):
        for copy in self.busy:
            if copy is not None:
                copy.wait_send()
        self.busy = [None, None]


def spread_grads(padded, group, pack):
    def later(values, amount):
        return pltpu.roll(values, amount, 0)

    one = take_group(padded, slice(0, pack + FINE), group, 48)
    two = one + pltpu.roll(later(one, 1), 48, 1)
    low, high = double_96(two, later(two, 2))
    near = jnp.concatenate(double_192(low, high, later(low, 4), later(high, 4)), axis=1)
    return jnp.concatenate([near, later(near, 8)], axis=1).astype(jnp.bfloat16)


def add_backward(total, tall, spread, weight, group, pack):
    edge = KERNEL // 2 - FINE
    tall[edge : edge + pack + FINE] = dot(spread, weight, (1, 1))

    def shift(base, moved, amount):
        return base[amount * FINE :] + moved[: base.shape[0] - amount * FINE]

    tiles = [tall[:, i * LANES : (i + 1) * LANES] for i in range(3)]
    add_group(total, fold_lanes(tiles, shift), group, 48)


def fused_backward_kernel(
    dims,
    weight, wide, down, patches, probs, grad_in, activated_in, middle_low_in, slope_in, unit_middle_in, attended_in,
    projected_in, unit_front_in, front_slope_in,
    gains, inverse_front, inverse_middle, last_gain_grad,
    conv_out, qkv_out, out_out, up_out, down_out, gain_out, both_grads, *scratch,
):
    arrays = CONV + 1
    n = CONV + CONV_PARTS
    stages, pairs = scratch[:arrays], scratch[arrays : 2 * arrays]
    hops = [scratch[2 * arrays + level * n : 2 * arrays + (level + 1) * n] for level in range(3)]
    conv_rows = [pl.ds(i * (384 // CONV_PARTS), 384 // CONV_PARTS) for i in range(CONV_PARTS)]

    def in_parts(refs):
        return list(refs[:CONV]) + [refs[CONV].at[:, rows] for rows in conv_rows]

    outs = [down_out, up_out, out_out, qkv_out, gain_out] + [conv_out.at[rows] for rows in conv_rows]
    (
        grad, activated, middle_low, slope, unit_middle, attended, projected, unit_front, front_slope,
        turned, grad_attended, grad_projected, padded, spread, tall, total, gain_grads, gain_wide,
        gain_box, tall_box, wide_box, tall_tiles, wide_tiles, prob_tiles, patch_tiles,
        pair_recv, hop_send, hop_recv, last_send, last_recv, box_sems, tile_sems, load_sems, input_sems,
    ) = scratch[2 * arrays + 3 * n :]
    core_index = lax.axis_index("seq")
    other = 1 - core_index
    pack, width = grad.shape
    inner = activated.shape[1]
    low = jnp.bfloat16
    heights = [out.shape[0] for out in outs]
    scatter = Scatter(
        dims, heights, in_parts(stages), in_parts(pairs), hops, outs, pairs[CONV],
        (pair_recv, hop_send, hop_recv, last_send, last_recv),
    )
    tall_stream, wide_stream = Stream(tall_tiles, tile_sems.at[0]), Stream(wide_tiles, tile_sems.at[1])
    prob_stream, patch_stream = Stream(prob_tiles, tile_sems.at[2]), Stream(patch_tiles, tile_sems.at[3])
    tall_out, wide_out_box = Outbox(tall_box, box_sems.at[0]), Outbox(wide_box, box_sems.at[1])

    def strip(index, base=0):
        return pl.ds(pl.multiple_of(base + index * STRIP, LANES), STRIP)

    up_base, out_base = 4 * width, 3 * width
    sources = (grad_in, activated_in, middle_low_in, slope_in, unit_middle_in, attended_in, projected_in,
               unit_front_in, front_slope_in)
    targets = (grad, activated, middle_low, slope, unit_middle, attended, projected, unit_front, front_slope)
    loads = [
        pltpu.make_async_copy(source, target, input_sems.at[i])
        for i, (source, target) in enumerate(zip(sources, targets))
    ]
    for load in loads:
        load.start()
    up_half, qkv_half, out_half = inner // 2, 3 * width // 2, width // 2
    up_strips, qkv_strips = up_half // STRIP, qkv_half // STRIP
    down_strips = inner // STRIP

    def ordered(index, strips):
        return (core_index if index % 2 else other) * strips + index // 2

    def up_start(index):
        which = ordered(index, up_strips)
        wide_stream.start(wide.at[:, strip(which, up_base)], index)
        tall_stream.start(down.at[strip(which)], index)

    up_start(0)
    greet(dims, scatter.position, core_index)

    def all_tasks(*wanted):
        return [[task for chunk, stage in wanted for task in scatter.tasks(core, chunk, stage)] for core in range(2)]

    def step(number):
        wanted = [(number - stage, stage) for stage in (3, 2, 1, 0) if 0 < number - stage < n]
        if number < 3:
            wanted.insert(0, (DOWN, number + 1))
        return all_tasks(*wanted)

    def gate(chunk, count, height, lanes):
        for index in range(count):
            ref = pairs[chunk].at[pl.ds(0, height), pl.ds(0, lanes)]
            pltpu.make_async_copy(ref, ref, pair_recv.at[chunk, index]).wait()

    own_lanes = pl.ds(pl.multiple_of(core_index * out_half, LANES), out_half)
    other_lanes = pl.ds(pl.multiple_of(other * out_half, LANES), out_half)
    loads[0].wait()
    loads[1].wait()
    grad_feed = grad[...].astype(low)
    spread[0:pack, :] = grad_feed
    first = [(i, j, 0) for j in near_first(dims[1]) + [0] for i in near_first(dims[0])[::-1] + [0]]
    strips = [place(dims, (0, 1, 2), scatter.position, offsets) // 2 for offsets in first]
    sends = [scatter.tasks(core, DOWN, 0) for core in range(2)]
    ahead = len(strips) // 2
    for index in range(down_strips + 1):
        if index < down_strips:
            slot, box = tall_out.free()
            rows = strip(strips[index])
            box[...] = dot(activated[:, rows], spread[0:pack, :], (0, 0)).astype(low)
            tall_out.send(slot, box.at[:, other_lanes], pairs[DOWN].at[rows], pair_recv.at[DOWN, index])
            stages[DOWN][rows, :] = box[:, own_lanes]
        if index > 0:
            came = pairs[DOWN].at[strip(strips[index - 1])]
            pltpu.make_async_copy(came, came, pair_recv.at[DOWN, index - 1]).wait()

            def early(core, index=index - 1):
                if core == 0:
                    sends[0][index]()
                elif index < ahead:
                    sends[1][index]()
                    sends[1][index + ahead]()

            by_core(core_index, early)
    loads[2].wait()
    loads[3].wait()
    turned[...] = jnp.transpose(middle_low[...].astype(jnp.float32)).astype(low)

    def give(chunk, index, values):
        lanes = pl.ds(index // 2 * STRIP, STRIP)
        if index % 2 == 0:
            slot, box = wide_out_box.free()
            box[...] = values
            wide_out_box.send(slot, box, pairs[chunk].at[:, lanes], pair_recv.at[chunk, index // 2])
        else:
            stages[chunk][:, lanes] = values

    def up_piece(index):
        def piece():
            if index + 1 < 2 * up_strips:
                up_start(index + 1)
            up_tile, down_tile = wide_stream.take(index), tall_stream.take(index)
            lanes = strip(ordered(index, up_strips))
            slopes = slope[:, lanes].astype(jnp.float32)
            grad_hidden = (dot(spread[0:pack, :], down_tile[...], (1, 1)) * slopes).astype(low)
            give(UP, index, dot(turned[...], grad_hidden).astype(low))
            grad[...] += dot(grad_hidden, up_tile[...], (1, 1))

        return piece

    weave(step(0), [up_piece(i) for i in range(2 * up_strips)])

    def prob_start(pair):
        prob_stream.start(probs.at[pl.ds(2 * pair, 2)], pair)

    for index in range(2):
        tall_stream.start(wide.at[strip(index), out_base : out_base + width], index)
    prob_start(0)
    gain_grads[...] = last_gain_grad[...]

    def middle_piece():
        for load in loads[4:]:
            load.wait()
        gate(UP, up_strips, width, STRIP)
        norm_back_rows(grad, unit_middle, inverse_middle, gains, 1, gain_grads)

    def out_piece():
        grad_branch = grad[...].astype(low)
        spread[0:pack, :] = grad_branch
        turned[...] = jnp.transpose(attended[...].astype(jnp.float32)).astype(low)
        for index, half in enumerate((other, core_index)):
            give(OUT, index, dot(turned[...], spread[0:pack, strip(half)]).astype(low))
            tile = tall_stream.take(index)
            lanes = slice(index * STRIP, (index + 1) * STRIP)
            grad_attended[:, lanes] = dot(grad_branch, tile[...], (1, 1)).astype(low)

    pairs_of_heads = width // LANES

    def attend_piece(pair):
        def piece():
            if pair + 1 < pairs_of_heads:
                prob_start(pair + 1)
            attend_back_pair(projected, grad_attended, prob_stream.take(pair), grad_projected, pair)

        return piece

    def qkv_start(index):
        wide_stream.start(wide.at[:, strip(ordered(index, qkv_strips))], index)

    def qkv_piece(index):
        def piece():
            if index == 0:
                qkv_start(0)
                turned[...] = jnp.transpose(unit_front[...] * gains[0:1, :]).astype(low)
            if index + 1 < 2 * qkv_strips:
                qkv_start(index + 1)
            tile = wide_stream.take(index)
            values = grad_projected[:, strip(ordered(index, qkv_strips))]
            give(QKV, index, dot(turned[...], values).astype(low))
            grad[...] += dot(values, tile[...], (1, 1))

        return piece

    places = sorted(offsets_of(dims), key=lambda o: (o[1] == 0) + (o[2] == 0))
    groups = [place(dims, (0, 1, 2), scatter.position, offsets) for offsets in places]

    def conv_start(number):
        tall_stream.start(weight.at[groups[number]], number)
        patch_stream.start(patches.at[groups[number]], number)

    def front_piece():
        conv_start(0)
        norm_back_rows(grad, unit_front, inverse_front, gains, 0, gain_grads)
        padded[...] = jnp.zeros_like(padded)
        tall[...] = jnp.zeros_like(tall)
        total[...] = jnp.zeros_like(total)
        total[:, :width] = grad[...]

        def body(rows):
            padded[rows, 0:width] = (grad[rows, :] * front_slope[rows, :]).astype(low).astype(jnp.float32)

        row_tiles(pack, body)
        gain_wide[...] = jnp.zeros_like(gain_wide)
        gain_wide[0:8, 0:width] = gain_grads[...]

        @pl.loop(0, scatter.count)
        def _(shard):
            one = take_group(gain_wide, slice(0, 16), shard, width // scatter.count)
            gain_box[shard] = one.astype(low)
            stages[GAIN][shard] = one.astype(low)

        gain_copy.start()

    gain_copy = pltpu.make_async_remote_copy(
        src_ref=gain_box,
        dst_ref=pairs[GAIN],
        send_sem=load_sems.at[1],
        recv_sem=load_sems.at[2],
        device_id={"seq": other},
        device_id_type=MESH,
    )

    def conv_piece(number):
        def piece():
            if number + 1 < len(groups):
                conv_start(number + 1)
            group = groups[number]
            tile, patch = tall_stream.take(number), patch_stream.take(number)
            spread[...] = spread_grads(padded, group, pack)
            slot, box = tall_out.free()
            box[...] = dot(patch[...], spread[...], (0, 0)).astype(low)
            tall_out.send(slot, box.at[:, other_lanes], pairs[CONV].at[group], pair_recv.at[CONV, group])
            stages[CONV][group] = box[:, own_lanes]
            add_backward(total, tall, spread[...], tile[...], group, pack)

        return piece

    middle_piece()
    weave(
        step(1),
        [out_piece]
        + [attend_piece(i) for i in range(pairs_of_heads)]
        + [qkv_piece(i) for i in range(2 * qkv_strips)]
        + [front_piece],
    )
    pieces = [conv_piece(i) for i in range(len(groups))]
    gate(OUT, 1, width, STRIP)
    weave(step(2), pieces[:5])
    gate(QKV, qkv_strips, width, STRIP)
    weave(step(3), pieces[5:11])
    gain_copy.wait()
    weave(step(4), pieces[11:])
    half = pack // 2
    here = pl.ds(pl.multiple_of(core_index * half, half), half)
    there = pl.ds(pl.multiple_of(other * half, half), half)
    frames_copy = pltpu.make_async_remote_copy(
        src_ref=total.at[there, pl.ds(0, width)],
        dst_ref=both_grads.at[core_index],
        send_sem=load_sems.at[3],
        recv_sem=load_sems.at[4],
        device_id={"seq": other},
        device_id_type=MESH,
    )
    frames_copy.start()
    both_grads[core_index] = total[here, 0:width]
    for number in range(5, n + 3):
        weave(step(number), [])
    by_core(core_index, scatter.finish)
    tall_out.drain()
    wide_out_box.drain()
    frames_copy.wait()


def fused_backward(weight, wide, down, patches, gains, kept, dp):
    dims = dp_factors(dp)
    (front_slope, grad_final, unit_front, inverse_front, projected, probs, attended, unit_middle,
     inverse_middle, middle_low, slope, activated, gain_grads) = kept
    pack, width = front_slope.shape
    inner = activated.shape[1]
    low, full = jnp.bfloat16, jnp.float32
    shape = jax.ShapeDtypeStruct
    vmem = pl.BlockSpec(memory_space=pltpu.VMEM)
    any_ = pl.BlockSpec(memory_space=pl.ANY)
    rows = width // dp
    flat = [(inner, width // 2), (width, inner // 2), (width, width // 2), (width, 3 * width // 2)]
    wholes = flat + [(dp, 16, LANES), (dp, 384, 384)]
    blocks = [(s[0] // dp, s[1]) for s in flat] + [(16, LANES)] + [(384 // CONV_PARTS, 384)] * CONV_PARTS
    n = len(blocks)
    scratch = [pltpu.VMEM(s, low) for s in wholes] * 2
    for level in range(3):
        for block, orders in zip(blocks, SCATTER_ORDERS):
            slots = max(hop_slots(dims, order)[level] for order in orders)
            scratch.append(pltpu.VMEM((slots,) + block, low))
    tall_rows = pack + FINE
    given = (grad_final, activated, middle_low, slope, unit_middle, attended, projected, unit_front, front_slope)
    scratch += [pltpu.VMEM(one.shape, one.dtype) for one in given]
    scratch += [
        pltpu.VMEM((width, pack), low),
        pltpu.VMEM((pack, width), low),
        pltpu.VMEM((pack, 3 * width), low),
        pltpu.VMEM((tall_rows, width + LANES), full),
        pltpu.VMEM((tall_rows, width), low),
        pltpu.VMEM((pack + KERNEL - FINE, 384), full),
        pltpu.VMEM((pack, width + LANES), full),
        pltpu.VMEM((8, width), full),
        pltpu.VMEM((16, width + LANES), full),
        pltpu.VMEM((dp, 16, LANES), low),
        pltpu.VMEM((2, STRIP, width), low),
        pltpu.VMEM((2, width, STRIP), low),
        pltpu.VMEM((2, STRIP, width), low),
        pltpu.VMEM((2, width, STRIP), low),
        pltpu.VMEM((2, 2, pack, pack), full),
        pltpu.VMEM((2, tall_rows, 384), low),
        pltpu.SemaphoreType.DMA((n, dp)),
        pltpu.SemaphoreType.DMA((n, dp)),
        pltpu.SemaphoreType.DMA((n, dp)),
        pltpu.SemaphoreType.DMA((n,)),
        pltpu.SemaphoreType.DMA((n,)),
        pltpu.SemaphoreType.DMA((2, 2)),
        pltpu.SemaphoreType.DMA((4, 2)),
        pltpu.SemaphoreType.DMA((5,)),
        pltpu.SemaphoreType.DMA((len(given),)),
    ]
    return pl.pallas_call(
        functools.partial(fused_backward_kernel, dims),
        out_shape=[
            shape((384, width), full),
            shape((rows, 3 * width), full),
            shape((rows, width), full),
            shape((rows, inner), full),
            shape((inner // dp, width), full),
            shape((16, 2 * LANES), full),
            shape((2, pack // 2, width), full),
        ],
        in_specs=[any_] * (5 + len(given)) + [vmem] * 4,
        out_specs=[vmem] * 7,
        scratch_shapes=scratch,
        compiler_params=pltpu.CompilerParams(
            collective_id=3, has_side_effects=True, vmem_limit_bytes=63 << 20
        ),
    )(weight, wide, down, patches, probs, *given, gains, inverse_front, inverse_middle, gain_grads)


GAIN_ROWS = 16


def chunks_of(conv_rows, conv_lanes, wide_rows, width, down_rows):
    both = range(2)
    quarter, half = conv_rows // 4, width // 2
    conv = [
        [(0, ((2 * part + core) * quarter, quarter), (0, conv_lanes)) for core in both] for part in both
    ]
    wide = [
        [(1, (0, wide_rows), ((2 * part + core) * 2 * width, 2 * width)) for core in both] for part in both
    ]
    down = [[(2, (0, down_rows), (core * half, half)) for core in both]]
    gain = [[(3, (core * GAIN_ROWS, GAIN_ROWS), (0, LANES)) for core in both]]
    return gain, conv, wide, down


def gather_chunks(chunks):
    return [
        (FIRST,) + tuple((array, array, rows, lanes[0], lanes[0], lanes[1]) for array, rows, lanes in chunk)
        for chunk in chunks
    ]


def fused_chunks(conv_rows, width, wide_rows, inner, down_rows):
    quarter = conv_rows // 4
    chunks = [(FIRST,) + tuple((5, 3, (core * GAIN_ROWS, GAIN_ROWS), 0, 0, LANES) for core in range(2))]
    for part, orders in enumerate((FIRST, FIRST)):
        chunks.append(
            (orders,) + tuple((0, 0, ((2 * part + core) * quarter, quarter), 0, 0, width) for core in range(2))
        )
    begin = 0
    for source, lanes, orders in ((1, 3 * width, FIRST), (2, width, FIRST), (3, inner, SECOND)):
        half = lanes // 2
        chunks.append(
            (orders,)
            + tuple((source, 1, (0, wide_rows), core * half, begin + core * half, half) for core in range(2))
        )
        begin += lanes
    half = width // 2
    chunks.append(
        (FIRST,) + tuple((4, 2, (0, down_rows), core * half, core * half, half) for core in range(2))
    )
    return chunks


def shards(
    frames,
    clip_lengths,
    conv_weight,
    front_gain,
    qkv_weight,
    out_weight,
    middle_gain,
    up_weight,
    down_weight,
    final_gain,
    cotangent,
):
    dp = lax.axis_size("dp")
    low = jnp.bfloat16
    width = frames.shape[2]
    columns = conv_weight.shape[2]
    group_width = conv_weight.shape[1]
    gain_width = front_gain.shape[0]
    conv_shard = (
        conv_weight.reshape(COARSE, FINE, group_width, columns)
        .transpose(0, 2, 1, 3)
        .reshape(COARSE * group_width, FINE * columns)
    )
    split = group_width // columns
    if split == 1:
        shards_in = (conv_shard, qkv_weight, out_weight, up_weight, down_weight) + tuple(
            gain[None] for gain in (front_gain, middle_gain, final_gain)
        )
        chunks = fused_chunks(conv_shard.shape[0], width, qkv_weight.shape[0], up_weight.shape[1], down_weight.shape[0])
        (weight, wide, down, patches, front_slope, unit_front, projected, probs, attended, unit_middle, middle_low,
         slope, activated, outputs, gains, grad_final, inverse_front, inverse_middle, last_gain_grad) = fused_forward(
            frames, cotangent, clip_lengths[:, 0], shards_in, chunks, dp
        )
        kept = (front_slope, grad_final, unit_front, inverse_front, projected, probs, attended, unit_middle,
                inverse_middle, middle_low, slope, activated, last_gain_grad)
    else:
        wide_shard = jnp.concatenate([qkv_weight, out_weight, up_weight], axis=1)
        gain_shard = jnp.pad(
            jnp.stack([front_gain, middle_gain, final_gain]),
            ((0, 2 * GAIN_ROWS - 3), (0, LANES - gain_width)),
        )
        parts = (conv_shard, wide_shard, down_weight, gain_shard)
        gain_chunk, conv_chunks, wide_chunks, down_chunk = chunks_of(
            *conv_shard.shape, wide_shard.shape[0], width, down_weight.shape[0]
        )
        chunks = gather_chunks(gain_chunk + conv_chunks + wide_chunks + down_chunk)
        conv_all, wide_all, down_all, gain_all = all_gather(parts, chunks, dp)
        weight = (
            conv_all.reshape(GROUPS, split, COARSE * group_width, FINE, columns)
            .transpose(0, 2, 3, 1, 4)
            .reshape(GROUPS, COARSE * group_width, FINE * group_width)
        )
        wide = wide_all.reshape(width, wide_shard.shape[1])
        down = down_all.reshape(-1, width)
        gains = gain_all[:, :3, :gain_width].transpose(1, 0, 2).reshape(3, width).astype(jnp.float32)
        gains = jnp.pad(gains, ((0, 5), (0, 0)))
        both = lax.all_to_all(
            jnp.stack([frames, cotangent], axis=1), "seq", split_axis=0, concat_axis=2, tiled=True
        )
        pack_frames, pack_cotangent = both[0, 0], both[0, 1]
        lengths = lax.dynamic_index_in_dim(clip_lengths[:, 0], lax.axis_index("seq"), 0)
        convolved, patches = conv_forward(pack_frames, weight)
        output, *kept = middle_forward(
            pack_frames, convolved, lengths, gains, wide, down, pack_cotangent
        )
        outputs = lax.all_to_all(output[None], "seq", split_axis=1, concat_axis=0, tiled=True)

    if split == 1:
        conv_sum, qkv_sum, out_sum, up_sum, down_sum, gain_sum, frame_grads = fused_backward(
            weight, wide, down, patches, gains, kept, dp
        )
    else:
        grad_mixed, grad_convolved, wide_grad, down_grad, gain_grads = middle_backward(
            gains, wide, down, kept
        )
        frame_grad, conv_grad = conv_backward(grad_convolved, grad_mixed, weight, patches)

        conv_blocks = (
            conv_grad.reshape(GROUPS, COARSE * group_width, FINE, split, columns)
            .transpose(0, 3, 1, 2, 4)
            .reshape((dp,) + conv_shard.shape)
        )
        gain_blocks = jnp.pad(
            gain_grads[:3].astype(low).reshape(3, dp, gain_width).transpose(1, 0, 2),
            ((0, 0), (0, 2 * GAIN_ROWS - 3), (0, LANES - gain_width)),
        )
        conv_sum, wide_sum, down_sum, gain_sum = reduce_scatter(
            (
                conv_blocks,
                wide_grad.reshape((dp,) + wide_shard.shape),
                down_grad.reshape((dp,) + down_weight.shape),
                gain_blocks,
            ),
            gain_chunk + down_chunk + wide_chunks[::-1] + conv_chunks,
            dp,
        )
        qkv_sum, out_sum, up_sum = (
            wide_sum[:, : 3 * width],
            wide_sum[:, 3 * width : 4 * width],
            wide_sum[:, 4 * width :],
        )
        frame_grads = lax.all_to_all(frame_grad[None], "seq", split_axis=1, concat_axis=0, tiled=True)

    conv_sum = (
        conv_sum.reshape(COARSE, group_width, FINE, columns)
        .transpose(1, 3, 0, 2)
        .reshape(group_width, columns, KERNEL)
        .transpose(2, 0, 1)
    )
    return (
        outputs,
        frame_grads,
        conv_sum,
        gain_sum[0, :gain_width],
        qkv_sum,
        out_sum,
        gain_sum[1, :gain_width],
        up_sum,
        down_sum,
        gain_sum[2, :gain_width],
    )


def solution(mesh):
    frames_spec = P(None, ("dp", "seq"), None)
    row, matrix, columns = P("dp"), P("dp", None), P(None, None, "dp")
    return jax.shard_map(
        shards,
        mesh=mesh,
        in_specs=(
            frames_spec,
            P(None, "dp", None),
            columns,
            row,
            matrix,
            matrix,
            row,
            matrix,
            matrix,
            row,
            frames_spec,
        ),
        out_specs=(
            frames_spec,
            frames_spec,
            columns,
            row,
            matrix,
            matrix,
            row,
            matrix,
            matrix,
            row,
        ),
        check_vma=False,
    )
```
